32 devices in a mesh: rep: 4 (over x, core), own: 8 (over z, y).
Axes of the slice: x: 2, y: 2, z: 4, core: 2. Of those that a mesh axis runs over, the one named last changes fastest.
Arguments:
- layer_input: float32 [8192, 1024], P(('rep', 'own')), may hold values from -6 to 6
- output_grad: float32 [8192, 1024], P(('rep', 'own')), may hold values from -12 to 12
- lengths: int32 [32, 3], P(('rep', 'own')), may hold values from 1 to 224, 256 in all within a row
- attention_gain: float32 [1024], replicated, may hold values from 0.25 to 1.75
- feed_gain: float32 [1024], replicated, may hold values from 0.25 to 1.75
- query_gain: float32 [128], replicated, may hold values from 0.25 to 1.75
- key_gain: float32 [128], replicated, may hold values from 0.25 to 1.75
- query_weight: float32 [1024, 2048], P('own'), may hold values from -0.1875 to 0.1875
- key_weight: float32 [1024, 1024], P('own'), may hold values from -0.1875 to 0.1875
- value_weight: float32 [1024, 1024], P('own'), may hold values from -0.1875 to 0.1875
- out_weight: float32 [2048, 1024], P('own'), may hold values from -0.75 to 0.75
- gate_weight: float32 [1024, 3072], P('own'), may hold values from -0.1875 to 0.1875
- up_weight: float32 [1024, 3072], P('own'), may hold values from -0.1875 to 0.1875
- down_weight: float32 [3072, 1024], P('own'), may hold values from -0.109375 to 0.109375
- query_moment: float32 [1024, 2048], P('own'), may hold values from -320 to 320
- key_moment: float32 [1024, 1024], P('own'), may hold values from -320 to 320
- value_moment: float32 [1024, 1024], P('own'), may hold values from -320 to 320
- out_moment: float32 [2048, 1024], P('own'), may hold values from -112 to 112
- gate_moment: float32 [1024, 3072], P('own'), may hold values from -224 to 224
- up_moment: float32 [1024, 3072], P('own'), may hold values from -224 to 224
- down_moment: float32 [3072, 1024], P('own'), may hold values from -448 to 448
Outputs:
- block_output: float32 [8192, 1024], P(('rep', 'own'))
- input_grad: float32 [8192, 1024], P(('rep', 'own'))
- norm_grads: float32 [2, 1024], replicated
- head_grads: float32 [2, 128], replicated
- query_updated: float32 [1024, 2048], P('own')
- key_updated: float32 [1024, 1024], P('own')
- value_updated: float32 [1024, 1024], P('own')
- out_updated: float32 [2048, 1024], P('own')
- gate_updated: float32 [1024, 3072], P('own')
- up_updated: float32 [1024, 3072], P('own')
- down_updated: float32 [3072, 1024], P('own')
- query_momentum: float32 [1024, 2048], P('own')
- key_momentum: float32 [1024, 1024], P('own')
- value_momentum: float32 [1024, 1024], P('own')
- out_momentum: float32 [2048, 1024], P('own')
- gate_momentum: float32 [1024, 3072], P('own')
- up_momentum: float32 [1024, 3072], P('own')
- down_momentum: float32 [3072, 1024], P('own')
The draws below stay inside these ranges and needn't reach their ends.
Inputs may be any that keep to these rules, and one draw needn't show every extreme that they name: Row d lists in order the lengths of the 3 sequences that fill device d's 256 rows; each row sums to 256 and its longest is 224.
All inputs are finite; a program needn't handle non-finite values.
Results may differ from the reference program's by a relative error of at most 0.029.
Values may be sent and summed in bfloat16 or wider, within the bound.
A program may use at most 448 MiB of HBM per device.

```python
import math
import jax
import jax.numpy as jnp
import numpy as np
from jax import lax

D = 1024
FF = 3072
HEADS = 16
KV_HEADS = 8
HEAD_DIM = 128
TOK_DEV = 256
SEQ_DEV = 3
NS_STEPS = 5
LONGEST = 224
TOKENS = 8192
N_OWN = 8
DEVICES = 32


def draw_output_grad(key, part):
    key = jax.random.fold_in(key, 11)
    device_ids = jnp.arange(TOKENS, dtype=jnp.int32) // TOK_DEV
    rep_count = DEVICES // N_OWN
    rep_place = (device_ids // N_OWN).astype(jnp.float32) / max(rep_count - 1, 1)
    own_place = (device_ids % N_OWN).astype(jnp.float32) / max(N_OWN - 1, 1)
    noise_field = jnp.clip(jax.random.normal(key, (TOKENS, D), jnp.float32), -4.0, 4.0)
    factor = 3.0 ** (rep_place + own_place - 1.0)
    return noise_field * factor[:, None]


def levels(stream_key, dims, cuts, least, largest):
    def one(dim, blocks):
        steps = jax.random.uniform(jax.random.fold_in(jax.random.fold_in(stream_key, 6), dim), (blocks,), jnp.float32, least / len(cuts), largest / len(cuts))
        return jnp.repeat(jnp.exp(steps), dims[dim] // blocks).reshape((-1,) + (1,) * (len(dims) - dim - 1))

    gain = one(*cuts[0])
    for cut in cuts[1:]:
        gain = gain * one(*cut)
    return gain


def length_profile(number_of, total, most, skew):
    portions = [(1 << 20) // math.isqrt(rank ** skew) + 1 for rank in range(2, number_of + 1)]
    surplus, holding = total - most - (number_of - 1), [1] * (number_of - 1)
    while surplus > 0:
        free = [i for i in range(number_of - 1) if holding[i] < most]
        pool, remaining = sum([portions[i] for i in free]), surplus
        for i in free:
            addition = min(most - holding[i], max(1, remaining * portions[i] // pool), surplus)
            holding[i] = holding[i] + addition
            surplus = surplus - addition
    return np.array([most] + holding)


def uneven_parts(rng, count, total, reach, lean):
    if count == 2:
        one = jax.random.randint(rng, (), max(1, total - reach), min(reach, total - 1) + 1)
        return jnp.stack([one, total - one])
    sizes = jnp.asarray(length_profile(count, total, reach, lean), jnp.int32)
    couples = (count - 1) // 2
    donor, sink = sizes[1:1 + 2 * couples:2], sizes[2:2 + 2 * couples:2]
    margin = jnp.minimum(donor - 1, reach - sink)
    moved = jax.random.randint(jax.random.fold_in(rng, 1), (couples,), 0, 1 << 20) % (margin + 1)
    sizes = sizes.at[1:1 + 2 * couples:2].set(donor - moved).at[2:2 + 2 * couples:2].set(sink + moved)
    return sizes[jax.random.permutation(jax.random.fold_in(rng, 2), count)]


def bell_draw(own_key, shape, scale, most, split=(), held_as=jnp.bfloat16):
    values = jax.random.normal(own_key, shape, jnp.float32) * scale
    if len(split) > 0:
        values = levels(own_key, shape, split, -0.22, 0.18) * values
    return jnp.clip(values, min=-most, max=most).astype(held_as)


def setup_inputs(seed: int = 0) -> dict:
    splits = jax.random.split(jax.random.key(seed), 22)
    layer_input = bell_draw(splits[0], (TOKENS, D), 1.0, 6.0, ((0, 32),), jnp.float32)
    output_grad = draw_output_grad(jax.random.fold_in(splits[21], 71), 0)
    lengths = jax.vmap(lambda own: uneven_parts(own, SEQ_DEV, TOK_DEV, LONGEST, 2))(jax.random.split(splits[2], DEVICES)).reshape((DEVICES, SEQ_DEV)).astype(jnp.int32)
    attention_gain = jnp.clip(1.0 + 0.15 * jax.random.normal(splits[3], (D,), jnp.float32), 0.25, 1.75)
    feed_gain = jnp.clip(1.0 + 0.15 * jax.random.normal(splits[4], (D,), jnp.float32), 0.25, 1.75)
    query_gain = jnp.clip(1.0 + 0.15 * jax.random.normal(splits[5], (HEAD_DIM,), jnp.float32), 0.25, 1.75)
    key_gain = jnp.clip(1.0 + 0.15 * jax.random.normal(splits[6], (HEAD_DIM,), jnp.float32), 0.25, 1.75)
    query_weight = bell_draw(splits[7], (D, HEADS * HEAD_DIM), D ** -0.5, 0.1875, ((0, 8),), jnp.float32)
    key_weight = bell_draw(splits[8], (D, KV_HEADS * HEAD_DIM), D ** -0.5, 0.1875, ((0, 8),), jnp.float32)
    value_weight = bell_draw(splits[9], (D, KV_HEADS * HEAD_DIM), D ** -0.5, 0.1875, ((0, 8),), jnp.float32)
    out_weight = bell_draw(splits[10], (HEADS * HEAD_DIM, D), (HEADS * HEAD_DIM * 8 // TOK_DEV) ** -0.5, 0.75, ((0, 8),), jnp.float32)
    gate_weight = bell_draw(splits[11], (D, FF), D ** -0.5, 0.1875, ((0, 8),), jnp.float32)
    up_weight = bell_draw(splits[12], (D, FF), D ** -0.5, 0.1875, ((0, 8),), jnp.float32)
    down_weight = bell_draw(splits[13], (FF, D), FF ** -0.5, 0.109375, ((0, 8),), jnp.float32)
    query_moment = bell_draw(splits[14], (D, HEADS * HEAD_DIM), (0.6 * TOKENS ** 0.5), 320.0, ((0, 8),), jnp.float32)
    key_moment = bell_draw(splits[15], (D, KV_HEADS * HEAD_DIM), (0.6 * TOKENS ** 0.5), 320.0, ((0, 8),), jnp.float32)
    value_moment = bell_draw(splits[16], (D, KV_HEADS * HEAD_DIM), (0.6 * TOKENS ** 0.5), 320.0, ((0, 8),), jnp.float32)
    out_moment = bell_draw(splits[17], (HEADS * HEAD_DIM, D), (1.2 * (8 * DEVICES) ** 0.5), 112.0, ((0, 8),), jnp.float32)
    gate_moment = bell_draw(splits[18], (D, FF), (0.4 * TOKENS ** 0.5), 224.0, ((0, 8),), jnp.float32)
    up_moment = bell_draw(splits[19], (D, FF), (0.4 * TOKENS ** 0.5), 224.0, ((0, 8),), jnp.float32)
    down_moment = bell_draw(splits[20], (FF, D), (0.8 * TOKENS ** 0.5), 448.0, ((0, 8),), jnp.float32)
    return dict(layer_input=layer_input, output_grad=output_grad, lengths=lengths, attention_gain=attention_gain, feed_gain=feed_gain, query_gain=query_gain, key_gain=key_gain, query_weight=query_weight, key_weight=key_weight, value_weight=value_weight, out_weight=out_weight, gate_weight=gate_weight, up_weight=up_weight, down_weight=down_weight, query_moment=query_moment, key_moment=key_moment, value_moment=value_moment, out_moment=out_moment, gate_moment=gate_moment, up_moment=up_moment, down_moment=down_moment)


EPSILON = 1e-06
ROPE_BASE = 1000000.0
MOMENTUM = 0.95
LEARN_RATE = 0.8
WEIGHT_DECAY = 0.01
NEWTON_A = 3.4445
NEWTON_B = -4.775
NEWTON_C = 2.0315
HIGHEST = lax.Precision.HIGHEST

@jax.custom_vjp
def low(v):
    return lax.optimization_barrier(v.astype(jnp.bfloat16)).astype(jnp.float32)

@jax.custom_vjp
def low_back(v):
    return v

def low_keep(v):
    return (low(v), None)

def low_pass(kept, grad):
    return (grad,)

def back_keep(v):
    return (v, None)

def back_low(kept, grad):
    return (low(grad),)
low.defvjp(low_keep, low_pass)
low_back.defvjp(back_keep, back_low)

def rms_scale(values, gain_vector):
    return values * lax.rsqrt(lax.optimization_barrier(jnp.mean(values * values, -1, keepdims=True)) + EPSILON) * gain_vector

def rotate(values, cosine_table, sine_table):
    half_dim = values.shape[-1] // 2
    first_half = values[..., :half_dim]
    second_half = values[..., half_dim:]
    return jnp.concatenate([first_half * cosine_table - second_half * sine_table, second_half * cosine_table + first_half * sine_table], -1)

def head_side(raw_value, gain_vector, cosine_table, sine_table):
    shaped = raw_value.reshape(raw_value.shape[0], -1, HEAD_DIM)
    return rotate(rms_scale(shaped, gain_vector), cosine_table, sine_table)

def swiglu(gate_value, up_value):
    return gate_value * jax.nn.sigmoid(gate_value) * up_value

def segments(lengths, row_count):
    lengths = lengths.astype(jnp.int32)
    seq_ends = jnp.cumsum(lengths).astype(jnp.int32)
    seq_starts = (seq_ends - lengths).astype(jnp.int32)
    row_ids = jnp.arange(row_count, dtype=jnp.int32)
    segment_ids = lax.optimization_barrier(jnp.sum((row_ids[:, None] >= seq_ends[None, :]).astype(jnp.int32), 1)).astype(jnp.int32)
    slot_ids = jnp.arange(lengths.shape[0], dtype=jnp.int32)
    row_starts = lax.optimization_barrier(jnp.sum(jnp.where(segment_ids[:, None] == slot_ids[None, :], seq_starts[None, :], 0), 1)).astype(jnp.int32)
    return (segment_ids, (row_ids - row_starts).astype(jnp.int32))

def rope_tables(positions):
    inverse = ROPE_BASE ** (-jnp.arange(0, HEAD_DIM, 2, dtype=jnp.float32) / HEAD_DIM)
    angles = positions.astype(jnp.float32)[:, None] * inverse[None, :]
    return (jnp.cos(angles)[:, None, :], jnp.sin(angles)[:, None, :])

def orthogonalize(update):
    row_count, column_count = update.shape
    scaled = update / (jnp.sqrt(jnp.sum(update * update)) + 1e-07)
    if row_count > column_count:
        scaled = scaled.T
    for step_index in range(NS_STEPS):
        gram_matrix = jnp.dot(scaled, scaled.T, precision=HIGHEST)
        polynomial = NEWTON_B * gram_matrix + NEWTON_C * jnp.dot(gram_matrix, gram_matrix, precision=HIGHEST)
        scaled = NEWTON_A * scaled + jnp.dot(polynomial, scaled, precision=HIGHEST)
    if row_count > column_count:
        scaled = scaled.T
    return scaled * max(1.0, row_count / column_count) ** 0.5

def layer(block, lengths, weight_set, gain_set):
    query_full, key_full, value_full, out_full, gate_full, up_full, down_full = weight_set
    attention_gain, feed_gain, query_gain, key_gain = gain_set
    row_count = block.shape[0]
    group_size = HEADS // KV_HEADS
    segment_ids, positions = segments(lengths, row_count)
    cosine_table, sine_table = rope_tables(positions)
    normed = low(rms_scale(block, attention_gain))
    query_raw = low_back(jnp.dot(normed, query_full, precision=HIGHEST))
    key_raw = low_back(jnp.dot(normed, key_full, precision=HIGHEST))
    value_raw = low_back(jnp.dot(normed, value_full, precision=HIGHEST))
    queries = low(head_side(query_raw, query_gain, cosine_table, sine_table)).reshape(row_count, KV_HEADS, group_size, HEAD_DIM)
    keys = low(head_side(key_raw, key_gain, cosine_table, sine_table))
    values = low(value_raw.reshape(row_count, KV_HEADS, HEAD_DIM))
    scores = low_back(jnp.einsum('tkgd,skd->kgts', queries, keys, precision=HIGHEST) * HEAD_DIM ** (-0.5))
    row_ids = jnp.arange(row_count, dtype=jnp.int32)
    allowed = (segment_ids[:, None] == segment_ids[None, :]) & (row_ids[:, None] >= row_ids[None, :])
    scores = jnp.where(allowed, scores, -1e+30)
    maximum = lax.optimization_barrier(jnp.max(scores, -1, keepdims=True))
    exponent = jnp.exp(scores - maximum)
    probabilities = exponent / lax.optimization_barrier(jnp.sum(exponent, -1, keepdims=True))
    context = jnp.einsum('kgts,skd->tkgd', low(probabilities), values, precision=HIGHEST)
    context = low(low_back(context)).reshape(row_count, HEADS * HEAD_DIM)
    middle = block + low_back(jnp.dot(context, out_full, precision=HIGHEST))
    hidden = low(rms_scale(middle, feed_gain))
    gate_value = low_back(jnp.dot(hidden, gate_full, precision=HIGHEST))
    up_value = low_back(jnp.dot(hidden, up_full, precision=HIGHEST))
    activated = low(swiglu(gate_value, up_value))
    return middle + low_back(jnp.dot(activated, down_full, precision=HIGHEST))

def reference(layer_input, output_grad, lengths, attention_gain, feed_gain, query_gain, key_gain, query_weight, key_weight, value_weight, out_weight, gate_weight, up_weight, down_weight, query_moment, key_moment, value_moment, out_moment, gate_moment, up_moment, down_moment):

    def forward(block_all, gain_set, weight_set):
        rounded = tuple((low(matrix) for matrix in weight_set))

        def per_device(device_pair):
            return layer(device_pair[0], device_pair[1], rounded, gain_set)
        outputs = lax.map(jax.checkpoint(per_device), (block_all.reshape(DEVICES, TOK_DEV, D), lengths))
        return outputs.reshape(TOKENS, D)
    gain_set = (attention_gain, feed_gain, query_gain, key_gain)
    weight_set = (query_weight, key_weight, value_weight, out_weight, gate_weight, up_weight, down_weight)
    moments = (query_moment, key_moment, value_moment, out_moment, gate_moment, up_moment, down_moment)
    block_output, pullback = jax.vjp(forward, layer_input, gain_set, weight_set)
    input_grad, gain_grads, weight_grads = pullback(output_grad)
    norm_grads = jnp.stack([gain_grads[0], gain_grads[1]])
    head_grads = jnp.stack([gain_grads[2], gain_grads[3]])
    results = []
    for matrix, moment, grad_sum in zip(weight_set, moments, weight_grads):
        moment_next = MOMENTUM * moment + grad_sum
        update = grad_sum + MOMENTUM * moment_next
        matrix_next = matrix * (1.0 - LEARN_RATE * WEIGHT_DECAY) - LEARN_RATE * orthogonalize(update)
        results.append((matrix_next, moment_next))
    return (block_output, input_grad, norm_grads, head_grads, results[0][0], results[1][0], results[2][0], results[3][0], results[4][0], results[5][0], results[6][0], results[0][1], results[1][1], results[2][1], results[3][1], results[4][1], results[5][1], results[6][1])
```

```python
import functools

import jax
import jax.numpy as jnp
from jax import lax
from jax.experimental import pallas as pl
from jax.experimental.pallas import tpu as pltpu
from jax.sharding import PartitionSpec as P

HEADS = 16
KV_HEADS = 8
HEAD_DIM = 128
NS_STEPS = 5

EPSILON = 1e-06
ROPE_BASE = 1000000.0
MOMENTUM = 0.95
LEARN_RATE = 0.8
WEIGHT_DECAY = 0.01
NEWTON_A = 3.4445
NEWTON_B = -4.775
NEWTON_C = 2.0315

BF16 = jnp.bfloat16
F32 = jnp.float32
MESH = pl.DeviceIdType.MESH
ANY = pl.BlockSpec(memory_space=pl.ANY)

QKV, OUT, GU, DOWN = range(4)


def rms_scale(values, gain_vector):
    return values * lax.rsqrt(jnp.mean(values * values, -1, keepdims=True) + EPSILON) * gain_vector


def rotate(values, cosine_table, sine_table):
    half_dim = values.shape[-1] // 2
    first_half = values[..., :half_dim]
    second_half = values[..., half_dim:]
    return jnp.concatenate(
        [
            first_half * cosine_table - second_half * sine_table,
            second_half * cosine_table + first_half * sine_table,
        ],
        -1,
    )


def head_side(raw_value, gain_vector, cosine_table, sine_table):
    shaped = raw_value.reshape(raw_value.shape[0], -1, HEAD_DIM)
    return rotate(rms_scale(shaped, gain_vector), cosine_table, sine_table)


def swiglu(gate_value, up_value):
    return gate_value * jax.nn.sigmoid(gate_value) * up_value


def segments(lengths, row_count):
    seq_ends = jnp.cumsum(lengths)
    seq_starts = seq_ends - lengths
    row_ids = jnp.arange(row_count, dtype=jnp.int32)
    segment_ids = jnp.sum((row_ids[:, None] >= seq_ends[None, :]).astype(jnp.int32), 1)
    slot_ids = jnp.arange(lengths.shape[0], dtype=jnp.int32)
    row_starts = jnp.sum(
        jnp.where(segment_ids[:, None] == slot_ids[None, :], seq_starts[None, :], 0), 1
    )
    return (segment_ids, row_ids - row_starts)


def rope_tables(positions):
    inverse = ROPE_BASE ** (-jnp.arange(0, HEAD_DIM, 2, dtype=jnp.float32) / HEAD_DIM)
    angles = positions.astype(jnp.float32)[:, None] * inverse[None, :]
    return (jnp.cos(angles)[:, None, :], jnp.sin(angles)[:, None, :])


class Place:
    def __init__(self, n):
        self.n = n
        self.rep = lax.axis_index("rep")
        self.own = lax.axis_index("own")
        self.x = self.rep // 2
        self.core = self.rep % 2
        odd, pair = self.own % 2, self.own // 2
        self.ring = pair * (1 - odd) + odd * (n - 1 - pair)

    def own_at(self, ring):
        odd = ring // (self.n // 2)
        return 2 * (ring * (1 - odd) + odd * (self.n - 1 - ring)) + odd

    def shard(self, distance):
        return self.own_at(lax.rem(self.ring + distance + self.n, self.n))

    def ring_neighbour(self, way):
        return (self.rep, self.shard(way))

    @property
    def core_partner(self):
        return (self.x * 2 + 1 - self.core, self.own)

    @property
    def x_partner(self):
        return ((1 - self.x) * 2 + self.core, self.own)


def greet(devices):
    barrier = pltpu.get_barrier_semaphore()
    for device in devices:
        pl.semaphore_signal(barrier, inc=1, device_id=device, device_id_type=MESH)
    pl.semaphore_wait(barrier, len(devices))


def remote(src, dst, send, recv, device):
    return pltpu.make_async_remote_copy(
        src_ref=src, dst_ref=dst, send_sem=send, recv_sem=recv, device_id=device, device_id_type=MESH
    )


def hops(n, way, kind):
    return n // 2 if (way == 0) == (kind == 0) else n // 2 - 1


def side_pieces(unit):
    sides = ([(QKV, 0, 4 * unit)], [(GU, 0, 4 * unit)])
    both = [(GU, 4 * unit, 2 * unit), (OUT, 0, unit), (DOWN, 0, unit)]
    return sides, both


def gather_kernel(n, rows, unit, *refs):
    shards, wholes = refs[:4], refs[4:8]
    local, ring_send, ring_recv, x_send, x_recv, core_send, core_recv = refs[8:]
    place = Place(n)
    cw, ccw = place.ring_neighbour(1), place.ring_neighbour(-1)
    greet([cw, ccw, place.core_partner, place.x_partner])
    sides, both = side_pieces(unit)

    def region(piece, own_index):
        array, first, columns = piece
        half = rows[array] // 2
        start = pl.multiple_of(own_index * rows[array] + place.core * half, half)
        return wholes[array].at[pl.ds(start, half), pl.ds(first, columns)]

    def shard_half(piece):
        array, first, columns = piece
        half = rows[array] // 2
        start = pl.multiple_of(place.core * half, half)
        return shards[array].at[pl.ds(start, half), pl.ds(first, columns)]

    def by_kind(kind, act):
        if kind == 1:
            act(both)
        else:
            for side in range(2):
                pl.when(place.x == side)(functools.partial(act, sides[side]))

    locals_ = []
    for array in range(4):
        start = pl.multiple_of(place.own * rows[array], rows[array])
        copy = pltpu.make_async_copy(
            shards[array], wholes[array].at[pl.ds(start, rows[array])], local.at[array]
        )
        copy.start()
        locals_.append(copy)

    top = n // 2
    ways = ((1, cw), (-1, ccw))

    def ring_copies(pieces, way, kind, hop, distance):
        slot = ((way * 2 + kind) * top + hop - 1) * 3
        step, target = ways[way]
        own_index = place.shard(distance)
        return [
            remote(
                shard_half(piece) if distance == 0 else region(piece, own_index),
                region(piece, own_index),
                ring_send.at[slot + i],
                ring_recv.at[slot + i],
                target,
            )
            for i, piece in enumerate(pieces)
        ]

    def core_copies(pieces, slot, distance):
        own_index = place.shard(distance)
        return [
            remote(
                region(piece, own_index),
                region(piece, own_index),
                core_send.at[slot + i],
                core_recv.at[slot + i],
                place.core_partner,
            )
            for i, piece in enumerate(pieces)
        ]

    def x_copies(pieces, way, hop, distance):
        slot = way * top + hop - 1
        own_index = place.shard(distance)
        return [
            remote(
                region(piece, own_index),
                region(piece, own_index),
                x_send.at[slot],
                x_recv.at[slot],
                place.x_partner,
            )
            for piece in pieces
        ]

    ring_slots = 2 * 2 * top * 3

    def start(copies):
        for copy in copies:
            copy.start()

    def wait_recv(copies):
        for copy in copies:
            copy.wait_recv()

    def wait_send(copies):
        for copy in copies:
            copy.wait_send()

    def other_side(act):
        for side in range(2):
            pl.when(place.x == 1 - side)(functools.partial(act, sides[side]))

    for kind in range(2):
        for way in range(2):
            by_kind(kind, lambda pieces: start(ring_copies(pieces, way, kind, 1, 0)))

    def take_x(way, hop):
        distance = -ways[way][0] * hop

        def act(pieces):
            wait_recv(x_copies(pieces, way, hop, distance))
            start(core_copies(pieces, ring_slots + way * top + hop - 1, distance))

        other_side(act)

    for hop in range(1, top + 1):
        for kind in range(2):
            for way in range(2):
                if hop > hops(n, way, kind):
                    continue
                distance = -ways[way][0] * hop

                def act(pieces):
                    wait_recv(ring_copies(pieces, way, kind, hop, distance))
                    if hop < hops(n, way, kind):
                        start(ring_copies(pieces, way, kind, hop + 1, distance))
                    if kind == 0:
                        start(x_copies(pieces, way, hop, distance))
                    start(core_copies(pieces, ((way * 2 + kind) * top + hop - 1) * 3, distance))

                by_kind(kind, act)
        if hop > 1:
            for way in range(2):
                if hop - 1 <= hops(n, way, 0):
                    take_x(way, hop - 1)
    for way in range(2):
        if top <= hops(n, way, 0):
            take_x(way, top)

    for copy in locals_:
        copy.wait()
    for hop in range(1, top + 1):
        for kind in range(2):
            for way in range(2):
                if hop > hops(n, way, kind):
                    continue
                distance = -ways[way][0] * hop
                slot = ((way * 2 + kind) * top + hop - 1) * 3

                def act(pieces):
                    wait_send(ring_copies(pieces, way, kind, hop, distance + ways[way][0]))
                    core = core_copies(pieces, slot, distance)
                    wait_send(core)
                    wait_recv(core)
                    if kind == 0:
                        wait_send(x_copies(pieces, way, hop, distance))

                by_kind(kind, act)
                if kind == 0:

                    def act_other(pieces):
                        core = core_copies(pieces, ring_slots + way * top + hop - 1, distance)
                        wait_send(core)
                        wait_recv(core)

                    other_side(act_other)


def gather_weights(shards, n, unit):
    rows = [shard.shape[0] for shard in shards]
    top = n // 2
    dma = pltpu.SemaphoreType.DMA
    return pl.pallas_call(
        functools.partial(gather_kernel, n, rows, unit),
        out_shape=[
            jax.ShapeDtypeStruct((n * shard.shape[0], shard.shape[1]), BF16) for shard in shards
        ],
        in_specs=[ANY] * 4,
        out_specs=[ANY] * 4,
        scratch_shapes=[
            dma((4,)),
            dma((12 * top,)),
            dma((12 * top,)),
            dma((2 * top,)),
            dma((2 * top,)),
            dma((14 * top,)),
            dma((14 * top,)),
        ],
        compiler_params=pltpu.CompilerParams(collective_id=0, has_side_effects=True),
    )(*shards)


def reduce_kernel(n, rows, unit, *refs):
    grads, gains_in = refs[:4], refs[4]
    outs, gains_out = refs[5:9], refs[9]
    (
        own_m, own_t, own_b, core_m, core_t, core_b, x_m, ring_m, ring_b, x_b, last_t,
        gain_mine, gain_core, gain_x, gain_all,
        load_sem, core_send, core_recv, x_send, x_recv,
        ring_send, ring_recv, end_send, end_recv, end_local,
        gain_send, gain_recv,
    ) = refs[10:]
    place = Place(n)
    cw, ccw = place.ring_neighbour(1), place.ring_neighbour(-1)
    greet([cw, ccw, place.core_partner, place.x_partner])
    sides, both = side_pieces(unit)
    top = n // 2
    ways = ((1, cw), (-1, ccw))
    half = rows[QKV] // 2
    order = [top]
    for distance in range(top - 1, 0, -1):
        order += [distance, -distance]
    order.append(0)
    last = n - 1

    def blocks(pieces):
        parts, at = [], 0
        for array, first, columns in pieces:
            height = rows[array] // 2
            for block in range(columns // unit):
                parts.append((array, first + block * unit, height, at))
                at += height
        return parts, at

    def from_grads(array, first, height, own_index, core):
        start = pl.multiple_of(own_index * rows[array] + core * height, height)
        return grads[array].at[pl.ds(start, height), pl.ds(first, unit)]

    def load(pieces, mine, theirs, i, which):
        own_index = place.shard(order[i])
        for array, first, height, at in blocks(pieces)[0]:
            remote(
                from_grads(array, first, height, own_index, 1 - place.core),
                theirs.at[i, pl.ds(at, height)],
                core_send.at[which, i],
                core_recv.at[which, i],
                place.core_partner,
            ).start()
            pltpu.make_async_copy(
                from_grads(array, first, height, own_index, place.core),
                mine.at[i, pl.ds(at, height)],
                load_sem.at[which, i],
            ).start()

    def wait_load(mine, theirs, i, which):
        pltpu.make_async_copy(theirs.at[i], mine.at[i], load_sem.at[which, i]).wait()
        remote(
            theirs.at[i], theirs.at[i], core_send.at[which, i], core_recv.at[which, i],
            place.core_partner,
        ).wait_recv()

    def gain_copy(src, dst, slot, device):
        return remote(src, dst, gain_send.at[slot], gain_recv.at[slot], device)

    gain_mine[...] = gains_in[...]
    gain_copy(gain_mine, gain_core, 0, place.core_partner).start()
    for i in range(n):
        for side in range(2):

            @pl.when(place.x == 1 - side)
            def _():
                load(sides[side], own_t, core_t, i, 0)

        for side in range(2):

            @pl.when(place.x == side)
            def _():
                load(sides[side], own_m, core_m, i, 1)

        load(both, own_b, core_b, i, 2)

    def add(target, i, others, height):
        step = half

        def body(k, carry):
            span = pl.ds(pl.multiple_of(k * step, step), step)
            total = target[i, span, :].astype(F32)
            for ref, index in others:
                total = total + ref[index + (span,)].astype(F32)
            target[i, span, :] = total.astype(BF16)
            return carry

        lax.fori_loop(0, height // step, body, 0)

    def x_copy(i):
        return remote(own_t.at[i], x_m.at[i], x_send.at[i], x_recv.at[i], place.x_partner)

    def to_x(i):
        wait_load(own_t, core_t, i, 0)
        add(own_t, i, [(core_t, (i,))], 4 * half)
        x_copy(i).start()

    buffers = ((own_m, ring_m), (own_b, ring_b))

    def ring_copy(kind, way, i, distance):
        mine, ring = buffers[kind]
        slot = (kind * 2 + way) * (top + 1) + distance
        return remote(
            mine.at[i], ring.at[way, distance - 1], ring_send.at[slot], ring_recv.at[slot],
            ways[way][1],
        )

    def arrival(kind, way, distance):
        mine, ring = buffers[kind]
        slot = (kind * 2 + way) * (top + 1) + distance + 1
        remote(
            ring.at[way, distance], ring.at[way, distance], ring_send.at[slot], ring_recv.at[slot],
            ways[way][1],
        ).wait_recv()
        return (ring, (way, distance))

    def sent_ways(kind, distance):
        if distance == top:
            return [0 if kind == 0 else 1]
        if distance == 0:
            return []
        return [0 if distance > 0 else 1]

    def taken_ways(kind, distance):
        if distance == top:
            return []
        found = [0, 1] if distance == 0 else [0 if distance > 0 else 1]
        return [way for way in found if abs(distance) + 1 <= hops(n, way, kind)]

    def ring_stage(i):
        distance = order[i]
        for kind in (1, 0):
            mine, _ = buffers[kind]
            if kind == 1:
                wait_load(own_b, core_b, i, 2)
                others = [(core_b, (i,))]
                height = 7 * half
            else:
                wait_load(own_m, core_m, i, 1)
                x_copy(i).wait_recv()
                others = [(core_m, (i,)), (x_m, (i,))]
                height = 4 * half
            for way in taken_ways(kind, distance):
                others.append(arrival(kind, way, abs(distance)))
            add(mine, i, others, height)
            for way in sent_ways(kind, distance):
                ring_copy(kind, way, i, abs(distance)).start()
            if distance == 0 and kind == 1:
                end_b().start()

    def end_b():
        return remote(own_b.at[last], x_b.at[0], end_send.at[0], end_recv.at[0], place.x_partner)

    def end_m():
        return remote(own_m.at[last], last_t.at[0], end_send.at[1], end_recv.at[1], place.x_partner)

    def gain_ring(way, hop, distance):
        spot = gain_all.at[place.shard(distance)]
        return gain_copy(spot, spot, 2 + way * top + hop - 1, ways[way][1])

    def gain_stage(hop):
        if hop == 0:
            gain_copy(gain_mine, gain_core, 0, place.core_partner).wait_recv()
            gain_core[...] = gain_mine[...] + gain_core[...]
            gain_copy(gain_core, gain_x, 1, place.x_partner).start()
            return
        if hop == 1:
            gain_copy(gain_core, gain_x, 1, place.x_partner).wait_recv()
            gain_all[place.own] = gain_core[...] + gain_x[...]
            for way in range(2):
                gain_ring(way, 1, 0).start()
        for way in range(2):
            if hop > 1 and hop - 1 <= hops(n, way, 0):
                distance = -ways[way][0] * (hop - 1)
                gain_ring(way, hop - 1, distance).wait_recv()
                if hop <= hops(n, way, 0):
                    gain_ring(way, hop, distance).start()

    lead = min(3, n)
    for i in range(lead):
        to_x(i)
    gain_stage(0)
    for i in range(n):
        ring_stage(i)
        if i + lead < n:
            to_x(i + lead)
        if i + 1 <= top + 1:
            gain_stage(i + 1)

    end_m().start()

    def result(piece_part, core):
        array, first, height, _ = piece_part
        start = pl.multiple_of(core * height, height)
        return outs[array].at[pl.ds(start, height), pl.ds(first, unit)]

    def hand_out(pieces, block, which):
        for part in blocks(pieces)[0]:
            array, first, height, at = part
            source = block.at[pl.ds(at, height)]
            remote(
                source, result(part, place.core), end_send.at[2 + which], end_recv.at[2 + which],
                place.core_partner,
            ).start()
            pltpu.make_async_copy(source, result(part, place.core), end_local.at[which]).start()

    for side in range(2):

        @pl.when(place.x == side)
        def _():
            hand_out(sides[side], own_m.at[last], 0)

    end_b().wait_recv()
    end_b().wait_send()
    add(own_b, last, [(x_b, (0,))], 7 * half)
    hand_out(both, own_b.at[last], 1)
    end_m().wait_recv()
    for side in range(2):

        @pl.when(place.x == 1 - side)
        def _():
            hand_out(sides[side], last_t.at[0], 2)

    total = gain_all[0]
    for k in range(1, n):
        total = total + gain_all[k]
    gains_out[...] = total

    end_m().wait_send()
    for which, block in enumerate((own_m.at[last], own_b.at[last], last_t.at[0])):
        remote(
            block, block, end_send.at[2 + which], end_recv.at[2 + which], place.core_partner
        ).wait()
        pltpu.make_async_copy(block, block, end_local.at[which]).wait()
    for i in range(n):
        x_copy(i).wait_send()
        for which, theirs in enumerate((core_t, core_m, core_b)):
            remote(
                theirs.at[i], theirs.at[i], core_send.at[which, i], core_recv.at[which, i],
                place.core_partner,
            ).wait_send()
        for kind in range(2):
            for way in sent_ways(kind, order[i]):
                ring_copy(kind, way, i, abs(order[i])).wait_send()
    gain_copy(gain_mine, gain_core, 0, place.core_partner).wait_send()
    gain_copy(gain_core, gain_x, 1, place.x_partner).wait_send()
    for way in range(2):
        for hop in range(1, hops(n, way, 0) + 1):
            gain_ring(way, hop, -ways[way][0] * (hop - 1)).wait_send()


def reduce_grads(grads, gains, n, unit):
    rows = [grad.shape[0] // n for grad in grads]
    top = n // 2
    half = rows[QKV] // 2
    dma = pltpu.SemaphoreType.DMA
    vmem = pltpu.VMEM
    m_block, b_block = (4 * half, unit), (7 * half, unit)
    return pl.pallas_call(
        functools.partial(reduce_kernel, n, rows, unit),
        out_shape=[
            jax.ShapeDtypeStruct((grad.shape[0] // n, grad.shape[1]), BF16) for grad in grads
        ]
        + [jax.ShapeDtypeStruct(gains.shape, F32)],
        in_specs=[ANY] * 4 + [pl.BlockSpec(memory_space=pltpu.VMEM)],
        out_specs=[ANY] * 4 + [pl.BlockSpec(memory_space=pltpu.VMEM)],
        scratch_shapes=[
            vmem((n,) + m_block, BF16),
            vmem((n,) + m_block, BF16),
            vmem((n,) + b_block, BF16),
            vmem((n,) + m_block, BF16),
            vmem((n,) + m_block, BF16),
            vmem((n,) + b_block, BF16),
            vmem((n,) + m_block, BF16),
            vmem((2, top) + m_block, BF16),
            vmem((2, top) + b_block, BF16),
            vmem((1,) + b_block, BF16),
            vmem((1,) + m_block, BF16),
            vmem(gains.shape, F32),
            vmem(gains.shape, F32),
            vmem(gains.shape, F32),
            vmem((n,) + gains.shape, F32),
            dma((3, n)),
            dma((3, n)),
            dma((3, n)),
            dma((n,)),
            dma((n,)),
            dma((4 * (top + 1),)),
            dma((4 * (top + 1),)),
            dma((5,)),
            dma((5,)),
            dma((3,)),
            dma((2 + 2 * top,)),
            dma((2 + 2 * top,)),
        ],
        compiler_params=pltpu.CompilerParams(
            collective_id=1, has_side_effects=True, vmem_limit_bytes=58 * 2**20
        ),
    )(*grads, gains)


OWNERS = (
    (QKV, 2, 1, False, 0, 3),
    (QKV, 3, 1, False, 2, 3),
    (QKV, 0, 2, False, 3, 5),
    (OUT, 0, 2, True, 3, 2),
    (GU, 0, 3, False, 0, 1),
    (GU, 3, 3, False, 1, 5),
    (DOWN, 0, 3, True, 2, 1),
)


def newton_kernel(n, rows, unit, *refs):
    sources, outs = refs[:4], refs[4:8]
    (
        whole, exact, low, gram, poly, sums,
        in_send, in_recv, in_local, out_send, out_recv, out_local, pass_send, pass_recv,
    ) = refs[8:]
    place = Place(n)
    others = [(place.rep, lax.rem(place.own + k, n)) for k in range(1, n)]
    greet(others + [place.core_partner, place.x_partner])
    base = rows[QKV]
    tile = min(512, unit // 2)
    small = min(256, unit // 2)
    tiles = unit // tile
    owner_of = [place.own_at(spot * n // 8) for *_, spot in OWNERS]
    in_lane = [place.rep == rep for *_, rep, _ in OWNERS]
    spot = place.rep * n + place.own
    is_owner = [spot == rep * n + owner for (*_, rep, _), owner in zip(OWNERS, owner_of)]
    not_owner = [spot != rep * n + owner for (*_, rep, _), owner in zip(OWNERS, owner_of)]
    count, tall = 0, 0
    for mine, (_, _, units, lies_tall, _, _) in zip(is_owner, OWNERS):
        count = count + units * mine.astype(jnp.int32)
        tall = tall + int(lies_tall) * mine.astype(jnp.int32)

    def row_block(start, size):
        return pl.ds(pl.multiple_of(start, size), size)

    def pieces(matrix, own_index):
        array, first, units, lies_tall, _, _ = OWNERS[matrix]
        if lies_tall:
            return [((pl.ds(0, units * base), pl.ds(0, unit)), row_block(own_index * units * base, units * base))]
        return [
            (
                (pl.ds(0, base), pl.ds((first + block) * unit, unit)),
                row_block(block * unit + own_index * base, base),
            )
            for block in range(units)
        ]

    for matrix, (array, *_) in enumerate(OWNERS):

        @pl.when(in_lane[matrix] & not_owner[matrix])
        def _():
            for at, span in pieces(matrix, place.own):
                remote(
                    sources[array].at[at], whole.at[span], in_send.at[matrix], in_recv.at[place.own],
                    (place.rep, owner_of[matrix]),
                ).start()

        @pl.when(is_owner[matrix])
        def _():
            for at, span in pieces(matrix, place.own):
                pltpu.make_async_copy(sources[array].at[at], whole.at[span], in_local).start()

    for matrix, (_, _, units, *_) in enumerate(OWNERS):

        @pl.when(is_owner[matrix])
        def _():
            size = units * base
            pltpu.make_async_copy(whole.at[pl.ds(0, size)], whole.at[pl.ds(0, size)], in_local).wait()
            for own_index in range(n):

                @pl.when(place.own != own_index)
                def _():
                    remote(
                        whole.at[pl.ds(0, size)], whole.at[pl.ds(0, size)],
                        in_send.at[matrix], in_recv.at[own_index], (place.rep, own_index),
                    ).wait_recv()

    @pl.when(count > 0)
    def _():
        sums[...] = jnp.zeros_like(sums)

        def square(k, carry):
            part = whole[row_block(k * small, small), :].astype(F32)
            sums[...] += jnp.sum((part * part).reshape(small // 8, 8, unit), 0)
            return carry

        lax.fori_loop(0, count * (unit // small), square, 0)
        total = jnp.sum(jnp.sum(sums[...], 1, keepdims=True), 0, keepdims=True)
        inverse = 1.0 / (jnp.sqrt(total) + 1e-07)

        @pl.when(tall == 0)
        def _():
            def scale(k, carry):
                span = row_block(k * small, small)
                part = whole[span, :].astype(F32) * inverse
                exact[span, :] = part
                low[0, span, :] = part.astype(BF16)
                return carry

            lax.fori_loop(0, count * (unit // small), scale, 0)

        @pl.when(tall == 1)
        def _():
            per = unit // small

            def scale(k, carry):
                block, row = k // per, k % per
                for column in range(per):
                    part = whole[
                        row_block(k * small, small), pl.ds(column * small, small)
                    ].astype(F32)
                    part = (part * inverse).T
                    span = row_block(block * unit + column * small, small)
                    columns = row_block(row * small, small)
                    exact[span, columns] = part
                    low[0, span, columns] = part.astype(BF16)
                return carry

            lax.fori_loop(0, count * per, scale, 0)

        def newton(step, carry):
            now, later = step % 2, 1 - step % 2

            def grams(i, carry):
                def part(block):
                    left = low[now, row_block(block * unit + i * tile, tile), :]
                    right = low[now, row_block(block * unit, unit), :]
                    return lax.dot_general(
                        left, right, (((1,), (1,)), ((), ())), preferred_element_type=F32
                    )

                sum_rows = row_block(i * tile, tile)
                gram[sum_rows, :] = part(0)

                def more(block, carry):
                    gram[sum_rows, :] += part(block)
                    return carry

                lax.fori_loop(1, count, more, 0)
                poly[0, sum_rows, :] = gram[sum_rows, :].astype(BF16)
                return carry

            lax.fori_loop(0, tiles, grams, 0)

            def polynomial(i, carry):
                span = row_block(i * tile, tile)
                part = poly[0, span, :]
                squared = jnp.dot(part, poly[0], preferred_element_type=F32)
                poly[1, span, :] = (NEWTON_B * part.astype(F32) + NEWTON_C * squared).astype(BF16)
                return carry

            lax.fori_loop(0, tiles, polynomial, 0)

            def advance(k, carry):
                block, i = k // tiles, k % tiles
                span = row_block(k * tile, tile)
                product = jnp.dot(
                    poly[1, row_block(i * tile, tile), :],
                    low[now, row_block(block * unit, unit), :],
                    preferred_element_type=F32,
                )
                value = NEWTON_A * exact[span, :] + product
                exact[span, :] = value
                low[later, span, :] = value.astype(BF16)
                return carry

            lax.fori_loop(0, count * tiles, advance, 0)
            return carry

        lax.fori_loop(0, NS_STEPS, newton, 0)

        @pl.when(tall == 1)
        def _():
            per = unit // small
            factor = jnp.sqrt(jnp.full((1, 1), count, jnp.int32).astype(F32))

            def lay(k, carry):
                block, row = k // per, k % per
                for column in range(per):
                    part = exact[row_block(k * small, small), pl.ds(column * small, small)] * factor
                    span = row_block(block * unit + column * small, small)
                    low[NS_STEPS % 2, span, row_block(row * small, small)] = part.T.astype(BF16)
                return carry

            lax.fori_loop(0, count * per, lay, 0)

    final = low.at[NS_STEPS % 2]
    for matrix, (array, _, units, *_) in enumerate(OWNERS):

        @pl.when(is_owner[matrix])
        def _():
            def send(k, carry):
                target = lax.rem(place.own + k, n)
                for at, span in pieces(matrix, target):
                    remote(
                        final.at[span], outs[array].at[at], out_send.at[target], out_recv.at[matrix],
                        (place.rep, target),
                    ).start()
                return carry

            lax.fori_loop(1, n, send, 0)
            for at, span in pieces(matrix, place.own):
                pltpu.make_async_copy(final.at[span], outs[array].at[at], out_local).start()

    def region(matrix):
        array, first, units, lies_tall, _, _ = OWNERS[matrix]
        if lies_tall:
            return outs[array].at[pl.ds(0, units * base), pl.ds(0, unit)]
        return outs[array].at[pl.ds(0, base), pl.ds(first * unit, units * unit)]

    def direct(matrix, target):
        return remote(
            region(matrix), region(matrix), out_send.at[target], out_recv.at[matrix],
            place.core_partner,
        )

    def hand_on(matrix, device, to):
        return remote(
            region(matrix), region(matrix), pass_send.at[matrix, to], pass_recv.at[matrix, to], device
        )

    for matrix, (array, _, units, _, rep, _) in enumerate(OWNERS):

        @pl.when(in_lane[matrix])
        def _():
            @pl.when(is_owner[matrix])
            def _():
                pltpu.make_async_copy(region(matrix), region(matrix), out_local).wait()

            @pl.when(not_owner[matrix])
            def _():
                direct(matrix, place.own).wait_recv()

            hand_on(matrix, place.x_partner, 0).start()
            hand_on(matrix, place.core_partner, 1).start()

        @pl.when((place.x != rep // 2) & (place.core == rep % 2))
        def _():
            hand_on(matrix, place.x_partner, 0).wait_recv()
            hand_on(matrix, place.core_partner, 1).start()

    for matrix, (array, _, units, _, rep, _) in enumerate(OWNERS):

        @pl.when(place.core != rep % 2)
        def _():
            hand_on(matrix, place.core_partner, 1).wait_recv()

        @pl.when(place.core == rep % 2)
        def _():
            hand_on(matrix, place.core_partner, 1).wait_send()

        @pl.when(in_lane[matrix])
        def _():
            hand_on(matrix, place.x_partner, 0).wait_send()

        @pl.when(is_owner[matrix])
        def _():
            def sent(k, carry):
                direct(matrix, lax.rem(place.own + k, n)).wait_send()
                return carry

            lax.fori_loop(1, n, sent, 0)

        @pl.when(in_lane[matrix] & not_owner[matrix])
        def _():
            size = units * base
            remote(
                whole.at[pl.ds(0, size)], whole.at[pl.ds(0, size)], in_send.at[matrix],
                in_recv.at[0], place.core_partner,
            ).wait_send()


def orthogonalize_all(sources, n, unit):
    rows = [source.shape[0] for source in sources]
    dma = pltpu.SemaphoreType.DMA
    vmem = pltpu.VMEM
    return pl.pallas_call(
        functools.partial(newton_kernel, n, rows, unit),
        out_shape=[jax.ShapeDtypeStruct(source.shape, BF16) for source in sources],
        in_specs=[ANY] * 4,
        out_specs=[ANY] * 4,
        scratch_shapes=[
            vmem((3 * unit, unit), BF16),
            vmem((3 * unit, unit), F32),
            vmem((2, 3 * unit, unit), BF16),
            vmem((unit, unit), F32),
            vmem((2, unit, unit), BF16),
            vmem((8, unit), F32),
            dma((7,)),
            dma((n,)),
            dma,
            dma((n,)),
            dma((7,)),
            dma,
            dma((7, 2)),
            dma((7, 2)),
        ],
        compiler_params=pltpu.CompilerParams(
            collective_id=2, has_side_effects=True, vmem_limit_bytes=58 * 2**20
        ),
    )(*sources)


def packed(matrices):
    query, key, value, out, gate, up, down = matrices
    return (
        jnp.concatenate([query, key, value], 1),
        out,
        jnp.concatenate([gate, up], 1),
        down,
    )


def unpacked(arrays, unit):
    qkv, out, gate_up, down = arrays
    return (
        qkv[:, : 2 * unit],
        qkv[:, 2 * unit : 3 * unit],
        qkv[:, 3 * unit :],
        out,
        gate_up[:, : 3 * unit],
        gate_up[:, 3 * unit :],
        down,
    )


def body(
    layer_input,
    output_grad,
    lengths,
    attention_gain,
    feed_gain,
    query_gain,
    key_gain,
    query_weight,
    key_weight,
    value_weight,
    out_weight,
    gate_weight,
    up_weight,
    down_weight,
    query_moment,
    key_moment,
    value_moment,
    out_moment,
    gate_moment,
    up_moment,
    down_moment,
):
    owned = (
        query_weight, key_weight, value_weight, out_weight, gate_weight, up_weight, down_weight,
    )
    moments = (
        query_moment, key_moment, value_moment, out_moment, gate_moment, up_moment, down_moment,
    )
    n = lax.axis_size("own")
    unit = layer_input.shape[1]
    q_width, kv_width, ff = 2 * unit, unit, 3 * unit
    low_shards = packed([matrix.astype(BF16) for matrix in owned])
    qkv_full, out_full, gu_full, down_full = gather_weights(low_shards, n, unit)

    row_count = layer_input.shape[0]
    group_size = HEADS // KV_HEADS
    segment_ids, positions = segments(lengths[0], row_count)
    cosine_table, sine_table = rope_tables(positions)
    normed_value, norm_pullback = jax.vjp(rms_scale, layer_input, attention_gain)
    normed = normed_value.astype(BF16)
    raw = jnp.dot(normed, qkv_full, preferred_element_type=F32)
    query_raw = raw[:, :q_width]
    key_raw = raw[:, q_width : q_width + kv_width]
    value_raw = raw[:, q_width + kv_width :]
    query_rot, query_pullback = jax.vjp(
        lambda raw_value, gain_vector: head_side(raw_value, gain_vector, cosine_table, sine_table),
        query_raw,
        query_gain,
    )
    key_rot, key_pullback = jax.vjp(
        lambda raw_value, gain_vector: head_side(raw_value, gain_vector, cosine_table, sine_table),
        key_raw,
        key_gain,
    )
    queries = query_rot.astype(BF16).reshape(row_count, KV_HEADS, group_size, HEAD_DIM)
    keys = key_rot.astype(BF16)
    values = value_raw.astype(BF16).reshape(row_count, KV_HEADS, HEAD_DIM)
    row_ids = jnp.arange(row_count, dtype=jnp.int32)
    score_scale = HEAD_DIM ** (-0.5)
    raw_scores = (
        jnp.einsum("tkgd,skd->kgts", queries, keys, preferred_element_type=F32) * score_scale
    )
    allowed = (segment_ids[:, None] == segment_ids[None, :]) & (
        row_ids[:, None] >= row_ids[None, :]
    )
    masked = jnp.where(allowed, raw_scores, -1e30)
    maximum = jnp.max(masked, -1, keepdims=True)
    exponent = jnp.exp(masked - maximum)
    totals = jnp.sum(exponent, -1, keepdims=True)
    probs_full = exponent / totals
    probs_low = probs_full.astype(BF16)
    context = jnp.einsum("kgts,skd->tkgd", probs_low, values, preferred_element_type=F32)
    context = context.reshape(row_count, q_width).astype(BF16)
    middle = layer_input + jnp.dot(context, out_full, preferred_element_type=F32)
    hidden_value, middle_pullback = jax.vjp(rms_scale, middle, feed_gain)
    hidden = hidden_value.astype(BF16)
    gate_up = jnp.dot(hidden, gu_full, preferred_element_type=F32)
    activated_value, swiglu_pullback = jax.vjp(swiglu, gate_up[:, :ff], gate_up[:, ff:])
    activated = activated_value.astype(BF16)
    block_output = middle + jnp.dot(activated, down_full, preferred_element_type=F32)

    out_low = output_grad.astype(BF16)
    grad_down = jnp.einsum("tf,td->fd", activated, out_low, preferred_element_type=F32)
    grad_activated = jnp.einsum("td,fd->tf", out_low, down_full, preferred_element_type=F32)
    grad_gate_value, grad_up_value = swiglu_pullback(grad_activated)
    gu_back = jnp.concatenate([grad_gate_value.astype(BF16), grad_up_value.astype(BF16)], 1)
    grad_gu = jnp.einsum("td,tf->df", hidden, gu_back, preferred_element_type=F32)
    grad_hidden = jnp.einsum("tf,df->td", gu_back, gu_full, preferred_element_type=F32)
    grad_middle_norm, grad_feed = middle_pullback(grad_hidden)
    grad_middle = output_grad + grad_middle_norm
    attended_low = grad_middle.astype(BF16)
    grad_out = jnp.einsum("ti,td->id", context, attended_low, preferred_element_type=F32)
    grad_context = jnp.einsum("td,id->ti", attended_low, out_full, preferred_element_type=F32)
    grad_context = grad_context.astype(BF16).reshape(row_count, KV_HEADS, group_size, HEAD_DIM)
    grad_values = jnp.einsum("kgts,tkgd->skd", probs_low, grad_context, preferred_element_type=F32)
    grad_probs = jnp.einsum("tkgd,skd->kgts", grad_context, values, preferred_element_type=F32)
    grad_scores = probs_full * (
        grad_probs - jnp.sum(probs_full * grad_probs, -1, keepdims=True)
    )
    grad_scores = grad_scores.astype(BF16)
    grad_queries = (
        jnp.einsum("kgts,skd->tkgd", grad_scores, keys, preferred_element_type=F32) * score_scale
    )
    grad_keys = (
        jnp.einsum("kgts,tkgd->skd", grad_scores, queries, preferred_element_type=F32)
        * score_scale
    )
    grad_query_raw, grad_query_gain = query_pullback(
        grad_queries.reshape(row_count, HEADS, HEAD_DIM)
    )
    grad_key_raw, grad_key_gain = key_pullback(grad_keys)
    qkv_back = jnp.concatenate(
        [
            grad_query_raw.astype(BF16),
            grad_key_raw.astype(BF16),
            grad_values.reshape(row_count, kv_width).astype(BF16),
        ],
        1,
    )
    grad_qkv = jnp.einsum("td,tq->dq", normed, qkv_back, preferred_element_type=F32)
    grad_normed = jnp.einsum("tq,dq->td", qkv_back, qkv_full, preferred_element_type=F32)
    grad_input_norm, grad_attention = norm_pullback(grad_normed)
    input_grad = grad_middle + grad_input_norm

    gains = jnp.concatenate([grad_attention, grad_feed, grad_query_gain, grad_key_gain])
    gains = jnp.pad(gains, (0, 24 * 128 - gains.shape[0])).reshape(24, 128)
    grads = [grad.astype(BF16) for grad in (grad_qkv, grad_out, grad_gu, grad_down)]
    *reduced, gain_sums = reduce_grads(grads, gains, n, unit)
    shards = [part.astype(F32) for part in unpacked(reduced, unit)]
    moments_next = [MOMENTUM * moment + grad_shard for moment, grad_shard in zip(moments, shards)]
    nesterov = packed(
        [
            (grad_shard + MOMENTUM * moment_next).astype(BF16)
            for grad_shard, moment_next in zip(shards, moments_next)
        ]
    )
    orth = unpacked(orthogonalize_all(nesterov, n, unit), unit)
    new_weights = [
        matrix * (1.0 - LEARN_RATE * WEIGHT_DECAY) - LEARN_RATE * part.astype(F32)
        for matrix, part in zip(owned, orth)
    ]
    gain_sums = gain_sums.reshape(-1)
    norm_grads = gain_sums[: 2 * unit].reshape(2, unit)
    head_grads = gain_sums[2 * unit : 2 * unit + 2 * HEAD_DIM].reshape(2, HEAD_DIM)
    return (block_output, input_grad, norm_grads, head_grads, *new_weights, *moments_next)


def solution(mesh):
    tokens, owned = P(("rep", "own"), None), P("own", None)
    return jax.shard_map(
        body,
        mesh=mesh,
        in_specs=(tokens,) * 3 + (P(),) * 4 + (owned,) * 14,
        out_specs=(tokens,) * 2 + (P(),) * 2 + (owned,) * 14,
        check_vma=False,
    )
```

```python
import functools

import jax
import jax.numpy as jnp
from jax import lax
from jax.experimental import pallas as pl
from jax.experimental.pallas import tpu as pltpu
from jax.sharding import PartitionSpec as P

HEADS = 16
KV_HEADS = 8
HEAD_DIM = 128
NS_STEPS = 5

EPSILON = 1e-06
ROPE_BASE = 1000000.0
MOMENTUM = 0.95
LEARN_RATE = 0.8
WEIGHT_DECAY = 0.01
NEWTON_A = 3.4445
NEWTON_B = -4.775
NEWTON_C = 2.0315

BF16 = jnp.bfloat16
F32 = jnp.float32
MESH = pl.DeviceIdType.MESH
ANY = pl.BlockSpec(memory_space=pltpu.HBM)

QKV, OUT, GU, DOWN = range(4)


def rms_scale(values, gain_vector):
    return values * lax.rsqrt(jnp.mean(values * values, -1, keepdims=True) + EPSILON) * gain_vector


def rotate(values, cosine_table, sine_table):
    half_dim = values.shape[-1] // 2
    first_half = values[..., :half_dim]
    second_half = values[..., half_dim:]
    return jnp.concatenate(
        [
            first_half * cosine_table - second_half * sine_table,
            second_half * cosine_table + first_half * sine_table,
        ],
        -1,
    )


def head_side(raw_value, gain_vector, cosine_table, sine_table):
    shaped = raw_value.reshape(raw_value.shape[0], -1, HEAD_DIM)
    return rotate(rms_scale(shaped, gain_vector), cosine_table, sine_table)


def swiglu(gate_value, up_value):
    return gate_value * jax.nn.sigmoid(gate_value) * up_value


def segments(lengths, row_count):
    seq_ends = jnp.cumsum(lengths)
    seq_starts = seq_ends - lengths
    row_ids = jnp.arange(row_count, dtype=jnp.int32)
    segment_ids = jnp.sum((row_ids[:, None] >= seq_ends[None, :]).astype(jnp.int32), 1)
    slot_ids = jnp.arange(lengths.shape[0], dtype=jnp.int32)
    row_starts = jnp.sum(
        jnp.where(segment_ids[:, None] == slot_ids[None, :], seq_starts[None, :], 0), 1
    )
    return (segment_ids, row_ids - row_starts)


def rope_tables(positions):
    inverse = ROPE_BASE ** (-jnp.arange(0, HEAD_DIM, 2, dtype=jnp.float32) / HEAD_DIM)
    angles = positions.astype(jnp.float32)[:, None] * inverse[None, :]
    return (jnp.cos(angles)[:, None, :], jnp.sin(angles)[:, None, :])


class Place:
    def __init__(self, n):
        self.n = n
        self.rep = lax.axis_index("rep")
        self.own = lax.axis_index("own")
        self.x = self.rep // 2
        self.core = self.rep % 2
        odd, pair = self.own % 2, self.own // 2
        self.ring = pair * (1 - odd) + odd * (n - 1 - pair)

    def own_at(self, ring):
        odd = ring // (self.n // 2)
        return 2 * (ring * (1 - odd) + odd * (self.n - 1 - ring)) + odd

    def shard(self, distance):
        return self.own_at(lax.rem(self.ring + distance + self.n, self.n))

    def ring_neighbour(self, way):
        return (self.rep, self.shard(way))

    @property
    def core_partner(self):
        return (self.x * 2 + 1 - self.core, self.own)

    @property
    def x_partner(self):
        return ((1 - self.x) * 2 + self.core, self.own)


def greet(devices):
    barrier = pltpu.get_barrier_semaphore()
    for device in devices:
        pl.semaphore_signal(barrier, inc=1, device_id=device, device_id_type=MESH)
    pl.semaphore_wait(barrier, len(devices))


def remote(src, dst, send, recv, device):
    return pltpu.make_async_remote_copy(
        src_ref=src, dst_ref=dst, send_sem=send, recv_sem=recv, device_id=device, device_id_type=MESH
    )


def hops(n, way, kind):
    return n // 2 if (way == 0) == (kind == 0) else n // 2 - 1


def side_pieces(unit):
    sides = ([(QKV, 0, 4 * unit)], [(GU, 0, 4 * unit)])
    both = [(GU, 4 * unit, 2 * unit), (OUT, 0, unit), (DOWN, 0, unit)]
    return sides, both


def gather_kernel(n, rows, unit, *refs):
    shards, wholes = refs[:4], refs[4:8]
    local, ring_send, ring_recv, x_send, x_recv, core_send, core_recv = refs[8:]
    place = Place(n)
    cw, ccw = place.ring_neighbour(1), place.ring_neighbour(-1)
    greet([cw, ccw, place.core_partner, place.x_partner])
    sides, both = side_pieces(unit)

    def region(piece, own_index):
        array, first, columns = piece
        half = rows[array] // 2
        start = pl.multiple_of(own_index * rows[array] + place.core * half, half)
        return wholes[array].at[pl.ds(start, half), pl.ds(first, columns)]

    def shard_half(piece):
        array, first, columns = piece
        half = rows[array] // 2
        start = pl.multiple_of(place.core * half, half)
        return shards[array].at[pl.ds(start, half), pl.ds(first, columns)]

    def by_kind(kind, act):
        if kind == 1:
            act(both)
        else:
            for side in range(2):
                pl.when(place.x == side)(functools.partial(act, sides[side]))

    locals_ = []
    for array in range(4):
        start = pl.multiple_of(place.own * rows[array], rows[array])
        copy = pltpu.make_async_copy(
            shards[array], wholes[array].at[pl.ds(start, rows[array])], local.at[array]
        )
        copy.start()
        locals_.append(copy)

    top = n // 2
    ways = ((1, cw), (-1, ccw))

    def ring_copies(pieces, way, kind, hop, distance):
        slot = ((way * 2 + kind) * top + hop - 1) * 3
        step, target = ways[way]
        own_index = place.shard(distance)
        return [
            remote(
                shard_half(piece) if distance == 0 else region(piece, own_index),
                region(piece, own_index),
                ring_send.at[slot + i],
                ring_recv.at[slot + i],
                target,
            )
            for i, piece in enumerate(pieces)
        ]

    def core_copies(pieces, slot, distance):
        own_index = place.shard(distance)
        return [
            remote(
                region(piece, own_index),
                region(piece, own_index),
                core_send.at[slot + i],
                core_recv.at[slot + i],
                place.core_partner,
            )
            for i, piece in enumerate(pieces)
        ]

    def x_copies(pieces, way, hop, distance):
        slot = way * top + hop - 1
        own_index = place.shard(distance)
        return [
            remote(
                region(piece, own_index),
                region(piece, own_index),
                x_send.at[slot],
                x_recv.at[slot],
                place.x_partner,
            )
            for piece in pieces
        ]

    ring_slots = 2 * 2 * top * 3

    def start(copies):
        for copy in copies:
            copy.start()

    def wait_recv(copies):
        for copy in copies:
            copy.wait_recv()

    def wait_send(copies):
        for copy in copies:
            copy.wait_send()

    def other_side(act):
        for side in range(2):
            pl.when(place.x == 1 - side)(functools.partial(act, sides[side]))

    for kind in range(2):
        for way in range(2):
            by_kind(kind, lambda pieces: start(ring_copies(pieces, way, kind, 1, 0)))

    def take_x(way, hop):
        distance = -ways[way][0] * hop

        def act(pieces):
            wait_recv(x_copies(pieces, way, hop, distance))
            start(core_copies(pieces, ring_slots + way * top + hop - 1, distance))

        other_side(act)

    for hop in range(1, top + 1):
        for kind in range(2):
            for way in range(2):
                if hop > hops(n, way, kind):
                    continue
                distance = -ways[way][0] * hop

                def act(pieces):
                    wait_recv(ring_copies(pieces, way, kind, hop, distance))
                    if hop < hops(n, way, kind):
                        start(ring_copies(pieces, way, kind, hop + 1, distance))
                    if kind == 0:
                        start(x_copies(pieces, way, hop, distance))
                    start(core_copies(pieces, ((way * 2 + kind) * top + hop - 1) * 3, distance))

                by_kind(kind, act)
        if hop > 1:
            for way in range(2):
                if hop - 1 <= hops(n, way, 0):
                    take_x(way, hop - 1)
    for way in range(2):
        if top <= hops(n, way, 0):
            take_x(way, top)

    for copy in locals_:
        copy.wait()
    for hop in range(1, top + 1):
        for kind in range(2):
            for way in range(2):
                if hop > hops(n, way, kind):
                    continue
                distance = -ways[way][0] * hop
                slot = ((way * 2 + kind) * top + hop - 1) * 3

                def act(pieces):
                    wait_send(ring_copies(pieces, way, kind, hop, distance + ways[way][0]))
                    core = core_copies(pieces, slot, distance)
                    wait_send(core)
                    wait_recv(core)
                    if kind == 0:
                        wait_send(x_copies(pieces, way, hop, distance))

                by_kind(kind, act)
                if kind == 0:

                    def act_other(pieces):
                        core = core_copies(pieces, ring_slots + way * top + hop - 1, distance)
                        wait_send(core)
                        wait_recv(core)

                    other_side(act_other)


def gather_weights(shards, n, unit):
    rows = [shard.shape[0] for shard in shards]
    top = n // 2
    dma = pltpu.SemaphoreType.DMA
    return pl.pallas_call(
        functools.partial(gather_kernel, n, rows, unit),
        out_shape=[
            jax.ShapeDtypeStruct((n * shard.shape[0], shard.shape[1]), BF16) for shard in shards
        ],
        in_specs=[ANY] * 4,
        out_specs=[ANY] * 4,
        scratch_shapes=[
            dma((4,)),
            dma((12 * top,)),
            dma((12 * top,)),
            dma((2 * top,)),
            dma((2 * top,)),
            dma((14 * top,)),
            dma((14 * top,)),
        ],
        compiler_params=pltpu.CompilerParams(collective_id=0, has_side_effects=True),
    )(*shards)


PHASES = ((DOWN, 3, False), (GU, 3, True), (OUT, 2, False), (QKV, 2, True))

OWNERS = (
    (3, 0, 1, False, 1, 2),
    (3, 1, 1, False, 1, 6),
    (3, 0, 2, False, 0, 2),
    (2, 0, 2, True, 1, 5),
    (1, 0, 3, False, 0, 5),
    (1, 0, 3, False, 1, 1),
    (0, 0, 3, True, 0, 1),
)
KEY, VALUE, QUERY, OUTM, GATE, UP, DOWNM = range(7)
RETURNS = (OUTM, KEY, VALUE, DOWNM, GATE, UP, QUERY)
MOMENTS = {0: ((6, 6),), 1: ((4,), (5,)), 2: ((3, 3),), 3: ((0,), (1, 2))}
TILE_SLOTS = 3
X_SLOTS = 3


def stage_order(n, order):
    top = n // 2
    ring = (top - 0.5) / n
    at = []
    for i in range(n):
        at.append((3 * i - 6.0, ("x", 1, i)))
        at.append((3 * n + 2 * i - 4.0, ("x", 3, i)))
        at.append((1 + 3 * ring * i, ("ring", 0, i)))
        at.append((3 * (i + 1) + 1.0, ("ring", 1, i)))
        at.append((3 * n + 2 + 2 * ring * i, ("ring", 2, i)))
        at.append((3 * n + 3 + max(2.0 * i, 2 * ring * (n + i)), ("ring", 3, i)))
    at.append((1 + 3 * ring * n + 9, ("final", 0, 0)))
    at.append((3 * n + 2 + 2 * ring * n + 6, ("final", 2, 0)))
    return [stage for _, stage in sorted(at)]


class Rows:
    def __init__(self):
        self.next = 0

    def take(self, rows):
        start = self.next
        self.next += rows
        return start


def layout(n, unit):
    base = unit // n
    top = n // 2
    sums = Rows()
    place = {
        "own": [sums.take(3 * base) for _ in range(TILE_SLOTS)],
        "land": [sums.take(3 * base) for _ in range(TILE_SLOTS)],
        "x_out": [sums.take(3 * base) for _ in range(X_SLOTS)],
        "x_in": {p: [sums.take(PHASES[p][1] * base) for _ in range(n)] for p in (1, 3)},
        "ring": [
            [[sums.take(PHASES[p][1] * base) for _ in range(top)] for _ in range(2)] for p in (0, 1)
        ],
    }
    place["ring"] += place["ring"]
    for name in ("far", "grad", "ahead"):
        place[name] = [sums.take(units * base) for _, units, _ in PHASES]
    for name in ("part", "other"):
        place[name] = [0 if split else sums.take(units * base) for _, units, split in PHASES]
    newton = Rows()
    place["high"] = [newton.take(3 * unit) for _ in range(2)]
    place["rest"] = newton.take(3 * unit)
    place["poly"] = [newton.take(unit) for _ in range(2)]
    return place, max(sums.next, newton.next)


def update_kernel(n, unit, *refs):
    grads, moments, gains_in = refs[:4], refs[4:11], refs[11]
    outs, orths, lands, gains_out = refs[12:16], refs[16:20], refs[20:24], refs[24]
    (
        pool, gram, squares, gain_mine, gain_core, gain_x, gain_all,
        land_send, land_recv, tile_sem, x_send, x_recv, ring_send, ring_recv, part_send, part_recv,
        moment_sem, grad_local, grad_send, grad_recv, in_send, in_recv,
        out_send, out_recv, pass_send, pass_recv, gain_send, gain_recv,
    ) = refs[25:]
    place = Place(n)
    base = unit // n
    top = n // 2
    at, _ = layout(n, unit)
    cw, ccw = place.ring_neighbour(1), place.ring_neighbour(-1)
    ways = ((1, cw), (-1, ccw))
    side = [(place.x * 2 + core, lax.rem(place.own + k, n)) for k in range(1, n) for core in range(2)]
    greet(side + [place.core_partner, place.x_partner])
    order = [top]
    for distance in range(top - 1, 0, -1):
        order += [distance, -distance]
    order.append(0)
    stages = stage_order(n, order)
    moment = gram
    height = [units * base for _, units, _ in PHASES]
    owners = [
        (xs * 2 + 1, place.own_at(spot * n // 8)) for _, _, _, _, xs, spot in OWNERS
    ]
    here = place.rep * n + place.own
    is_owner = [here == rep * n + own for rep, own in owners]

    def rows(start, size):
        if isinstance(start, int):
            return pl.ds(start, size)
        return pl.ds(pl.multiple_of(start, size), size)

    def block(start, size):
        return pool.at[rows(start, size)]

    def first_column(phase, x):
        return x * PHASES[phase][1] * unit

    def parts(phase, x):
        _, units, split = PHASES[phase]
        if not split:
            return [(pl.ds(0, unit), 0, units * base)]
        first = first_column(phase, x)
        return [
            (pl.ds(pl.multiple_of(first + k * unit, unit), unit), k * base, base)
            for k in range(units)
        ]

    def shard_rows(phase, own_index):
        size = height[phase] if not PHASES[phase][2] else base
        return rows(own_index * size, size)

    def land_copy(phase, i):
        array = PHASES[phase][0]
        span = shard_rows(phase, place.shard(order[i]))
        return remote(
            grads[array].at[span], lands[array].at[span],
            land_send.at[phase * n + i], land_recv.at[phase * n + i], place.core_partner,
        )

    def x_copy(phase, i):
        index = (phase // 2) * n + i
        slot = at["x_out"][index % X_SLOTS]
        return remote(
            block(slot, height[phase]), block(at["x_in"][phase][i], height[phase]),
            x_send.at[index], x_recv.at[index], place.x_partner,
        )

    def ring_copy(phase, way, distance, source, part):
        size = height[phase]
        target = at["ring"][phase][way][distance - 1]
        if part is not None:
            size //= 2
            source, target = source + part * size, target + part * size
        index = (phase * 2 + way) * top + distance - 1
        return remote(
            block(source, size), block(target, size), ring_send.at[index], ring_recv.at[index],
            ways[way][1],
        )

    def ring_out(phase, distance):
        if distance == 0:
            return []
        if distance == top:
            return [ring_copy(phase, way, top, at["far"][phase], way) for way in range(2)]
        way = 0 if distance > 0 else 1
        far = abs(distance)
        return [ring_copy(phase, way, far, at["ring"][phase][way][far], None)]

    def part_copy(phase):
        return remote(
            block(at["part"][phase], height[phase]), block(at["other"][phase], height[phase]),
            part_send.at[phase // 2], part_recv.at[phase // 2], place.x_partner,
        )

    def gain_copy(src, dst, slot, device):
        return remote(src, dst, gain_send.at[slot], gain_recv.at[slot], device)

    def gain_core_copy():
        return gain_copy(gain_mine, gain_core, 0, place.core_partner)

    def gain_x_copy():
        return gain_copy(gain_core, gain_x, 1, place.x_partner)

    def gain_back_copy():
        return gain_copy(gain_mine, gain_x, 2, place.core_partner)

    def gain_ring(way, hop, distance):
        spot = gain_all.at[place.shard(distance)]
        return gain_copy(spot, spot, 3 + way * top + hop - 1, ways[way][1])

    def grad_place(phase, x, which):
        array = PHASES[phase][0]
        return [
            (outs[array].at[:, columns], block(at[which][phase] + first, size))
            for columns, first, size in parts(phase, x)
        ]

    def grad_span(phase, x):
        array, units, split = PHASES[phase]
        if not split:
            return outs[array]
        first = pl.multiple_of(first_column(phase, x), unit)
        return outs[array].at[:, pl.ds(first, units * unit)]

    def grad_sent(phase, to, device, x):
        span = grad_span(phase, x)
        return remote(span, span, grad_send.at[phase, to], grad_recv.at[phase, to], device)

    def matrix_rows(matrix, own_index):
        phase, first, units, tall, _, _ = OWNERS[matrix]
        if tall:
            return [(0, own_index * units * base, units * base)]
        return [
            ((first + k) * base, k * unit + own_index * base, base) for k in range(units)
        ]

    def matrix_span(matrix):
        phase, first, units, tall, xs, _ = OWNERS[matrix]
        array = PHASES[phase][0]
        if tall:
            return orths[array]
        start = (xs * PHASES[phase][1] + first) * unit
        return orths[array].at[:, pl.ds(start, units * unit)]

    def matrix_parts(matrix):
        phase, first, units, tall, xs, _ = OWNERS[matrix]
        array = PHASES[phase][0]
        if tall:
            return [orths[array]]
        start = (xs * PHASES[phase][1] + first) * unit
        return [orths[array].at[:, pl.ds(start + k * unit, unit)] for k in range(units)]

    def handed(matrix, to, device):
        span = matrix_span(matrix)
        return remote(span, span, pass_send.at[matrix, to], pass_recv.at[matrix, to], device)

    def answered(matrix, target):
        span = matrix_span(matrix)
        return remote(
            span, span, out_send.at[target], out_recv.at[matrix], (place.x * 2, target)
        )

    def summed(pieces, size, store):
        step = base // 2

        def body(k, carry):
            shift = k * step
            total = None
            for start in pieces:
                value = pool[rows_at(start, shift, step), :].astype(F32)
                total = value if total is None else total + value
            store(shift, step, total)
            return carry

        lax.fori_loop(0, size // step, body, 0)

    def rows_at(start, shift, step):
        return pl.ds(pl.multiple_of(start + shift, step), step)

    def keep(start):
        def store(shift, step, total):
            pool[rows_at(start, shift, step), :] = total.astype(BF16)

        return store

    def tile_copies(k):
        kind, phase, i = stages[k]
        slot = k_slot[k]
        x = place.x if kind == "ring" else 1 - place.x
        array = PHASES[phase][0]
        span = shard_rows(phase, place.shard(order[i]))
        copies = []
        for which, (name, source) in enumerate((("own", grads), ("land", lands))):
            for columns, first, size in parts(phase, x):
                copies.append(
                    pltpu.make_async_copy(
                        source[array].at[span, columns], block(at[name][slot] + first, size),
                        tile_sem.at[slot, which],
                    )
                )
        return copies

    tiled = [k for k, stage in enumerate(stages) if stage[0] != "final"]
    k_slot = {k: index % TILE_SLOTS for index, k in enumerate(tiled)}

    def prefetch(index, seen):
        if index >= len(tiled):
            return
        k = tiled[index]
        _, phase, i = stages[k]
        if (phase, i) not in seen:
            seen.add((phase, i))
            land_copy(phase, i).wait_recv()
        for copy in tile_copies(k):
            copy.start()

    def wait_tiles(k):
        _, phase, _ = stages[k]
        slot = k_slot[k]
        for which, name in enumerate(("own", "land")):
            span = block(at[name][slot], height[phase])
            pltpu.make_async_copy(span, span, tile_sem.at[slot, which]).wait()

    def moment_copies(phase, act):
        for x in range(2):

            @pl.when(place.x == x)
            def _():
                sources = MOMENTS[phase][x if PHASES[phase][2] else 0]
                if not PHASES[phase][2]:
                    act(moments[sources[0]], moment.at[pl.ds(0, height[phase])])
                    return
                each = PHASES[phase][1] // len(sources)
                for s, source in enumerate(sources):
                    for k in range(each):
                        act(
                            moments[source].at[:, pl.ds(k * unit, unit)],
                            moment.at[pl.ds((s * each + k) * base, base)],
                        )

    def load_moment(phase):
        moment_copies(
            phase, lambda src, dst: pltpu.make_async_copy(src, dst, moment_sem.at[phase]).start()
        )

    def finish(phase, pieces):
        span = moment.at[pl.ds(0, height[phase])]
        pltpu.make_async_copy(span, span, moment_sem.at[phase]).wait()

        def store(shift, step, total):
            pool[rows_at(at["grad"][phase], shift, step), :] = total.astype(BF16)
            ahead = (1.0 + MOMENTUM) * total + MOMENTUM**2 * moment[rows_at(0, shift, step), :]
            pool[rows_at(at["ahead"][phase], shift, step), :] = ahead.astype(BF16)

        summed(pieces, height[phase], store)
        for matrix, (its_phase, _, _, _, xs, _) in enumerate(OWNERS):
            if its_phase != phase:
                continue

            @pl.when(place.x == xs)
            def _():
                for source, target, size in matrix_rows(matrix, place.own):
                    remote(
                        block(at["ahead"][phase] + source, size), block(at["high"][1] + target, size),
                        in_send.at[matrix], in_recv.at[place.own], owners[matrix],
                    ).start()

        for target, source in grad_place(phase, place.x, "grad"):
            pltpu.make_async_copy(source, target, grad_local.at[phase]).start()
            remote(
                source, target, grad_send.at[phase, 0], grad_recv.at[phase, 0], place.core_partner
            ).start()
            if PHASES[phase][2]:
                remote(
                    source, target, grad_send.at[phase, 1], grad_recv.at[phase, 1], place.x_partner
                ).start()
        after = {0: 1, 1: 2, 2: 3, 3: None}[phase]
        if after is not None:
            load_moment(after)

    def stage_x(k, phase, i):
        wait_tiles(k)
        index = (phase // 2) * n + i
        if index >= X_SLOTS:
            before = index - X_SLOTS
            x_copy(1 if before < n else 3, before % n).wait_send()
        slot = k_slot[k]
        summed(
            [at["own"][slot], at["land"][slot]], height[phase], keep(at["x_out"][index % X_SLOTS])
        )
        x_copy(phase, i).start()

    def stage_ring(k, phase, i):
        distance = order[i]
        slot = k_slot[k]
        wait_tiles(k)
        pieces = [at["own"][slot], at["land"][slot]]
        if PHASES[phase][2]:
            x_copy(phase, i).wait_recv()
            pieces.append(at["x_in"][phase][i])
        size = height[phase]
        if distance == top:
            summed(pieces, size, keep(at["far"][phase]))
        elif distance == 0:
            for way in range(2):
                ring_copy(phase, way, 1, at["ring"][phase][way][0], None).wait_recv()
                pieces.append(at["ring"][phase][way][0])
            if PHASES[phase][2]:
                finish(phase, pieces)
            else:
                summed(pieces, size, keep(at["part"][phase]))
                part_copy(phase).start()
        else:
            way = 0 if distance > 0 else 1
            far = abs(distance)
            held = at["ring"][phase][way][far]
            if far + 1 == top:
                ring_copy(phase, way, top, at["far"][phase], way).wait_recv()
                mid = size // 2
                for part in range(2):
                    starts = [start + part * mid for start in pieces]
                    if part == way:
                        starts.append(held + part * mid)
                    summed(starts, mid, keep(held + part * mid))
            else:
                ring_copy(phase, way, far + 1, held, None).wait_recv()
                summed(pieces + [held], size, keep(held))
        if abs(distance) == 1 and 0 < phase < 3:
            ring_sent(phase - 1)
        for copy in ring_out(phase, distance):
            copy.start()

    def ring_sent(phase):
        if phase not in ring_waited:
            ring_waited.add(phase)
            for distance in order:
                for copy in ring_out(phase, distance):
                    copy.wait_send()

    ring_waited = set()

    def gain_stage(hop):
        if hop == 0:
            gain_core_copy().wait_recv()
            gain_core[...] = gain_mine[...] + gain_core[...]
            gain_x_copy().start()
            return
        if hop == 1:
            gain_x_copy().wait_recv()
            gain_all[place.own] = gain_core[...] + gain_x[...]
            for way in range(2):
                gain_ring(way, 1, 0).start()
        for way in range(2):
            if 1 < hop <= hops(n, way, 0) + 1:
                distance = -ways[way][0] * (hop - 1)
                gain_ring(way, hop - 1, distance).wait_recv()
                if hop <= hops(n, way, 0):
                    gain_ring(way, hop, distance).start()

    gain_mine[...] = gains_in[...]

    @pl.when(place.core == 0)
    def _():
        load_moment(0)
        seen = set()
        for index in range(TILE_SLOTS - 1):
            prefetch(index, seen)
        done = 0
        hop = 0
        for k, (kind, phase, i) in enumerate(stages):
            if kind == "final":
                part_copy(phase).wait_recv()
                finish(phase, [at["part"][phase], at["other"][phase]])
                continue
            prefetch(done + TILE_SLOTS - 1, seen)
            done += 1
            if kind == "x":
                stage_x(k, phase, i)
            else:
                stage_ring(k, phase, i)
            if done % 3 == 0 and hop <= top + 1:
                gain_stage(hop)
                hop += 1

        total = gain_all[0]
        for k in range(1, n):
            total = total + gain_all[k]
        gains_out[...] = total
        gain_mine[...] = total
        gain_back_copy().start()

        for phase in (1, 3):
            grad_sent(phase, 1, place.x_partner, 1 - place.x).wait_recv()
            grad_sent(phase, 2, place.core_partner, 1 - place.x).start()

        for matrix in RETURNS:
            xs = OWNERS[matrix][4]

            @pl.when(place.x == xs)
            def _():
                answered(matrix, place.own).wait_recv()
                handed(matrix, 0, place.x_partner).start()
                handed(matrix, 1, place.core_partner).start()

            @pl.when(place.x != xs)
            def _():
                handed(matrix, 0, place.x_partner).wait_recv()
                handed(matrix, 1, place.core_partner).start()

        for matrix, (phase, _, units, _, xs, _) in enumerate(OWNERS):
            handed(matrix, 1, place.core_partner).wait_send()

            @pl.when(place.x == xs)
            def _():
                handed(matrix, 0, place.x_partner).wait_send()
                span = block(at["high"][1], units * base)
                remote(
                    span, span, in_send.at[matrix], in_recv.at[0], place.core_partner
                ).wait_send()

        for phase, (_, _, split) in enumerate(PHASES):
            span = block(at["grad"][phase], height[phase])
            pltpu.make_async_copy(span, span, grad_local.at[phase]).wait()
            remote(
                span, span, grad_send.at[phase, 0], grad_recv.at[phase, 0], place.core_partner
            ).wait_send()
            if split:
                remote(
                    span, span, grad_send.at[phase, 1], grad_recv.at[phase, 1], place.x_partner
                ).wait_send()
                grad_sent(phase, 2, place.core_partner, 1 - place.x).wait_send()
            else:
                part_copy(phase).wait_send()
            ring_sent(phase)
        for index in range(2 * n - X_SLOTS, 2 * n):
            x_copy(1 if index < n else 3, index % n).wait_send()
        gain_x_copy().wait_send()
        gain_back_copy().wait_send()
        for way in range(2):
            for h in range(1, hops(n, way, 0) + 1):
                gain_ring(way, h, -ways[way][0] * (h - 1)).wait_send()

    @pl.when(place.core == 1)
    def _():
        gain_core_copy().start()
        needed = []
        for kind, phase, i in stages:
            if kind != "final" and (phase, i) not in needed:
                needed.append((phase, i))
        ahead = 4
        for index, (phase, i) in enumerate(needed):
            if index >= ahead:
                land_copy(*needed[index - ahead]).wait_send()
            land_copy(phase, i).start()
        for phase, i in needed[-ahead:]:
            land_copy(phase, i).wait_send()
        newton_part(n, unit, place, pool, gram, squares, at, is_owner, in_recv)
        for matrix, (_, _, units, tall, _, _) in enumerate(OWNERS):

            @pl.when(is_owner[matrix])
            def _():
                final = at["high"][1 - NS_STEPS % 2 if tall else NS_STEPS % 2]

                def send(k, carry):
                    target = lax.rem(place.own + k, n)
                    for part, (_, row, size) in zip(matrix_parts(matrix), matrix_rows(matrix, target)):
                        remote(
                            block(final + row, size), part, out_send.at[target], out_recv.at[matrix],
                            (place.x * 2, target),
                        ).start()
                    return carry

                lax.fori_loop(0, n, send, 0)

                def sent(k, carry):
                    answered(matrix, lax.rem(place.own + k, n)).wait_send()
                    return carry

                lax.fori_loop(0, n, sent, 0)

        gain_core_copy().wait_send()
        gain_back_copy().wait_recv()
        gains_out[...] = gain_x[...]
        for phase, (_, _, split) in enumerate(PHASES):
            grad_sent(phase, 0, place.core_partner, place.x).wait_recv()
            if split:
                grad_sent(phase, 2, place.core_partner, 1 - place.x).wait_recv()
        for matrix in RETURNS:
            handed(matrix, 1, place.core_partner).wait_recv()


def newton_part(n, unit, place, pool, gram, squares, at, is_owner, in_recv):
    base = unit // n
    tile = unit // 2
    small = min(256, unit // 2)
    per = unit // small
    count, tall = 0, 0
    for mine, (_, _, units, lies_tall, _, _) in zip(is_owner, OWNERS):
        count = count + units * mine.astype(jnp.int32)
        tall = tall + int(lies_tall) * mine.astype(jnp.int32)
    high, rest, poly = at["high"], at["rest"], at["poly"]

    def rows(start, size):
        return pl.ds(pl.multiple_of(start, size), size)

    for matrix, (_, _, units, *_) in enumerate(OWNERS):

        @pl.when(is_owner[matrix])
        def _():
            span = pool.at[pl.ds(high[1], units * base)]
            for own_index in range(n):
                remote(
                    span, span, in_recv.at[own_index], in_recv.at[own_index], place.core_partner
                ).wait_recv()

    @pl.when(count > 0)
    def _():
        squares[...] = jnp.zeros_like(squares)

        def square(k, carry):
            part = pool[rows(high[1] + k * small, small), :].astype(F32)
            squares[...] += jnp.sum((part * part).reshape(small // 8, 8, unit), 0)
            return carry

        lax.fori_loop(0, count * per, square, 0)
        total = jnp.sum(jnp.sum(squares[...], 1, keepdims=True), 0, keepdims=True)
        inverse = 1.0 / (jnp.sqrt(total) + 1e-07)

        def keep(span, shift, columns, value, to):
            low = value.astype(BF16)
            pool[rows(to + shift, span), columns] = low
            pool[rows(rest + shift, span), columns] = (value - low.astype(F32)).astype(BF16)

        @pl.when(tall == 0)
        def _():
            def scale(k, carry):
                part = pool[rows(high[1] + k * small, small), :].astype(F32)
                keep(small, k * small, slice(None), part * inverse, high[0])
                return carry

            lax.fori_loop(0, count * per, scale, 0)

        @pl.when(tall == 1)
        def _():
            def scale(k, carry):
                block, row = k // per, k % per
                for column in range(per):
                    part = pool[
                        rows(high[1] + k * small, small), pl.ds(column * small, small)
                    ].astype(F32)
                    keep(
                        small, block * unit + column * small, rows(row * small, small),
                        (part * inverse).T, high[0],
                    )
                return carry

            lax.fori_loop(0, count * per, scale, 0)

        def newton(step, carry):
            even = step % 2
            now = high[0] + even * (high[1] - high[0])
            later = high[1] - even * (high[1] - high[0])

            def gram_part(block, upper):
                left = pool[rows(now + block * unit + upper * tile, tile), :]
                right = (
                    pool[rows(now + block * unit, unit), :]
                    if upper == 0
                    else pool[rows(now + block * unit + tile, tile), :]
                )
                return lax.dot_general(
                    left, right, (((1,), (1,)), ((), ())), preferred_element_type=F32
                )

            gram[:tile, :] = gram_part(0, 0)
            gram[tile:, tile:] = gram_part(0, 1)

            def more(block, carry):
                gram[:tile, :] += gram_part(block, 0)
                gram[tile:, tile:] += gram_part(block, 1)
                return carry

            lax.fori_loop(1, count, more, 0)
            pool[pl.ds(poly[0], tile), :] = gram[:tile, :].astype(BF16)
            pool[pl.ds(poly[0] + tile, tile), tile:] = gram[tile:, tile:].astype(BF16)
            pool[pl.ds(poly[0] + tile, tile), :tile] = gram[:tile, tile:].T.astype(BF16)

            def squared(left, right):
                part = pool[pl.ds(poly[0] + left, tile), right:]
                product = lax.dot_general(
                    pool[pl.ds(poly[0] + left, tile), :], pool[pl.ds(poly[0], unit), right:],
                    (((1,), (0,)), ((), ())), preferred_element_type=F32,
                )
                return NEWTON_B * part.astype(F32) + NEWTON_C * product

            upper = squared(0, 0)
            pool[pl.ds(poly[1], tile), :] = upper.astype(BF16)
            pool[pl.ds(poly[1] + tile, tile), :tile] = upper[:, tile:].T.astype(BF16)
            pool[pl.ds(poly[1] + tile, tile), tile:] = squared(tile, tile).astype(BF16)

            def advance(k, carry):
                block, i = k // 2, k % 2
                product = jnp.dot(
                    pool[rows(poly[1] + i * tile, tile), :],
                    pool[rows(now + block * unit, unit), :],
                    preferred_element_type=F32,
                )
                exact = pool[rows(now + k * tile, tile), :].astype(F32) + pool[
                    rows(rest + k * tile, tile), :
                ].astype(F32)
                keep(tile, k * tile, slice(None), NEWTON_A * exact + product, later)
                return carry

            lax.fori_loop(0, count * 2, advance, 0)
            return carry

        lax.fori_loop(0, NS_STEPS, newton, 0)

        @pl.when(tall == 1)
        def _():
            last, free = high[NS_STEPS % 2], high[1 - NS_STEPS % 2]
            factor = jnp.sqrt(jnp.full((1, 1), count, jnp.int32).astype(F32))

            def lay(k, carry):
                block, row = k // per, k % per
                for column in range(per):
                    columns = pl.ds(column * small, small)
                    part = pool[rows(last + k * small, small), columns].astype(F32) + pool[
                        rows(rest + k * small, small), columns
                    ].astype(F32)
                    pool[
                        rows(free + block * unit + column * small, small), rows(row * small, small)
                    ] = (part * factor).T.astype(BF16)
                return carry

            lax.fori_loop(0, count * per, lay, 0)


def update_all(grads, moments, gains, n, unit):
    top = n // 2
    dma = pltpu.SemaphoreType.DMA
    vmem = pltpu.VMEM
    _, pool_rows = layout(n, unit)
    own = [jax.ShapeDtypeStruct((grad.shape[0] // n, grad.shape[1]), BF16) for grad in grads]
    whole = [jax.ShapeDtypeStruct(grad.shape, BF16) for grad in grads]
    in_vmem = pl.BlockSpec(memory_space=pltpu.VMEM)
    results = pl.pallas_call(
        functools.partial(update_kernel, n, unit),
        out_shape=own + own + whole + [jax.ShapeDtypeStruct(gains.shape, F32)],
        in_specs=[ANY] * 11 + [in_vmem],
        out_specs=[ANY] * 12 + [in_vmem],
        scratch_shapes=[
            vmem((pool_rows, unit), BF16),
            vmem((unit, unit), F32),
            vmem((8, unit), F32),
            vmem(gains.shape, F32),
            vmem(gains.shape, F32),
            vmem(gains.shape, F32),
            vmem((n,) + gains.shape, F32),
            dma((4 * n,)),
            dma((4 * n,)),
            dma((TILE_SLOTS, 2)),
            dma((2 * n,)),
            dma((2 * n,)),
            dma((8 * top,)),
            dma((8 * top,)),
            dma((2,)),
            dma((2,)),
            dma((4,)),
            dma((4,)),
            dma((4, 3)),
            dma((4, 3)),
            dma((7,)),
            dma((n,)),
            dma((n,)),
            dma((7,)),
            dma((7, 2)),
            dma((7, 2)),
            dma((3 + 2 * top,)),
            dma((3 + 2 * top,)),
        ],
        compiler_params=pltpu.CompilerParams(
            collective_id=1, has_side_effects=True, vmem_limit_bytes=56 * 2**20
        ),
    )(*grads, *moments, gains)
    return results[:4], results[4:8], results[12]


def packed(matrices):
    query, key, value, out, gate, up, down = matrices
    return (
        jnp.concatenate([query, key, value], 1),
        out,
        jnp.concatenate([gate, up], 1),
        down,
    )


def unpacked(arrays, unit):
    qkv, out, gate_up, down = arrays
    return (
        qkv[:, : 2 * unit],
        qkv[:, 2 * unit : 3 * unit],
        qkv[:, 3 * unit :],
        out,
        gate_up[:, : 3 * unit],
        gate_up[:, 3 * unit :],
        down,
    )


def body(
    layer_input,
    output_grad,
    lengths,
    attention_gain,
    feed_gain,
    query_gain,
    key_gain,
    query_weight,
    key_weight,
    value_weight,
    out_weight,
    gate_weight,
    up_weight,
    down_weight,
    query_moment,
    key_moment,
    value_moment,
    out_moment,
    gate_moment,
    up_moment,
    down_moment,
):
    owned = (
        query_weight, key_weight, value_weight, out_weight, gate_weight, up_weight, down_weight,
    )
    moments = (
        query_moment, key_moment, value_moment, out_moment, gate_moment, up_moment, down_moment,
    )
    n = lax.axis_size("own")
    unit = layer_input.shape[1]
    q_width, kv_width, ff = 2 * unit, unit, 3 * unit
    low_shards = packed([matrix.astype(BF16) for matrix in owned])
    qkv_full, out_full, gu_full, down_full = gather_weights(low_shards, n, unit)

    row_count = layer_input.shape[0]
    group_size = HEADS // KV_HEADS
    segment_ids, positions = segments(lengths[0], row_count)
    cosine_table, sine_table = rope_tables(positions)
    normed_value, norm_pullback = jax.vjp(rms_scale, layer_input, attention_gain)
    normed = normed_value.astype(BF16)
    raw = jnp.dot(normed, qkv_full, preferred_element_type=F32)
    query_raw = raw[:, :q_width]
    key_raw = raw[:, q_width : q_width + kv_width]
    value_raw = raw[:, q_width + kv_width :]
    query_rot, query_pullback = jax.vjp(
        lambda raw_value, gain_vector: head_side(raw_value, gain_vector, cosine_table, sine_table),
        query_raw,
        query_gain,
    )
    key_rot, key_pullback = jax.vjp(
        lambda raw_value, gain_vector: head_side(raw_value, gain_vector, cosine_table, sine_table),
        key_raw,
        key_gain,
    )
    queries = query_rot.astype(BF16).reshape(row_count, KV_HEADS, group_size, HEAD_DIM)
    keys = key_rot.astype(BF16)
    values = value_raw.astype(BF16).reshape(row_count, KV_HEADS, HEAD_DIM)
    row_ids = jnp.arange(row_count, dtype=jnp.int32)
    score_scale = HEAD_DIM ** (-0.5)
    raw_scores = (
        jnp.einsum("tkgd,skd->kgts", queries, keys, preferred_element_type=F32) * score_scale
    )
    allowed = (segment_ids[:, None] == segment_ids[None, :]) & (
        row_ids[:, None] >= row_ids[None, :]
    )
    masked = jnp.where(allowed, raw_scores, -1e30)
    maximum = jnp.max(masked, -1, keepdims=True)
    exponent = jnp.exp(masked - maximum)
    totals = jnp.sum(exponent, -1, keepdims=True)
    probs_full = exponent / totals
    probs_low = probs_full.astype(BF16)
    context = jnp.einsum("kgts,skd->tkgd", probs_low, values, preferred_element_type=F32)
    context = context.reshape(row_count, q_width).astype(BF16)
    middle = layer_input + jnp.dot(context, out_full, preferred_element_type=F32)
    hidden_value, middle_pullback = jax.vjp(rms_scale, middle, feed_gain)
    hidden = hidden_value.astype(BF16)
    gate_up = jnp.dot(hidden, gu_full, preferred_element_type=F32)
    activated_value, swiglu_pullback = jax.vjp(swiglu, gate_up[:, :ff], gate_up[:, ff:])
    activated = activated_value.astype(BF16)
    block_output = middle + jnp.dot(activated, down_full, preferred_element_type=F32)

    out_low = output_grad.astype(BF16)
    grad_down = jnp.einsum("tf,td->fd", activated, out_low, preferred_element_type=F32)
    grad_activated = jnp.einsum("td,fd->tf", out_low, down_full, preferred_element_type=F32)
    grad_gate_value, grad_up_value = swiglu_pullback(grad_activated)
    gu_back = jnp.concatenate([grad_gate_value.astype(BF16), grad_up_value.astype(BF16)], 1)
    grad_gu = jnp.einsum("td,tf->df", hidden, gu_back, preferred_element_type=F32)
    grad_hidden = jnp.einsum("tf,df->td", gu_back, gu_full, preferred_element_type=F32)
    grad_middle_norm, grad_feed = middle_pullback(grad_hidden)
    grad_middle = output_grad + grad_middle_norm
    attended_low = grad_middle.astype(BF16)
    grad_out = jnp.einsum("ti,td->id", context, attended_low, preferred_element_type=F32)
    grad_context = jnp.einsum("td,id->ti", attended_low, out_full, preferred_element_type=F32)
    grad_context = grad_context.astype(BF16).reshape(row_count, KV_HEADS, group_size, HEAD_DIM)
    grad_values = jnp.einsum("kgts,tkgd->skd", probs_low, grad_context, preferred_element_type=F32)
    grad_probs = jnp.einsum("tkgd,skd->kgts", grad_context, values, preferred_element_type=F32)
    grad_scores = probs_full * (
        grad_probs - jnp.sum(probs_full * grad_probs, -1, keepdims=True)
    )
    grad_scores = grad_scores.astype(BF16)
    grad_queries = (
        jnp.einsum("kgts,skd->tkgd", grad_scores, keys, preferred_element_type=F32) * score_scale
    )
    grad_keys = (
        jnp.einsum("kgts,tkgd->skd", grad_scores, queries, preferred_element_type=F32)
        * score_scale
    )
    grad_query_raw, grad_query_gain = query_pullback(
        grad_queries.reshape(row_count, HEADS, HEAD_DIM)
    )
    grad_key_raw, grad_key_gain = key_pullback(grad_keys)
    qkv_back = jnp.concatenate(
        [
            grad_query_raw.astype(BF16),
            grad_key_raw.astype(BF16),
            grad_values.reshape(row_count, kv_width).astype(BF16),
        ],
        1,
    )
    grad_qkv = jnp.einsum("td,tq->dq", normed, qkv_back, preferred_element_type=F32)
    grad_normed = jnp.einsum("tq,dq->td", qkv_back, qkv_full, preferred_element_type=F32)
    grad_input_norm, grad_attention = norm_pullback(grad_normed)
    input_grad = grad_middle + grad_input_norm

    gains = jnp.concatenate([grad_attention, grad_feed, grad_query_gain, grad_key_gain])
    gains = jnp.pad(gains, (0, 24 * 128 - gains.shape[0])).reshape(24, 128)
    grads = [grad.astype(BF16) for grad in (grad_qkv, grad_out, grad_gu, grad_down)]
    reduced, orth, gain_sums = update_all(grads, moments, gains, n, unit)
    moments_next = [
        MOMENTUM * moment + part.astype(F32) for moment, part in zip(moments, unpacked(reduced, unit))
    ]
    new_weights = [
        matrix * (1.0 - LEARN_RATE * WEIGHT_DECAY) - LEARN_RATE * part.astype(F32)
        for matrix, part in zip(owned, unpacked(orth, unit))
    ]
    gain_sums = gain_sums.reshape(-1)
    norm_grads = gain_sums[: 2 * unit].reshape(2, unit)
    head_grads = gain_sums[2 * unit : 2 * unit + 2 * HEAD_DIM].reshape(2, HEAD_DIM)
    return (block_output, input_grad, norm_grads, head_grads, *new_weights, *moments_next)


def solution(mesh):
    tokens, owned = P(("rep", "own"), None), P("own", None)
    return jax.shard_map(
        body,
        mesh=mesh,
        in_specs=(tokens,) * 3 + (P(),) * 4 + (owned,) * 14,
        out_specs=(tokens,) * 2 + (P(),) * 2 + (owned,) * 14,
        check_vma=False,
    )
```

```python
import functools

import jax
import jax.numpy as jnp
from jax import lax
from jax.experimental import pallas as pl
from jax.experimental.pallas import tpu as pltpu
from jax.sharding import PartitionSpec as P

HEADS = 16
KV_HEADS = 8
HEAD_DIM = 128
NS_STEPS = 5

EPSILON = 1e-06
ROPE_BASE = 1000000.0
MOMENTUM = 0.95
LEARN_RATE = 0.8
WEIGHT_DECAY = 0.01
NEWTON_A = 3.4445
NEWTON_B = -4.775
NEWTON_C = 2.0315

BF16 = jnp.bfloat16
F32 = jnp.float32
MESH = pl.DeviceIdType.MESH
ANY = pl.BlockSpec(memory_space=pltpu.HBM)

QKV, OUT, GU, DOWN = range(4)


def rms_scale(values, gain_vector):
    return values * lax.rsqrt(jnp.mean(values * values, -1, keepdims=True) + EPSILON) * gain_vector


def rotate(values, cosine_table, sine_table):
    half_dim = values.shape[-1] // 2
    first_half = values[..., :half_dim]
    second_half = values[..., half_dim:]
    return jnp.concatenate(
        [
            first_half * cosine_table - second_half * sine_table,
            second_half * cosine_table + first_half * sine_table,
        ],
        -1,
    )


def head_side(raw_value, gain_vector, cosine_table, sine_table):
    shaped = raw_value.reshape(raw_value.shape[0], -1, HEAD_DIM)
    return rotate(rms_scale(shaped, gain_vector), cosine_table, sine_table)


def swiglu(gate_value, up_value):
    return gate_value * jax.nn.sigmoid(gate_value) * up_value


def segments(lengths, row_count):
    seq_ends = jnp.cumsum(lengths)
    seq_starts = seq_ends - lengths
    row_ids = jnp.arange(row_count, dtype=jnp.int32)
    segment_ids = jnp.sum((row_ids[:, None] >= seq_ends[None, :]).astype(jnp.int32), 1)
    slot_ids = jnp.arange(lengths.shape[0], dtype=jnp.int32)
    row_starts = jnp.sum(
        jnp.where(segment_ids[:, None] == slot_ids[None, :], seq_starts[None, :], 0), 1
    )
    return (segment_ids, row_ids - row_starts)


def rope_tables(positions):
    inverse = ROPE_BASE ** (-jnp.arange(0, HEAD_DIM, 2, dtype=jnp.float32) / HEAD_DIM)
    angles = positions.astype(jnp.float32)[:, None] * inverse[None, :]
    return (jnp.cos(angles)[:, None, :], jnp.sin(angles)[:, None, :])


class Place:
    def __init__(self, n):
        self.n = n
        self.rep = lax.axis_index("rep")
        self.own = lax.axis_index("own")
        self.x = self.rep // 2
        self.core = self.rep % 2
        odd, pair = self.own % 2, self.own // 2
        self.ring = pair * (1 - odd) + odd * (n - 1 - pair)

    def own_at(self, ring):
        odd = ring // (self.n // 2)
        return 2 * (ring * (1 - odd) + odd * (self.n - 1 - ring)) + odd

    def shard(self, distance):
        return self.own_at(lax.rem(self.ring + distance + self.n, self.n))

    def ring_neighbour(self, way):
        return (self.rep, self.shard(way))

    @property
    def core_partner(self):
        return (self.x * 2 + 1 - self.core, self.own)

    @property
    def x_partner(self):
        return ((1 - self.x) * 2 + self.core, self.own)


def greet(devices):
    barrier = pltpu.get_barrier_semaphore()
    for device in devices:
        pl.semaphore_signal(barrier, inc=1, device_id=device, device_id_type=MESH)
    pl.semaphore_wait(barrier, len(devices))


def remote(src, dst, send, recv, device):
    return pltpu.make_async_remote_copy(
        src_ref=src, dst_ref=dst, send_sem=send, recv_sem=recv, device_id=device, device_id_type=MESH
    )


def hops(n, way, kind):
    return n // 2 if (way == 0) == (kind == 0) else n // 2 - 1


def side_pieces(unit):
    sides = ([(QKV, 0, 4 * unit)], [(GU, 0, 4 * unit)])
    both = [(GU, 4 * unit, 2 * unit), (OUT, 0, unit), (DOWN, 0, unit)]
    return sides, both


def gather_kernel(n, rows, unit, *refs):
    shards, wholes = refs[:4], refs[4:8]
    local, ring_send, ring_recv, x_send, x_recv, core_send, core_recv = refs[8:]
    place = Place(n)
    cw, ccw = place.ring_neighbour(1), place.ring_neighbour(-1)
    greet([cw, ccw, place.core_partner, place.x_partner])
    sides, both = side_pieces(unit)

    def region(piece, own_index):
        array, first, columns = piece
        half = rows[array] // 2
        start = pl.multiple_of(own_index * rows[array] + place.core * half, half)
        return wholes[array].at[pl.ds(start, half), pl.ds(first, columns)]

    def shard_half(piece):
        array, first, columns = piece
        half = rows[array] // 2
        start = pl.multiple_of(place.core * half, half)
        return shards[array].at[pl.ds(start, half), pl.ds(first, columns)]

    def by_kind(kind, act):
        if kind == 1:
            act(both)
        else:
            for side in range(2):
                pl.when(place.x == side)(functools.partial(act, sides[side]))

    locals_ = []
    for array in range(4):
        start = pl.multiple_of(place.own * rows[array], rows[array])
        copy = pltpu.make_async_copy(
            shards[array], wholes[array].at[pl.ds(start, rows[array])], local.at[array]
        )
        copy.start()
        locals_.append(copy)

    top = n // 2
    ways = ((1, cw), (-1, ccw))

    def ring_copies(pieces, way, kind, hop, distance):
        slot = ((way * 2 + kind) * top + hop - 1) * 3
        step, target = ways[way]
        own_index = place.shard(distance)
        return [
            remote(
                shard_half(piece) if distance == 0 else region(piece, own_index),
                region(piece, own_index),
                ring_send.at[slot + i],
                ring_recv.at[slot + i],
                target,
            )
            for i, piece in enumerate(pieces)
        ]

    def core_copies(pieces, slot, distance):
        own_index = place.shard(distance)
        return [
            remote(
                region(piece, own_index),
                region(piece, own_index),
                core_send.at[slot + i],
                core_recv.at[slot + i],
                place.core_partner,
            )
            for i, piece in enumerate(pieces)
        ]

    def x_copies(pieces, way, hop, distance):
        slot = way * top + hop - 1
        own_index = place.shard(distance)
        return [
            remote(
                region(piece, own_index),
                region(piece, own_index),
                x_send.at[slot],
                x_recv.at[slot],
                place.x_partner,
            )
            for piece in pieces
        ]

    ring_slots = 2 * 2 * top * 3

    def start(copies):
        for copy in copies:
            copy.start()

    def wait_recv(copies):
        for copy in copies:
            copy.wait_recv()

    def wait_send(copies):
        for copy in copies:
            copy.wait_send()

    def other_side(act):
        for side in range(2):
            pl.when(place.x == 1 - side)(functools.partial(act, sides[side]))

    for kind in range(2):
        for way in range(2):
            by_kind(kind, lambda pieces: start(ring_copies(pieces, way, kind, 1, 0)))

    def take_x(way, hop):
        distance = -ways[way][0] * hop

        def act(pieces):
            wait_recv(x_copies(pieces, way, hop, distance))
            start(core_copies(pieces, ring_slots + way * top + hop - 1, distance))

        other_side(act)

    for hop in range(1, top + 1):
        for kind in range(2):
            for way in range(2):
                if hop > hops(n, way, kind):
                    continue
                distance = -ways[way][0] * hop

                def act(pieces):
                    wait_recv(ring_copies(pieces, way, kind, hop, distance))
                    if hop < hops(n, way, kind):
                        start(ring_copies(pieces, way, kind, hop + 1, distance))
                    if kind == 0:
                        start(x_copies(pieces, way, hop, distance))
                    start(core_copies(pieces, ((way * 2 + kind) * top + hop - 1) * 3, distance))

                by_kind(kind, act)
        if hop > 1:
            for way in range(2):
                if hop - 1 <= hops(n, way, 0):
                    take_x(way, hop - 1)
    for way in range(2):
        if top <= hops(n, way, 0):
            take_x(way, top)

    for copy in locals_:
        copy.wait()
    for hop in range(1, top + 1):
        for kind in range(2):
            for way in range(2):
                if hop > hops(n, way, kind):
                    continue
                distance = -ways[way][0] * hop
                slot = ((way * 2 + kind) * top + hop - 1) * 3

                def act(pieces):
                    wait_send(ring_copies(pieces, way, kind, hop, distance + ways[way][0]))
                    core = core_copies(pieces, slot, distance)
                    wait_send(core)
                    wait_recv(core)
                    if kind == 0:
                        wait_send(x_copies(pieces, way, hop, distance))

                by_kind(kind, act)
                if kind == 0:

                    def act_other(pieces):
                        core = core_copies(pieces, ring_slots + way * top + hop - 1, distance)
                        wait_send(core)
                        wait_recv(core)

                    other_side(act_other)


def gather_weights(shards, n, unit):
    rows = [shard.shape[0] for shard in shards]
    top = n // 2
    dma = pltpu.SemaphoreType.DMA
    return pl.pallas_call(
        functools.partial(gather_kernel, n, rows, unit),
        out_shape=[
            jax.ShapeDtypeStruct((n * shard.shape[0], shard.shape[1]), BF16) for shard in shards
        ],
        in_specs=[ANY] * 4,
        out_specs=[ANY] * 4,
        scratch_shapes=[
            dma((4,)),
            dma((12 * top,)),
            dma((12 * top,)),
            dma((2 * top,)),
            dma((2 * top,)),
            dma((14 * top,)),
            dma((14 * top,)),
        ],
        compiler_params=pltpu.CompilerParams(collective_id=0, has_side_effects=True),
    )(*shards)


PHASES = ((DOWN, 3, False), (GU, 3, True), (OUT, 2, False), (QKV, 2, True))

OWNERS = (
    (3, 0, 1, False, 1, 2),
    (3, 1, 1, False, 1, 6),
    (3, 0, 2, False, 0, 2),
    (2, 0, 2, True, 1, 5),
    (1, 0, 3, False, 0, 5),
    (1, 0, 3, False, 1, 1),
    (0, 0, 3, True, 0, 1),
)
KEY, VALUE, QUERY, OUTM, GATE, UP, DOWNM = range(7)
RETURNS = (OUTM, KEY, VALUE, DOWNM, GATE, UP, QUERY)
MOMENTS = {0: ((6, 6),), 1: ((4,), (5,)), 2: ((3, 3),), 3: ((0,), (1, 2))}
TILE_SLOTS = 3
X_SLOTS = 3


def stage_order(n, order):
    top = n // 2
    ring = (top - 0.5) / n
    at = []
    for i in range(n):
        at.append((3 * i - 6.0, ("x", 1, i)))
        at.append((3 * n + 2 * i - 4.0, ("x", 3, i)))
        at.append((1 + 3 * ring * i, ("ring", 0, i)))
        at.append((3 * (i + 1) + 1.0, ("ring", 1, i)))
        at.append((3 * n + 2 + 2 * ring * i, ("ring", 2, i)))
        at.append((3 * n + 3 + max(2.0 * i, 2 * ring * (n + i)), ("ring", 3, i)))
    at.append((1 + 3 * ring * n + 9, ("final", 0, 0)))
    at.append((3 * n + 2 + 2 * ring * n + 6, ("final", 2, 0)))
    return [stage for _, stage in sorted(at)]


class Rows:
    def __init__(self):
        self.next = 0

    def take(self, rows):
        start = self.next
        self.next += rows
        return start


def layout(n, unit):
    base = unit // n
    top = n // 2
    sums = Rows()

    def shared(take):
        first = [take(PHASES[p][1] * base) for p in (0, 1)]
        return first + first

    x_in = [sums.take(PHASES[1][1] * base) for _ in range(n)]
    place = {
        "own": [sums.take(3 * base) for _ in range(TILE_SLOTS)],
        "land": [sums.take(3 * base) for _ in range(TILE_SLOTS)],
        "x_out": [sums.take(3 * base) for _ in range(X_SLOTS)],
        "x_in": {1: x_in, 3: x_in},
        "ring": shared(
            lambda rows: [[sums.take(rows) for _ in range(top)] for _ in range(2)]
        ),
    }
    for name in ("far", "grad", "ahead"):
        place[name] = shared(sums.take)
    for name in ("part", "other"):
        place[name] = [0 if split else sums.take(units * base) for _, units, split in PHASES]
    newton = Rows()
    place["high"] = [newton.take(3 * unit) for _ in range(2)]
    place["poly"] = [newton.take(unit) for _ in range(2)]
    return place, max(sums.next, newton.next)


def update_kernel(n, unit, *refs):
    grads, moments, gains_in = refs[:4], refs[4:11], refs[11]
    outs, orths, lands, gains_out = refs[12:16], refs[16:20], refs[20:24], refs[24]
    (
        pool, exact, gram, squares, gain_mine, gain_core, gain_x, gain_all,
        land_send, land_recv, tile_sem, x_send, x_recv, x_free, ring_send, ring_recv, part_send, part_recv,
        moment_sem, grad_local, grad_send, grad_recv, in_send, in_recv,
        out_send, out_recv, pass_send, pass_recv, gain_send, gain_recv,
    ) = refs[25:]
    place = Place(n)
    base = unit // n
    top = n // 2
    at, _ = layout(n, unit)
    cw, ccw = place.ring_neighbour(1), place.ring_neighbour(-1)
    ways = ((1, cw), (-1, ccw))
    side = [(place.x * 2 + core, lax.rem(place.own + k, n)) for k in range(1, n) for core in range(2)]
    greet(side + [place.core_partner, place.x_partner])
    order = [top]
    for distance in range(top - 1, 0, -1):
        order += [distance, -distance]
    order.append(0)
    stages = stage_order(n, order)
    moment = exact
    height = [units * base for _, units, _ in PHASES]
    owners = [
        (xs * 2 + 1, place.own_at(spot * n // 8)) for _, _, _, _, xs, spot in OWNERS
    ]
    here = place.rep * n + place.own
    is_owner = [here == rep * n + own for rep, own in owners]

    def rows(start, size):
        if isinstance(start, int):
            return pl.ds(start, size)
        return pl.ds(pl.multiple_of(start, size), size)

    def block(start, size):
        return pool.at[rows(start, size)]

    def first_column(phase, x):
        return x * PHASES[phase][1] * unit

    def parts(phase, x):
        _, units, split = PHASES[phase]
        if not split:
            return [(pl.ds(0, unit), 0, units * base)]
        first = first_column(phase, x)
        return [
            (pl.ds(pl.multiple_of(first + k * unit, unit), unit), k * base, base)
            for k in range(units)
        ]

    def shard_rows(phase, own_index):
        size = height[phase] if not PHASES[phase][2] else base
        return rows(own_index * size, size)

    def land_copy(phase, i):
        array = PHASES[phase][0]
        span = shard_rows(phase, place.shard(order[i]))
        return remote(
            grads[array].at[span], lands[array].at[span],
            land_send.at[phase * n + i], land_recv.at[phase * n + i], place.core_partner,
        )

    def x_copy(phase, i):
        index = (phase // 2) * n + i
        slot = at["x_out"][index % X_SLOTS]
        return remote(
            block(slot, height[phase]), block(at["x_in"][phase][i], height[phase]),
            x_send.at[index], x_recv.at[index], place.x_partner,
        )

    def ring_copy(phase, way, distance, source, part):
        size = height[phase] // 2
        target = at["ring"][phase][way][distance - 1] + part * size
        index = ((phase * 2 + way) * top + distance - 1) * 2 + part
        return remote(
            block(source + part * size, size), block(target, size),
            ring_send.at[index], ring_recv.at[index], ways[way][1],
        )

    def ring_out(phase, distance, part):
        if distance == 0:
            return []
        if distance == top:
            return [ring_copy(phase, part, top, at["far"][phase], part)]
        way = 0 if distance > 0 else 1
        far = abs(distance)
        return [ring_copy(phase, way, far, at["ring"][phase][way][far], part)]

    def part_copy(phase):
        return remote(
            block(at["part"][phase], height[phase]), block(at["other"][phase], height[phase]),
            part_send.at[phase // 2], part_recv.at[phase // 2], place.x_partner,
        )

    def gain_copy(src, dst, slot, device):
        return remote(src, dst, gain_send.at[slot], gain_recv.at[slot], device)

    def gain_core_copy():
        return gain_copy(gain_mine, gain_core, 0, place.core_partner)

    def gain_x_copy():
        return gain_copy(gain_core, gain_x, 1, place.x_partner)

    def gain_back_copy():
        return gain_copy(gain_mine, gain_x, 2, place.core_partner)

    def gain_ring(way, hop, distance):
        spot = gain_all.at[place.shard(distance)]
        return gain_copy(spot, spot, 3 + way * top + hop - 1, ways[way][1])

    def grad_place(phase, x, which):
        array = PHASES[phase][0]
        return [
            (outs[array].at[:, columns], block(at[which][phase] + first, size))
            for columns, first, size in parts(phase, x)
        ]

    def grad_span(phase, x):
        array, units, split = PHASES[phase]
        if not split:
            return outs[array]
        first = pl.multiple_of(first_column(phase, x), unit)
        return outs[array].at[:, pl.ds(first, units * unit)]

    def grad_sent(phase, to, device, x):
        span = grad_span(phase, x)
        return remote(span, span, grad_send.at[phase, to], grad_recv.at[phase, to], device)

    def matrix_rows(matrix, own_index):
        phase, first, units, tall, _, _ = OWNERS[matrix]
        if tall:
            return [(0, own_index * units * base, units * base)]
        return [
            ((first + k) * base, k * unit + own_index * base, base) for k in range(units)
        ]

    def matrix_span(matrix):
        phase, first, units, tall, xs, _ = OWNERS[matrix]
        array = PHASES[phase][0]
        if tall:
            return orths[array]
        start = (xs * PHASES[phase][1] + first) * unit
        return orths[array].at[:, pl.ds(start, units * unit)]

    def matrix_parts(matrix):
        phase, first, units, tall, xs, _ = OWNERS[matrix]
        array = PHASES[phase][0]
        if tall:
            return [orths[array]]
        start = (xs * PHASES[phase][1] + first) * unit
        return [orths[array].at[:, pl.ds(start + k * unit, unit)] for k in range(units)]

    def handed(matrix, to, device):
        span = matrix_span(matrix)
        return remote(span, span, pass_send.at[matrix, to], pass_recv.at[matrix, to], device)

    def answered(matrix, target):
        span = matrix_span(matrix)
        return remote(
            span, span, out_send.at[target], out_recv.at[matrix], (place.x * 2, target)
        )

    def summed(pieces, size, store):
        step = 16
        steps = 4 if size % (4 * step) == 0 else 1

        def body(k, carry):
            for j in range(steps):
                shift = (k * steps + j) * step
                total = None
                for start in pieces:
                    value = pool[rows_at(start, shift, step), :].astype(F32)
                    total = value if total is None else total + value
                store(shift, step, total)
            return carry

        lax.fori_loop(0, size // (step * steps), body, 0)

    def rows_at(start, shift, step):
        return pl.ds(pl.multiple_of(start + shift, step), step)

    def keep(start):
        def store(shift, step, total):
            pool[rows_at(start, shift, step), :] = total.astype(BF16)

        return store

    def tile_copies(k):
        kind, phase, i = stages[k]
        slot = k_slot[k]
        x = place.x if kind == "ring" else 1 - place.x
        array = PHASES[phase][0]
        span = shard_rows(phase, place.shard(order[i]))
        copies = []
        for which, (name, source) in enumerate((("own", grads), ("land", lands))):
            for columns, first, size in parts(phase, x):
                copies.append(
                    pltpu.make_async_copy(
                        source[array].at[span, columns], block(at[name][slot] + first, size),
                        tile_sem.at[slot, which],
                    )
                )
        return copies

    tiled = [k for k, stage in enumerate(stages) if stage[0] != "final"]
    k_slot = {k: index % TILE_SLOTS for index, k in enumerate(tiled)}

    def prefetch(index, seen):
        if index >= len(tiled):
            return
        k = tiled[index]
        _, phase, i = stages[k]
        if (phase, i) not in seen:
            seen.add((phase, i))
            land_copy(phase, i).wait_recv()
        for copy in tile_copies(k):
            copy.start()

    def wait_tiles(k):
        _, phase, _ = stages[k]
        slot = k_slot[k]
        for which, name in enumerate(("own", "land")):
            span = block(at[name][slot], height[phase])
            pltpu.make_async_copy(span, span, tile_sem.at[slot, which]).wait()

    def moment_copies(phase, act):
        for x in range(2):

            @pl.when(place.x == x)
            def _():
                sources = MOMENTS[phase][x if PHASES[phase][2] else 0]
                if not PHASES[phase][2]:
                    act(moments[sources[0]], moment.at[pl.ds(0, height[phase])])
                    return
                each = PHASES[phase][1] // len(sources)
                for s, source in enumerate(sources):
                    for k in range(each):
                        act(
                            moments[source].at[:, pl.ds(k * unit, unit)],
                            moment.at[pl.ds((s * each + k) * base, base)],
                        )

    def load_moment(phase):
        moment_copies(
            phase, lambda src, dst: pltpu.make_async_copy(src, dst, moment_sem.at[phase]).start()
        )

    def finish(phase, pieces):
        span = moment.at[pl.ds(0, height[phase])]
        pltpu.make_async_copy(span, span, moment_sem.at[phase]).wait()

        if phase >= 2:
            settle(phase - 2)

        def store(shift, step, total):
            pool[rows_at(at["grad"][phase], shift, step), :] = total.astype(BF16)
            ahead = (1.0 + MOMENTUM) * total + MOMENTUM**2 * moment[rows_at(0, shift, step), :]
            pool[rows_at(at["ahead"][phase], shift, step), :] = ahead.astype(BF16)

        summed(pieces, height[phase], store)
        for matrix, (its_phase, _, _, _, xs, _) in enumerate(OWNERS):
            if its_phase != phase:
                continue

            @pl.when(place.x == xs)
            def _():
                for source, target, size in matrix_rows(matrix, place.own):
                    remote(
                        block(at["ahead"][phase] + source, size), block(at["high"][1] + target, size),
                        in_send.at[matrix], in_recv.at[place.own], owners[matrix],
                    ).start()

        for target, source in grad_place(phase, place.x, "grad"):
            pltpu.make_async_copy(source, target, grad_local.at[phase]).start()
            remote(
                source, target, grad_send.at[phase, 0], grad_recv.at[phase, 0], place.core_partner
            ).start()
            if PHASES[phase][2]:
                remote(
                    source, target, grad_send.at[phase, 1], grad_recv.at[phase, 1], place.x_partner
                ).start()
        after = {0: 1, 1: 2, 2: 3, 3: None}[phase]
        if after is not None:
            load_moment(after)

    def settle(phase):
        span = block(at["grad"][phase], height[phase])
        pltpu.make_async_copy(span, span, grad_local.at[phase]).wait()
        remote(
            span, span, grad_send.at[phase, 0], grad_recv.at[phase, 0], place.core_partner
        ).wait_send()
        if PHASES[phase][2]:
            remote(
                span, span, grad_send.at[phase, 1], grad_recv.at[phase, 1], place.x_partner
            ).wait_send()
        for matrix, (its_phase, _, units, _, xs, _) in enumerate(OWNERS):
            if its_phase != phase:
                continue

            @pl.when(place.x == xs)
            def _():
                span = block(at["high"][1], units * base)
                remote(
                    span, span, in_send.at[matrix], in_recv.at[0], place.core_partner
                ).wait_send()

    def stage_x(k, phase, i):
        wait_tiles(k)
        index = (phase // 2) * n + i
        if index >= X_SLOTS:
            before = index - X_SLOTS
            x_copy(1 if before < n else 3, before % n).wait_send()
        slot = k_slot[k]
        summed(
            [at["own"][slot], at["land"][slot]], height[phase], keep(at["x_out"][index % X_SLOTS])
        )
        if phase == 3:
            pl.semaphore_wait(x_free, 1)
        x_copy(phase, i).start()

    def stage_ring(k, phase, i):
        distance = order[i]
        slot = k_slot[k]
        wait_tiles(k)
        pieces = [at["own"][slot], at["land"][slot]]
        if PHASES[phase][2]:
            x_copy(phase, i).wait_recv()
            pieces.append(at["x_in"][phase][i])
        size = height[phase]
        mid = size // 2
        if abs(distance) == 1 and 0 < phase < 3:
            ring_sent(phase - 1)
        if distance == 0:
            for way in range(2):
                held = at["ring"][phase][way][0]
                for part in range(2):
                    ring_copy(phase, way, 1, held, part).wait_recv()
                pieces.append(held)
            if PHASES[phase][2]:
                finish(phase, pieces)
            else:
                summed(pieces, size, keep(at["part"][phase]))
                part_copy(phase).start()
        else:
            way = 0 if distance > 0 else 1
            far = abs(distance)
            held = at["far"][phase] if far == top else at["ring"][phase][way][far]
            for part in (1 - way, way):
                starts = [start + part * mid for start in pieces]
                if far + 1 < top or (far + 1 == top and part == way):
                    ring_copy(phase, way, far + 1, held, part).wait_recv()
                    starts.append(held + part * mid)
                summed(starts, mid, keep(held + part * mid))
                for copy in ring_out(phase, distance, part):
                    copy.start()
        if phase == 1:
            pl.semaphore_signal(x_free, inc=1, device_id=place.x_partner, device_id_type=MESH)

    def ring_sent(phase):
        if phase not in ring_waited:
            ring_waited.add(phase)
            for distance in order:
                for part in range(2):
                    for copy in ring_out(phase, distance, part):
                        copy.wait_send()

    ring_waited = set()

    def gain_stage(hop):
        if hop == 0:
            gain_core_copy().wait_recv()
            gain_core[...] = gain_mine[...] + gain_core[...]
            gain_x_copy().start()
            return
        if hop == 1:
            gain_x_copy().wait_recv()
            gain_all[place.own] = gain_core[...] + gain_x[...]
            for way in range(2):
                gain_ring(way, 1, 0).start()
        for way in range(2):
            if 1 < hop <= hops(n, way, 0) + 1:
                distance = -ways[way][0] * (hop - 1)
                gain_ring(way, hop - 1, distance).wait_recv()
                if hop <= hops(n, way, 0):
                    gain_ring(way, hop, distance).start()

    gain_mine[...] = gains_in[...]

    @pl.when(place.core == 0)
    def _():
        load_moment(0)
        seen = set()
        for index in range(TILE_SLOTS - 1):
            prefetch(index, seen)
        done = 0
        hop = 0
        for k, (kind, phase, i) in enumerate(stages):
            if kind == "final":
                part_copy(phase).wait_recv()
                finish(phase, [at["part"][phase], at["other"][phase]])
                continue
            prefetch(done + TILE_SLOTS - 1, seen)
            done += 1
            if kind == "x":
                stage_x(k, phase, i)
            else:
                stage_ring(k, phase, i)
            if done % 3 == 0 and hop <= top + 1:
                gain_stage(hop)
                hop += 1

        total = gain_all[0]
        for k in range(1, n):
            total = total + gain_all[k]
        gains_out[...] = total
        gain_mine[...] = total
        gain_back_copy().start()

        for phase in (1, 3):
            grad_sent(phase, 1, place.x_partner, 1 - place.x).wait_recv()
            grad_sent(phase, 2, place.core_partner, 1 - place.x).start()

        for matrix in RETURNS:
            xs = OWNERS[matrix][4]

            @pl.when(place.x == xs)
            def _():
                answered(matrix, place.own).wait_recv()
                handed(matrix, 0, place.x_partner).start()
                handed(matrix, 1, place.core_partner).start()

            @pl.when(place.x != xs)
            def _():
                handed(matrix, 0, place.x_partner).wait_recv()
                handed(matrix, 1, place.core_partner).start()

        for matrix, (phase, _, units, _, xs, _) in enumerate(OWNERS):
            handed(matrix, 1, place.core_partner).wait_send()

            @pl.when(place.x == xs)
            def _():
                handed(matrix, 0, place.x_partner).wait_send()

        for phase, (_, _, split) in enumerate(PHASES):
            if phase >= 2:
                settle(phase)
            if split:
                grad_sent(phase, 2, place.core_partner, 1 - place.x).wait_send()
            else:
                part_copy(phase).wait_send()
            ring_sent(phase)
        for index in range(2 * n - X_SLOTS, 2 * n):
            x_copy(1 if index < n else 3, index % n).wait_send()
        gain_x_copy().wait_send()
        gain_back_copy().wait_send()
        for way in range(2):
            for h in range(1, hops(n, way, 0) + 1):
                gain_ring(way, h, -ways[way][0] * (h - 1)).wait_send()

    @pl.when(place.core == 1)
    def _():
        gain_core_copy().start()
        needed = []
        for kind, phase, i in stages:
            if kind != "final" and (phase, i) not in needed:
                needed.append((phase, i))
        ahead = 4
        for index, (phase, i) in enumerate(needed):
            if index >= ahead:
                land_copy(*needed[index - ahead]).wait_send()
            land_copy(phase, i).start()
        for phase, i in needed[-ahead:]:
            land_copy(phase, i).wait_send()
        newton_part(n, unit, place, pool, exact, gram, squares, at, is_owner, in_recv)
        for matrix, (_, _, units, tall, _, _) in enumerate(OWNERS):

            @pl.when(is_owner[matrix])
            def _():
                final = at["high"][1 - NS_STEPS % 2 if tall else NS_STEPS % 2]

                def send(k, carry):
                    target = lax.rem(place.own + k, n)
                    for part, (_, row, size) in zip(matrix_parts(matrix), matrix_rows(matrix, target)):
                        remote(
                            block(final + row, size), part, out_send.at[target], out_recv.at[matrix],
                            (place.x * 2, target),
                        ).start()
                    return carry

                lax.fori_loop(0, n, send, 0)

                def sent(k, carry):
                    answered(matrix, lax.rem(place.own + k, n)).wait_send()
                    return carry

                lax.fori_loop(0, n, sent, 0)

        gain_core_copy().wait_send()
        gain_back_copy().wait_recv()
        gains_out[...] = gain_x[...]
        for phase, (_, _, split) in enumerate(PHASES):
            grad_sent(phase, 0, place.core_partner, place.x).wait_recv()
            if split:
                grad_sent(phase, 2, place.core_partner, 1 - place.x).wait_recv()
        for matrix in RETURNS:
            handed(matrix, 1, place.core_partner).wait_recv()


def newton_part(n, unit, place, pool, exact, gram, squares, at, is_owner, in_recv):
    base = unit // n
    small = min(256, unit // 2)
    per = unit // small
    few = 32
    count, tall = 0, 0
    for mine, (_, _, units, lies_tall, _, _) in zip(is_owner, OWNERS):
        count = count + units * mine.astype(jnp.int32)
        tall = tall + int(lies_tall) * mine.astype(jnp.int32)
    high, poly = at["high"], at["poly"]

    def rows(start, size):
        return pl.ds(pl.multiple_of(start, size), size)

    for matrix, (_, _, units, *_) in enumerate(OWNERS):

        @pl.when(is_owner[matrix])
        def _():
            span = pool.at[pl.ds(high[1], units * base)]
            for own_index in range(n):
                remote(
                    span, span, in_recv.at[own_index], in_recv.at[own_index], place.core_partner
                ).wait_recv()

    @pl.when(count > 0)
    def _():
        squares[...] = jnp.zeros_like(squares)

        def square(k, carry):
            part = pool[rows(high[1] + k * few, few), :].astype(F32)
            squares[...] += jnp.sum((part * part).reshape(few // 8, 8, unit), 0)
            return carry

        lax.fori_loop(0, count * (unit // few), square, 0)
        total = jnp.sum(jnp.sum(squares[...], 1, keepdims=True), 0, keepdims=True)
        inverse = 1.0 / (jnp.sqrt(total) + 1e-07)

        @pl.when(tall == 0)
        def _():
            def scale(k, carry):
                value = pool[rows(high[1] + k * few, few), :].astype(F32) * inverse
                exact[rows(k * few, few), :] = value
                pool[rows(high[0] + k * few, few), :] = value.astype(BF16)
                return carry

            lax.fori_loop(0, count * (unit // few), scale, 0)

        @pl.when(tall == 1)
        def _():
            def scale(k, carry):
                block, row = k // per, k % per
                for column in range(per):
                    part = pool[
                        rows(high[1] + k * small, small), pl.ds(column * small, small)
                    ].astype(F32)
                    value = (part * inverse).T
                    shift = block * unit + column * small
                    columns = rows(row * small, small)
                    exact[rows(shift, small), columns] = value
                    pool[rows(high[0] + shift, small), columns] = value.astype(BF16)
                return carry

            lax.fori_loop(0, count * per, scale, 0)

        def newton(step, carry):
            even = step % 2
            now = high[0] + even * (high[1] - high[0])
            later = high[1] - even * (high[1] - high[0])

            def keep_symmetric(to, chunk, value):
                pool[pl.ds(to, (chunk + 1) * small), pl.ds(chunk * small, small)] = value.astype(BF16)
                for row in range(chunk):
                    pool[pl.ds(to + chunk * small, small), pl.ds(row * small, small)] = (
                        value[row * small : (row + 1) * small].T.astype(BF16)
                    )

            for chunk in range(per):
                down = (chunk + 1) * small

                def product(block):
                    left = pool[pl.ds(pl.multiple_of(now + block * unit, unit), down), :]
                    right = pool[rows(now + block * unit + chunk * small, small), :]
                    return lax.dot_general(
                        left, right, (((1,), (1,)), ((), ())), preferred_element_type=F32
                    )

                gram[:down, :] = product(0)

                def more(block, carry):
                    gram[:down, :] += product(block)
                    return carry

                lax.fori_loop(1, count, more, 0)
                keep_symmetric(poly[0], chunk, gram[:down, :])

            for chunk in range(per):
                down = (chunk + 1) * small
                columns = pl.ds(chunk * small, small)
                squared = jnp.dot(
                    pool[pl.ds(poly[0], down), :], pool[pl.ds(poly[0], unit), columns],
                    preferred_element_type=F32,
                )
                plain = pool[pl.ds(poly[0], down), columns].astype(F32)
                keep_symmetric(poly[1], chunk, NEWTON_B * plain + NEWTON_C * squared)

            def advance(block, carry):
                for chunk in range(per):
                    columns = pl.ds(chunk * small, small)
                    value = NEWTON_A * exact[rows(block * unit, unit), columns] + jnp.dot(
                        pool[pl.ds(poly[1], unit), :],
                        pool[rows(now + block * unit, unit), columns],
                        preferred_element_type=F32,
                    )
                    exact[rows(block * unit, unit), columns] = value
                    pool[rows(later + block * unit, unit), columns] = value.astype(BF16)
                return carry

            lax.fori_loop(0, count, advance, 0)
            return carry

        lax.fori_loop(0, NS_STEPS, newton, 0)

        @pl.when(tall == 1)
        def _():
            free = high[1 - NS_STEPS % 2]
            factor = jnp.sqrt(jnp.full((1, 1), count, jnp.int32).astype(F32))

            def lay(k, carry):
                block, row = k // per, k % per
                for column in range(per):
                    columns = pl.ds(column * small, small)
                    part = exact[rows(k * small, small), columns]
                    pool[
                        rows(free + block * unit + column * small, small), rows(row * small, small)
                    ] = (part * factor).T.astype(BF16)
                return carry

            lax.fori_loop(0, count * per, lay, 0)


def update_all(grads, moments, gains, n, unit):
    top = n // 2
    dma = pltpu.SemaphoreType.DMA
    vmem = pltpu.VMEM
    _, pool_rows = layout(n, unit)
    own = [jax.ShapeDtypeStruct((grad.shape[0] // n, grad.shape[1]), BF16) for grad in grads]
    whole = [jax.ShapeDtypeStruct(grad.shape, BF16) for grad in grads]
    in_vmem = pl.BlockSpec(memory_space=pltpu.VMEM)
    results = pl.pallas_call(
        functools.partial(update_kernel, n, unit),
        out_shape=own + own + whole + [jax.ShapeDtypeStruct(gains.shape, F32)],
        in_specs=[ANY] * 11 + [in_vmem],
        out_specs=[ANY] * 12 + [in_vmem],
        scratch_shapes=[
            vmem((pool_rows, unit), BF16),
            vmem((3 * unit, unit), F32),
            vmem((unit, min(256, unit // 2)), F32),
            vmem((8, unit), F32),
            vmem(gains.shape, F32),
            vmem(gains.shape, F32),
            vmem(gains.shape, F32),
            vmem((n,) + gains.shape, F32),
            dma((4 * n,)),
            dma((4 * n,)),
            dma((TILE_SLOTS, 2)),
            dma((2 * n,)),
            dma((2 * n,)),
            pltpu.SemaphoreType.REGULAR,
            dma((16 * top,)),
            dma((16 * top,)),
            dma((2,)),
            dma((2,)),
            dma((4,)),
            dma((4,)),
            dma((4, 3)),
            dma((4, 3)),
            dma((7,)),
            dma((n,)),
            dma((n,)),
            dma((7,)),
            dma((7, 2)),
            dma((7, 2)),
            dma((3 + 2 * top,)),
            dma((3 + 2 * top,)),
        ],
        compiler_params=pltpu.CompilerParams(
            collective_id=1, has_side_effects=True, vmem_limit_bytes=56 * 2**20
        ),
    )(*grads, *moments, gains)
    return results[:4], results[4:8], results[12]


def packed(matrices):
    query, key, value, out, gate, up, down = matrices
    return (
        jnp.concatenate([query, key, value], 1),
        out,
        jnp.concatenate([gate, up], 1),
        down,
    )


def unpacked(arrays, unit):
    qkv, out, gate_up, down = arrays
    return (
        qkv[:, : 2 * unit],
        qkv[:, 2 * unit : 3 * unit],
        qkv[:, 3 * unit :],
        out,
        gate_up[:, : 3 * unit],
        gate_up[:, 3 * unit :],
        down,
    )


def body(
    layer_input,
    output_grad,
    lengths,
    attention_gain,
    feed_gain,
    query_gain,
    key_gain,
    query_weight,
    key_weight,
    value_weight,
    out_weight,
    gate_weight,
    up_weight,
    down_weight,
    query_moment,
    key_moment,
    value_moment,
    out_moment,
    gate_moment,
    up_moment,
    down_moment,
):
    owned = (
        query_weight, key_weight, value_weight, out_weight, gate_weight, up_weight, down_weight,
    )
    moments = (
        query_moment, key_moment, value_moment, out_moment, gate_moment, up_moment, down_moment,
    )
    n = lax.axis_size("own")
    unit = layer_input.shape[1]
    q_width, kv_width, ff = 2 * unit, unit, 3 * unit
    low_shards = packed([matrix.astype(BF16) for matrix in owned])
    qkv_full, out_full, gu_full, down_full = gather_weights(low_shards, n, unit)

    row_count = layer_input.shape[0]
    group_size = HEADS // KV_HEADS
    segment_ids, positions = segments(lengths[0], row_count)
    cosine_table, sine_table = rope_tables(positions)
    normed_value, norm_pullback = jax.vjp(rms_scale, layer_input, attention_gain)
    normed = normed_value.astype(BF16)
    raw = jnp.dot(normed, qkv_full, preferred_element_type=F32)
    query_raw = raw[:, :q_width]
    key_raw = raw[:, q_width : q_width + kv_width]
    value_raw = raw[:, q_width + kv_width :]
    query_rot, query_pullback = jax.vjp(
        lambda raw_value, gain_vector: head_side(raw_value, gain_vector, cosine_table, sine_table),
        query_raw,
        query_gain,
    )
    key_rot, key_pullback = jax.vjp(
        lambda raw_value, gain_vector: head_side(raw_value, gain_vector, cosine_table, sine_table),
        key_raw,
        key_gain,
    )
    queries = query_rot.astype(BF16).reshape(row_count, KV_HEADS, group_size, HEAD_DIM)
    keys = key_rot.astype(BF16)
    values = value_raw.astype(BF16).reshape(row_count, KV_HEADS, HEAD_DIM)
    row_ids = jnp.arange(row_count, dtype=jnp.int32)
    score_scale = HEAD_DIM ** (-0.5)
    raw_scores = (
        jnp.einsum("tkgd,skd->kgts", queries, keys, preferred_element_type=F32) * score_scale
    )
    allowed = (segment_ids[:, None] == segment_ids[None, :]) & (
        row_ids[:, None] >= row_ids[None, :]
    )
    masked = jnp.where(allowed, raw_scores, -1e30)
    maximum = jnp.max(masked, -1, keepdims=True)
    exponent = jnp.exp(masked - maximum)
    totals = jnp.sum(exponent, -1, keepdims=True)
    probs_full = exponent / totals
    probs_low = probs_full.astype(BF16)
    context = jnp.einsum("kgts,skd->tkgd", probs_low, values, preferred_element_type=F32)
    context = context.reshape(row_count, q_width).astype(BF16)
    middle = layer_input + jnp.dot(context, out_full, preferred_element_type=F32)
    hidden_value, middle_pullback = jax.vjp(rms_scale, middle, feed_gain)
    hidden = hidden_value.astype(BF16)
    gate_up = jnp.dot(hidden, gu_full, preferred_element_type=F32)
    activated_value, swiglu_pullback = jax.vjp(swiglu, gate_up[:, :ff], gate_up[:, ff:])
    activated = activated_value.astype(BF16)
    block_output = middle + jnp.dot(activated, down_full, preferred_element_type=F32)

    out_low = output_grad.astype(BF16)
    grad_down = jnp.einsum("tf,td->fd", activated, out_low, preferred_element_type=F32)
    grad_activated = jnp.einsum("td,fd->tf", out_low, down_full, preferred_element_type=F32)
    grad_gate_value, grad_up_value = swiglu_pullback(grad_activated)
    gu_back = jnp.concatenate([grad_gate_value.astype(BF16), grad_up_value.astype(BF16)], 1)
    grad_gu = jnp.einsum("td,tf->df", hidden, gu_back, preferred_element_type=F32)
    grad_hidden = jnp.einsum("tf,df->td", gu_back, gu_full, preferred_element_type=F32)
    grad_middle_norm, grad_feed = middle_pullback(grad_hidden)
    grad_middle = output_grad + grad_middle_norm
    attended_low = grad_middle.astype(BF16)
    grad_out = jnp.einsum("ti,td->id", context, attended_low, preferred_element_type=F32)
    grad_context = jnp.einsum("td,id->ti", attended_low, out_full, preferred_element_type=F32)
    grad_context = grad_context.astype(BF16).reshape(row_count, KV_HEADS, group_size, HEAD_DIM)
    grad_values = jnp.einsum("kgts,tkgd->skd", probs_low, grad_context, preferred_element_type=F32)
    grad_probs = jnp.einsum("tkgd,skd->kgts", grad_context, values, preferred_element_type=F32)
    grad_scores = probs_full * (
        grad_probs - jnp.sum(probs_full * grad_probs, -1, keepdims=True)
    )
    grad_scores = grad_scores.astype(BF16)
    grad_queries = (
        jnp.einsum("kgts,skd->tkgd", grad_scores, keys, preferred_element_type=F32) * score_scale
    )
    grad_keys = (
        jnp.einsum("kgts,tkgd->skd", grad_scores, queries, preferred_element_type=F32)
        * score_scale
    )
    grad_query_raw, grad_query_gain = query_pullback(
        grad_queries.reshape(row_count, HEADS, HEAD_DIM)
    )
    grad_key_raw, grad_key_gain = key_pullback(grad_keys)
    qkv_back = jnp.concatenate(
        [
            grad_query_raw.astype(BF16),
            grad_key_raw.astype(BF16),
            grad_values.reshape(row_count, kv_width).astype(BF16),
        ],
        1,
    )
    grad_qkv = jnp.einsum("td,tq->dq", normed, qkv_back, preferred_element_type=F32)
    grad_normed = jnp.einsum("tq,dq->td", qkv_back, qkv_full, preferred_element_type=F32)
    grad_input_norm, grad_attention = norm_pullback(grad_normed)
    input_grad = grad_middle + grad_input_norm

    gains = jnp.concatenate([grad_attention, grad_feed, grad_query_gain, grad_key_gain])
    gains = jnp.pad(gains, (0, 24 * 128 - gains.shape[0])).reshape(24, 128)
    grads = [grad.astype(BF16) for grad in (grad_qkv, grad_out, grad_gu, grad_down)]
    reduced, orth, gain_sums = update_all(grads, moments, gains, n, unit)
    moments_next = [
        MOMENTUM * moment + part.astype(F32) for moment, part in zip(moments, unpacked(reduced, unit))
    ]
    new_weights = [
        matrix * (1.0 - LEARN_RATE * WEIGHT_DECAY) - LEARN_RATE * part.astype(F32)
        for matrix, part in zip(owned, unpacked(orth, unit))
    ]
    gain_sums = gain_sums.reshape(-1)
    norm_grads = gain_sums[: 2 * unit].reshape(2, unit)
    head_grads = gain_sums[2 * unit : 2 * unit + 2 * HEAD_DIM].reshape(2, HEAD_DIM)
    return (block_output, input_grad, norm_grads, head_grads, *new_weights, *moments_next)


def solution(mesh):
    tokens, owned = P(("rep", "own"), None), P("own", None)
    return jax.shard_map(
        body,
        mesh=mesh,
        in_specs=(tokens,) * 3 + (P(),) * 4 + (owned,) * 14,
        out_specs=(tokens,) * 2 + (P(),) * 2 + (owned,) * 14,
        check_vma=False,
    )
```

```python
import functools

import jax
import jax.numpy as jnp
from jax import lax
from jax.experimental import pallas as pl
from jax.experimental.pallas import tpu as pltpu
from jax.sharding import PartitionSpec as P

HEADS = 16
KV_HEADS = 8
HEAD_DIM = 128
NS_STEPS = 5

EPSILON = 1e-06
ROPE_BASE = 1000000.0
MOMENTUM = 0.95
LEARN_RATE = 0.8
WEIGHT_DECAY = 0.01
NEWTON_A = 3.4445
NEWTON_B = -4.775
NEWTON_C = 2.0315

BF16 = jnp.bfloat16
F32 = jnp.float32
MESH = pl.DeviceIdType.MESH
ANY = pl.BlockSpec(memory_space=pltpu.HBM)

QKV, OUT, GU, DOWN = range(4)


def rms_scale(values, gain_vector):
    return values * lax.rsqrt(jnp.mean(values * values, -1, keepdims=True) + EPSILON) * gain_vector


def rotate(values, cosine_table, sine_table):
    half_dim = values.shape[-1] // 2
    first_half = values[..., :half_dim]
    second_half = values[..., half_dim:]
    return jnp.concatenate(
        [
            first_half * cosine_table - second_half * sine_table,
            second_half * cosine_table + first_half * sine_table,
        ],
        -1,
    )


def head_side(raw_value, gain_vector, cosine_table, sine_table):
    shaped = raw_value.reshape(raw_value.shape[0], -1, HEAD_DIM)
    return rotate(rms_scale(shaped, gain_vector), cosine_table, sine_table)


def swiglu(gate_value, up_value):
    return gate_value * jax.nn.sigmoid(gate_value) * up_value


def segments(lengths, row_count):
    seq_ends = jnp.cumsum(lengths)
    seq_starts = seq_ends - lengths
    row_ids = jnp.arange(row_count, dtype=jnp.int32)
    segment_ids = jnp.sum((row_ids[:, None] >= seq_ends[None, :]).astype(jnp.int32), 1)
    slot_ids = jnp.arange(lengths.shape[0], dtype=jnp.int32)
    row_starts = jnp.sum(
        jnp.where(segment_ids[:, None] == slot_ids[None, :], seq_starts[None, :], 0), 1
    )
    return (segment_ids, row_ids - row_starts)


def rope_tables(positions):
    inverse = ROPE_BASE ** (-jnp.arange(0, HEAD_DIM, 2, dtype=jnp.float32) / HEAD_DIM)
    angles = positions.astype(jnp.float32)[:, None] * inverse[None, :]
    return (jnp.cos(angles)[:, None, :], jnp.sin(angles)[:, None, :])


class Place:
    def __init__(self, n):
        self.n = n
        self.rep = lax.axis_index("rep")
        self.own = lax.axis_index("own")
        self.x = self.rep // 2
        self.core = self.rep % 2
        odd, pair = self.own % 2, self.own // 2
        self.ring = pair * (1 - odd) + odd * (n - 1 - pair)

    def own_at(self, ring):
        odd = ring // (self.n // 2)
        return 2 * (ring * (1 - odd) + odd * (self.n - 1 - ring)) + odd

    def shard(self, distance):
        return self.own_at(lax.rem(self.ring + distance + self.n, self.n))

    def ring_neighbour(self, way):
        return (self.rep, self.shard(way))

    @property
    def core_partner(self):
        return (self.x * 2 + 1 - self.core, self.own)

    @property
    def x_partner(self):
        return ((1 - self.x) * 2 + self.core, self.own)


def greet(devices):
    barrier = pltpu.get_barrier_semaphore()
    for device in devices:
        pl.semaphore_signal(barrier, inc=1, device_id=device, device_id_type=MESH)
    pl.semaphore_wait(barrier, len(devices))


class Several:
    def __init__(self, whole, copies):
        self.whole = whole
        self.copies = copies

    def start(self):
        for copy in self.copies:
            copy().start()

    def wait_send(self):
        self.whole().wait_send()

    def wait_recv(self):
        self.whole().wait_recv()


def remote(src, dst, send, recv, device):
    return pltpu.make_async_remote_copy(
        src_ref=src, dst_ref=dst, send_sem=send, recv_sem=recv, device_id=device, device_id_type=MESH
    )


def hops(n, way, kind):
    return n // 2 if (way == 0) == (kind == 0) else n // 2 - 1


def side_pieces(unit):
    sides = ([(QKV, 0, 4 * unit)], [(GU, 0, 4 * unit)])
    both = [(GU, 4 * unit, 2 * unit), (OUT, 0, unit), (DOWN, 0, unit)]
    return sides, both


def gather_kernel(n, rows, unit, *refs):
    shards, wholes = refs[:4], refs[4:8]
    local, ring_send, ring_recv, x_send, x_recv, core_send, core_recv = refs[8:]
    place = Place(n)
    cw, ccw = place.ring_neighbour(1), place.ring_neighbour(-1)
    greet([cw, ccw, place.core_partner, place.x_partner])
    sides, both = side_pieces(unit)

    def region(piece, own_index):
        array, first, columns = piece
        half = rows[array] // 2
        start = pl.multiple_of(own_index * rows[array] + place.core * half, half)
        return wholes[array].at[pl.ds(start, half), pl.ds(first, columns)]

    def shard_half(piece):
        array, first, columns = piece
        half = rows[array] // 2
        start = pl.multiple_of(place.core * half, half)
        return shards[array].at[pl.ds(start, half), pl.ds(first, columns)]

    def by_kind(kind, act):
        if kind == 1:
            act(both)
        else:
            for side in range(2):
                pl.when(place.x == side)(functools.partial(act, sides[side]))

    locals_ = []
    for array in range(4):
        start = pl.multiple_of(place.own * rows[array], rows[array])
        copy = pltpu.make_async_copy(
            shards[array], wholes[array].at[pl.ds(start, rows[array])], local.at[array]
        )
        copy.start()
        locals_.append(copy)

    top = n // 2
    ways = ((1, cw), (-1, ccw))

    def ring_copies(pieces, way, kind, hop, distance):
        slot = ((way * 2 + kind) * top + hop - 1) * 3
        step, target = ways[way]
        own_index = place.shard(distance)
        return [
            remote(
                shard_half(piece) if distance == 0 else region(piece, own_index),
                region(piece, own_index),
                ring_send.at[slot + i],
                ring_recv.at[slot + i],
                target,
            )
            for i, piece in enumerate(pieces)
        ]

    def core_copies(pieces, slot, distance):
        own_index = place.shard(distance)
        return [
            remote(
                region(piece, own_index),
                region(piece, own_index),
                core_send.at[slot + i],
                core_recv.at[slot + i],
                place.core_partner,
            )
            for i, piece in enumerate(pieces)
        ]

    def x_copies(pieces, way, hop, distance):
        slot = way * top + hop - 1
        own_index = place.shard(distance)
        return [
            remote(
                region(piece, own_index),
                region(piece, own_index),
                x_send.at[slot],
                x_recv.at[slot],
                place.x_partner,
            )
            for piece in pieces
        ]

    ring_slots = 2 * 2 * top * 3

    def start(copies):
        for copy in copies:
            copy.start()

    def wait_recv(copies):
        for copy in copies:
            copy.wait_recv()

    def wait_send(copies):
        for copy in copies:
            copy.wait_send()

    def other_side(act):
        for side in range(2):
            pl.when(place.x == 1 - side)(functools.partial(act, sides[side]))

    for kind in range(2):
        for way in range(2):
            by_kind(kind, lambda pieces: start(ring_copies(pieces, way, kind, 1, 0)))

    def take_x(way, hop):
        distance = -ways[way][0] * hop

        def act(pieces):
            wait_recv(x_copies(pieces, way, hop, distance))
            start(core_copies(pieces, ring_slots + way * top + hop - 1, distance))

        other_side(act)

    for hop in range(1, top + 1):
        for kind in range(2):
            for way in range(2):
                if hop > hops(n, way, kind):
                    continue
                distance = -ways[way][0] * hop

                def act(pieces):
                    wait_recv(ring_copies(pieces, way, kind, hop, distance))
                    if hop < hops(n, way, kind):
                        start(ring_copies(pieces, way, kind, hop + 1, distance))
                    if kind == 0:
                        start(x_copies(pieces, way, hop, distance))
                    start(core_copies(pieces, ((way * 2 + kind) * top + hop - 1) * 3, distance))

                by_kind(kind, act)
        if hop > 1:
            for way in range(2):
                if hop - 1 <= hops(n, way, 0):
                    take_x(way, hop - 1)
    for way in range(2):
        if top <= hops(n, way, 0):
            take_x(way, top)

    for copy in locals_:
        copy.wait()
    for hop in range(1, top + 1):
        for kind in range(2):
            for way in range(2):
                if hop > hops(n, way, kind):
                    continue
                distance = -ways[way][0] * hop
                slot = ((way * 2 + kind) * top + hop - 1) * 3

                def act(pieces):
                    wait_send(ring_copies(pieces, way, kind, hop, distance + ways[way][0]))
                    core = core_copies(pieces, slot, distance)
                    wait_send(core)
                    wait_recv(core)
                    if kind == 0:
                        wait_send(x_copies(pieces, way, hop, distance))

                by_kind(kind, act)
                if kind == 0:

                    def act_other(pieces):
                        core = core_copies(pieces, ring_slots + way * top + hop - 1, distance)
                        wait_send(core)
                        wait_recv(core)

                    other_side(act_other)


def gather_weights(shards, n, unit):
    rows = [shard.shape[0] for shard in shards]
    top = n // 2
    dma = pltpu.SemaphoreType.DMA
    return pl.pallas_call(
        functools.partial(gather_kernel, n, rows, unit),
        out_shape=[
            jax.ShapeDtypeStruct((n * shard.shape[0], shard.shape[1]), BF16) for shard in shards
        ],
        in_specs=[ANY] * 4,
        out_specs=[ANY] * 4,
        scratch_shapes=[
            dma((4,)),
            dma((12 * top,)),
            dma((12 * top,)),
            dma((2 * top,)),
            dma((2 * top,)),
            dma((14 * top,)),
            dma((14 * top,)),
        ],
        compiler_params=pltpu.CompilerParams(collective_id=0, has_side_effects=True),
    )(*shards)


PHASES = ((DOWN, 3, False), (GU, 3, True), (OUT, 2, False), (QKV, 2, True))

OWNERS = (
    (3, 0, 1, False, 1, 2),
    (3, 1, 1, False, 1, 6),
    (3, 0, 2, False, 0, 2),
    (2, 0, 2, True, 1, 5),
    (1, 0, 3, False, 0, 5),
    (1, 0, 3, False, 1, 1),
    (0, 0, 3, True, 0, 1),
)
KEY, VALUE, QUERY, OUTM, GATE, UP, DOWNM = range(7)
RETURNS = (OUTM, KEY, VALUE, DOWNM, GATE, UP, QUERY)
MOMENTS = {0: ((6, 6),), 1: ((4,), (5,)), 2: ((3, 3),), 3: ((0,), (1, 2))}
TILE_SLOTS = 3
X_SLOTS = 3


def stage_order(n, order):
    top = n // 2
    ring = (top - 0.5) / n
    at = []
    for i in range(n):
        at.append((3 * i - 6.0, ("x", 1, i)))
        at.append((3 * n + 2 * i - 4.0, ("x", 3, i)))
        at.append((1 + 3 * ring * i, ("ring", 0, i)))
        at.append((3 * (i + 1) + 1.0, ("ring", 1, i)))
        at.append((3 * n + 2 + 2 * ring * i, ("ring", 2, i)))
        at.append((3 * n + 3 + max(2.0 * i, 2 * ring * (n + i)), ("ring", 3, i)))
    at.append((1 + 3 * ring * n + 9, ("final", 0, 0)))
    at.append((3 * n + 2 + 2 * ring * n + 6, ("final", 2, 0)))
    return [stage for _, stage in sorted(at)]


class Rows:
    def __init__(self):
        self.next = 0

    def take(self, rows):
        start = self.next
        self.next += rows
        return start


def layout(n, unit):
    base = unit // n
    top = n // 2
    sums = Rows()

    def shared(take):
        first = [take(PHASES[p][1] * base) for p in (0, 1)]
        return first + first

    x_in = [sums.take(PHASES[1][1] * base) for _ in range(n)]
    place = {
        "own": [sums.take(3 * base) for _ in range(TILE_SLOTS)],
        "land": [sums.take(3 * base) for _ in range(TILE_SLOTS)],
        "x_out": [sums.take(3 * base) for _ in range(X_SLOTS)],
        "x_in": {1: x_in, 3: x_in},
        "ring": shared(
            lambda rows: [[sums.take(rows) for _ in range(top)] for _ in range(2)]
        ),
    }
    for name in ("far", "grad", "ahead"):
        place[name] = shared(sums.take)
    for name in ("part", "other"):
        place[name] = [0 if split else sums.take(units * base) for _, units, split in PHASES]
    newton = Rows()
    place["high"] = [newton.take(3 * unit) for _ in range(2)]
    place["poly"] = [newton.take(unit) for _ in range(2)]
    return place, max(sums.next, newton.next)


def update_kernel(n, unit, *refs):
    grads, moments, gains_in = refs[:4], refs[4:11], refs[11]
    outs, orths, lands, gains_out = refs[12:16], refs[16:20], refs[20:24], refs[24]
    (
        pool, exact, gram, squares, gain_mine, gain_core, gain_x, gain_all,
        land_send, land_recv, tile_sem, x_send, x_recv, x_free, ring_send, ring_recv, part_send, part_recv,
        moment_sem, grad_local, grad_send, grad_recv, in_send, in_recv,
        out_send, out_recv, pass_send, pass_recv, gain_send, gain_recv,
    ) = refs[25:]
    place = Place(n)
    base = unit // n
    top = n // 2
    at, _ = layout(n, unit)
    cw, ccw = place.ring_neighbour(1), place.ring_neighbour(-1)
    ways = ((1, cw), (-1, ccw))
    side = [(place.x * 2 + core, lax.rem(place.own + k, n)) for k in range(1, n) for core in range(2)]
    greet(side + [place.core_partner, place.x_partner])
    order = [top]
    for distance in range(top - 1, 0, -1):
        order += [distance, -distance]
    order.append(0)
    stages = stage_order(n, order)
    moment = exact
    height = [units * base for _, units, _ in PHASES]
    owners = [
        (xs * 2 + 1, place.own_at(spot * n // 8)) for _, _, _, _, xs, spot in OWNERS
    ]
    here = place.rep * n + place.own
    is_owner = [here == rep * n + own for rep, own in owners]

    def rows(start, size):
        if isinstance(start, int):
            return pl.ds(start, size)
        return pl.ds(pl.multiple_of(start, size), size)

    def block(start, size):
        return pool.at[rows(start, size)]

    def first_column(phase, x):
        return x * PHASES[phase][1] * unit

    def parts(phase, x):
        _, units, split = PHASES[phase]
        if not split:
            return [(pl.ds(0, unit), 0, units * base)]
        first = first_column(phase, x)
        return [
            (pl.ds(pl.multiple_of(first + k * unit, unit), unit), k * base, base)
            for k in range(units)
        ]

    def shard_rows(phase, own_index):
        size = height[phase] if not PHASES[phase][2] else base
        return rows(own_index * size, size)

    def spread(source, target, size, send, recv, device):
        step = base // 2 if size % (base // 2) == 0 else size

        def copy(k, count):
            return remote(block(source + k, count), block(target + k, count), send, recv, device)

        return Several(
            functools.partial(copy, 0, size),
            [functools.partial(copy, k, step) for k in range(0, size, step)],
        )

    def land_copy(phase, i):
        array = PHASES[phase][0]
        own_index = place.shard(order[i])
        size = height[phase] if not PHASES[phase][2] else base

        def copy(span):
            return remote(
                grads[array].at[span], lands[array].at[span],
                land_send.at[phase * n + i], land_recv.at[phase * n + i], place.core_partner,
            )

        step = base // 2
        pieces = [
            functools.partial(copy, pl.ds(pl.multiple_of(own_index * size + k * step, step), step))
            for k in range(size // step)
        ]
        return Several(functools.partial(copy, rows(own_index * size, size)), pieces)

    def x_copy(phase, i):
        index = (phase // 2) * n + i
        slot = at["x_out"][index % X_SLOTS]
        return spread(
            slot, at["x_in"][phase][i], height[phase],
            x_send.at[index], x_recv.at[index], place.x_partner,
        )

    def ring_copy(phase, way, distance, source, part):
        size = height[phase] // 2
        target = at["ring"][phase][way][distance - 1] + part * size
        index = ((phase * 2 + way) * top + distance - 1) * 2 + part
        return spread(
            source + part * size, target, size,
            ring_send.at[index], ring_recv.at[index], ways[way][1],
        )

    def ring_out(phase, distance, part):
        if distance == 0:
            return []
        if distance == top:
            return [ring_copy(phase, part, top, at["far"][phase], part)]
        way = 0 if distance > 0 else 1
        far = abs(distance)
        return [ring_copy(phase, way, far, at["ring"][phase][way][far], part)]

    def part_copy(phase):
        return spread(
            at["part"][phase], at["other"][phase], height[phase],
            part_send.at[phase // 2], part_recv.at[phase // 2], place.x_partner,
        )

    def gain_copy(src, dst, slot, device):
        return remote(src, dst, gain_send.at[slot], gain_recv.at[slot], device)

    def gain_core_copy():
        return gain_copy(gain_mine, gain_core, 0, place.core_partner)

    def gain_x_copy():
        return gain_copy(gain_core, gain_x, 1, place.x_partner)

    def gain_back_copy():
        return gain_copy(gain_mine, gain_x, 2, place.core_partner)

    def gain_ring(way, hop, distance):
        spot = gain_all.at[place.shard(distance)]
        return gain_copy(spot, spot, 3 + way * top + hop - 1, ways[way][1])

    def grad_place(phase, x, which):
        array = PHASES[phase][0]
        return [
            (outs[array].at[:, columns], block(at[which][phase] + first, size))
            for columns, first, size in parts(phase, x)
        ]

    def grad_span(phase, x):
        array, units, split = PHASES[phase]
        if not split:
            return outs[array]
        first = pl.multiple_of(first_column(phase, x), unit)
        return outs[array].at[:, pl.ds(first, units * unit)]

    def grad_sent(phase, to, device, x):
        span = grad_span(phase, x)
        return remote(span, span, grad_send.at[phase, to], grad_recv.at[phase, to], device)

    def matrix_rows(matrix, own_index):
        phase, first, units, tall, _, _ = OWNERS[matrix]
        if tall:
            return [(0, own_index * units * base, units * base)]
        return [
            ((first + k) * base, k * unit + own_index * base, base) for k in range(units)
        ]

    def matrix_span(matrix):
        phase, first, units, tall, xs, _ = OWNERS[matrix]
        array = PHASES[phase][0]
        if tall:
            return orths[array]
        start = (xs * PHASES[phase][1] + first) * unit
        return orths[array].at[:, pl.ds(start, units * unit)]

    def matrix_parts(matrix):
        phase, first, units, tall, xs, _ = OWNERS[matrix]
        array = PHASES[phase][0]
        if tall:
            return [orths[array]]
        start = (xs * PHASES[phase][1] + first) * unit
        return [orths[array].at[:, pl.ds(start + k * unit, unit)] for k in range(units)]

    def handed(matrix, to, device):
        span = matrix_span(matrix)
        return remote(span, span, pass_send.at[matrix, to], pass_recv.at[matrix, to], device)

    def answered(matrix, target):
        span = matrix_span(matrix)
        return remote(
            span, span, out_send.at[target], out_recv.at[matrix], (place.x * 2, target)
        )

    def summed(pieces, size, store):
        step = 16
        steps = 4 if size % (4 * step) == 0 else 1

        def body(k, carry):
            for j in range(steps):
                shift = (k * steps + j) * step
                total = None
                for start in pieces:
                    value = pool[rows_at(start, shift, step), :].astype(F32)
                    total = value if total is None else total + value
                store(shift, step, total)
            return carry

        lax.fori_loop(0, size // (step * steps), body, 0)

    def rows_at(start, shift, step):
        return pl.ds(pl.multiple_of(start + shift, step), step)

    def keep(start):
        def store(shift, step, total):
            pool[rows_at(start, shift, step), :] = total.astype(BF16)

        return store

    def tile_copies(k):
        kind, phase, i = stages[k]
        slot = k_slot[k]
        x = place.x if kind == "ring" else 1 - place.x
        array = PHASES[phase][0]
        span = shard_rows(phase, place.shard(order[i]))
        copies = []
        for which, (name, source) in enumerate((("own", grads), ("land", lands))):
            for columns, first, size in parts(phase, x):
                copies.append(
                    pltpu.make_async_copy(
                        source[array].at[span, columns], block(at[name][slot] + first, size),
                        tile_sem.at[slot, which],
                    )
                )
        return copies

    tiled = [k for k, stage in enumerate(stages) if stage[0] != "final"]
    k_slot = {k: index % TILE_SLOTS for index, k in enumerate(tiled)}

    def prefetch(index, seen):
        if index >= len(tiled):
            return
        k = tiled[index]
        _, phase, i = stages[k]
        if (phase, i) not in seen:
            seen.add((phase, i))
            land_copy(phase, i).wait_recv()
        for copy in tile_copies(k):
            copy.start()

    def wait_tiles(k):
        _, phase, _ = stages[k]
        slot = k_slot[k]
        for which, name in enumerate(("own", "land")):
            span = block(at[name][slot], height[phase])
            pltpu.make_async_copy(span, span, tile_sem.at[slot, which]).wait()

    def moment_copies(phase, act):
        for x in range(2):

            @pl.when(place.x == x)
            def _():
                sources = MOMENTS[phase][x if PHASES[phase][2] else 0]
                if not PHASES[phase][2]:
                    act(moments[sources[0]], moment.at[pl.ds(0, height[phase])])
                    return
                each = PHASES[phase][1] // len(sources)
                for s, source in enumerate(sources):
                    for k in range(each):
                        act(
                            moments[source].at[:, pl.ds(k * unit, unit)],
                            moment.at[pl.ds((s * each + k) * base, base)],
                        )

    def load_moment(phase):
        moment_copies(
            phase, lambda src, dst: pltpu.make_async_copy(src, dst, moment_sem.at[phase]).start()
        )

    def finish(phase, pieces):
        span = moment.at[pl.ds(0, height[phase])]
        pltpu.make_async_copy(span, span, moment_sem.at[phase]).wait()

        if phase >= 2:
            settle(phase - 2)

        def store(shift, step, total):
            pool[rows_at(at["grad"][phase], shift, step), :] = total.astype(BF16)
            ahead = (1.0 + MOMENTUM) * total + MOMENTUM**2 * moment[rows_at(0, shift, step), :]
            pool[rows_at(at["ahead"][phase], shift, step), :] = ahead.astype(BF16)

        summed(pieces, height[phase], store)
        for matrix, (its_phase, _, _, _, xs, _) in enumerate(OWNERS):
            if its_phase != phase:
                continue

            @pl.when(place.x == xs)
            def _():
                for source, target, size in matrix_rows(matrix, place.own):
                    remote(
                        block(at["ahead"][phase] + source, size), block(at["high"][1] + target, size),
                        in_send.at[matrix], in_recv.at[place.own], owners[matrix],
                    ).start()

        for target, source in grad_place(phase, place.x, "grad"):
            pltpu.make_async_copy(source, target, grad_local.at[phase]).start()
            remote(
                source, target, grad_send.at[phase, 0], grad_recv.at[phase, 0], place.core_partner
            ).start()
            if PHASES[phase][2]:
                remote(
                    source, target, grad_send.at[phase, 1], grad_recv.at[phase, 1], place.x_partner
                ).start()
        after = {0: 1, 1: 2, 2: 3, 3: None}[phase]
        if after is not None:
            load_moment(after)

    def settle(phase):
        span = block(at["grad"][phase], height[phase])
        pltpu.make_async_copy(span, span, grad_local.at[phase]).wait()
        remote(
            span, span, grad_send.at[phase, 0], grad_recv.at[phase, 0], place.core_partner
        ).wait_send()
        if PHASES[phase][2]:
            remote(
                span, span, grad_send.at[phase, 1], grad_recv.at[phase, 1], place.x_partner
            ).wait_send()
        for matrix, (its_phase, _, units, _, xs, _) in enumerate(OWNERS):
            if its_phase != phase:
                continue

            @pl.when(place.x == xs)
            def _():
                span = block(at["high"][1], units * base)
                remote(
                    span, span, in_send.at[matrix], in_recv.at[0], place.core_partner
                ).wait_send()

    def stage_x(k, phase, i):
        wait_tiles(k)
        index = (phase // 2) * n + i
        if index >= X_SLOTS:
            before = index - X_SLOTS
            x_copy(1 if before < n else 3, before % n).wait_send()
        slot = k_slot[k]
        summed(
            [at["own"][slot], at["land"][slot]], height[phase], keep(at["x_out"][index % X_SLOTS])
        )
        if phase == 3:
            pl.semaphore_wait(x_free, 1)
        x_copy(phase, i).start()

    def stage_ring(k, phase, i):
        distance = order[i]
        slot = k_slot[k]
        wait_tiles(k)
        pieces = [at["own"][slot], at["land"][slot]]
        if PHASES[phase][2]:
            x_copy(phase, i).wait_recv()
            pieces.append(at["x_in"][phase][i])
        size = height[phase]
        mid = size // 2
        if abs(distance) == 1 and 0 < phase < 3:
            ring_sent(phase - 1)
        if distance == 0:
            for way in range(2):
                held = at["ring"][phase][way][0]
                for part in range(2):
                    ring_copy(phase, way, 1, held, part).wait_recv()
                pieces.append(held)
            if PHASES[phase][2]:
                finish(phase, pieces)
            else:
                summed(pieces, size, keep(at["part"][phase]))
                part_copy(phase).start()
        else:
            way = 0 if distance > 0 else 1
            far = abs(distance)
            held = at["far"][phase] if far == top else at["ring"][phase][way][far]
            for part in (1 - way, way):
                starts = [start + part * mid for start in pieces]
                if far + 1 < top or (far + 1 == top and part == way):
                    ring_copy(phase, way, far + 1, held, part).wait_recv()
                    starts.append(held + part * mid)
                summed(starts, mid, keep(held + part * mid))
                for copy in ring_out(phase, distance, part):
                    copy.start()
        if phase == 1:
            pl.semaphore_signal(x_free, inc=1, device_id=place.x_partner, device_id_type=MESH)

    def ring_sent(phase):
        if phase not in ring_waited:
            ring_waited.add(phase)
            for distance in order:
                for part in range(2):
                    for copy in ring_out(phase, distance, part):
                        copy.wait_send()

    ring_waited = set()

    def gain_stage(hop):
        if hop == 0:
            gain_core_copy().wait_recv()
            gain_core[...] = gain_mine[...] + gain_core[...]
            gain_x_copy().start()
            return
        if hop == 1:
            gain_x_copy().wait_recv()
            gain_all[place.own] = gain_core[...] + gain_x[...]
            for way in range(2):
                gain_ring(way, 1, 0).start()
        for way in range(2):
            if 1 < hop <= hops(n, way, 0) + 1:
                distance = -ways[way][0] * (hop - 1)
                gain_ring(way, hop - 1, distance).wait_recv()
                if hop <= hops(n, way, 0):
                    gain_ring(way, hop, distance).start()

    gain_mine[...] = gains_in[...]

    @pl.when(place.core == 0)
    def _():
        load_moment(0)
        seen = set()
        for index in range(TILE_SLOTS - 1):
            prefetch(index, seen)
        done = 0
        hop = 0
        for k, (kind, phase, i) in enumerate(stages):
            if kind == "final":
                part_copy(phase).wait_recv()
                finish(phase, [at["part"][phase], at["other"][phase]])
                continue
            prefetch(done + TILE_SLOTS - 1, seen)
            done += 1
            if kind == "x":
                stage_x(k, phase, i)
            else:
                stage_ring(k, phase, i)
            if done % 3 == 0 and hop <= top + 1:
                gain_stage(hop)
                hop += 1

        total = gain_all[0]
        for k in range(1, n):
            total = total + gain_all[k]
        gains_out[...] = total
        gain_mine[...] = total
        gain_back_copy().start()

        for phase in (1, 3):
            grad_sent(phase, 1, place.x_partner, 1 - place.x).wait_recv()
            grad_sent(phase, 2, place.core_partner, 1 - place.x).start()

        for matrix in RETURNS:
            xs = OWNERS[matrix][4]

            @pl.when(place.x == xs)
            def _():
                answered(matrix, place.own).wait_recv()
                handed(matrix, 0, place.x_partner).start()
                handed(matrix, 1, place.core_partner).start()

            @pl.when(place.x != xs)
            def _():
                handed(matrix, 0, place.x_partner).wait_recv()
                handed(matrix, 1, place.core_partner).start()

        for matrix, (phase, _, units, _, xs, _) in enumerate(OWNERS):
            handed(matrix, 1, place.core_partner).wait_send()

            @pl.when(place.x == xs)
            def _():
                handed(matrix, 0, place.x_partner).wait_send()

        for phase, (_, _, split) in enumerate(PHASES):
            if phase >= 2:
                settle(phase)
            if split:
                grad_sent(phase, 2, place.core_partner, 1 - place.x).wait_send()
            else:
                part_copy(phase).wait_send()
            ring_sent(phase)
        for index in range(2 * n - X_SLOTS, 2 * n):
            x_copy(1 if index < n else 3, index % n).wait_send()
        gain_x_copy().wait_send()
        gain_back_copy().wait_send()
        for way in range(2):
            for h in range(1, hops(n, way, 0) + 1):
                gain_ring(way, h, -ways[way][0] * (h - 1)).wait_send()

    @pl.when(place.core == 1)
    def _():
        gain_core_copy().start()
        needed = []
        for kind, phase, i in stages:
            if kind != "final" and (phase, i) not in needed:
                needed.append((phase, i))
        ahead = 8
        for index, (phase, i) in enumerate(needed):
            if index >= ahead:
                land_copy(*needed[index - ahead]).wait_send()
            land_copy(phase, i).start()
        for phase, i in needed[-ahead:]:
            land_copy(phase, i).wait_send()
        newton_part(n, unit, place, pool, exact, gram, squares, at, is_owner, in_recv)
        for matrix, (_, _, units, tall, _, _) in enumerate(OWNERS):

            @pl.when(is_owner[matrix])
            def _():
                final = at["high"][1 - NS_STEPS % 2 if tall else NS_STEPS % 2]

                def send(k, carry):
                    target = lax.rem(place.own + k, n)
                    for part, (_, row, size) in zip(matrix_parts(matrix), matrix_rows(matrix, target)):
                        remote(
                            block(final + row, size), part, out_send.at[target], out_recv.at[matrix],
                            (place.x * 2, target),
                        ).start()
                    return carry

                lax.fori_loop(0, n, send, 0)

                def sent(k, carry):
                    answered(matrix, lax.rem(place.own + k, n)).wait_send()
                    return carry

                lax.fori_loop(0, n, sent, 0)

        gain_core_copy().wait_send()
        gain_back_copy().wait_recv()
        gains_out[...] = gain_x[...]
        for phase, (_, _, split) in enumerate(PHASES):
            grad_sent(phase, 0, place.core_partner, place.x).wait_recv()
            if split:
                grad_sent(phase, 2, place.core_partner, 1 - place.x).wait_recv()
        for matrix in RETURNS:
            handed(matrix, 1, place.core_partner).wait_recv()


def newton_part(n, unit, place, pool, exact, gram, squares, at, is_owner, in_recv):
    base = unit // n
    small = min(256, unit // 2)
    per = unit // small
    few = 32
    count, tall = 0, 0
    for mine, (_, _, units, lies_tall, _, _) in zip(is_owner, OWNERS):
        count = count + units * mine.astype(jnp.int32)
        tall = tall + int(lies_tall) * mine.astype(jnp.int32)
    high, poly = at["high"], at["poly"]

    def rows(start, size):
        return pl.ds(pl.multiple_of(start, size), size)

    for matrix, (_, _, units, *_) in enumerate(OWNERS):

        @pl.when(is_owner[matrix])
        def _():
            span = pool.at[pl.ds(high[1], units * base)]
            for own_index in range(n):
                remote(
                    span, span, in_recv.at[own_index], in_recv.at[own_index], place.core_partner
                ).wait_recv()

    @pl.when(count > 0)
    def _():
        squares[...] = jnp.zeros_like(squares)

        def square(k, carry):
            part = pool[rows(high[1] + k * few, few), :].astype(F32)
            squares[...] += jnp.sum((part * part).reshape(few // 8, 8, unit), 0)
            return carry

        lax.fori_loop(0, count * (unit // few), square, 0)
        total = jnp.sum(jnp.sum(squares[...], 1, keepdims=True), 0, keepdims=True)
        inverse = 1.0 / (jnp.sqrt(total) + 1e-07)

        @pl.when(tall == 0)
        def _():
            def scale(k, carry):
                value = pool[rows(high[1] + k * few, few), :].astype(F32) * inverse
                exact[rows(k * few, few), :] = value
                pool[rows(high[0] + k * few, few), :] = value.astype(BF16)
                return carry

            lax.fori_loop(0, count * (unit // few), scale, 0)

        @pl.when(tall == 1)
        def _():
            def scale(k, carry):
                block, row = k // per, k % per
                for column in range(per):
                    part = pool[
                        rows(high[1] + k * small, small), pl.ds(column * small, small)
                    ].astype(F32)
                    value = (part * inverse).T
                    shift = block * unit + column * small
                    columns = rows(row * small, small)
                    exact[rows(shift, small), columns] = value
                    pool[rows(high[0] + shift, small), columns] = value.astype(BF16)
                return carry

            lax.fori_loop(0, count * per, scale, 0)

        def newton(step, carry):
            even = step % 2
            now = high[0] + even * (high[1] - high[0])
            later = high[1] - even * (high[1] - high[0])

            def keep_symmetric(to, chunk, value):
                pool[pl.ds(to, (chunk + 1) * small), pl.ds(chunk * small, small)] = value.astype(BF16)
                for row in range(chunk):
                    pool[pl.ds(to + chunk * small, small), pl.ds(row * small, small)] = (
                        value[row * small : (row + 1) * small].T.astype(BF16)
                    )

            for chunk in range(per):
                down = (chunk + 1) * small

                def product(block):
                    left = pool[pl.ds(pl.multiple_of(now + block * unit, unit), down), :]
                    right = pool[rows(now + block * unit + chunk * small, small), :]
                    return lax.dot_general(
                        left, right, (((1,), (1,)), ((), ())), preferred_element_type=F32
                    )

                gram[:down, :] = product(0)

                def more(block, carry):
                    gram[:down, :] += product(block)
                    return carry

                lax.fori_loop(1, count, more, 0)
                keep_symmetric(poly[0], chunk, gram[:down, :])

            for chunk in range(per):
                down = (chunk + 1) * small
                columns = pl.ds(chunk * small, small)
                squared = jnp.dot(
                    pool[pl.ds(poly[0], down), :], pool[pl.ds(poly[0], unit), columns],
                    preferred_element_type=F32,
                )
                plain = pool[pl.ds(poly[0], down), columns].astype(F32)
                keep_symmetric(poly[1], chunk, NEWTON_B * plain + NEWTON_C * squared)

            def advance(block, carry):
                for chunk in range(per):
                    columns = pl.ds(chunk * small, small)
                    value = NEWTON_A * exact[rows(block * unit, unit), columns] + jnp.dot(
                        pool[pl.ds(poly[1], unit), :],
                        pool[rows(now + block * unit, unit), columns],
                        preferred_element_type=F32,
                    )
                    exact[rows(block * unit, unit), columns] = value
                    pool[rows(later + block * unit, unit), columns] = value.astype(BF16)
                return carry

            lax.fori_loop(0, count, advance, 0)
            return carry

        lax.fori_loop(0, NS_STEPS, newton, 0)

        @pl.when(tall == 1)
        def _():
            free = high[1 - NS_STEPS % 2]
            factor = jnp.sqrt(jnp.full((1, 1), count, jnp.int32).astype(F32))

            def lay(k, carry):
                block, row = k // per, k % per
                for column in range(per):
                    columns = pl.ds(column * small, small)
                    part = exact[rows(k * small, small), columns]
                    pool[
                        rows(free + block * unit + column * small, small), rows(row * small, small)
                    ] = (part * factor).T.astype(BF16)
                return carry

            lax.fori_loop(0, count * per, lay, 0)


def update_all(grads, moments, gains, n, unit):
    top = n // 2
    dma = pltpu.SemaphoreType.DMA
    vmem = pltpu.VMEM
    _, pool_rows = layout(n, unit)
    own = [jax.ShapeDtypeStruct((grad.shape[0] // n, grad.shape[1]), BF16) for grad in grads]
    whole = [jax.ShapeDtypeStruct(grad.shape, BF16) for grad in grads]
    in_vmem = pl.BlockSpec(memory_space=pltpu.VMEM)
    results = pl.pallas_call(
        functools.partial(update_kernel, n, unit),
        out_shape=own + own + whole + [jax.ShapeDtypeStruct(gains.shape, F32)],
        in_specs=[ANY] * 11 + [in_vmem],
        out_specs=[ANY] * 12 + [in_vmem],
        scratch_shapes=[
            vmem((pool_rows, unit), BF16),
            vmem((3 * unit, unit), F32),
            vmem((unit, min(256, unit // 2)), F32),
            vmem((8, unit), F32),
            vmem(gains.shape, F32),
            vmem(gains.shape, F32),
            vmem(gains.shape, F32),
            vmem((n,) + gains.shape, F32),
            dma((4 * n,)),
            dma((4 * n,)),
            dma((TILE_SLOTS, 2)),
            dma((2 * n,)),
            dma((2 * n,)),
            pltpu.SemaphoreType.REGULAR,
            dma((16 * top,)),
            dma((16 * top,)),
            dma((2,)),
            dma((2,)),
            dma((4,)),
            dma((4,)),
            dma((4, 3)),
            dma((4, 3)),
            dma((7,)),
            dma((n,)),
            dma((n,)),
            dma((7,)),
            dma((7, 2)),
            dma((7, 2)),
            dma((3 + 2 * top,)),
            dma((3 + 2 * top,)),
        ],
        compiler_params=pltpu.CompilerParams(
            collective_id=1, has_side_effects=True, vmem_limit_bytes=56 * 2**20
        ),
    )(*grads, *moments, gains)
    return results[:4], results[4:8], results[12]


def packed(matrices):
    query, key, value, out, gate, up, down = matrices
    return (
        jnp.concatenate([query, key, value], 1),
        out,
        jnp.concatenate([gate, up], 1),
        down,
    )


def unpacked(arrays, unit):
    qkv, out, gate_up, down = arrays
    return (
        qkv[:, : 2 * unit],
        qkv[:, 2 * unit : 3 * unit],
        qkv[:, 3 * unit :],
        out,
        gate_up[:, : 3 * unit],
        gate_up[:, 3 * unit :],
        down,
    )


def body(
    layer_input,
    output_grad,
    lengths,
    attention_gain,
    feed_gain,
    query_gain,
    key_gain,
    query_weight,
    key_weight,
    value_weight,
    out_weight,
    gate_weight,
    up_weight,
    down_weight,
    query_moment,
    key_moment,
    value_moment,
    out_moment,
    gate_moment,
    up_moment,
    down_moment,
):
    owned = (
        query_weight, key_weight, value_weight, out_weight, gate_weight, up_weight, down_weight,
    )
    moments = (
        query_moment, key_moment, value_moment, out_moment, gate_moment, up_moment, down_moment,
    )
    n = lax.axis_size("own")
    unit = layer_input.shape[1]
    q_width, kv_width, ff = 2 * unit, unit, 3 * unit
    low_shards = packed([matrix.astype(BF16) for matrix in owned])
    qkv_full, out_full, gu_full, down_full = gather_weights(low_shards, n, unit)

    row_count = layer_input.shape[0]
    group_size = HEADS // KV_HEADS
    segment_ids, positions = segments(lengths[0], row_count)
    cosine_table, sine_table = rope_tables(positions)
    normed_value, norm_pullback = jax.vjp(rms_scale, layer_input, attention_gain)
    normed = normed_value.astype(BF16)
    raw = jnp.dot(normed, qkv_full, preferred_element_type=F32)
    query_raw = raw[:, :q_width]
    key_raw = raw[:, q_width : q_width + kv_width]
    value_raw = raw[:, q_width + kv_width :]
    query_rot, query_pullback = jax.vjp(
        lambda raw_value, gain_vector: head_side(raw_value, gain_vector, cosine_table, sine_table),
        query_raw,
        query_gain,
    )
    key_rot, key_pullback = jax.vjp(
        lambda raw_value, gain_vector: head_side(raw_value, gain_vector, cosine_table, sine_table),
        key_raw,
        key_gain,
    )
    queries = query_rot.astype(BF16).reshape(row_count, KV_HEADS, group_size, HEAD_DIM)
    keys = key_rot.astype(BF16)
    values = value_raw.astype(BF16).reshape(row_count, KV_HEADS, HEAD_DIM)
    row_ids = jnp.arange(row_count, dtype=jnp.int32)
    score_scale = HEAD_DIM ** (-0.5)
    raw_scores = (
        jnp.einsum("tkgd,skd->kgts", queries, keys, preferred_element_type=F32) * score_scale
    )
    allowed = (segment_ids[:, None] == segment_ids[None, :]) & (
        row_ids[:, None] >= row_ids[None, :]
    )
    masked = jnp.where(allowed, raw_scores, -1e30)
    maximum = jnp.max(masked, -1, keepdims=True)
    exponent = jnp.exp(masked - maximum)
    totals = jnp.sum(exponent, -1, keepdims=True)
    probs_full = exponent / totals
    probs_low = probs_full.astype(BF16)
    context = jnp.einsum("kgts,skd->tkgd", probs_low, values, preferred_element_type=F32)
    context = context.reshape(row_count, q_width).astype(BF16)
    middle = layer_input + jnp.dot(context, out_full, preferred_element_type=F32)
    hidden_value, middle_pullback = jax.vjp(rms_scale, middle, feed_gain)
    hidden = hidden_value.astype(BF16)
    gate_up = jnp.dot(hidden, gu_full, preferred_element_type=F32)
    activated_value, swiglu_pullback = jax.vjp(swiglu, gate_up[:, :ff], gate_up[:, ff:])
    activated = activated_value.astype(BF16)
    block_output = middle + jnp.dot(activated, down_full, preferred_element_type=F32)

    out_low = output_grad.astype(BF16)
    grad_down = jnp.einsum("tf,td->fd", activated, out_low, preferred_element_type=F32)
    grad_activated = jnp.einsum("td,fd->tf", out_low, down_full, preferred_element_type=F32)
    grad_gate_value, grad_up_value = swiglu_pullback(grad_activated)
    gu_back = jnp.concatenate([grad_gate_value.astype(BF16), grad_up_value.astype(BF16)], 1)
    grad_gu = jnp.einsum("td,tf->df", hidden, gu_back, preferred_element_type=F32)
    grad_hidden = jnp.einsum("tf,df->td", gu_back, gu_full, preferred_element_type=F32)
    grad_middle_norm, grad_feed = middle_pullback(grad_hidden)
    grad_middle = output_grad + grad_middle_norm
    attended_low = grad_middle.astype(BF16)
    grad_out = jnp.einsum("ti,td->id", context, attended_low, preferred_element_type=F32)
    grad_context = jnp.einsum("td,id->ti", attended_low, out_full, preferred_element_type=F32)
    grad_context = grad_context.astype(BF16).reshape(row_count, KV_HEADS, group_size, HEAD_DIM)
    grad_values = jnp.einsum("kgts,tkgd->skd", probs_low, grad_context, preferred_element_type=F32)
    grad_probs = jnp.einsum("tkgd,skd->kgts", grad_context, values, preferred_element_type=F32)
    grad_scores = probs_full * (
        grad_probs - jnp.sum(probs_full * grad_probs, -1, keepdims=True)
    )
    grad_scores = grad_scores.astype(BF16)
    grad_queries = (
        jnp.einsum("kgts,skd->tkgd", grad_scores, keys, preferred_element_type=F32) * score_scale
    )
    grad_keys = (
        jnp.einsum("kgts,tkgd->skd", grad_scores, queries, preferred_element_type=F32)
        * score_scale
    )
    grad_query_raw, grad_query_gain = query_pullback(
        grad_queries.reshape(row_count, HEADS, HEAD_DIM)
    )
    grad_key_raw, grad_key_gain = key_pullback(grad_keys)
    qkv_back = jnp.concatenate(
        [
            grad_query_raw.astype(BF16),
            grad_key_raw.astype(BF16),
            grad_values.reshape(row_count, kv_width).astype(BF16),
        ],
        1,
    )
    grad_qkv = jnp.einsum("td,tq->dq", normed, qkv_back, preferred_element_type=F32)
    grad_normed = jnp.einsum("tq,dq->td", qkv_back, qkv_full, preferred_element_type=F32)
    grad_input_norm, grad_attention = norm_pullback(grad_normed)
    input_grad = grad_middle + grad_input_norm

    gains = jnp.concatenate([grad_attention, grad_feed, grad_query_gain, grad_key_gain])
    gains = jnp.pad(gains, (0, 24 * 128 - gains.shape[0])).reshape(24, 128)
    grads = [grad.astype(BF16) for grad in (grad_qkv, grad_out, grad_gu, grad_down)]
    reduced, orth, gain_sums = update_all(grads, moments, gains, n, unit)
    moments_next = [
        MOMENTUM * moment + part.astype(F32) for moment, part in zip(moments, unpacked(reduced, unit))
    ]
    new_weights = [
        matrix * (1.0 - LEARN_RATE * WEIGHT_DECAY) - LEARN_RATE * part.astype(F32)
        for matrix, part in zip(owned, unpacked(orth, unit))
    ]
    gain_sums = gain_sums.reshape(-1)
    norm_grads = gain_sums[: 2 * unit].reshape(2, unit)
    head_grads = gain_sums[2 * unit : 2 * unit + 2 * HEAD_DIM].reshape(2, HEAD_DIM)
    return (block_output, input_grad, norm_grads, head_grads, *new_weights, *moments_next)


def solution(mesh):
    tokens, owned = P(("rep", "own"), None), P("own", None)
    return jax.shard_map(
        body,
        mesh=mesh,
        in_specs=(tokens,) * 3 + (P(),) * 4 + (owned,) * 14,
        out_specs=(tokens,) * 2 + (P(),) * 2 + (owned,) * 14,
        check_vma=False,
    )
```

```python
import functools

import jax
import jax.numpy as jnp
from jax import lax
from jax.experimental import pallas as pl
from jax.experimental.pallas import tpu as pltpu
from jax.sharding import PartitionSpec as P

HEADS = 16
KV_HEADS = 8
HEAD_DIM = 128
NS_STEPS = 5

EPSILON = 1e-06
ROPE_BASE = 1000000.0
MOMENTUM = 0.95
LEARN_RATE = 0.8
WEIGHT_DECAY = 0.01
NEWTON_A = 3.4445
NEWTON_B = -4.775
NEWTON_C = 2.0315

BF16 = jnp.bfloat16
F32 = jnp.float32
MESH = pl.DeviceIdType.MESH
ANY = pl.BlockSpec(memory_space=pltpu.HBM)

QKV, OUT, GU, DOWN = range(4)


def segments(lengths, row_count):
    seq_ends = jnp.cumsum(lengths)
    seq_starts = seq_ends - lengths
    row_ids = jnp.arange(row_count, dtype=jnp.int32)
    segment_ids = jnp.sum((row_ids[:, None] >= seq_ends[None, :]).astype(jnp.int32), 1)
    slot_ids = jnp.arange(lengths.shape[0], dtype=jnp.int32)
    row_starts = jnp.sum(
        jnp.where(segment_ids[:, None] == slot_ids[None, :], seq_starts[None, :], 0), 1
    )
    return (segment_ids, row_ids - row_starts)


def rope_tables(positions):
    inverse = ROPE_BASE ** (-jnp.arange(0, HEAD_DIM, 2, dtype=jnp.float32) / HEAD_DIM)
    angles = positions.astype(jnp.float32)[:, None] * inverse[None, :]
    return (jnp.cos(angles)[:, None, :], jnp.sin(angles)[:, None, :])


class Place:
    def __init__(self, n):
        self.n = n
        self.rep = lax.axis_index("rep")
        self.own = lax.axis_index("own")
        self.x = self.rep // 2
        self.core = self.rep % 2
        odd, pair = self.own % 2, self.own // 2
        self.ring = pair * (1 - odd) + odd * (n - 1 - pair)

    def own_at(self, ring):
        odd = ring // (self.n // 2)
        return 2 * (ring * (1 - odd) + odd * (self.n - 1 - ring)) + odd

    def shard(self, distance):
        return self.own_at(lax.rem(self.ring + distance + self.n, self.n))

    def ring_neighbour(self, way):
        return (self.rep, self.shard(way))

    @property
    def core_partner(self):
        return (self.x * 2 + 1 - self.core, self.own)

    @property
    def x_partner(self):
        return ((1 - self.x) * 2 + self.core, self.own)


def greet(devices):
    barrier = pltpu.get_barrier_semaphore()
    for device in devices:
        pl.semaphore_signal(barrier, inc=1, device_id=device, device_id_type=MESH)
    pl.semaphore_wait(barrier, len(devices))


class Several:
    def __init__(self, whole, copies):
        self.whole = whole
        self.copies = copies

    def start(self):
        for copy in self.copies:
            copy().start()

    def wait_send(self):
        self.whole().wait_send()

    def wait_recv(self):
        self.whole().wait_recv()


def remote(src, dst, send, recv, device):
    return pltpu.make_async_remote_copy(
        src_ref=src, dst_ref=dst, send_sem=send, recv_sem=recv, device_id=device, device_id_type=MESH
    )


def hops(n, way, kind):
    return n // 2 if (way == 0) == (kind == 0) else n // 2 - 1


SPREADS = ((QKV, True), (OUT, False), (GU, True), (DOWN, False))


def layer_kernel(n, tokens, unit, *refs):
    (
        x_ref, back_ref, table_ref, attention_gain, feed_gain, query_gain, key_gain,
    ) = refs[:7]
    shards = refs[7:11]
    output, input_grad, grad_attention, grad_feed, grad_query_gain, grad_key_gain = refs[11:17]
    grads = refs[17:21]
    (
        w_qkv, w_out, w_gu, w_down, normed, raw, low, probs, context, hidden, out_low, attended,
        grad_context, activated, gu_back, part, sent, got, middle, tables, stage, gain_sums,
        local, ring_send, ring_recv, x_send, x_recv, swap_send, swap_recv, stage_sem,
    ) = refs[21:]
    weights = (w_qkv, w_out, w_gu, w_down)
    place = Place(n)
    top = n // 2
    cw, ccw = place.ring_neighbour(1), place.ring_neighbour(-1)
    ways = ((1, cw), (-1, ccw))
    greet([cw, ccw, place.core_partner, place.x_partner])
    both = 2 * tokens
    mine = pl.multiple_of(place.core * tokens, tokens)
    theirs = pl.multiple_of((1 - place.core) * tokens, tokens)
    my_rows, their_rows = pl.ds(mine, tokens), pl.ds(theirs, tokens)
    chunk = unit // 4
    ff = 3 * unit // 2
    few = 32
    base = unit // n
    heads = unit // HEAD_DIM
    kv_heads = heads // 2
    scale = HEAD_DIM ** (-0.5)

    def holds(which, own_index, act):
        if SPREADS[which][1]:
            act()
        else:
            pl.when(own_index // top == place.core)(act)

    def region(which, own_index, x):
        array, split = SPREADS[which]
        height = shards[which].shape[0]
        if split:
            width = weights[which].shape[1] // 2
            start = pl.multiple_of(own_index * height, height)
            return weights[which].at[pl.ds(start, height), pl.ds(pl.multiple_of(x * width, width), width)]
        start = pl.multiple_of(lax.rem(own_index, top) * height, height)
        return weights[which].at[pl.ds(start, height)]

    def own_copy(which):
        height = shards[which].shape[0]
        index = place.own if SPREADS[which][1] else lax.rem(place.own, top)
        start = pl.multiple_of(index * height, height)
        return pltpu.make_async_copy(
            shards[which], weights[which].at[pl.ds(start, height)], local.at[which]
        )

    def reach(which, way):
        return hops(n, way, 0 if SPREADS[which][1] else 1)

    def ring_copy(which, way, hop, act):
        step, target = ways[way]
        own_index = place.shard(-step * (hop if act == "wait_recv" else hop - 1))
        spot = region(which, own_index, place.x)
        index = (which * 2 + way) * top + hop - 1

        def do():
            copy = remote(spot, spot, ring_send.at[index], ring_recv.at[index], target)
            getattr(copy, act)()

        holds(which, own_index, do)

    def send_on(which, way, hop):
        ring_copy(which, way, hop, "start")

    def x_copy(which, way, hop, x):
        spot = region(which, place.shard(-ways[way][0] * hop), x)
        index = (which // 2 * 2 + way) * top + hop - 1
        return remote(spot, spot, x_send.at[index], x_recv.at[index], place.x_partner)

    def serve(which, hop):
        for way in range(2):
            if hop > reach(which, way):
                continue
            ring_copy(which, way, hop, "wait_recv")
            if hop < reach(which, way):
                send_on(which, way, hop + 1)
            if SPREADS[which][1]:
                x_copy(which, way, hop, place.x).start()

    def begin(which):
        def act():
            own_copy(which).wait()

        holds(which, place.own, act)
        for way in range(2):
            if reach(which, way) > 0:
                send_on(which, way, 1)

    def take_x(which):
        for way in range(2):
            for hop in range(1, reach(which, way) + 1):
                x_copy(which, way, hop, 1 - place.x).wait_recv()

    def swap(index, src, dst):
        return remote(src, dst, swap_send.at[index], swap_recv.at[index], place.core_partner)

    def rows_swap(index, ref):
        return swap(index, ref.at[my_rows], ref.at[my_rows])

    def part_swap(index, slot):
        return swap(index, sent.at[slot], got.at[slot])

    def loop(size, step, act):
        def body(k, carry):
            act(pl.multiple_of(k * step, step))
            return carry

        lax.fori_loop(0, size // step, body, 0)

    def normalize(source, gain, target):
        def act(k):
            value = source[pl.ds(k, few), :]
            value = value * lax.rsqrt(jnp.mean(value * value, -1, keepdims=True) + EPSILON)
            target[pl.ds(pl.multiple_of(mine + k, few), few), :] = (value * gain[...]).astype(BF16)

        loop(tokens, few, act)

    def normalize_back(k, source, gain, grad):
        value = source[pl.ds(k, few), :]
        inverse = lax.rsqrt(jnp.mean(value * value, -1, keepdims=True) + EPSILON)
        unscaled = value * inverse
        inner = grad * gain[...]
        back = inverse * (inner - unscaled * jnp.mean(inner * unscaled, -1, keepdims=True))
        return back, jnp.sum((grad * unscaled).reshape(few // 8, 8, unit), 0)

    def dot(left, right, across):
        return lax.dot_general(left, right, ((across[0], across[1]), ((), ())), preferred_element_type=F32)

    NN, NT, TN = ((1,), (0,)), ((1,), (1,)), ((0,), (0,))

    def partial_product(index, slot, left, right, across, by_rows):
        def act(k):
            span = pl.ds(k, chunk)
            factor = right[span, :] if by_rows else right[:, span]
            part[:, span] = dot(left[...], factor, across)

        loop(unit, chunk, act)

        def pack(k):
            sent[slot, pl.ds(k, few), :] = part[
                pl.ds(pl.multiple_of(theirs + k, few), few), :
            ].astype(BF16)

        loop(tokens, few, pack)
        part_swap(index, slot).start()

    def whole_rows(k, slot):
        own = part[pl.ds(pl.multiple_of(mine + k, few), few), :]
        return own + got[slot, pl.ds(k, few), :].astype(F32)

    staged = [0]

    def weight_grad(which, left, right, rows, columns):
        height, width = rows, min(columns, unit)
        blocks = [(r, c) for r in range(0, left.shape[1], height) for c in range(0, columns, width)]
        per_row = columns // width
        count = len(blocks)

        def act(k, carry):
            row = pl.multiple_of(k // per_row * height, height)
            column = pl.multiple_of(k % per_row * width, width)
            slot = lax.rem(k, 2)

            @pl.when(k >= 2)
            def _():
                stage_copy(which, slot, row, column, height, width).wait()

            value = dot(left[:, pl.ds(row, height)], right[:, pl.ds(column, width)], TN)
            stage[slot] = value.astype(BF16)
            stage_copy(which, slot, row, column, height, width).start()
            return carry

        lax.fori_loop(0, count, act, 0)
        for slot in range(2):
            stage_copy(which, slot, 0, 0, height, width).wait()

    def stage_copy(which, slot, row, column, height, width):
        return pltpu.make_async_copy(
            stage.at[slot], grads[which].at[pl.ds(row, height), pl.ds(column, width)],
            stage_sem.at[slot],
        )

    for which in range(4):
        holds(which, place.own, lambda: own_copy(which).start())
    tables[my_rows, :] = table_ref[...]
    normalize(x_ref, attention_gain, normed)
    rows_swap(0, normed).start()
    rows_swap(1, tables).start()
    begin(0)
    begin(1)

    def round_back(k):
        out_low[pl.ds(pl.multiple_of(mine + k, few), few), :] = back_ref[pl.ds(k, few), :].astype(BF16)

    loop(tokens, few, round_back)
    rows_swap(2, out_low).start()
    gain_sums[...] = jnp.zeros_like(gain_sums)

    late = [(1, top)] if top < 3 else [(1, h) for h in range(3, top + 1)]
    serve(0, 1)
    serve(1, 1)
    begin(2)
    for hop in range(2, top + 1):
        serve(0, hop)
        if (1, hop) not in late:
            serve(1, hop)
        if hop == 2:
            serve(2, 1)
    take_x(0)
    begin(3)
    pending = late + [(2, h) for h in range(2, top)] + [(3, 1), (2, top)]
    pending += [(3, h) for h in range(2, top + 1)]
    for name in (0, 1):
        rows_swap(name, (normed, tables)[name]).wait_recv()

    def project(k):
        span = pl.ds(k, chunk)
        raw[:, span] = dot(normed[...], w_qkv[:, span], NN)

    loop(2 * unit, chunk, project)
    serve(*pending.pop(0))

    def turned(value, rows):
        return value * tables[rows, pl.ds(0, HEAD_DIM)] + pltpu.roll(
            value, HEAD_DIM // 2, 1
        ) * tables[rows, pl.ds(HEAD_DIM, HEAD_DIM)]

    def turned_back(value, rows):
        return value * tables[rows, pl.ds(0, HEAD_DIM)] - pltpu.roll(
            value, HEAD_DIM // 2, 1
        ) * tables[rows, pl.ds(HEAD_DIM, HEAD_DIM)]

    def head_norm(first, count, gain):
        def act(k):
            for half in range(2):
                rows = pl.ds(half * tokens, tokens)
                columns = pl.ds(pl.multiple_of(first + k, HEAD_DIM), HEAD_DIM)
                value = raw[rows, columns]
                inverse = lax.rsqrt(jnp.mean(value * value, -1, keepdims=True) + EPSILON)
                low[rows, columns] = turned(value * inverse * gain[...], rows).astype(BF16)

        loop(count * HEAD_DIM, HEAD_DIM, act)

    head_norm(0, heads, query_gain)
    if pending:
        serve(*pending.pop(0))
    head_norm(unit, kv_heads, key_gain)
    low[:, pl.ds(unit + unit // 2, unit // 2)] = raw[:, pl.ds(unit + unit // 2, unit // 2)].astype(BF16)

    def spans(k, half):
        queries = [pl.ds(pl.multiple_of((2 * k + g) * HEAD_DIM, HEAD_DIM), HEAD_DIM) for g in range(2)]
        keys = pl.ds(pl.multiple_of(unit + k * HEAD_DIM, HEAD_DIM), HEAD_DIM)
        values = pl.ds(pl.multiple_of(unit + unit // 2 + k * HEAD_DIM, HEAD_DIM), HEAD_DIM)
        return queries, keys, values, pl.ds(half * tokens, tokens)

    def attend(k, half):
        queries, keys, values, rows = spans(k, half)
        row_id = lax.broadcasted_iota(jnp.int32, (tokens, tokens), 0)
        column_id = lax.broadcasted_iota(jnp.int32, (tokens, tokens), 1)
        start = tables[rows, pl.ds(2 * HEAD_DIM, HEAD_DIM)][:, :1]
        allowed = (column_id <= row_id) & (column_id.astype(F32) >= start)
        for g in range(2):
            scores = dot(low[rows, queries[g]], low[rows, keys], NT) * scale
            scores = jnp.where(allowed, scores, -1e30)
            exponent = jnp.exp(scores - jnp.max(scores, -1, keepdims=True))
            value = exponent / jnp.sum(exponent, -1, keepdims=True)
            probs[(k * 2 + half) * 2 + g] = value
            context[rows, queries[g]] = dot(value.astype(BF16), low[rows, values], NN).astype(BF16)

    for k in range(kv_heads):
        for half in range(2):
            attend(k, half)
        if pending and k % 2 == 0:
            serve(*pending.pop(0))

    while pending and pending[0][0] == 1:
        serve(*pending.pop(0))
    partial_product(3, 0, context, w_out, NN, False)
    if pending and pending[0][0] == 2:
        serve(*pending.pop(0))
    part_swap(3, 0).wait_recv()

    def add_middle(k):
        middle[pl.ds(k, few), :] = x_ref[pl.ds(k, few), :] + whole_rows(k, 0)

    loop(tokens, few, add_middle)
    normalize(middle, feed_gain, hidden)
    rows_swap(4, hidden).start()
    while pending:
        serve(*pending.pop(0))
    take_x(2)
    rows_swap(4, hidden).wait_recv()
    rows_swap(2, out_low).wait_recv()

    def feed(k):
        span = pl.ds(k, chunk)
        gate = dot(hidden[...], w_gu[:, span], NN)
        up_columns = pl.ds(pl.multiple_of(ff + k, chunk), chunk)
        up = dot(hidden[...], w_gu[:, up_columns], NN)
        grad = dot(out_low[...], w_down[span, :], NT)
        sigmoid = 1.0 / (1.0 + jnp.exp(-gate))
        swish = gate * sigmoid
        activated[:, span] = (swish * up).astype(BF16)
        gu_back[:, span] = (grad * up * (sigmoid + swish * (1.0 - sigmoid))).astype(BF16)
        gu_back[:, up_columns] = (grad * swish).astype(BF16)

    loop(ff, chunk, feed)
    part_swap(3, 0).wait_send()
    partial_product(6, 0, gu_back, w_gu, NT, True)
    weight_grad(3, activated, out_low, chunk, unit)
    part_swap(6, 0).wait_recv()

    def middle_back(k):
        back, gain_part = normalize_back(k, middle, feed_gain, whole_rows(k, 0))
        back = back_ref[pl.ds(k, few), :] + back
        input_grad[pl.ds(k, few), :] = back
        attended[pl.ds(pl.multiple_of(mine + k, few), few), :] = back.astype(BF16)
        gain_sums[1] += gain_part

    loop(tokens, few, middle_back)
    rows_swap(7, attended).start()
    partial_product(5, 1, activated, w_down, NN, False)
    weight_grad(2, hidden, gu_back, chunk, 3 * unit)
    part_swap(5, 1).wait_recv()

    def add_output(k):
        output[pl.ds(k, few), :] = middle[pl.ds(k, few), :] + whole_rows(k, 1)

    loop(tokens, few, add_output)
    rows_swap(7, attended).wait_recv()

    def context_back(k):
        span = pl.ds(k, chunk)
        grad_context[:, span] = dot(attended[...], w_out[span, :], NT).astype(BF16)

    loop(unit, chunk, context_back)
    weight_grad(1, context, attended, chunk, unit)

    def head_back(rows, columns, gain, grad, index):
        value = raw[rows, columns]
        inverse = lax.rsqrt(jnp.mean(value * value, -1, keepdims=True) + EPSILON)
        unscaled = value * inverse
        grad = turned_back(grad, rows)
        gain_sums[index, :, pl.ds(0, HEAD_DIM)] += jnp.sum(
            (grad * unscaled).reshape(tokens // 8, 8, HEAD_DIM), 0
        )
        inner = grad * gain[...]
        back = inverse * (inner - unscaled * jnp.mean(inner * unscaled, -1, keepdims=True))
        low[rows, columns] = back.astype(BF16)

    def attend_back(k, half):
        queries, keys, values, rows = spans(k, half)
        grad_keys, grad_values = 0.0, 0.0
        grad_queries = []
        for g in range(2):
            prob = probs[(k * 2 + half) * 2 + g]
            above = grad_context[rows, queries[g]]
            grad_values = grad_values + dot(prob.astype(BF16), above, TN)
            grad_probs = dot(above, low[rows, values], NT)
            grad_scores = prob * (grad_probs - jnp.sum(prob * grad_probs, -1, keepdims=True))
            grad_scores = grad_scores.astype(BF16)
            grad_queries.append(dot(grad_scores, low[rows, keys], NN) * scale)
            grad_keys = grad_keys + dot(grad_scores, low[rows, queries[g]], TN)
        for g in range(2):
            head_back(rows, queries[g], query_gain, grad_queries[g], 2)
        head_back(rows, keys, key_gain, grad_keys * scale, 3)
        low[rows, values] = grad_values.astype(BF16)

    for half in range(2):

        def body(k, carry):
            attend_back(k, half)
            return carry

        lax.fori_loop(0, kv_heads, body, 0)

    part_swap(6, 0).wait_send()
    partial_product(8, 0, low, w_qkv, NT, True)
    weight_grad(0, normed, low, chunk, 2 * unit)
    part_swap(8, 0).wait_recv()

    def input_back(k):
        back, gain_part = normalize_back(k, x_ref, attention_gain, whole_rows(k, 0))
        input_grad[pl.ds(k, few), :] += back
        gain_sums[0] += gain_part

    loop(tokens, few, input_back)
    grad_attention[...] = jnp.sum(gain_sums[0], 0, keepdims=True)
    grad_feed[...] = jnp.sum(gain_sums[1], 0, keepdims=True)
    grad_query_gain[...] = jnp.sum(gain_sums[2, :, pl.ds(0, HEAD_DIM)], 0, keepdims=True)
    grad_key_gain[...] = jnp.sum(gain_sums[3, :, pl.ds(0, HEAD_DIM)], 0, keepdims=True)

    for index, ref in ((0, normed), (1, tables), (2, out_low), (4, hidden), (7, attended)):
        rows_swap(index, ref).wait_send()
    part_swap(5, 1).wait_send()
    part_swap(8, 0).wait_send()
    for which in range(4):
        for way in range(2):
            for hop in range(1, reach(which, way) + 1):
                ring_copy(which, way, hop, "wait_send")
                if SPREADS[which][1]:
                    x_copy(which, way, hop, place.x).wait_send()


def layer_pass(values, back, table, gains, shards, n):
    tokens, unit = values.shape
    top = n // 2
    dma = pltpu.SemaphoreType.DMA
    vmem = pltpu.VMEM
    both = 2 * tokens
    heads = unit // HEAD_DIM
    in_vmem = pl.BlockSpec(memory_space=pltpu.VMEM)
    row = lambda width: jax.ShapeDtypeStruct((1, width), F32)
    shapes = [(unit, 2 * unit), (unit, unit), (unit, 3 * unit), (3 * unit // 2, unit)]
    results = pl.pallas_call(
        functools.partial(layer_kernel, n, tokens, unit),
        out_shape=[jax.ShapeDtypeStruct((tokens, unit), F32)] * 2
        + [row(unit), row(unit), row(HEAD_DIM), row(HEAD_DIM)]
        + [jax.ShapeDtypeStruct(shape, BF16) for shape in shapes],
        in_specs=[in_vmem] * 7 + [ANY] * 4,
        out_specs=[in_vmem] * 6 + [ANY] * 4,
        scratch_shapes=[vmem(shape, BF16) for shape in shapes]
        + [
            vmem((both, unit), BF16),
            vmem((both, 2 * unit), F32),
            vmem((both, 2 * unit), BF16),
            vmem((2 * heads, tokens, tokens), F32),
            vmem((both, unit), BF16),
            vmem((both, unit), BF16),
            vmem((both, unit), BF16),
            vmem((both, unit), BF16),
            vmem((both, unit), BF16),
            vmem((both, 3 * unit // 2), BF16),
            vmem((both, 3 * unit), BF16),
            vmem((both, unit), F32),
            vmem((2, tokens, unit), BF16),
            vmem((2, tokens, unit), BF16),
            vmem((tokens, unit), F32),
            vmem((both, 3 * HEAD_DIM), F32),
            vmem((2, unit // 4, unit), BF16),
            vmem((4, 8, unit), F32),
            dma((4,)),
            dma((8 * top,)),
            dma((8 * top,)),
            dma((4 * top,)),
            dma((4 * top,)),
            dma((9,)),
            dma((9,)),
            dma((2,)),
        ],
        compiler_params=pltpu.CompilerParams(
            collective_id=0, has_side_effects=True, vmem_limit_bytes=56 * 2**20
        ),
    )(values, back, table, *gains, *shards)
    return results[:2], results[2:6], results[6:]


PHASES = ((DOWN, 3, False), (GU, 3, True), (OUT, 2, False), (QKV, 2, True))

OWNERS = (
    (3, 0, 1, False, 1, 2),
    (3, 1, 1, False, 1, 6),
    (3, 0, 2, False, 0, 2),
    (2, 0, 2, True, 1, 5),
    (1, 0, 3, False, 0, 5),
    (1, 0, 3, False, 1, 1),
    (0, 0, 3, True, 0, 1),
)
KEY, VALUE, QUERY, OUTM, GATE, UP, DOWNM = range(7)
RETURNS = (OUTM, KEY, VALUE, DOWNM, GATE, UP, QUERY)
TILE_SLOTS = 4
X_SLOTS = 3


def stage_order(n, order):
    top = n // 2
    ring = (top - 0.5) / n
    at = []
    for i in range(n):
        at.append((3 * i - 6.0, ("x", 1, i)))
        at.append((3 * n + 2 * i - 4.0, ("x", 3, i)))
        at.append((1 + 3 * ring * i, ("ring", 0, i)))
        at.append((3 * (i + 1) + 1.0, ("ring", 1, i)))
        at.append((3 * n + 2 + 2 * ring * i, ("ring", 2, i)))
        at.append((3 * n + 3 + max(2.0 * i, 2 * ring * (n + i)), ("ring", 3, i)))
    at.append((1 + 3 * ring * n + 9, ("final", 0, 0)))
    at.append((3 * n + 2 + 2 * ring * n + 6, ("final", 2, 0)))
    return [stage for _, stage in sorted(at)]


class Rows:
    def __init__(self):
        self.next = 0

    def take(self, rows):
        start = self.next
        self.next += rows
        return start


def layout(n, unit):
    base = unit // n
    top = n // 2
    sums = Rows()

    def shared(take):
        first = [take(PHASES[p][1] * base) for p in (0, 1)]
        return first + first

    x_in = [sums.take(PHASES[1][1] * base) for _ in range(n)]
    place = {
        "own": [sums.take(3 * base) for _ in range(TILE_SLOTS)],
        "x_in": {1: x_in, 3: x_in},
        "ring": shared(
            lambda rows: [[sums.take(rows) for _ in range(top)] for _ in range(2)]
        ),
    }
    for name in ("far", "grad", "ahead"):
        place[name] = shared(sums.take)
    for name in ("part", "other"):
        place[name] = [0 if split else sums.take(units * base) for _, units, split in PHASES]
    newton = Rows()
    place["high"] = [newton.take(3 * unit) for _ in range(2)]
    place["poly"] = [newton.take(unit) for _ in range(2)]
    return place, max(sums.next, newton.next)


def update_kernel(n, unit, *refs):
    grads, moments, gains_in = refs[:4], refs[4:11], refs[11]
    outs, orths, lands, gains_out = refs[12:16], refs[16:20], refs[20:24], refs[24]
    (
        pool, exact, gram, squares, gain_mine, gain_core, gain_x, gain_all,
        land_send, land_recv, tile_sem, x_send, x_recv, x_free, ring_send, ring_recv, part_send, part_recv,
        moment_sem, grad_local, grad_send, grad_recv, in_send, in_recv,
        out_send, out_recv, pass_send, pass_recv, gain_send, gain_recv,
    ) = refs[25:]
    place = Place(n)
    base = unit // n
    top = n // 2
    at, _ = layout(n, unit)
    cw, ccw = place.ring_neighbour(1), place.ring_neighbour(-1)
    ways = ((1, cw), (-1, ccw))
    side = [(place.x * 2 + core, lax.rem(place.own + k, n)) for k in range(1, n) for core in range(2)]
    greet(side + [place.core_partner, place.x_partner])
    order = [top]
    for distance in range(top - 1, 0, -1):
        order += [distance, -distance]
    order.append(0)
    stages = stage_order(n, order)
    moment = exact
    height = [units * base for _, units, _ in PHASES]
    owners = [
        (xs * 2 + 1, place.own_at(spot * n // 8)) for _, _, _, _, xs, spot in OWNERS
    ]
    here = place.rep * n + place.own
    is_owner = [here == rep * n + own for rep, own in owners]

    def rows(start, size):
        if isinstance(start, int):
            return pl.ds(start, size)
        return pl.ds(pl.multiple_of(start, size), size)

    def block(start, size):
        return pool.at[rows(start, size)]

    def pieces_of(phase, x):
        array, units, _ = PHASES[phase]
        half = unit // 2
        found = []
        for core in range(2):
            for b in range(units):
                if array == GU:
                    column = x * 3 * unit + core * (3 * half) + b * half
                else:
                    column = x * 2 * unit + core * (unit - x * half) + b * (half + x * half)
                found.append((core, b, x * units * half + b * half, column))
        return found

    def columns(start):
        return pl.ds(pl.multiple_of(start, unit // 2), unit // 2)

    def in_block(start, core, b):
        return pool.at[pl.ds(start + b * base, base), pl.ds(core * (unit // 2), unit // 2)]

    def shard_rows(phase, own_index):
        if PHASES[phase][2]:
            return rows(own_index * base, base)
        return rows(lax.rem(own_index, top) * height[phase], height[phase])

    def landing(phase, own_index, act):
        if PHASES[phase][2]:
            act()
        else:
            pl.when(own_index // top == 1)(act)

    def spread(source, target, size, send, recv, device):
        step = base // 2 if size % (base // 2) == 0 else size

        def copy(k, count):
            return remote(block(source + k, count), block(target + k, count), send, recv, device)

        return Several(
            functools.partial(copy, 0, size),
            [functools.partial(copy, k, step) for k in range(0, size, step)],
        )

    def land_copy(phase, i, act):
        array = PHASES[phase][0]
        own_index = place.shard(order[i])
        span = shard_rows(phase, own_index)
        size = base if PHASES[phase][2] else height[phase]
        step = base // 2

        def copy(span):
            return remote(
                grads[array].at[span], lands[array].at[span],
                land_send.at[phase * n + i], land_recv.at[phase * n + i], place.core_partner,
            )

        def do():
            if act == "start":
                for k in range(size // step):
                    copy(pl.ds(pl.multiple_of(span.start + k * step, step), step)).start()
            else:
                getattr(copy(span), act)()

        landing(phase, own_index, do)

    def x_index(phase, i):
        return (phase // 2) * n + i

    def x_copy(phase, i):
        index = x_index(phase, i)
        array = PHASES[phase][0]
        span = shard_rows(phase, place.shard(order[i]))
        target = at["x_in"][phase][i]

        def copy(core, b, column):
            return remote(
                (grads, lands)[core][array].at[span, columns(column)], in_block(target, core, b),
                x_send.at[index], x_recv.at[index], place.x_partner,
            )

        def whole():
            spot = block(target, height[phase])
            return remote(spot, spot, x_send.at[index], x_recv.at[index], place.x_partner)

        return Several(
            whole,
            [
                functools.partial(copy, core, b, column)
                for core, b, column, _ in pieces_of(phase, 1 - place.x)
            ],
        )

    def ring_copy(phase, way, distance, source, part):
        size = height[phase] // 2
        target = at["ring"][phase][way][distance - 1] + part * size
        index = ((phase * 2 + way) * top + distance - 1) * 2 + part
        return spread(
            source + part * size, target, size,
            ring_send.at[index], ring_recv.at[index], ways[way][1],
        )

    def ring_out(phase, distance, part):
        if distance == 0:
            return []
        if distance == top:
            return [ring_copy(phase, part, top, at["far"][phase], part)]
        way = 0 if distance > 0 else 1
        far = abs(distance)
        return [ring_copy(phase, way, far, at["ring"][phase][way][far], part)]

    def part_copy(phase):
        return spread(
            at["part"][phase], at["other"][phase], height[phase],
            part_send.at[phase // 2], part_recv.at[phase // 2], place.x_partner,
        )

    def gain_copy(src, dst, slot, device):
        return remote(src, dst, gain_send.at[slot], gain_recv.at[slot], device)

    def gain_core_copy():
        return gain_copy(gain_mine, gain_core, 0, place.core_partner)

    def gain_x_copy():
        return gain_copy(gain_core, gain_x, 1, place.x_partner)

    def gain_back_copy():
        return gain_copy(gain_mine, gain_x, 2, place.core_partner)

    def gain_ring(way, hop, distance):
        spot = gain_all.at[place.shard(distance)]
        return gain_copy(spot, spot, 3 + way * top + hop - 1, ways[way][1])

    def grad_place(phase, x):
        array = PHASES[phase][0]
        start = at["grad"][phase]
        if not PHASES[phase][2]:
            return [(outs[array], block(start, height[phase]))]
        return [
            (outs[array].at[:, columns(column)], in_block(start, core, b))
            for core, b, _, column in pieces_of(phase, x)
        ]

    def grad_span(phase, x):
        array, units, split = PHASES[phase]
        if not split:
            return outs[array]
        first = pl.multiple_of(x * units * unit, unit)
        return outs[array].at[:, pl.ds(first, units * unit)]

    def grad_sent(phase, to, device, x):
        span = grad_span(phase, x)
        return remote(span, span, grad_send.at[phase, to], grad_recv.at[phase, to], device)

    def matrix_rows(matrix, own_index):
        phase, first, units, tall, _, _ = OWNERS[matrix]
        if tall:
            return [(0, own_index * units * base, units * base)]
        return [
            ((first + k) * base, k * unit + own_index * base, base) for k in range(units)
        ]

    def matrix_span(matrix):
        phase, first, units, tall, xs, _ = OWNERS[matrix]
        array = PHASES[phase][0]
        if tall:
            return orths[array]
        start = (xs * PHASES[phase][1] + first) * unit
        return orths[array].at[:, pl.ds(start, units * unit)]

    def answer_parts(matrix, final, own_index):
        phase, first, units, tall, xs, _ = OWNERS[matrix]
        array = PHASES[phase][0]
        if tall:
            return [(block(final + own_index * units * base, units * base), orths[array])]
        return [
            (
                pool.at[
                    rows(final + (b - first) * unit + own_index * base, base),
                    pl.ds(core * (unit // 2), unit // 2),
                ],
                orths[array].at[:, columns(column)],
            )
            for core, b, _, column in pieces_of(phase, xs)
            if first <= b < first + units
        ]

    def handed(matrix, to, device):
        span = matrix_span(matrix)
        return remote(span, span, pass_send.at[matrix, to], pass_recv.at[matrix, to], device)

    def answered(matrix, target):
        span = matrix_span(matrix)
        return remote(
            span, span, out_send.at[target], out_recv.at[matrix], (place.x * 2, target)
        )

    def summed(pieces, size, store):
        step = 16
        steps = 4 if size % (4 * step) == 0 else 1

        def body(k, carry):
            for j in range(steps):
                shift = (k * steps + j) * step
                total = None
                for start in pieces:
                    value = pool[rows_at(start, shift, step), :].astype(F32)
                    total = value if total is None else total + value
                store(shift, step, total)
            return carry

        lax.fori_loop(0, size // (step * steps), body, 0)

    def rows_at(start, shift, step):
        return pl.ds(pl.multiple_of(start + shift, step), step)

    def keep(start):
        def store(shift, step, total):
            pool[rows_at(start, shift, step), :] = total.astype(BF16)

        return store

    def load_tile(k):
        _, phase, i = stages[k]
        array, _, split = PHASES[phase]
        slot = k_slot[k]
        own_index = place.shard(order[i])
        span = shard_rows(phase, own_index)

        def load(source, target):
            pltpu.make_async_copy(source, target, tile_sem.at[slot]).start()

        if split:
            for core, b, column, _ in pieces_of(phase, place.x):
                load(
                    (grads, lands)[core][array].at[span, columns(column)],
                    in_block(at["own"][slot], core, b),
                )
            return
        for core in range(2):

            @pl.when(own_index // top == core)
            def _():
                load((grads, lands)[core][array].at[span], block(at["own"][slot], height[phase]))

    tiled = [k for k, stage in enumerate(stages) if stage[0] == "ring"]
    k_slot = {k: index % TILE_SLOTS for index, k in enumerate(tiled)}
    seen = set()

    def landed(phase, i):
        if (phase, i) not in seen:
            seen.add((phase, i))
            land_copy(phase, i, "wait_recv")

    def prefetch(index):
        if index >= len(tiled):
            return
        k = tiled[index]
        landed(*stages[k][1:])
        load_tile(k)

    def wait_tile(k):
        span = block(at["own"][k_slot[k]], height[stages[k][1]])
        pltpu.make_async_copy(span, span, tile_sem.at[k_slot[k]]).wait()

    def moment_copies(phase, act):
        array, units, split = PHASES[phase]
        if not split:
            act(moments[3 if array == OUT else 6], moment.at[pl.ds(0, height[phase])])
            return
        half = unit // 2
        for x in range(2):

            @pl.when(place.x == x)
            def _():
                for core, b, _, column in pieces_of(phase, x):
                    if array == GU:
                        source, first = 4 + x, x * 3 * unit
                    elif x == 0:
                        source, first = 0, 0
                    else:
                        source, first = 1 + b, (2 + b) * unit
                    act(
                        moments[source].at[:, pl.ds(column - first, half)],
                        moment.at[pl.ds(b * base, base), pl.ds(core * half, half)],
                    )

    def load_moment(phase):
        moment_copies(
            phase, lambda src, dst: pltpu.make_async_copy(src, dst, moment_sem.at[phase]).start()
        )

    def finish(phase, pieces):
        span = moment.at[pl.ds(0, height[phase])]
        pltpu.make_async_copy(span, span, moment_sem.at[phase]).wait()

        if phase >= 2:
            settle(phase - 2)

        def store(shift, step, total):
            pool[rows_at(at["grad"][phase], shift, step), :] = total.astype(BF16)
            ahead = (1.0 + MOMENTUM) * total + MOMENTUM**2 * moment[rows_at(0, shift, step), :]
            pool[rows_at(at["ahead"][phase], shift, step), :] = ahead.astype(BF16)

        summed(pieces, height[phase], store)
        for matrix, (its_phase, _, _, _, xs, _) in enumerate(OWNERS):
            if its_phase != phase:
                continue

            @pl.when(place.x == xs)
            def _():
                for source, target, size in matrix_rows(matrix, place.own):
                    remote(
                        block(at["ahead"][phase] + source, size), block(at["high"][1] + target, size),
                        in_send.at[matrix], in_recv.at[place.own], owners[matrix],
                    ).start()

        for target, source in grad_place(phase, place.x):
            pltpu.make_async_copy(source, target, grad_local.at[phase]).start()
            remote(
                source, target, grad_send.at[phase, 0], grad_recv.at[phase, 0], place.core_partner
            ).start()
            if PHASES[phase][2]:
                remote(
                    source, target, grad_send.at[phase, 1], grad_recv.at[phase, 1], place.x_partner
                ).start()
        after = {0: 1, 1: 2, 2: 3, 3: None}[phase]
        if after is not None:
            load_moment(after)

    def settle(phase):
        span = block(at["grad"][phase], height[phase])
        pltpu.make_async_copy(span, span, grad_local.at[phase]).wait()
        remote(
            span, span, grad_send.at[phase, 0], grad_recv.at[phase, 0], place.core_partner
        ).wait_send()
        if PHASES[phase][2]:
            remote(
                span, span, grad_send.at[phase, 1], grad_recv.at[phase, 1], place.x_partner
            ).wait_send()
        for matrix, (its_phase, _, units, _, xs, _) in enumerate(OWNERS):
            if its_phase != phase:
                continue

            @pl.when(place.x == xs)
            def _():
                span = block(at["high"][1], units * base)
                remote(
                    span, span, in_send.at[matrix], in_recv.at[0], place.core_partner
                ).wait_send()

    def stage_x(phase, i):
        landed(phase, i)
        index = x_index(phase, i)
        if index >= X_SLOTS:
            before = index - X_SLOTS
            x_copy(1 if before < n else 3, before % n).wait_send()
        if phase == 3:
            pl.semaphore_wait(x_free, 1)
        x_copy(phase, i).start()

    def stage_ring(k, phase, i):
        distance = order[i]
        wait_tile(k)
        pieces = [at["own"][k_slot[k]]]
        if PHASES[phase][2]:
            x_copy(phase, i).wait_recv()
            pieces.append(at["x_in"][phase][i])
        size = height[phase]
        mid = size // 2
        if abs(distance) == 1 and 0 < phase < 3:
            ring_sent(phase - 1)
        if distance == 0:
            for way in range(2):
                held = at["ring"][phase][way][0]
                for part in range(2):
                    ring_copy(phase, way, 1, held, part).wait_recv()
                pieces.append(held)
            if PHASES[phase][2]:
                finish(phase, pieces)
            else:
                summed(pieces, size, keep(at["part"][phase]))
                part_copy(phase).start()
        else:
            way = 0 if distance > 0 else 1
            far = abs(distance)
            held = at["far"][phase] if far == top else at["ring"][phase][way][far]
            for part in (1 - way, way):
                starts = [start + part * mid for start in pieces]
                if far + 1 < top or (far + 1 == top and part == way):
                    ring_copy(phase, way, far + 1, held, part).wait_recv()
                    starts.append(held + part * mid)
                summed(starts, mid, keep(held + part * mid))
                for copy in ring_out(phase, distance, part):
                    copy.start()
        if phase == 1:
            pl.semaphore_signal(x_free, inc=1, device_id=place.x_partner, device_id_type=MESH)

    def ring_sent(phase):
        if phase not in ring_waited:
            ring_waited.add(phase)
            for distance in order:
                for part in range(2):
                    for copy in ring_out(phase, distance, part):
                        copy.wait_send()

    ring_waited = set()

    def gain_stage(hop):
        if hop == 0:
            gain_core_copy().wait_recv()
            gain_core[...] = gain_mine[...] + gain_core[...]
            gain_x_copy().start()
            return
        if hop == 1:
            gain_x_copy().wait_recv()
            gain_all[place.own] = gain_core[...] + gain_x[...]
            for way in range(2):
                gain_ring(way, 1, 0).start()
        for way in range(2):
            if 1 < hop <= hops(n, way, 0) + 1:
                distance = -ways[way][0] * (hop - 1)
                gain_ring(way, hop - 1, distance).wait_recv()
                if hop <= hops(n, way, 0):
                    gain_ring(way, hop, distance).start()

    gain_mine[...] = gains_in[...]

    @pl.when(place.core == 0)
    def _():
        load_moment(0)
        for index in range(TILE_SLOTS - 1):
            prefetch(index)
        done = 0
        hop = 0
        for k, (kind, phase, i) in enumerate(stages):
            if kind == "final":
                part_copy(phase).wait_recv()
                finish(phase, [at["part"][phase], at["other"][phase]])
                continue
            if kind == "x":
                stage_x(phase, i)
                continue
            prefetch(done + TILE_SLOTS - 1)
            done += 1
            stage_ring(k, phase, i)
            if done % 2 == 0 and hop <= top + 1:
                gain_stage(hop)
                hop += 1

        total = gain_all[0]
        for k in range(1, n):
            total = total + gain_all[k]
        gains_out[...] = total
        gain_mine[...] = total
        gain_back_copy().start()

        for phase in (1, 3):
            grad_sent(phase, 1, place.x_partner, 1 - place.x).wait_recv()
            grad_sent(phase, 2, place.core_partner, 1 - place.x).start()

        for matrix in RETURNS:
            xs = OWNERS[matrix][4]

            @pl.when(place.x == xs)
            def _():
                answered(matrix, place.own).wait_recv()
                handed(matrix, 0, place.x_partner).start()
                handed(matrix, 1, place.core_partner).start()

            @pl.when(place.x != xs)
            def _():
                handed(matrix, 0, place.x_partner).wait_recv()
                handed(matrix, 1, place.core_partner).start()

        for matrix, (phase, _, units, _, xs, _) in enumerate(OWNERS):
            handed(matrix, 1, place.core_partner).wait_send()

            @pl.when(place.x == xs)
            def _():
                handed(matrix, 0, place.x_partner).wait_send()

        for phase, (_, _, split) in enumerate(PHASES):
            if phase >= 2:
                settle(phase)
            if split:
                grad_sent(phase, 2, place.core_partner, 1 - place.x).wait_send()
            else:
                part_copy(phase).wait_send()
            ring_sent(phase)
        for index in range(2 * n - X_SLOTS, 2 * n):
            x_copy(1 if index < n else 3, index % n).wait_send()
        gain_x_copy().wait_send()
        gain_back_copy().wait_send()
        for way in range(2):
            for h in range(1, hops(n, way, 0) + 1):
                gain_ring(way, h, -ways[way][0] * (h - 1)).wait_send()

    @pl.when(place.core == 1)
    def _():
        gain_core_copy().start()
        needed = []
        for kind, phase, i in stages:
            if kind != "final" and (phase, i) not in needed:
                needed.append((phase, i))
        ahead = 8
        for index, (phase, i) in enumerate(needed):
            if index >= ahead:
                land_copy(*needed[index - ahead], "wait_send")
            land_copy(phase, i, "start")
        for phase, i in needed[-ahead:]:
            land_copy(phase, i, "wait_send")
        newton_part(n, unit, place, pool, exact, gram, squares, at, is_owner, in_recv)
        for matrix, (_, _, units, tall, _, _) in enumerate(OWNERS):

            @pl.when(is_owner[matrix])
            def _():
                final = at["high"][1 - NS_STEPS % 2 if tall else NS_STEPS % 2]

                def send(k, carry):
                    target = lax.rem(place.own + k, n)
                    for source, part in answer_parts(matrix, final, target):
                        remote(
                            source, part, out_send.at[target], out_recv.at[matrix],
                            (place.x * 2, target),
                        ).start()
                    return carry

                lax.fori_loop(0, n, send, 0)

                def sent(k, carry):
                    answered(matrix, lax.rem(place.own + k, n)).wait_send()
                    return carry

                lax.fori_loop(0, n, sent, 0)

        gain_core_copy().wait_send()
        gain_back_copy().wait_recv()
        gains_out[...] = gain_x[...]
        for phase, (_, _, split) in enumerate(PHASES):
            grad_sent(phase, 0, place.core_partner, place.x).wait_recv()
            if split:
                grad_sent(phase, 2, place.core_partner, 1 - place.x).wait_recv()
        for matrix in RETURNS:
            handed(matrix, 1, place.core_partner).wait_recv()


def newton_part(n, unit, place, pool, exact, gram, squares, at, is_owner, in_recv):
    base = unit // n
    small = min(256, unit // 2)
    per = unit // small
    few = 32
    count, tall = 0, 0
    for mine, (_, _, units, lies_tall, _, _) in zip(is_owner, OWNERS):
        count = count + units * mine.astype(jnp.int32)
        tall = tall + int(lies_tall) * mine.astype(jnp.int32)
    high, poly = at["high"], at["poly"]

    def rows(start, size):
        return pl.ds(pl.multiple_of(start, size), size)

    for matrix, (_, _, units, *_) in enumerate(OWNERS):

        @pl.when(is_owner[matrix])
        def _():
            span = pool.at[pl.ds(high[1], units * base)]
            for own_index in range(n):
                remote(
                    span, span, in_recv.at[own_index], in_recv.at[own_index], place.core_partner
                ).wait_recv()

    @pl.when(count > 0)
    def _():
        squares[...] = jnp.zeros_like(squares)

        def square(k, carry):
            part = pool[rows(high[1] + k * few, few), :].astype(F32)
            squares[...] += jnp.sum((part * part).reshape(few // 8, 8, unit), 0)
            return carry

        lax.fori_loop(0, count * (unit // few), square, 0)
        total = jnp.sum(jnp.sum(squares[...], 1, keepdims=True), 0, keepdims=True)
        inverse = 1.0 / (jnp.sqrt(total) + 1e-07)

        @pl.when(tall == 0)
        def _():
            def scale(k, carry):
                value = pool[rows(high[1] + k * few, few), :].astype(F32) * inverse
                exact[rows(k * few, few), :] = value
                pool[rows(high[0] + k * few, few), :] = value.astype(BF16)
                return carry

            lax.fori_loop(0, count * (unit // few), scale, 0)

        @pl.when(tall == 1)
        def _():
            def scale(k, carry):
                block, row = k // per, k % per
                for column in range(per):
                    part = pool[
                        rows(high[1] + k * small, small), pl.ds(column * small, small)
                    ].astype(F32)
                    value = (part * inverse).T
                    shift = block * unit + column * small
                    columns = rows(row * small, small)
                    exact[rows(shift, small), columns] = value
                    pool[rows(high[0] + shift, small), columns] = value.astype(BF16)
                return carry

            lax.fori_loop(0, count * per, scale, 0)

        def newton(step, carry):
            even = step % 2
            now = high[0] + even * (high[1] - high[0])
            later = high[1] - even * (high[1] - high[0])

            def keep_symmetric(to, chunk, value):
                pool[pl.ds(to, (chunk + 1) * small), pl.ds(chunk * small, small)] = value.astype(BF16)
                for row in range(chunk):
                    pool[pl.ds(to + chunk * small, small), pl.ds(row * small, small)] = (
                        value[row * small : (row + 1) * small].T.astype(BF16)
                    )

            for chunk in range(per):
                down = (chunk + 1) * small

                def product(block):
                    left = pool[pl.ds(pl.multiple_of(now + block * unit, unit), down), :]
                    right = pool[rows(now + block * unit + chunk * small, small), :]
                    return lax.dot_general(
                        left, right, (((1,), (1,)), ((), ())), preferred_element_type=F32
                    )

                gram[:down, :] = product(0)

                def more(block, carry):
                    gram[:down, :] += product(block)
                    return carry

                lax.fori_loop(1, count, more, 0)
                keep_symmetric(poly[0], chunk, gram[:down, :])

            for chunk in range(per):
                down = (chunk + 1) * small
                columns = pl.ds(chunk * small, small)
                squared = jnp.dot(
                    pool[pl.ds(poly[0], down), :], pool[pl.ds(poly[0], unit), columns],
                    preferred_element_type=F32,
                )
                plain = pool[pl.ds(poly[0], down), columns].astype(F32)
                keep_symmetric(poly[1], chunk, NEWTON_B * plain + NEWTON_C * squared)

            def advance(block, carry):
                for chunk in range(per):
                    columns = pl.ds(chunk * small, small)
                    value = NEWTON_A * exact[rows(block * unit, unit), columns] + jnp.dot(
                        pool[pl.ds(poly[1], unit), :],
                        pool[rows(now + block * unit, unit), columns],
                        preferred_element_type=F32,
                    )
                    exact[rows(block * unit, unit), columns] = value
                    pool[rows(later + block * unit, unit), columns] = value.astype(BF16)
                return carry

            lax.fori_loop(0, count, advance, 0)
            return carry

        lax.fori_loop(0, NS_STEPS, newton, 0)

        @pl.when(tall == 1)
        def _():
            free = high[1 - NS_STEPS % 2]
            factor = jnp.sqrt(jnp.full((1, 1), count, jnp.int32).astype(F32))

            def lay(k, carry):
                block, row = k // per, k % per
                for column in range(per):
                    columns = pl.ds(column * small, small)
                    part = exact[rows(k * small, small), columns]
                    pool[
                        rows(free + block * unit + column * small, small), rows(row * small, small)
                    ] = (part * factor).T.astype(BF16)
                return carry

            lax.fori_loop(0, count * per, lay, 0)


def update_all(grads, moments, gains, n, unit):
    top = n // 2
    dma = pltpu.SemaphoreType.DMA
    vmem = pltpu.VMEM
    _, pool_rows = layout(n, unit)
    shapes = [(unit // n, 4 * unit), (2 * unit // n, unit), (unit // n, 6 * unit), (3 * unit // n, unit)]
    own = [jax.ShapeDtypeStruct(shape, BF16) for shape in shapes]
    whole = [jax.ShapeDtypeStruct(grad.shape, BF16) for grad in grads]
    in_vmem = pl.BlockSpec(memory_space=pltpu.VMEM)
    results = pl.pallas_call(
        functools.partial(update_kernel, n, unit),
        out_shape=own + own + whole + [jax.ShapeDtypeStruct(gains.shape, F32)],
        in_specs=[ANY] * 11 + [in_vmem],
        out_specs=[ANY] * 12 + [in_vmem],
        scratch_shapes=[
            vmem((pool_rows, unit), BF16),
            vmem((3 * unit, unit), F32),
            vmem((unit, min(256, unit // 2)), F32),
            vmem((8, unit), F32),
            vmem(gains.shape, F32),
            vmem(gains.shape, F32),
            vmem(gains.shape, F32),
            vmem((n,) + gains.shape, F32),
            dma((4 * n,)),
            dma((4 * n,)),
            dma((TILE_SLOTS,)),
            dma((2 * n,)),
            dma((2 * n,)),
            pltpu.SemaphoreType.REGULAR,
            dma((16 * top,)),
            dma((16 * top,)),
            dma((2,)),
            dma((2,)),
            dma((4,)),
            dma((4,)),
            dma((4, 3)),
            dma((4, 3)),
            dma((7,)),
            dma((n,)),
            dma((n,)),
            dma((7,)),
            dma((7, 2)),
            dma((7, 2)),
            dma((3 + 2 * top,)),
            dma((3 + 2 * top,)),
        ],
        compiler_params=pltpu.CompilerParams(
            collective_id=1, has_side_effects=True, vmem_limit_bytes=56 * 2**20
        ),
    )(*grads, *moments, gains)
    return results[:4], results[4:8], results[12]


def unpacked(arrays, unit):
    qkv, out, gate_up, down = arrays
    return (
        qkv[:, : 2 * unit],
        qkv[:, 2 * unit : 3 * unit],
        qkv[:, 3 * unit :],
        out,
        gate_up[:, : 3 * unit],
        gate_up[:, 3 * unit :],
        down,
    )


def body(
    layer_input,
    output_grad,
    lengths,
    attention_gain,
    feed_gain,
    query_gain,
    key_gain,
    query_weight,
    key_weight,
    value_weight,
    out_weight,
    gate_weight,
    up_weight,
    down_weight,
    query_moment,
    key_moment,
    value_moment,
    out_moment,
    gate_moment,
    up_moment,
    down_moment,
):
    owned = (
        query_weight, key_weight, value_weight, out_weight, gate_weight, up_weight, down_weight,
    )
    moments = (
        query_moment, key_moment, value_moment, out_moment, gate_moment, up_moment, down_moment,
    )
    n = lax.axis_size("own")
    unit = layer_input.shape[1]
    core = lax.axis_index("rep") % 2

    def halves(*matrices):
        parts = []
        for matrix in matrices:
            width = matrix.shape[1] // 2
            parts.append(lax.dynamic_slice_in_dim(matrix, core * width, width, 1))
        return jnp.concatenate(parts, 1).astype(BF16)

    shards = (
        halves(query_weight, key_weight, value_weight),
        out_weight.astype(BF16),
        halves(gate_weight, up_weight),
        down_weight.astype(BF16),
    )
    row_count = layer_input.shape[0]
    _, positions = segments(lengths[0], row_count)
    cosine_table, sine_table = rope_tables(positions)
    starts = (jnp.arange(row_count, dtype=jnp.int32) - positions).astype(F32)
    table = jnp.concatenate(
        [
            cosine_table[:, 0], cosine_table[:, 0], -sine_table[:, 0], sine_table[:, 0],
            jnp.broadcast_to(starts[:, None], (row_count, HEAD_DIM)),
        ],
        1,
    )
    gain_rows = [gain[None, :] for gain in (attention_gain, feed_gain, query_gain, key_gain)]
    (block_output, input_grad), gain_grads, grads = layer_pass(
        layer_input, output_grad, table, gain_rows, shards, n
    )
    gains = jnp.concatenate([grad[0] for grad in gain_grads])
    gains = jnp.pad(gains, (0, 24 * 128 - gains.shape[0])).reshape(24, 128)
    reduced, orth, gain_sums = update_all(grads, moments, gains, n, unit)
    moments_next = [
        MOMENTUM * moment + part.astype(F32) for moment, part in zip(moments, unpacked(reduced, unit))
    ]
    new_weights = [
        matrix * (1.0 - LEARN_RATE * WEIGHT_DECAY) - LEARN_RATE * part.astype(F32)
        for matrix, part in zip(owned, unpacked(orth, unit))
    ]
    gain_sums = gain_sums.reshape(-1)
    norm_grads = gain_sums[: 2 * unit].reshape(2, unit)
    head_grads = gain_sums[2 * unit : 2 * unit + 2 * HEAD_DIM].reshape(2, HEAD_DIM)
    return (block_output, input_grad, norm_grads, head_grads, *new_weights, *moments_next)


def solution(mesh):
    tokens, owned = P(("rep", "own"), None), P("own", None)
    return jax.shard_map(
        body,
        mesh=mesh,
        in_specs=(tokens,) * 3 + (P(),) * 4 + (owned,) * 14,
        out_specs=(tokens,) * 2 + (P(),) * 2 + (owned,) * 14,
        check_vma=False,
    )
```

```python
import functools

import jax
import jax.numpy as jnp
from jax import lax
from jax.experimental import pallas as pl
from jax.experimental.pallas import tpu as pltpu
from jax.sharding import PartitionSpec as P

HEADS = 16
KV_HEADS = 8
HEAD_DIM = 128
NS_STEPS = 5

EPSILON = 1e-06
ROPE_BASE = 1000000.0
MOMENTUM = 0.95
LEARN_RATE = 0.8
WEIGHT_DECAY = 0.01
NEWTON_A = 3.4445
NEWTON_B = -4.775
NEWTON_C = 2.0315

BF16 = jnp.bfloat16
F32 = jnp.float32
MESH = pl.DeviceIdType.MESH
ANY = pl.BlockSpec(memory_space=pltpu.HBM)

QKV, OUT, GU, DOWN = range(4)


def segments(lengths, row_count):
    seq_ends = jnp.cumsum(lengths)
    seq_starts = seq_ends - lengths
    row_ids = jnp.arange(row_count, dtype=jnp.int32)
    segment_ids = jnp.sum((row_ids[:, None] >= seq_ends[None, :]).astype(jnp.int32), 1)
    slot_ids = jnp.arange(lengths.shape[0], dtype=jnp.int32)
    row_starts = jnp.sum(
        jnp.where(segment_ids[:, None] == slot_ids[None, :], seq_starts[None, :], 0), 1
    )
    return (segment_ids, row_ids - row_starts)


def rope_tables(positions):
    inverse = ROPE_BASE ** (-jnp.arange(0, HEAD_DIM, 2, dtype=jnp.float32) / HEAD_DIM)
    angles = positions.astype(jnp.float32)[:, None] * inverse[None, :]
    return (jnp.cos(angles)[:, None, :], jnp.sin(angles)[:, None, :])


class Place:
    def __init__(self, n):
        self.n = n
        self.rep = lax.axis_index("rep")
        self.own = lax.axis_index("own")
        self.x = self.rep // 2
        self.core = self.rep % 2
        odd, pair = self.own % 2, self.own // 2
        self.ring = pair * (1 - odd) + odd * (n - 1 - pair)

    def own_at(self, ring):
        odd = ring // (self.n // 2)
        return 2 * (ring * (1 - odd) + odd * (self.n - 1 - ring)) + odd

    def shard(self, distance):
        return self.own_at(lax.rem(self.ring + distance + self.n, self.n))

    def ring_neighbour(self, way):
        return (self.rep, self.shard(way))

    @property
    def core_partner(self):
        return (self.x * 2 + 1 - self.core, self.own)

    @property
    def x_partner(self):
        return ((1 - self.x) * 2 + self.core, self.own)


def greet(devices):
    barrier = pltpu.get_barrier_semaphore()
    for device in devices:
        pl.semaphore_signal(barrier, inc=1, device_id=device, device_id_type=MESH)
    pl.semaphore_wait(barrier, len(devices))


class Several:
    def __init__(self, whole, copies):
        self.whole = whole
        self.copies = copies

    def start(self):
        for copy in self.copies:
            copy().start()

    def wait_send(self):
        self.whole().wait_send()

    def wait_recv(self):
        self.whole().wait_recv()


def remote(src, dst, send, recv, device):
    return pltpu.make_async_remote_copy(
        src_ref=src, dst_ref=dst, send_sem=send, recv_sem=recv, device_id=device, device_id_type=MESH
    )


def hops(n, way, kind):
    return n // 2 if (way == 0) == (kind == 0) else n // 2 - 1


SPREADS = ((QKV, True), (OUT, False), (GU, True), (DOWN, False))


def layer_kernel(n, tokens, unit, *refs):
    (
        x_ref, back_ref, table_ref, attention_gain, feed_gain, query_gain, key_gain,
    ) = refs[:7]
    shards = refs[7:11]
    output, input_grad, grad_attention, grad_feed, grad_query_gain, grad_key_gain = refs[11:17]
    grads = refs[17:21]
    (
        w_qkv, w_out, w_gu, w_down, normed, raw, low, probs, context, hidden, out_low, attended,
        grad_context, activated, gu_back, part, sent, got, middle, tables, stage, turned_left, gain_sums,
        local, ring_send, ring_recv, x_send, x_recv, swap_send, swap_recv, stage_sem,
    ) = refs[21:]
    weights = (w_qkv, w_out, w_gu, w_down)
    place = Place(n)
    top = n // 2
    cw, ccw = place.ring_neighbour(1), place.ring_neighbour(-1)
    ways = ((1, cw), (-1, ccw))
    greet([cw, ccw, place.core_partner, place.x_partner])
    both = 2 * tokens
    mine = pl.multiple_of(place.core * tokens, tokens)
    theirs = pl.multiple_of((1 - place.core) * tokens, tokens)
    my_rows, their_rows = pl.ds(mine, tokens), pl.ds(theirs, tokens)
    chunk = unit // 2
    ff = 3 * unit // 2
    few = 32
    base = unit // n
    heads = unit // HEAD_DIM
    kv_heads = heads // 2
    scale = HEAD_DIM ** (-0.5)

    def holds(which, own_index, act):
        if SPREADS[which][1]:
            act()
        else:
            pl.when(own_index // top == place.core)(act)

    def region(which, own_index, x):
        array, split = SPREADS[which]
        height = shards[which].shape[0]
        if split:
            width = weights[which].shape[1] // 2
            start = pl.multiple_of(own_index * height, height)
            return weights[which].at[pl.ds(start, height), pl.ds(pl.multiple_of(x * width, width), width)]
        start = pl.multiple_of(lax.rem(own_index, top) * height, height)
        return weights[which].at[pl.ds(start, height)]

    def own_copy(which):
        height = shards[which].shape[0]
        index = place.own if SPREADS[which][1] else lax.rem(place.own, top)
        start = pl.multiple_of(index * height, height)
        return pltpu.make_async_copy(
            shards[which], weights[which].at[pl.ds(start, height)], local.at[which]
        )

    def reach(which, way):
        return hops(n, way, 0 if SPREADS[which][1] else 1)

    def ring_copy(which, way, hop, act):
        step, target = ways[way]
        own_index = place.shard(-step * (hop if act == "wait_recv" else hop - 1))
        spot = region(which, own_index, place.x)
        index = (which * 2 + way) * top + hop - 1

        def do():
            copy = remote(spot, spot, ring_send.at[index], ring_recv.at[index], target)
            getattr(copy, act)()

        holds(which, own_index, do)

    def send_on(which, way, hop):
        ring_copy(which, way, hop, "start")

    def x_copy(which, way, hop, x):
        spot = region(which, place.shard(-ways[way][0] * hop), x)
        index = (which // 2 * 2 + way) * top + hop - 1
        return remote(spot, spot, x_send.at[index], x_recv.at[index], place.x_partner)

    def serve(which, hop):
        for way in range(2):
            if hop > reach(which, way):
                continue
            ring_copy(which, way, hop, "wait_recv")
            if hop < reach(which, way):
                send_on(which, way, hop + 1)
            if SPREADS[which][1]:
                x_copy(which, way, hop, place.x).start()

    def begin(which):
        def act():
            own_copy(which).wait()

        holds(which, place.own, act)
        for way in range(2):
            if reach(which, way) > 0:
                send_on(which, way, 1)

    def take_x(which):
        for way in range(2):
            for hop in range(1, reach(which, way) + 1):
                x_copy(which, way, hop, 1 - place.x).wait_recv()

    def swap(index, src, dst):
        return remote(src, dst, swap_send.at[index], swap_recv.at[index], place.core_partner)

    def rows_swap(index, ref):
        return swap(index, ref.at[my_rows], ref.at[my_rows])

    def part_swap(index, slot):
        return swap(index, sent.at[slot], got.at[slot])

    def loop(size, step, act):
        def body(k, carry):
            act(pl.multiple_of(k * step, step))
            return carry

        lax.fori_loop(0, size // step, body, 0)

    def normalize(source, gain, target):
        def act(k):
            value = source[pl.ds(k, few), :]
            value = value * lax.rsqrt(jnp.mean(value * value, -1, keepdims=True) + EPSILON)
            target[pl.ds(pl.multiple_of(mine + k, few), few), :] = (value * gain[...]).astype(BF16)

        loop(tokens, few, act)

    def normalize_back(k, source, gain, grad):
        value = source[pl.ds(k, few), :]
        inverse = lax.rsqrt(jnp.mean(value * value, -1, keepdims=True) + EPSILON)
        unscaled = value * inverse
        inner = grad * gain[...]
        back = inverse * (inner - unscaled * jnp.mean(inner * unscaled, -1, keepdims=True))
        return back, jnp.sum((grad * unscaled).reshape(few // 8, 8, unit), 0)

    def dot(left, right, across):
        return lax.dot_general(left, right, ((across[0], across[1]), ((), ())), preferred_element_type=F32)

    NN, NT, TN = ((1,), (0,)), ((1,), (1,)), ((0,), (0,))

    def partial_product(index, slot, left, right, across, by_rows):
        def act(k):
            span = pl.ds(k, chunk)
            factor = right[span, :] if by_rows else right[:, span]
            part[:, span] = dot(left[...], factor, across)

        loop(unit, chunk, act)

        def pack(k):
            sent[slot, pl.ds(k, few), :] = part[
                pl.ds(pl.multiple_of(theirs + k, few), few), :
            ].astype(BF16)

        loop(tokens, few, pack)
        part_swap(index, slot).start()

    def whole_rows(k, slot):
        own = part[pl.ds(pl.multiple_of(mine + k, few), few), :]
        return own + got[slot, pl.ds(k, few), :].astype(F32)

    def weight_grad(which, left, right):
        columns = right.shape[1] // unit

        def by_rows(r, carry):
            row = pl.multiple_of(r * chunk, chunk)
            turned_left[...] = left[:, pl.ds(row, chunk)].T

            def by_columns(c, carry):
                column = pl.multiple_of(c * unit, unit)
                index = r * columns + c
                slot = lax.rem(index, 2)

                @pl.when(index >= 2)
                def _():
                    stage_copy(which, slot, row, column, chunk, unit).wait()

                value = dot(turned_left[...], right[:, pl.ds(column, unit)], NN)
                stage[slot] = value.astype(BF16)
                stage_copy(which, slot, row, column, chunk, unit).start()
                return carry

            lax.fori_loop(0, columns, by_columns, 0)
            return carry

        lax.fori_loop(0, left.shape[1] // chunk, by_rows, 0)
        for slot in range(2):
            stage_copy(which, slot, 0, 0, chunk, unit).wait()

    def stage_copy(which, slot, row, column, height, width):
        return pltpu.make_async_copy(
            stage.at[slot], grads[which].at[pl.ds(row, height), pl.ds(column, width)],
            stage_sem.at[slot],
        )

    for which in range(4):
        holds(which, place.own, lambda: own_copy(which).start())
    tables[my_rows, :] = table_ref[...]
    normalize(x_ref, attention_gain, normed)
    rows_swap(0, normed).start()
    rows_swap(1, tables).start()
    begin(0)
    begin(1)

    def round_back(k):
        out_low[pl.ds(pl.multiple_of(mine + k, few), few), :] = back_ref[pl.ds(k, few), :].astype(BF16)

    loop(tokens, few, round_back)
    rows_swap(2, out_low).start()
    gain_sums[...] = jnp.zeros_like(gain_sums)

    late = [(1, top)] if top < 3 else [(1, h) for h in range(3, top + 1)]
    serve(0, 1)
    serve(1, 1)
    begin(2)
    for hop in range(2, top + 1):
        serve(0, hop)
        if (1, hop) not in late:
            serve(1, hop)
        if hop == 2:
            serve(2, 1)
    take_x(0)
    begin(3)
    pending = late + [(2, h) for h in range(2, top)] + [(3, 1), (2, top)]
    pending += [(3, h) for h in range(2, top + 1)]
    for name in (0, 1):
        rows_swap(name, (normed, tables)[name]).wait_recv()

    def project(k):
        span = pl.ds(k, chunk)
        raw[:, span] = dot(normed[...], w_qkv[:, span], NN)

    loop(3 * unit // 2, chunk, project)
    values_at = pl.ds(3 * unit // 2, chunk)
    low[:, values_at] = dot(normed[...], w_qkv[:, values_at], NN).astype(BF16)
    serve(*pending.pop(0))

    def turned(value, rows):
        return value * tables[rows, pl.ds(0, HEAD_DIM)] + pltpu.roll(
            value, HEAD_DIM // 2, 1
        ) * tables[rows, pl.ds(HEAD_DIM, HEAD_DIM)]

    def turned_back(value, rows):
        return value * tables[rows, pl.ds(0, HEAD_DIM)] - pltpu.roll(
            value, HEAD_DIM // 2, 1
        ) * tables[rows, pl.ds(HEAD_DIM, HEAD_DIM)]

    def head_norm(first, count, gain):
        def act(k):
            for half in range(2):
                rows = pl.ds(half * tokens, tokens)
                columns = pl.ds(pl.multiple_of(first + k, HEAD_DIM), HEAD_DIM)
                value = raw[rows, columns]
                inverse = lax.rsqrt(jnp.mean(value * value, -1, keepdims=True) + EPSILON)
                low[rows, columns] = turned(value * inverse * gain[...], rows).astype(BF16)

        loop(count * HEAD_DIM, HEAD_DIM, act)

    head_norm(0, heads, query_gain)
    if pending:
        serve(*pending.pop(0))
    head_norm(unit, kv_heads, key_gain)

    def spans(k, half):
        queries = [pl.ds(pl.multiple_of((2 * k + g) * HEAD_DIM, HEAD_DIM), HEAD_DIM) for g in range(2)]
        keys = pl.ds(pl.multiple_of(unit + k * HEAD_DIM, HEAD_DIM), HEAD_DIM)
        values = pl.ds(pl.multiple_of(unit + unit // 2 + k * HEAD_DIM, HEAD_DIM), HEAD_DIM)
        return queries, keys, values, pl.ds(half * tokens, tokens)

    def attend(k, half):
        queries, keys, values, rows = spans(k, half)
        row_id = lax.broadcasted_iota(jnp.int32, (tokens, tokens), 0)
        column_id = lax.broadcasted_iota(jnp.int32, (tokens, tokens), 1)
        start = tables[rows, pl.ds(2 * HEAD_DIM, HEAD_DIM)][:, :1]
        allowed = (column_id <= row_id) & (column_id.astype(F32) >= start)
        for g in range(2):
            scores = dot(low[rows, queries[g]], low[rows, keys], NT) * scale
            scores = jnp.where(allowed, scores, -1e30)
            exponent = jnp.exp(scores - jnp.max(scores, -1, keepdims=True))
            value = exponent / jnp.sum(exponent, -1, keepdims=True)
            probs[(k * 2 + half) * 2 + g] = value
            context[rows, queries[g]] = dot(value.astype(BF16), low[rows, values], NN).astype(BF16)

    for k in range(kv_heads):
        for half in range(2):
            attend(k, half)
        if pending and k % 2 == 0:
            serve(*pending.pop(0))

    while pending and pending[0][0] == 1:
        serve(*pending.pop(0))
    partial_product(3, 0, context, w_out, NN, False)
    if pending and pending[0][0] == 2:
        serve(*pending.pop(0))
    part_swap(3, 0).wait_recv()

    def add_middle(k):
        middle[pl.ds(k, few), :] = x_ref[pl.ds(k, few), :] + whole_rows(k, 0)

    loop(tokens, few, add_middle)
    normalize(middle, feed_gain, hidden)
    rows_swap(4, hidden).start()
    while pending:
        serve(*pending.pop(0))
    take_x(2)
    rows_swap(4, hidden).wait_recv()
    rows_swap(2, out_low).wait_recv()

    def feed(k):
        span = pl.ds(k, chunk)
        gate = dot(hidden[...], w_gu[:, span], NN)
        up_columns = pl.ds(pl.multiple_of(ff + k, chunk), chunk)
        up = dot(hidden[...], w_gu[:, up_columns], NN)
        grad = dot(out_low[...], w_down[span, :], NT)
        sigmoid = 1.0 / (1.0 + jnp.exp(-gate))
        swish = gate * sigmoid
        activated[:, span] = (swish * up).astype(BF16)
        gu_back[:, span] = (grad * up * (sigmoid + swish * (1.0 - sigmoid))).astype(BF16)
        gu_back[:, up_columns] = (grad * swish).astype(BF16)

    loop(ff, chunk, feed)
    part_swap(3, 0).wait_send()
    partial_product(6, 0, gu_back, w_gu, NT, True)
    weight_grad(3, activated, out_low)
    part_swap(6, 0).wait_recv()

    def middle_back(k):
        back, gain_part = normalize_back(k, middle, feed_gain, whole_rows(k, 0))
        back = back_ref[pl.ds(k, few), :] + back
        input_grad[pl.ds(k, few), :] = back
        attended[pl.ds(pl.multiple_of(mine + k, few), few), :] = back.astype(BF16)
        gain_sums[1] += gain_part

    loop(tokens, few, middle_back)
    rows_swap(7, attended).start()
    partial_product(5, 1, activated, w_down, NN, False)
    weight_grad(2, hidden, gu_back)
    part_swap(5, 1).wait_recv()

    def add_output(k):
        output[pl.ds(k, few), :] = middle[pl.ds(k, few), :] + whole_rows(k, 1)

    loop(tokens, few, add_output)
    rows_swap(7, attended).wait_recv()

    def context_back(k):
        span = pl.ds(k, chunk)
        grad_context[:, span] = dot(attended[...], w_out[span, :], NT).astype(BF16)

    loop(unit, chunk, context_back)
    weight_grad(1, context, attended)

    def head_back(rows, columns, gain, grad, index):
        value = raw[rows, columns]
        inverse = lax.rsqrt(jnp.mean(value * value, -1, keepdims=True) + EPSILON)
        unscaled = value * inverse
        grad = turned_back(grad, rows)
        gain_sums[index, :, pl.ds(0, HEAD_DIM)] += jnp.sum(
            (grad * unscaled).reshape(tokens // 8, 8, HEAD_DIM), 0
        )
        inner = grad * gain[...]
        back = inverse * (inner - unscaled * jnp.mean(inner * unscaled, -1, keepdims=True))
        low[rows, columns] = back.astype(BF16)

    def attend_back(k, half):
        queries, keys, values, rows = spans(k, half)
        grad_keys, grad_values = 0.0, 0.0
        grad_queries = []
        for g in range(2):
            prob = probs[(k * 2 + half) * 2 + g]
            above = grad_context[rows, queries[g]]
            grad_values = grad_values + dot(prob.astype(BF16), above, TN)
            grad_probs = dot(above, low[rows, values], NT)
            grad_scores = prob * (grad_probs - jnp.sum(prob * grad_probs, -1, keepdims=True))
            grad_scores = grad_scores.astype(BF16)
            grad_queries.append(dot(grad_scores, low[rows, keys], NN) * scale)
            grad_keys = grad_keys + dot(grad_scores, low[rows, queries[g]], TN)
        for g in range(2):
            head_back(rows, queries[g], query_gain, grad_queries[g], 2)
        head_back(rows, keys, key_gain, grad_keys * scale, 3)
        low[rows, values] = grad_values.astype(BF16)

    for half in range(2):

        def body(k, carry):
            attend_back(k, half)
            return carry

        lax.fori_loop(0, kv_heads, body, 0)

    part_swap(6, 0).wait_send()
    partial_product(8, 0, low, w_qkv, NT, True)
    weight_grad(0, normed, low)
    part_swap(8, 0).wait_recv()

    def input_back(k):
        back, gain_part = normalize_back(k, x_ref, attention_gain, whole_rows(k, 0))
        input_grad[pl.ds(k, few), :] += back
        gain_sums[0] += gain_part

    loop(tokens, few, input_back)
    grad_attention[...] = jnp.sum(gain_sums[0], 0, keepdims=True)
    grad_feed[...] = jnp.sum(gain_sums[1], 0, keepdims=True)
    grad_query_gain[...] = jnp.sum(gain_sums[2, :, pl.ds(0, HEAD_DIM)], 0, keepdims=True)
    grad_key_gain[...] = jnp.sum(gain_sums[3, :, pl.ds(0, HEAD_DIM)], 0, keepdims=True)

    for index, ref in ((0, normed), (1, tables), (2, out_low), (4, hidden), (7, attended)):
        rows_swap(index, ref).wait_send()
    part_swap(5, 1).wait_send()
    part_swap(8, 0).wait_send()
    for which in range(4):
        for way in range(2):
            for hop in range(1, reach(which, way) + 1):
                ring_copy(which, way, hop, "wait_send")
                if SPREADS[which][1]:
                    x_copy(which, way, hop, place.x).wait_send()


def layer_pass(values, back, table, gains, shards, n):
    tokens, unit = values.shape
    top = n // 2
    dma = pltpu.SemaphoreType.DMA
    vmem = pltpu.VMEM
    both = 2 * tokens
    heads = unit // HEAD_DIM
    in_vmem = pl.BlockSpec(memory_space=pltpu.VMEM)
    row = lambda width: jax.ShapeDtypeStruct((1, width), F32)
    shapes = [(unit, 2 * unit), (unit, unit), (unit, 3 * unit), (3 * unit // 2, unit)]
    results = pl.pallas_call(
        functools.partial(layer_kernel, n, tokens, unit),
        out_shape=[jax.ShapeDtypeStruct((tokens, unit), F32)] * 2
        + [row(unit), row(unit), row(HEAD_DIM), row(HEAD_DIM)]
        + [jax.ShapeDtypeStruct(shape, BF16) for shape in shapes],
        in_specs=[in_vmem] * 7 + [ANY] * 4,
        out_specs=[in_vmem] * 6 + [ANY] * 4,
        scratch_shapes=[vmem(shape, BF16) for shape in shapes]
        + [
            vmem((both, unit), BF16),
            vmem((both, 3 * unit // 2), F32),
            vmem((both, 2 * unit), BF16),
            vmem((2 * heads, tokens, tokens), F32),
            vmem((both, unit), BF16),
            vmem((both, unit), BF16),
            vmem((both, unit), BF16),
            vmem((both, unit), BF16),
            vmem((both, unit), BF16),
            vmem((both, 3 * unit // 2), BF16),
            vmem((both, 3 * unit), BF16),
            vmem((both, unit), F32),
            vmem((2, tokens, unit), BF16),
            vmem((2, tokens, unit), BF16),
            vmem((tokens, unit), F32),
            vmem((both, 3 * HEAD_DIM), F32),
            vmem((2, unit // 2, unit), BF16),
            vmem((unit // 2, both), BF16),
            vmem((4, 8, unit), F32),
            dma((4,)),
            dma((8 * top,)),
            dma((8 * top,)),
            dma((4 * top,)),
            dma((4 * top,)),
            dma((9,)),
            dma((9,)),
            dma((2,)),
        ],
        compiler_params=pltpu.CompilerParams(
            collective_id=0, has_side_effects=True, vmem_limit_bytes=56 * 2**20
        ),
    )(values, back, table, *gains, *shards)
    return results[:2], results[2:6], results[6:]


PHASES = ((DOWN, 3, False), (GU, 3, True), (OUT, 2, False), (QKV, 2, True))

OWNERS = (
    (3, 0, 1, False, 1, 2),
    (3, 1, 1, False, 1, 6),
    (3, 0, 2, False, 0, 2),
    (2, 0, 2, True, 1, 5),
    (1, 0, 3, False, 0, 5),
    (1, 0, 3, False, 1, 1),
    (0, 0, 3, True, 0, 1),
)
KEY, VALUE, QUERY, OUTM, GATE, UP, DOWNM = range(7)
RETURNS = (OUTM, KEY, VALUE, DOWNM, GATE, UP, QUERY)
TILE_SLOTS = 4
X_SLOTS = 3


def stage_order(n, order):
    top = n // 2
    ring = (top - 0.5) / n
    at = []
    for i in range(n):
        at.append((3 * i - 6.0, ("x", 1, i)))
        at.append((3 * n + 2 * i - 4.0, ("x", 3, i)))
        at.append((1 + 3 * ring * i, ("ring", 0, i)))
        at.append((3 * (i + 1) + 1.0, ("ring", 1, i)))
        at.append((3 * n + 2 + 2 * ring * i, ("ring", 2, i)))
        at.append((3 * n + 3 + max(2.0 * i, 2 * ring * (n + i)), ("ring", 3, i)))
    at.append((1 + 3 * ring * n + 9, ("final", 0, 0)))
    at.append((3 * n + 2 + 2 * ring * n + 6, ("final", 2, 0)))
    return [stage for _, stage in sorted(at)]


class Rows:
    def __init__(self):
        self.next = 0

    def take(self, rows):
        start = self.next
        self.next += rows
        return start


def layout(n, unit):
    base = unit // n
    top = n // 2
    sums = Rows()

    def shared(take):
        first = [take(PHASES[p][1] * base) for p in (0, 1)]
        return first + first

    x_in = [sums.take(PHASES[1][1] * base) for _ in range(n)]
    place = {
        "own": [sums.take(3 * base) for _ in range(TILE_SLOTS)],
        "x_in": {1: x_in, 3: x_in},
        "ring": shared(
            lambda rows: [[sums.take(rows) for _ in range(top)] for _ in range(2)]
        ),
    }
    for name in ("far", "grad", "ahead"):
        place[name] = shared(sums.take)
    for name in ("part", "other"):
        place[name] = [0 if split else sums.take(units * base) for _, units, split in PHASES]
    newton = Rows()
    place["high"] = [newton.take(3 * unit) for _ in range(2)]
    place["poly"] = [newton.take(unit) for _ in range(2)]
    return place, max(sums.next, newton.next)


def update_kernel(n, unit, *refs):
    grads, moments, gains_in = refs[:4], refs[4:11], refs[11]
    outs, orths, lands, gains_out = refs[12:16], refs[16:20], refs[20:24], refs[24]
    (
        pool, exact, gram, squares, gain_mine, gain_core, gain_x, gain_all,
        land_send, land_recv, tile_sem, x_send, x_recv, x_free, ring_send, ring_recv, part_send, part_recv,
        moment_sem, grad_local, grad_send, grad_recv, in_send, in_recv,
        out_send, out_recv, pass_send, pass_recv, gain_send, gain_recv,
    ) = refs[25:]
    place = Place(n)
    base = unit // n
    top = n // 2
    at, _ = layout(n, unit)
    cw, ccw = place.ring_neighbour(1), place.ring_neighbour(-1)
    ways = ((1, cw), (-1, ccw))
    side = [(place.x * 2 + core, lax.rem(place.own + k, n)) for k in range(1, n) for core in range(2)]
    greet(side + [place.core_partner, place.x_partner])
    order = [top]
    for distance in range(top - 1, 0, -1):
        order += [distance, -distance]
    order.append(0)
    stages = stage_order(n, order)
    moment = exact
    height = [units * base for _, units, _ in PHASES]
    owners = [
        (xs * 2 + 1, place.own_at(spot * n // 8)) for _, _, _, _, xs, spot in OWNERS
    ]
    here = place.rep * n + place.own
    is_owner = [here == rep * n + own for rep, own in owners]

    def rows(start, size):
        if isinstance(start, int):
            return pl.ds(start, size)
        return pl.ds(pl.multiple_of(start, size), size)

    def block(start, size):
        return pool.at[rows(start, size)]

    def pieces_of(phase, x):
        array, units, _ = PHASES[phase]
        half = unit // 2
        found = []
        for core in range(2):
            for b in range(units):
                if array == GU:
                    column = x * 3 * unit + core * (3 * half) + b * half
                else:
                    column = x * 2 * unit + core * (unit - x * half) + b * (half + x * half)
                found.append((core, b, x * units * half + b * half, column))
        return found

    def columns(start):
        return pl.ds(pl.multiple_of(start, unit // 2), unit // 2)

    def in_block(start, core, b):
        return pool.at[pl.ds(start + b * base, base), pl.ds(core * (unit // 2), unit // 2)]

    def shard_rows(phase, own_index):
        if PHASES[phase][2]:
            return rows(own_index * base, base)
        return rows(lax.rem(own_index, top) * height[phase], height[phase])

    def landing(phase, own_index, act):
        if PHASES[phase][2]:
            act()
        else:
            pl.when(own_index // top == 1)(act)

    def spread(source, target, size, send, recv, device):
        step = size

        def copy(k, count):
            return remote(block(source + k, count), block(target + k, count), send, recv, device)

        return Several(
            functools.partial(copy, 0, size),
            [functools.partial(copy, k, step) for k in range(0, size, step)],
        )

    def land_copy(phase, i, act):
        array = PHASES[phase][0]
        own_index = place.shard(order[i])
        span = shard_rows(phase, own_index)

        def copy(span):
            return remote(
                grads[array].at[span], lands[array].at[span],
                land_send.at[phase * n + i], land_recv.at[phase * n + i], place.core_partner,
            )

        def do():
            getattr(copy(span), act)()

        landing(phase, own_index, do)

    def x_index(phase, i):
        return (phase // 2) * n + i

    def x_copy(phase, i):
        index = x_index(phase, i)
        array = PHASES[phase][0]
        span = shard_rows(phase, place.shard(order[i]))
        target = at["x_in"][phase][i]

        def copy(core, b, column):
            return remote(
                (grads, lands)[core][array].at[span, columns(column)], in_block(target, core, b),
                x_send.at[index], x_recv.at[index], place.x_partner,
            )

        def whole():
            spot = block(target, height[phase])
            return remote(spot, spot, x_send.at[index], x_recv.at[index], place.x_partner)

        return Several(
            whole,
            [
                functools.partial(copy, core, b, column)
                for core, b, column, _ in pieces_of(phase, 1 - place.x)
            ],
        )

    def ring_copy(phase, way, distance, source, part):
        size = height[phase] // 2
        target = at["ring"][phase][way][distance - 1] + part * size
        index = ((phase * 2 + way) * top + distance - 1) * 2 + part
        return spread(
            source + part * size, target, size,
            ring_send.at[index], ring_recv.at[index], ways[way][1],
        )

    def ring_out(phase, distance, part):
        if distance == 0:
            return []
        if distance == top:
            return [ring_copy(phase, part, top, at["far"][phase], part)]
        way = 0 if distance > 0 else 1
        far = abs(distance)
        return [ring_copy(phase, way, far, at["ring"][phase][way][far], part)]

    def part_copy(phase):
        return spread(
            at["part"][phase], at["other"][phase], height[phase],
            part_send.at[phase // 2], part_recv.at[phase // 2], place.x_partner,
        )

    def gain_copy(src, dst, slot, device):
        return remote(src, dst, gain_send.at[slot], gain_recv.at[slot], device)

    def gain_core_copy():
        return gain_copy(gain_mine, gain_core, 0, place.core_partner)

    def gain_x_copy():
        return gain_copy(gain_core, gain_x, 1, place.x_partner)

    def gain_back_copy():
        return gain_copy(gain_mine, gain_x, 2, place.core_partner)

    def gain_ring(way, hop, distance):
        spot = gain_all.at[place.shard(distance)]
        return gain_copy(spot, spot, 3 + way * top + hop - 1, ways[way][1])

    def grad_place(phase, x):
        array = PHASES[phase][0]
        start = at["grad"][phase]
        if not PHASES[phase][2]:
            return [(outs[array], block(start, height[phase]))]
        return [
            (outs[array].at[:, columns(column)], in_block(start, core, b))
            for core, b, _, column in pieces_of(phase, x)
        ]

    def grad_span(phase, x):
        array, units, split = PHASES[phase]
        if not split:
            return outs[array]
        first = pl.multiple_of(x * units * unit, unit)
        return outs[array].at[:, pl.ds(first, units * unit)]

    def grad_sent(phase, to, device, x):
        span = grad_span(phase, x)
        return remote(span, span, grad_send.at[phase, to], grad_recv.at[phase, to], device)

    def matrix_rows(matrix, own_index):
        phase, first, units, tall, _, _ = OWNERS[matrix]
        if tall:
            return [(0, own_index * units * base, units * base)]
        return [
            ((first + k) * base, k * unit + own_index * base, base) for k in range(units)
        ]

    def matrix_span(matrix):
        phase, first, units, tall, xs, _ = OWNERS[matrix]
        array = PHASES[phase][0]
        if tall:
            return orths[array]
        start = (xs * PHASES[phase][1] + first) * unit
        return orths[array].at[:, pl.ds(start, units * unit)]

    def answer_parts(matrix, final, own_index):
        phase, first, units, tall, xs, _ = OWNERS[matrix]
        array = PHASES[phase][0]
        if tall:
            return [(block(final + own_index * units * base, units * base), orths[array])]
        return [
            (
                pool.at[
                    rows(final + (b - first) * unit + own_index * base, base),
                    pl.ds(core * (unit // 2), unit // 2),
                ],
                orths[array].at[:, columns(column)],
            )
            for core, b, _, column in pieces_of(phase, xs)
            if first <= b < first + units
        ]

    def handed(matrix, to, device):
        span = matrix_span(matrix)
        return remote(span, span, pass_send.at[matrix, to], pass_recv.at[matrix, to], device)

    def answered(matrix, target):
        span = matrix_span(matrix)
        return remote(
            span, span, out_send.at[target], out_recv.at[matrix], (place.x * 2, target)
        )

    def summed(pieces, size, store):
        step = 16
        steps = 4 if size % (4 * step) == 0 else 1

        def body(k, carry):
            for j in range(steps):
                shift = (k * steps + j) * step
                total = None
                for start in pieces:
                    value = pool[rows_at(start, shift, step), :].astype(F32)
                    total = value if total is None else total + value
                store(shift, step, total)
            return carry

        lax.fori_loop(0, size // (step * steps), body, 0)

    def rows_at(start, shift, step):
        return pl.ds(pl.multiple_of(start + shift, step), step)

    def keep(start):
        def store(shift, step, total):
            pool[rows_at(start, shift, step), :] = total.astype(BF16)

        return store

    def load_tile(k):
        _, phase, i = stages[k]
        array, _, split = PHASES[phase]
        slot = k_slot[k]
        own_index = place.shard(order[i])
        span = shard_rows(phase, own_index)

        def load(source, target):
            pltpu.make_async_copy(source, target, tile_sem.at[slot]).start()

        if split:
            for core, b, column, _ in pieces_of(phase, place.x):
                load(
                    (grads, lands)[core][array].at[span, columns(column)],
                    in_block(at["own"][slot], core, b),
                )
            return
        for core in range(2):

            @pl.when(own_index // top == core)
            def _():
                load((grads, lands)[core][array].at[span], block(at["own"][slot], height[phase]))

    tiled = [k for k, stage in enumerate(stages) if stage[0] == "ring"]
    k_slot = {k: index % TILE_SLOTS for index, k in enumerate(tiled)}
    seen = set()

    def landed(phase, i):
        if (phase, i) not in seen:
            seen.add((phase, i))
            land_copy(phase, i, "wait_recv")

    def prefetch(index):
        if index >= len(tiled):
            return
        k = tiled[index]
        landed(*stages[k][1:])
        load_tile(k)

    def wait_tile(k):
        span = block(at["own"][k_slot[k]], height[stages[k][1]])
        pltpu.make_async_copy(span, span, tile_sem.at[k_slot[k]]).wait()

    def moment_copies(phase, act):
        array, units, split = PHASES[phase]
        if not split:
            act(moments[3 if array == OUT else 6], moment.at[pl.ds(0, height[phase])])
            return
        half = unit // 2
        for x in range(2):

            @pl.when(place.x == x)
            def _():
                for core, b, _, column in pieces_of(phase, x):
                    if array == GU:
                        source, first = 4 + x, x * 3 * unit
                    elif x == 0:
                        source, first = 0, 0
                    else:
                        source, first = 1 + b, (2 + b) * unit
                    act(
                        moments[source].at[:, pl.ds(column - first, half)],
                        moment.at[pl.ds(b * base, base), pl.ds(core * half, half)],
                    )

    def load_moment(phase):
        moment_copies(
            phase, lambda src, dst: pltpu.make_async_copy(src, dst, moment_sem.at[phase]).start()
        )

    def finish(phase, pieces):
        span = moment.at[pl.ds(0, height[phase])]
        pltpu.make_async_copy(span, span, moment_sem.at[phase]).wait()

        if phase >= 2:
            settle(phase - 2)

        def store(shift, step, total):
            pool[rows_at(at["grad"][phase], shift, step), :] = total.astype(BF16)
            ahead = (1.0 + MOMENTUM) * total + MOMENTUM**2 * moment[rows_at(0, shift, step), :]
            pool[rows_at(at["ahead"][phase], shift, step), :] = ahead.astype(BF16)

        summed(pieces, height[phase], store)
        for matrix, (its_phase, _, _, _, xs, _) in enumerate(OWNERS):
            if its_phase != phase:
                continue

            @pl.when(place.x == xs)
            def _():
                for source, target, size in matrix_rows(matrix, place.own):
                    remote(
                        block(at["ahead"][phase] + source, size), block(at["high"][1] + target, size),
                        in_send.at[matrix], in_recv.at[place.own], owners[matrix],
                    ).start()

        for target, source in grad_place(phase, place.x):
            pltpu.make_async_copy(source, target, grad_local.at[phase]).start()
            remote(
                source, target, grad_send.at[phase, 0], grad_recv.at[phase, 0], place.core_partner
            ).start()
            if PHASES[phase][2]:
                remote(
                    source, target, grad_send.at[phase, 1], grad_recv.at[phase, 1], place.x_partner
                ).start()
        after = {0: 1, 1: 2, 2: 3, 3: None}[phase]
        if after is not None:
            load_moment(after)

    def settle(phase):
        span = block(at["grad"][phase], height[phase])
        pltpu.make_async_copy(span, span, grad_local.at[phase]).wait()
        remote(
            span, span, grad_send.at[phase, 0], grad_recv.at[phase, 0], place.core_partner
        ).wait_send()
        if PHASES[phase][2]:
            remote(
                span, span, grad_send.at[phase, 1], grad_recv.at[phase, 1], place.x_partner
            ).wait_send()
        for matrix, (its_phase, _, units, _, xs, _) in enumerate(OWNERS):
            if its_phase != phase:
                continue

            @pl.when(place.x == xs)
            def _():
                span = block(at["high"][1], units * base)
                remote(
                    span, span, in_send.at[matrix], in_recv.at[0], place.core_partner
                ).wait_send()

    def stage_x(phase, i):
        landed(phase, i)
        index = x_index(phase, i)
        if index >= X_SLOTS:
            before = index - X_SLOTS
            x_copy(1 if before < n else 3, before % n).wait_send()
        if phase == 3:
            pl.semaphore_wait(x_free, 1)
        x_copy(phase, i).start()

    def stage_ring(k, phase, i):
        distance = order[i]
        wait_tile(k)
        pieces = [at["own"][k_slot[k]]]
        if PHASES[phase][2]:
            x_copy(phase, i).wait_recv()
            pieces.append(at["x_in"][phase][i])
        size = height[phase]
        mid = size // 2
        if abs(distance) == 1 and 0 < phase < 3:
            ring_sent(phase - 1)
        if distance == 0:
            for way in range(2):
                held = at["ring"][phase][way][0]
                for part in range(2):
                    ring_copy(phase, way, 1, held, part).wait_recv()
                pieces.append(held)
            if PHASES[phase][2]:
                finish(phase, pieces)
            else:
                summed(pieces, size, keep(at["part"][phase]))
                part_copy(phase).start()
        else:
            way = 0 if distance > 0 else 1
            far = abs(distance)
            held = at["far"][phase] if far == top else at["ring"][phase][way][far]
            for part in (1 - way, way):
                starts = [start + part * mid for start in pieces]
                if far + 1 < top or (far + 1 == top and part == way):
                    ring_copy(phase, way, far + 1, held, part).wait_recv()
                    starts.append(held + part * mid)
                summed(starts, mid, keep(held + part * mid))
                for copy in ring_out(phase, distance, part):
                    copy.start()
        if phase == 1:
            pl.semaphore_signal(x_free, inc=1, device_id=place.x_partner, device_id_type=MESH)

    def ring_sent(phase):
        if phase not in ring_waited:
            ring_waited.add(phase)
            for distance in order:
                for part in range(2):
                    for copy in ring_out(phase, distance, part):
                        copy.wait_send()

    ring_waited = set()

    def gain_stage(hop):
        if hop == 0:
            gain_core_copy().wait_recv()
            gain_core[...] = gain_mine[...] + gain_core[...]
            gain_x_copy().start()
            return
        if hop == 1:
            gain_x_copy().wait_recv()
            gain_all[place.own] = gain_core[...] + gain_x[...]
            for way in range(2):
                gain_ring(way, 1, 0).start()
        for way in range(2):
            if 1 < hop <= hops(n, way, 0) + 1:
                distance = -ways[way][0] * (hop - 1)
                gain_ring(way, hop - 1, distance).wait_recv()
                if hop <= hops(n, way, 0):
                    gain_ring(way, hop, distance).start()

    gain_mine[...] = gains_in[...]

    @pl.when(place.core == 0)
    def _():
        load_moment(0)
        for index in range(TILE_SLOTS - 1):
            prefetch(index)
        done = 0
        hop = 0
        for k, (kind, phase, i) in enumerate(stages):
            if kind == "final":
                part_copy(phase).wait_recv()
                finish(phase, [at["part"][phase], at["other"][phase]])
                continue
            if kind == "x":
                stage_x(phase, i)
                continue
            prefetch(done + TILE_SLOTS - 1)
            done += 1
            stage_ring(k, phase, i)
            if done % 2 == 0 and hop <= top + 1:
                gain_stage(hop)
                hop += 1

        total = gain_all[0]
        for k in range(1, n):
            total = total + gain_all[k]
        gains_out[...] = total
        gain_mine[...] = total
        gain_back_copy().start()

        for phase in (1, 3):
            grad_sent(phase, 1, place.x_partner, 1 - place.x).wait_recv()
            grad_sent(phase, 2, place.core_partner, 1 - place.x).start()

        for matrix in RETURNS:
            xs = OWNERS[matrix][4]

            @pl.when(place.x == xs)
            def _():
                answered(matrix, place.own).wait_recv()
                handed(matrix, 0, place.x_partner).start()
                handed(matrix, 1, place.core_partner).start()

            @pl.when(place.x != xs)
            def _():
                handed(matrix, 0, place.x_partner).wait_recv()
                handed(matrix, 1, place.core_partner).start()

        for matrix, (phase, _, units, _, xs, _) in enumerate(OWNERS):
            handed(matrix, 1, place.core_partner).wait_send()

            @pl.when(place.x == xs)
            def _():
                handed(matrix, 0, place.x_partner).wait_send()

        for phase, (_, _, split) in enumerate(PHASES):
            if phase >= 2:
                settle(phase)
            if split:
                grad_sent(phase, 2, place.core_partner, 1 - place.x).wait_send()
            else:
                part_copy(phase).wait_send()
            ring_sent(phase)
        for index in range(2 * n - X_SLOTS, 2 * n):
            x_copy(1 if index < n else 3, index % n).wait_send()
        gain_x_copy().wait_send()
        gain_back_copy().wait_send()
        for way in range(2):
            for h in range(1, hops(n, way, 0) + 1):
                gain_ring(way, h, -ways[way][0] * (h - 1)).wait_send()

    @pl.when(place.core == 1)
    def _():
        gain_core_copy().start()
        needed = []
        for kind, phase, i in stages:
            if kind != "final" and (phase, i) not in needed:
                needed.append((phase, i))
        ahead = 8
        for index, (phase, i) in enumerate(needed):
            if index >= ahead:
                land_copy(*needed[index - ahead], "wait_send")
            land_copy(phase, i, "start")
        for phase, i in needed[-ahead:]:
            land_copy(phase, i, "wait_send")
        newton_part(n, unit, place, pool, exact, gram, squares, at, is_owner, in_recv)
        for matrix, (_, _, units, tall, _, _) in enumerate(OWNERS):

            @pl.when(is_owner[matrix])
            def _():
                final = at["high"][1 - NS_STEPS % 2 if tall else NS_STEPS % 2]

                def send(k, carry):
                    target = lax.rem(place.own + k, n)
                    for source, part in answer_parts(matrix, final, target):
                        remote(
                            source, part, out_send.at[target], out_recv.at[matrix],
                            (place.x * 2, target),
                        ).start()
                    return carry

                lax.fori_loop(0, n, send, 0)

                def sent(k, carry):
                    answered(matrix, lax.rem(place.own + k, n)).wait_send()
                    return carry

                lax.fori_loop(0, n, sent, 0)

        gain_core_copy().wait_send()
        gain_back_copy().wait_recv()
        gains_out[...] = gain_x[...]
        for phase, (_, _, split) in enumerate(PHASES):
            grad_sent(phase, 0, place.core_partner, place.x).wait_recv()
            if split:
                grad_sent(phase, 2, place.core_partner, 1 - place.x).wait_recv()
        for matrix in RETURNS:
            handed(matrix, 1, place.core_partner).wait_recv()


def newton_part(n, unit, place, pool, exact, gram, squares, at, is_owner, in_recv):
    base = unit // n
    small = min(256, unit // 2)
    per = unit // small
    wide = unit // 2
    few = 32
    count, tall = 0, 0
    for mine, (_, _, units, lies_tall, _, _) in zip(is_owner, OWNERS):
        count = count + units * mine.astype(jnp.int32)
        tall = tall + int(lies_tall) * mine.astype(jnp.int32)
    high, poly = at["high"], at["poly"]

    def rows(start, size):
        return pl.ds(pl.multiple_of(start, size), size)

    for matrix, (_, _, units, *_) in enumerate(OWNERS):

        @pl.when(is_owner[matrix])
        def _():
            span = pool.at[pl.ds(high[1], units * base)]
            for own_index in range(n):
                remote(
                    span, span, in_recv.at[own_index], in_recv.at[own_index], place.core_partner
                ).wait_recv()

    @pl.when(count > 0)
    def _():
        squares[...] = jnp.zeros_like(squares)

        def square(k, carry):
            part = pool[rows(high[1] + k * few, few), :].astype(F32)
            squares[...] += jnp.sum((part * part).reshape(few // 8, 8, unit), 0)
            return carry

        lax.fori_loop(0, count * (unit // few), square, 0)
        total = jnp.sum(jnp.sum(squares[...], 1, keepdims=True), 0, keepdims=True)
        inverse = 1.0 / (jnp.sqrt(total) + 1e-07)

        @pl.when(tall == 0)
        def _():
            def scale(k, carry):
                value = pool[rows(high[1] + k * few, few), :].astype(F32) * inverse
                exact[rows(k * few, few), :] = value
                pool[rows(high[0] + k * few, few), :] = value.astype(BF16)
                return carry

            lax.fori_loop(0, count * (unit // few), scale, 0)

        @pl.when(tall == 1)
        def _():
            def scale(k, carry):
                block, row = k // per, k % per
                for column in range(per):
                    part = pool[
                        rows(high[1] + k * small, small), pl.ds(column * small, small)
                    ].astype(F32)
                    value = (part * inverse).T
                    shift = block * unit + column * small
                    columns = rows(row * small, small)
                    exact[rows(shift, small), columns] = value
                    pool[rows(high[0] + shift, small), columns] = value.astype(BF16)
                return carry

            lax.fori_loop(0, count * per, scale, 0)

        def newton(step, carry):
            even = step % 2
            now = high[0] + even * (high[1] - high[0])
            later = high[1] - even * (high[1] - high[0])

            def keep_symmetric(to, chunk, value):
                pool[pl.ds(to, (chunk + 1) * wide), pl.ds(chunk * wide, wide)] = value.astype(BF16)
                if chunk == 1:
                    pool[pl.ds(to + wide, wide), pl.ds(0, wide)] = value[:wide].T.astype(BF16)

            for chunk in range(2):
                down = (chunk + 1) * wide

                def product(block):
                    left = pool[pl.ds(pl.multiple_of(now + block * unit, unit), down), :]
                    right = pool[rows(now + block * unit + chunk * wide, wide), :]
                    return lax.dot_general(
                        left, right, (((1,), (1,)), ((), ())), preferred_element_type=F32
                    )

                gram[:down, :] = product(0)

                def more(block, carry):
                    gram[:down, :] += product(block)
                    return carry

                lax.fori_loop(1, count, more, 0)
                keep_symmetric(poly[0], chunk, gram[:down, :])

            for chunk in range(2):
                down = (chunk + 1) * wide
                columns = pl.ds(chunk * wide, wide)
                squared = jnp.dot(
                    pool[pl.ds(poly[0], down), :], pool[pl.ds(poly[0], unit), columns],
                    preferred_element_type=F32,
                )
                plain = pool[pl.ds(poly[0], down), columns].astype(F32)
                keep_symmetric(poly[1], chunk, NEWTON_B * plain + NEWTON_C * squared)

            def advance(block, carry):
                for chunk in range(2):
                    columns = pl.ds(chunk * wide, wide)
                    value = NEWTON_A * exact[rows(block * unit, unit), columns] + jnp.dot(
                        pool[pl.ds(poly[1], unit), :],
                        pool[rows(now + block * unit, unit), columns],
                        preferred_element_type=F32,
                    )
                    exact[rows(block * unit, unit), columns] = value
                    pool[rows(later + block * unit, unit), columns] = value.astype(BF16)
                return carry

            lax.fori_loop(0, count, advance, 0)
            return carry

        lax.fori_loop(0, NS_STEPS, newton, 0)

        @pl.when(tall == 1)
        def _():
            free = high[1 - NS_STEPS % 2]
            factor = jnp.sqrt(jnp.full((1, 1), count, jnp.int32).astype(F32))

            def lay(k, carry):
                block, row = k // per, k % per
                for column in range(per):
                    columns = pl.ds(column * small, small)
                    part = exact[rows(k * small, small), columns]
                    pool[
                        rows(free + block * unit + column * small, small), rows(row * small, small)
                    ] = (part * factor).T.astype(BF16)
                return carry

            lax.fori_loop(0, count * per, lay, 0)


def update_all(grads, moments, gains, n, unit):
    top = n // 2
    dma = pltpu.SemaphoreType.DMA
    vmem = pltpu.VMEM
    _, pool_rows = layout(n, unit)
    shapes = [(unit // n, 4 * unit), (2 * unit // n, unit), (unit // n, 6 * unit), (3 * unit // n, unit)]
    own = [jax.ShapeDtypeStruct(shape, BF16) for shape in shapes]
    whole = [jax.ShapeDtypeStruct(grad.shape, BF16) for grad in grads]
    in_vmem = pl.BlockSpec(memory_space=pltpu.VMEM)
    results = pl.pallas_call(
        functools.partial(update_kernel, n, unit),
        out_shape=own + own + whole + [jax.ShapeDtypeStruct(gains.shape, F32)],
        in_specs=[ANY] * 11 + [in_vmem],
        out_specs=[ANY] * 12 + [in_vmem],
        scratch_shapes=[
            vmem((pool_rows, unit), BF16),
            vmem((3 * unit, unit), F32),
            vmem((unit, unit // 2), F32),
            vmem((8, unit), F32),
            vmem(gains.shape, F32),
            vmem(gains.shape, F32),
            vmem(gains.shape, F32),
            vmem((n,) + gains.shape, F32),
            dma((4 * n,)),
            dma((4 * n,)),
            dma((TILE_SLOTS,)),
            dma((2 * n,)),
            dma((2 * n,)),
            pltpu.SemaphoreType.REGULAR,
            dma((16 * top,)),
            dma((16 * top,)),
            dma((2,)),
            dma((2,)),
            dma((4,)),
            dma((4,)),
            dma((4, 3)),
            dma((4, 3)),
            dma((7,)),
            dma((n,)),
            dma((n,)),
            dma((7,)),
            dma((7, 2)),
            dma((7, 2)),
            dma((3 + 2 * top,)),
            dma((3 + 2 * top,)),
        ],
        compiler_params=pltpu.CompilerParams(
            collective_id=1, has_side_effects=True, vmem_limit_bytes=56 * 2**20
        ),
    )(*grads, *moments, gains)
    return results[:4], results[4:8], results[12]


def unpacked(arrays, unit):
    qkv, out, gate_up, down = arrays
    return (
        qkv[:, : 2 * unit],
        qkv[:, 2 * unit : 3 * unit],
        qkv[:, 3 * unit :],
        out,
        gate_up[:, : 3 * unit],
        gate_up[:, 3 * unit :],
        down,
    )


def body(
    layer_input,
    output_grad,
    lengths,
    attention_gain,
    feed_gain,
    query_gain,
    key_gain,
    query_weight,
    key_weight,
    value_weight,
    out_weight,
    gate_weight,
    up_weight,
    down_weight,
    query_moment,
    key_moment,
    value_moment,
    out_moment,
    gate_moment,
    up_moment,
    down_moment,
):
    owned = (
        query_weight, key_weight, value_weight, out_weight, gate_weight, up_weight, down_weight,
    )
    moments = (
        query_moment, key_moment, value_moment, out_moment, gate_moment, up_moment, down_moment,
    )
    n = lax.axis_size("own")
    unit = layer_input.shape[1]
    core = lax.axis_index("rep") % 2

    def halves(*matrices):
        parts = []
        for matrix in matrices:
            width = matrix.shape[1] // 2
            parts.append(lax.dynamic_slice_in_dim(matrix, core * width, width, 1))
        return jnp.concatenate(parts, 1).astype(BF16)

    shards = (
        halves(query_weight, key_weight, value_weight),
        out_weight.astype(BF16),
        halves(gate_weight, up_weight),
        down_weight.astype(BF16),
    )
    row_count = layer_input.shape[0]
    _, positions = segments(lengths[0], row_count)
    cosine_table, sine_table = rope_tables(positions)
    starts = (jnp.arange(row_count, dtype=jnp.int32) - positions).astype(F32)
    table = jnp.concatenate(
        [
            cosine_table[:, 0], cosine_table[:, 0], -sine_table[:, 0], sine_table[:, 0],
            jnp.broadcast_to(starts[:, None], (row_count, HEAD_DIM)),
        ],
        1,
    )
    gain_rows = [gain[None, :] for gain in (attention_gain, feed_gain, query_gain, key_gain)]
    (block_output, input_grad), gain_grads, grads = layer_pass(
        layer_input, output_grad, table, gain_rows, shards, n
    )
    gains = jnp.concatenate([grad[0] for grad in gain_grads])
    gains = jnp.pad(gains, (0, 24 * 128 - gains.shape[0])).reshape(24, 128)
    reduced, orth, gain_sums = update_all(grads, moments, gains, n, unit)
    moments_next = [
        MOMENTUM * moment + part.astype(F32) for moment, part in zip(moments, unpacked(reduced, unit))
    ]
    new_weights = [
        matrix * (1.0 - LEARN_RATE * WEIGHT_DECAY) - LEARN_RATE * part.astype(F32)
        for matrix, part in zip(owned, unpacked(orth, unit))
    ]
    gain_sums = gain_sums.reshape(-1)
    norm_grads = gain_sums[: 2 * unit].reshape(2, unit)
    head_grads = gain_sums[2 * unit : 2 * unit + 2 * HEAD_DIM].reshape(2, HEAD_DIM)
    return (block_output, input_grad, norm_grads, head_grads, *new_weights, *moments_next)


def solution(mesh):
    tokens, owned = P(("rep", "own"), None), P("own", None)
    return jax.shard_map(
        body,
        mesh=mesh,
        in_specs=(tokens,) * 3 + (P(),) * 4 + (owned,) * 14,
        out_specs=(tokens,) * 2 + (P(),) * 2 + (owned,) * 14,
        check_vma=False,
    )
```

```python
import functools

import jax
import jax.numpy as jnp
from jax import lax
from jax.experimental import pallas as pl
from jax.experimental.pallas import tpu as pltpu
from jax.sharding import PartitionSpec as P

HEADS = 16
KV_HEADS = 8
HEAD_DIM = 128
NS_STEPS = 5

EPSILON = 1e-06
ROPE_BASE = 1000000.0
MOMENTUM = 0.95
LEARN_RATE = 0.8
WEIGHT_DECAY = 0.01
NEWTON_A = 3.4445
NEWTON_B = -4.775
NEWTON_C = 2.0315

BF16 = jnp.bfloat16
F32 = jnp.float32
MESH = pl.DeviceIdType.MESH
ANY = pl.BlockSpec(memory_space=pltpu.HBM)

QKV, OUT, GU, DOWN = range(4)


def segments(lengths, row_count):
    seq_ends = jnp.cumsum(lengths)
    seq_starts = seq_ends - lengths
    row_ids = jnp.arange(row_count, dtype=jnp.int32)
    segment_ids = jnp.sum((row_ids[:, None] >= seq_ends[None, :]).astype(jnp.int32), 1)
    slot_ids = jnp.arange(lengths.shape[0], dtype=jnp.int32)
    row_starts = jnp.sum(
        jnp.where(segment_ids[:, None] == slot_ids[None, :], seq_starts[None, :], 0), 1
    )
    return (segment_ids, row_ids - row_starts)


def rope_tables(positions):
    inverse = ROPE_BASE ** (-jnp.arange(0, HEAD_DIM, 2, dtype=jnp.float32) / HEAD_DIM)
    angles = positions.astype(jnp.float32)[:, None] * inverse[None, :]
    return (jnp.cos(angles)[:, None, :], jnp.sin(angles)[:, None, :])


class Place:
    def __init__(self, n):
        self.n = n
        self.rep = lax.axis_index("rep")
        self.own = lax.axis_index("own")
        self.x = self.rep // 2
        self.core = self.rep % 2
        odd, pair = self.own % 2, self.own // 2
        self.ring = pair * (1 - odd) + odd * (n - 1 - pair)

    def own_at(self, ring):
        odd = ring // (self.n // 2)
        return 2 * (ring * (1 - odd) + odd * (self.n - 1 - ring)) + odd

    def shard(self, distance):
        return self.own_at(lax.rem(self.ring + distance + self.n, self.n))

    def ring_neighbour(self, way):
        return (self.rep, self.shard(way))

    @property
    def core_partner(self):
        return (self.x * 2 + 1 - self.core, self.own)

    @property
    def x_partner(self):
        return ((1 - self.x) * 2 + self.core, self.own)


def greet(devices):
    barrier = pltpu.get_barrier_semaphore()
    for device in devices:
        pl.semaphore_signal(barrier, inc=1, device_id=device, device_id_type=MESH)
    pl.semaphore_wait(barrier, len(devices))


class Several:
    def __init__(self, whole, copies):
        self.whole = whole
        self.copies = copies

    def start(self):
        for copy in self.copies:
            copy().start()

    def wait_send(self):
        self.whole().wait_send()

    def wait_recv(self):
        self.whole().wait_recv()


def remote(src, dst, send, recv, device):
    return pltpu.make_async_remote_copy(
        src_ref=src, dst_ref=dst, send_sem=send, recv_sem=recv, device_id=device, device_id_type=MESH
    )


def hops(n, way, kind):
    return n // 2 if (way == 0) == (kind == 0) else n // 2 - 1


SPREADS = ((QKV, True), (OUT, False), (GU, True), (DOWN, False))


def layer_kernel(n, tokens, unit, *refs):
    (
        x_ref, back_ref, table_ref, attention_gain, feed_gain, query_gain, key_gain,
    ) = refs[:7]
    shards = refs[7:11]
    output, input_grad, grad_attention, grad_feed, grad_query_gain, grad_key_gain = refs[11:17]
    grads = refs[17:21]
    (
        w_qkv, w_out, w_gu, w_down, normed, raw, low, probs, context, hidden, out_low, attended,
        grad_context, activated, gu_back, part, sent, got, middle, tables, stage, turned_left, gain_sums,
        local, ring_send, ring_recv, x_send, x_recv, swap_send, swap_recv, stage_sem,
    ) = refs[21:]
    weights = (w_qkv, w_out, w_gu, w_down)
    place = Place(n)
    top = n // 2
    cw, ccw = place.ring_neighbour(1), place.ring_neighbour(-1)
    ways = ((1, cw), (-1, ccw))
    greet([cw, ccw, place.core_partner, place.x_partner])
    both = 2 * tokens
    mine = pl.multiple_of(place.core * tokens, tokens)
    theirs = pl.multiple_of((1 - place.core) * tokens, tokens)
    my_rows, their_rows = pl.ds(mine, tokens), pl.ds(theirs, tokens)
    chunk = unit // 2
    ff = 3 * unit // 2
    few = 32
    base = unit // n
    heads = unit // HEAD_DIM
    kv_heads = heads // 2
    scale = HEAD_DIM ** (-0.5)

    def holds(which, own_index, act):
        if SPREADS[which][1]:
            act()
        else:
            pl.when(own_index // top == place.core)(act)

    def region(which, own_index, x):
        array, split = SPREADS[which]
        height = shards[which].shape[0]
        if split:
            width = weights[which].shape[1] // 2
            start = pl.multiple_of(own_index * height, height)
            return weights[which].at[pl.ds(start, height), pl.ds(pl.multiple_of(x * width, width), width)]
        start = pl.multiple_of(lax.rem(own_index, top) * height, height)
        return weights[which].at[pl.ds(start, height)]

    def own_copy(which):
        height = shards[which].shape[0]
        index = place.own if SPREADS[which][1] else lax.rem(place.own, top)
        start = pl.multiple_of(index * height, height)
        return pltpu.make_async_copy(
            shards[which], weights[which].at[pl.ds(start, height)], local.at[which]
        )

    def reach(which, way):
        return hops(n, way, 0 if SPREADS[which][1] else 1)

    def ring_copy(which, way, hop, act):
        step, target = ways[way]
        own_index = place.shard(-step * (hop if act == "wait_recv" else hop - 1))
        spot = region(which, own_index, place.x)
        index = (which * 2 + way) * top + hop - 1

        def do():
            copy = remote(spot, spot, ring_send.at[index], ring_recv.at[index], target)
            getattr(copy, act)()

        holds(which, own_index, do)

    def send_on(which, way, hop):
        ring_copy(which, way, hop, "start")

    def x_copy(which, way, hop, x):
        spot = region(which, place.shard(-ways[way][0] * hop), x)
        index = (which // 2 * 2 + way) * top + hop - 1
        return remote(spot, spot, x_send.at[index], x_recv.at[index], place.x_partner)

    def serve(which, hop):
        for way in range(2):
            if hop > reach(which, way):
                continue
            ring_copy(which, way, hop, "wait_recv")
            if hop < reach(which, way):
                send_on(which, way, hop + 1)
            if SPREADS[which][1]:
                x_copy(which, way, hop, place.x).start()

    def begin(which):
        def act():
            own_copy(which).wait()

        holds(which, place.own, act)
        for way in range(2):
            if reach(which, way) > 0:
                send_on(which, way, 1)

    def take_x(which):
        for way in range(2):
            for hop in range(1, reach(which, way) + 1):
                x_copy(which, way, hop, 1 - place.x).wait_recv()

    def swap(index, src, dst):
        return remote(src, dst, swap_send.at[index], swap_recv.at[index], place.core_partner)

    def rows_swap(index, ref):
        return swap(index, ref.at[my_rows], ref.at[my_rows])

    def part_swap(index, slot):
        return swap(index, sent.at[slot], got.at[slot])

    def loop(size, step, act):
        def body(k, carry):
            act(pl.multiple_of(k * step, step))
            return carry

        lax.fori_loop(0, size // step, body, 0)

    def normalize(source, gain, target):
        def act(k):
            value = source[pl.ds(k, few), :]
            value = value * lax.rsqrt(jnp.mean(value * value, -1, keepdims=True) + EPSILON)
            target[pl.ds(pl.multiple_of(mine + k, few), few), :] = (value * gain[...]).astype(BF16)

        loop(tokens, few, act)

    def normalize_back(k, source, gain, grad):
        value = source[pl.ds(k, few), :]
        inverse = lax.rsqrt(jnp.mean(value * value, -1, keepdims=True) + EPSILON)
        unscaled = value * inverse
        inner = grad * gain[...]
        back = inverse * (inner - unscaled * jnp.mean(inner * unscaled, -1, keepdims=True))
        return back, jnp.sum((grad * unscaled).reshape(few // 8, 8, unit), 0)

    def dot(left, right, across):
        return lax.dot_general(left, right, ((across[0], across[1]), ((), ())), preferred_element_type=F32)

    NN, NT, TN = ((1,), (0,)), ((1,), (1,)), ((0,), (0,))

    def partial_product(index, slot, left, right, across):
        part[...] = dot(left[...], right[...], across)

        def pack(k):
            sent[slot, pl.ds(k, few), :] = part[
                pl.ds(pl.multiple_of(theirs + k, few), few), :
            ].astype(BF16)

        loop(tokens, few, pack)
        part_swap(index, slot).start()

    def whole_rows(k, slot):
        own = part[pl.ds(pl.multiple_of(mine + k, few), few), :]
        return own + got[slot, pl.ds(k, few), :].astype(F32)

    def weight_grad(which, left, right):
        columns = right.shape[1] // unit

        def by_rows(r, carry):
            row = pl.multiple_of(r * chunk, chunk)
            turned_left[...] = left[:, pl.ds(row, chunk)].T

            def by_columns(c, carry):
                column = pl.multiple_of(c * unit, unit)
                index = r * columns + c
                slot = lax.rem(index, 2)

                @pl.when(index >= 2)
                def _():
                    stage_copy(which, slot, row, column, chunk, unit).wait()

                value = dot(turned_left[...], right[:, pl.ds(column, unit)], NN)
                stage[slot] = value.astype(BF16)
                stage_copy(which, slot, row, column, chunk, unit).start()
                return carry

            lax.fori_loop(0, columns, by_columns, 0)
            return carry

        lax.fori_loop(0, left.shape[1] // chunk, by_rows, 0)
        for slot in range(2):
            stage_copy(which, slot, 0, 0, chunk, unit).wait()

    def stage_copy(which, slot, row, column, height, width):
        return pltpu.make_async_copy(
            stage.at[slot], grads[which].at[pl.ds(row, height), pl.ds(column, width)],
            stage_sem.at[slot],
        )

    for which in range(4):
        holds(which, place.own, lambda: own_copy(which).start())
    tables[my_rows, :] = table_ref[...]
    normalize(x_ref, attention_gain, normed)
    rows_swap(0, normed).start()
    rows_swap(1, tables).start()
    begin(0)
    begin(1)

    def round_back(k):
        out_low[pl.ds(pl.multiple_of(mine + k, few), few), :] = back_ref[pl.ds(k, few), :].astype(BF16)

    loop(tokens, few, round_back)
    rows_swap(2, out_low).start()
    gain_sums[...] = jnp.zeros_like(gain_sums)

    late = [(1, top)] if top < 3 else [(1, h) for h in range(3, top + 1)]
    serve(0, 1)
    serve(1, 1)
    begin(2)
    for hop in range(2, top + 1):
        serve(0, hop)
        if (1, hop) not in late:
            serve(1, hop)
        if hop == 2:
            serve(2, 1)
    take_x(0)
    begin(3)
    pending = late + [(2, h) for h in range(2, top)] + [(3, 1), (2, top)]
    pending += [(3, h) for h in range(2, top + 1)]
    for name in (0, 1):
        rows_swap(name, (normed, tables)[name]).wait_recv()

    raw[:, pl.ds(0, unit)] = dot(normed[...], w_qkv[:, pl.ds(0, unit)], NN)
    keys_values = dot(normed[...], w_qkv[:, pl.ds(unit, unit)], NN)
    raw[:, pl.ds(unit, chunk)] = keys_values[:, :chunk]
    low[:, pl.ds(unit + chunk, chunk)] = keys_values[:, chunk:].astype(BF16)
    serve(*pending.pop(0))

    def turned(value, rows):
        return value * tables[rows, pl.ds(0, HEAD_DIM)] + pltpu.roll(
            value, HEAD_DIM // 2, 1
        ) * tables[rows, pl.ds(HEAD_DIM, HEAD_DIM)]

    def turned_back(value, rows):
        return value * tables[rows, pl.ds(0, HEAD_DIM)] - pltpu.roll(
            value, HEAD_DIM // 2, 1
        ) * tables[rows, pl.ds(HEAD_DIM, HEAD_DIM)]

    def head_norm(first, count, gain):
        def act(k):
            for half in range(2):
                rows = pl.ds(half * tokens, tokens)
                columns = pl.ds(pl.multiple_of(first + k, HEAD_DIM), HEAD_DIM)
                value = raw[rows, columns]
                inverse = lax.rsqrt(jnp.mean(value * value, -1, keepdims=True) + EPSILON)
                low[rows, columns] = turned(value * inverse * gain[...], rows).astype(BF16)

        loop(count * HEAD_DIM, HEAD_DIM, act)

    head_norm(0, heads, query_gain)
    if pending:
        serve(*pending.pop(0))
    head_norm(unit, kv_heads, key_gain)

    def spans(k, half):
        queries = [pl.ds(pl.multiple_of((2 * k + g) * HEAD_DIM, HEAD_DIM), HEAD_DIM) for g in range(2)]
        keys = pl.ds(pl.multiple_of(unit + k * HEAD_DIM, HEAD_DIM), HEAD_DIM)
        values = pl.ds(pl.multiple_of(unit + unit // 2 + k * HEAD_DIM, HEAD_DIM), HEAD_DIM)
        return queries, keys, values, pl.ds(half * tokens, tokens)

    def stacked(ref, rows, columns):
        return jnp.concatenate([ref[rows, columns[0]], ref[rows, columns[1]]], 0)

    def attend(k, half):
        queries, keys, values, rows = spans(k, half)
        row_id = lax.broadcasted_iota(jnp.int32, (tokens, tokens), 0)
        column_id = lax.broadcasted_iota(jnp.int32, (tokens, tokens), 1)
        start = tables[rows, pl.ds(2 * HEAD_DIM, HEAD_DIM)][:, :1]
        allowed = (column_id <= row_id) & (column_id.astype(F32) >= start)
        masks = jnp.where(allowed, 0.0, -1e30)
        scores = dot(stacked(low, rows, queries), low[rows, keys], NT) * scale
        scores = scores + jnp.concatenate([masks, masks], 0)
        exponent = jnp.exp(scores - jnp.max(scores, -1, keepdims=True))
        value = exponent / jnp.sum(exponent, -1, keepdims=True)
        probs[k * 2 + half] = value
        result = dot(value.astype(BF16), low[rows, values], NN).astype(BF16)
        for g in range(2):
            context[rows, queries[g]] = result[g * tokens : (g + 1) * tokens]

    for k in range(kv_heads):
        for half in range(2):
            attend(k, half)
        if pending and k % 2 == 0:
            serve(*pending.pop(0))

    while pending and pending[0][0] == 1:
        serve(*pending.pop(0))
    partial_product(3, 0, context, w_out, NN)
    if pending and pending[0][0] == 2:
        serve(*pending.pop(0))
    part_swap(3, 0).wait_recv()

    def add_middle(k):
        middle[pl.ds(k, few), :] = x_ref[pl.ds(k, few), :] + whole_rows(k, 0)

    loop(tokens, few, add_middle)
    normalize(middle, feed_gain, hidden)
    rows_swap(4, hidden).start()
    while pending:
        serve(*pending.pop(0))
    take_x(2)
    rows_swap(4, hidden).wait_recv()
    rows_swap(2, out_low).wait_recv()

    def feed(k):
        span = pl.ds(k, chunk)
        pair = pl.ds(pl.multiple_of(2 * k, unit), unit)
        gate_up = dot(hidden[...], w_gu[:, pair], NN)
        gate, up = gate_up[:, :chunk], gate_up[:, chunk:]
        grad = dot(out_low[...], w_down[span, :], NT)
        sigmoid = 1.0 / (1.0 + jnp.exp(-gate))
        swish = gate * sigmoid
        activated[:, span] = (swish * up).astype(BF16)
        gu_back[:, pl.ds(pl.multiple_of(2 * k, chunk), chunk)] = (
            grad * up * (sigmoid + swish * (1.0 - sigmoid))
        ).astype(BF16)
        gu_back[:, pl.ds(pl.multiple_of(2 * k + chunk, chunk), chunk)] = (grad * swish).astype(BF16)

    loop(ff, chunk, feed)
    part_swap(3, 0).wait_send()
    partial_product(6, 0, gu_back, w_gu, NT)
    weight_grad(3, activated, out_low)
    part_swap(6, 0).wait_recv()

    def middle_back(k):
        back, gain_part = normalize_back(k, middle, feed_gain, whole_rows(k, 0))
        back = back_ref[pl.ds(k, few), :] + back
        input_grad[pl.ds(k, few), :] = back
        attended[pl.ds(pl.multiple_of(mine + k, few), few), :] = back.astype(BF16)
        gain_sums[1] += gain_part

    loop(tokens, few, middle_back)
    rows_swap(7, attended).start()
    partial_product(5, 1, activated, w_down, NN)
    weight_grad(2, hidden, gu_back)
    part_swap(5, 1).wait_recv()

    def add_output(k):
        output[pl.ds(k, few), :] = middle[pl.ds(k, few), :] + whole_rows(k, 1)

    loop(tokens, few, add_output)
    rows_swap(7, attended).wait_recv()

    grad_context[...] = dot(attended[...], w_out[...], NT).astype(BF16)
    weight_grad(1, context, attended)

    def head_back(rows, columns, gain, grad, index):
        value = raw[rows, columns]
        inverse = lax.rsqrt(jnp.mean(value * value, -1, keepdims=True) + EPSILON)
        unscaled = value * inverse
        grad = turned_back(grad, rows)
        gain_sums[index, :, pl.ds(0, HEAD_DIM)] += jnp.sum(
            (grad * unscaled).reshape(tokens // 8, 8, HEAD_DIM), 0
        )
        inner = grad * gain[...]
        back = inverse * (inner - unscaled * jnp.mean(inner * unscaled, -1, keepdims=True))
        low[rows, columns] = back.astype(BF16)

    def attend_back(k, half):
        queries, keys, values, rows = spans(k, half)
        prob = probs[k * 2 + half]
        above = stacked(grad_context, rows, queries)
        query_pair = stacked(low, rows, queries)
        grad_values = dot(prob.astype(BF16), above, TN)
        grad_probs = dot(above, low[rows, values], NT)
        grad_scores = prob * (grad_probs - jnp.sum(prob * grad_probs, -1, keepdims=True))
        grad_scores = grad_scores.astype(BF16)
        grad_queries = dot(grad_scores, low[rows, keys], NN) * scale
        grad_keys = dot(grad_scores, query_pair, TN) * scale
        for g in range(2):
            head_back(rows, queries[g], query_gain, grad_queries[g * tokens : (g + 1) * tokens], 2)
        head_back(rows, keys, key_gain, grad_keys, 3)
        low[rows, values] = grad_values.astype(BF16)

    def back_body(k, carry):
        for half in range(2):
            attend_back(k, half)
        return carry

    lax.fori_loop(0, kv_heads, back_body, 0)

    part_swap(6, 0).wait_send()
    partial_product(8, 0, low, w_qkv, NT)
    weight_grad(0, normed, low)
    part_swap(8, 0).wait_recv()

    def input_back(k):
        back, gain_part = normalize_back(k, x_ref, attention_gain, whole_rows(k, 0))
        input_grad[pl.ds(k, few), :] += back
        gain_sums[0] += gain_part

    loop(tokens, few, input_back)
    grad_attention[...] = jnp.sum(gain_sums[0], 0, keepdims=True)
    grad_feed[...] = jnp.sum(gain_sums[1], 0, keepdims=True)
    grad_query_gain[...] = jnp.sum(gain_sums[2, :, pl.ds(0, HEAD_DIM)], 0, keepdims=True)
    grad_key_gain[...] = jnp.sum(gain_sums[3, :, pl.ds(0, HEAD_DIM)], 0, keepdims=True)

    for index, ref in ((0, normed), (1, tables), (2, out_low), (4, hidden), (7, attended)):
        rows_swap(index, ref).wait_send()
    part_swap(5, 1).wait_send()
    part_swap(8, 0).wait_send()
    for which in range(4):
        for way in range(2):
            for hop in range(1, reach(which, way) + 1):
                ring_copy(which, way, hop, "wait_send")
                if SPREADS[which][1]:
                    x_copy(which, way, hop, place.x).wait_send()


def layer_pass(values, back, table, gains, shards, n):
    tokens, unit = values.shape
    top = n // 2
    dma = pltpu.SemaphoreType.DMA
    vmem = pltpu.VMEM
    both = 2 * tokens
    heads = unit // HEAD_DIM
    in_vmem = pl.BlockSpec(memory_space=pltpu.VMEM)
    row = lambda width: jax.ShapeDtypeStruct((1, width), F32)
    shapes = [(unit, 2 * unit), (unit, unit), (unit, 3 * unit), (3 * unit // 2, unit)]
    results = pl.pallas_call(
        functools.partial(layer_kernel, n, tokens, unit),
        out_shape=[jax.ShapeDtypeStruct((tokens, unit), F32)] * 2
        + [row(unit), row(unit), row(HEAD_DIM), row(HEAD_DIM)]
        + [jax.ShapeDtypeStruct(shape, BF16) for shape in shapes],
        in_specs=[in_vmem] * 7 + [ANY] * 4,
        out_specs=[in_vmem] * 6 + [ANY] * 4,
        scratch_shapes=[vmem(shape, BF16) for shape in shapes]
        + [
            vmem((both, unit), BF16),
            vmem((both, 3 * unit // 2), F32),
            vmem((both, 2 * unit), BF16),
            vmem((heads, both, tokens), F32),
            vmem((both, unit), BF16),
            vmem((both, unit), BF16),
            vmem((both, unit), BF16),
            vmem((both, unit), BF16),
            vmem((both, unit), BF16),
            vmem((both, 3 * unit // 2), BF16),
            vmem((both, 3 * unit), BF16),
            vmem((both, unit), F32),
            vmem((2, tokens, unit), BF16),
            vmem((2, tokens, unit), BF16),
            vmem((tokens, unit), F32),
            vmem((both, 3 * HEAD_DIM), F32),
            vmem((2, unit // 2, unit), BF16),
            vmem((unit // 2, both), BF16),
            vmem((4, 8, unit), F32),
            dma((4,)),
            dma((8 * top,)),
            dma((8 * top,)),
            dma((4 * top,)),
            dma((4 * top,)),
            dma((9,)),
            dma((9,)),
            dma((2,)),
        ],
        compiler_params=pltpu.CompilerParams(
            collective_id=0, has_side_effects=True, vmem_limit_bytes=56 * 2**20
        ),
    )(values, back, table, *gains, *shards)
    return results[:2], results[2:6], results[6:]


PHASES = ((DOWN, 3, False), (GU, 3, True), (OUT, 2, False), (QKV, 2, True))

OWNERS = (
    (3, 0, 1, False, 1, 2),
    (3, 1, 1, False, 1, 6),
    (3, 0, 2, False, 0, 2),
    (2, 0, 2, True, 1, 5),
    (1, 0, 3, False, 0, 5),
    (1, 0, 3, False, 1, 1),
    (0, 0, 3, True, 0, 1),
)
KEY, VALUE, QUERY, OUTM, GATE, UP, DOWNM = range(7)
RETURNS = (OUTM, KEY, VALUE, DOWNM, GATE, UP, QUERY)
TILE_SLOTS = 3
X_AHEAD = 3


def stage_order(n):
    rings = ((1.0, 1.05), (4.8, 2.65), (23.4, 1.12), (26.6, 1.06))
    crossings = {1: (-6.0, 2.5), 3: (21.5, 1.27)}
    slots = x_slots(n)
    keys, needs = {}, {}
    crossed = []
    for phase in (1, 3):
        for i in range(n):
            first, step = crossings[phase]
            keys["x", phase, i] = first + step * i * 8 / n
            needs["x", phase, i] = [("x", phase, i - 1)] if i else [("x", 1, n - 1)] * (phase == 3)
            if len(crossed) >= slots:
                needs["x", phase, i].append(("ring",) + crossed[len(crossed) - slots])
            crossed.append((phase, i))
    for phase in range(4):
        for i in range(n):
            first, step = rings[phase]
            keys["ring", phase, i] = first + step * i * 8 / n
            needs["ring", phase, i] = [("ring", phase, i - 1)] if i else []
            if phase in crossings:
                needs["ring", phase, i].append(("x", phase, i))
    needs["ring", 2, 0].append(("ring", 1, n - 1))
    for phase, key in ((0, 16.0), (2, 44.0)):
        keys["final", phase, 0] = key
        needs["final", phase, 0] = [("ring", phase, n - 1)]
    needs["ring", 1, n - 1].append(("final", 0, 0))
    left, found = sorted(keys, key=lambda stage: (keys[stage], stage)), []
    while left:
        stage = next(stage for stage in left if all(need in found for need in needs[stage]))
        left.remove(stage)
        found.append(stage)
    return found


def x_slots(n):
    return max(2, 5 * n // 8)


class Rows:
    def __init__(self):
        self.next = 0

    def take(self, rows):
        start = self.next
        self.next += rows
        return start


def layout(n, unit):
    base = unit // n
    top = n // 2
    sums = Rows()

    def shared(take):
        found = [take(PHASES[p][1] * base) for p in (0, 1, 3)]
        return [found[0], found[1], found[0], found[2]]

    place = {
        "own": [sums.take(3 * base) for _ in range(TILE_SLOTS)],
        "x_in": [sums.take(3 * base) for _ in range(x_slots(n))],
        "ring": shared(
            lambda rows: [[sums.take(rows) for _ in range(top)] for _ in range(2)]
        ),
    }
    for name in ("far", "grad", "ahead"):
        place[name] = shared(sums.take)
    for name in ("part", "other"):
        place[name] = [0 if split else sums.take(units * base) for _, units, split in PHASES]
    newton = Rows()
    place["high"] = [newton.take(3 * unit) for _ in range(2)]
    place["poly"] = [newton.take(unit) for _ in range(2)]
    return place, max(sums.next, newton.next)


def update_kernel(n, unit, *refs):
    grads, moments, gains_in = refs[:4], refs[4:11], refs[11]
    outs, orths, lands, gains_out = refs[12:16], refs[16:20], refs[20:24], refs[24]
    (
        pool, exact, gram, squares, gain_mine, gain_core, gain_x, gain_all,
        land_send, land_recv, tile_sem, x_send, x_recv, x_free, ring_send, ring_recv, part_send, part_recv,
        moment_sem, grad_local, grad_send, grad_recv, in_send, in_recv,
        out_send, out_recv, pass_send, pass_recv, gain_send, gain_recv,
    ) = refs[25:]
    place = Place(n)
    base = unit // n
    top = n // 2
    at, _ = layout(n, unit)
    cw, ccw = place.ring_neighbour(1), place.ring_neighbour(-1)
    ways = ((1, cw), (-1, ccw))
    side = [(place.x * 2 + core, lax.rem(place.own + k, n)) for k in range(1, n) for core in range(2)]
    greet(side + [place.core_partner, place.x_partner])
    order = [top]
    for distance in range(top - 1, 0, -1):
        order += [distance, -distance]
    order.append(0)
    stages = stage_order(n)
    slots = x_slots(n)
    moment = exact
    height = [units * base for _, units, _ in PHASES]
    moment_at = [sum(height[:phase]) for phase in range(4)]
    owners = [
        (xs * 2 + 1, place.own_at(spot * n // 8)) for _, _, _, _, xs, spot in OWNERS
    ]
    here = place.rep * n + place.own
    is_owner = [here == rep * n + own for rep, own in owners]

    def rows(start, size):
        if isinstance(start, int):
            return pl.ds(start, size)
        return pl.ds(pl.multiple_of(start, size), size)

    def block(start, size):
        return pool.at[rows(start, size)]

    def pieces_of(phase, x):
        array, units, _ = PHASES[phase]
        half = unit // 2
        found = []
        for core in range(2):
            for b in range(units):
                if array == GU:
                    own_column = b * unit + x * half
                    column = x * 3 * unit + core * (3 * half) + b * half
                else:
                    own_column = x * units * half + b * half
                    column = x * 2 * unit + core * (unit - x * half) + b * (half + x * half)
                found.append((core, b, own_column, column))
        return found

    def columns(start):
        return pl.ds(pl.multiple_of(start, unit // 2), unit // 2)

    def in_block(start, core, b):
        return pool.at[pl.ds(start + b * base, base), pl.ds(core * (unit // 2), unit // 2)]

    def shard_rows(phase, own_index):
        if PHASES[phase][2]:
            return rows(own_index * base, base)
        return rows(lax.rem(own_index, top) * height[phase], height[phase])

    def landing(phase, own_index, act):
        if PHASES[phase][2]:
            act()
        else:
            pl.when(own_index // top == 1)(act)

    def spread(source, target, size, send, recv, device):
        step = size

        def copy(k, count):
            return remote(block(source + k, count), block(target + k, count), send, recv, device)

        return Several(
            functools.partial(copy, 0, size),
            [functools.partial(copy, k, step) for k in range(0, size, step)],
        )

    def land_copy(phase, i, act):
        array = PHASES[phase][0]
        own_index = place.shard(order[i])
        span = shard_rows(phase, own_index)

        def copy(span):
            return remote(
                grads[array].at[span], lands[array].at[span],
                land_send.at[phase * n + i], land_recv.at[phase * n + i], place.core_partner,
            )

        def do():
            getattr(copy(span), act)()

        landing(phase, own_index, do)

    def x_index(phase, i):
        return (phase // 2) * n + i

    def x_copy(phase, i):
        index = x_index(phase, i)
        array = PHASES[phase][0]
        span = shard_rows(phase, place.shard(order[i]))
        target = at["x_in"][index % slots]

        def copy(core, b, column):
            return remote(
                (grads, lands)[core][array].at[span, columns(column)], in_block(target, core, b),
                x_send.at[index], x_recv.at[index], place.x_partner,
            )

        def whole():
            spot = block(target, height[phase])
            return remote(spot, spot, x_send.at[index], x_recv.at[index], place.x_partner)

        return Several(
            whole,
            [
                functools.partial(copy, core, b, column)
                for core, b, column, _ in pieces_of(phase, 1 - place.x)
            ],
        )

    def ring_copy(phase, way, distance, source, part):
        size = height[phase] // 2
        target = at["ring"][phase][way][distance - 1] + part * size
        index = ((phase * 2 + way) * top + distance - 1) * 2 + part
        return spread(
            source + part * size, target, size,
            ring_send.at[index], ring_recv.at[index], ways[way][1],
        )

    def ring_out(phase, distance, part):
        if distance == 0:
            return []
        if distance == top:
            return [ring_copy(phase, part, top, at["far"][phase], part)]
        way = 0 if distance > 0 else 1
        far = abs(distance)
        return [ring_copy(phase, way, far, at["ring"][phase][way][far], part)]

    def part_copy(phase):
        return spread(
            at["part"][phase], at["other"][phase], height[phase],
            part_send.at[phase // 2], part_recv.at[phase // 2], place.x_partner,
        )

    def gain_copy(src, dst, slot, device):
        return remote(src, dst, gain_send.at[slot], gain_recv.at[slot], device)

    def gain_core_copy():
        return gain_copy(gain_mine, gain_core, 0, place.core_partner)

    def gain_x_copy():
        return gain_copy(gain_core, gain_x, 1, place.x_partner)

    def gain_back_copy():
        return gain_copy(gain_mine, gain_x, 2, place.core_partner)

    def gain_ring(way, hop, distance):
        spot = gain_all.at[place.shard(distance)]
        return gain_copy(spot, spot, 3 + way * top + hop - 1, ways[way][1])

    def grad_place(phase, x):
        array = PHASES[phase][0]
        start = at["grad"][phase]
        if not PHASES[phase][2]:
            return [(outs[array], block(start, height[phase]))]
        return [
            (outs[array].at[:, columns(column)], in_block(start, core, b))
            for core, b, _, column in pieces_of(phase, x)
        ]

    def grad_span(phase, x):
        array, units, split = PHASES[phase]
        if not split:
            return outs[array]
        first = pl.multiple_of(x * units * unit, unit)
        return outs[array].at[:, pl.ds(first, units * unit)]

    def grad_sent(phase, to, device, x):
        span = grad_span(phase, x)
        return remote(span, span, grad_send.at[phase, to], grad_recv.at[phase, to], device)

    def matrix_rows(matrix, own_index):
        phase, first, units, tall, _, _ = OWNERS[matrix]
        if tall:
            return [(0, own_index * units * base, units * base)]
        return [
            ((first + k) * base, k * unit + own_index * base, base) for k in range(units)
        ]

    def matrix_span(matrix):
        phase, first, units, tall, xs, _ = OWNERS[matrix]
        array = PHASES[phase][0]
        if tall:
            return orths[array]
        start = (xs * PHASES[phase][1] + first) * unit
        return orths[array].at[:, pl.ds(start, units * unit)]

    def answer_parts(matrix, final, own_index):
        phase, first, units, tall, xs, _ = OWNERS[matrix]
        array = PHASES[phase][0]
        if tall:
            return [(block(final + own_index * units * base, units * base), orths[array])]
        return [
            (
                pool.at[
                    rows(final + (b - first) * unit + own_index * base, base),
                    pl.ds(core * (unit // 2), unit // 2),
                ],
                orths[array].at[:, columns(column)],
            )
            for core, b, _, column in pieces_of(phase, xs)
            if first <= b < first + units
        ]

    def handed(matrix, to, device):
        span = matrix_span(matrix)
        return remote(span, span, pass_send.at[matrix, to], pass_recv.at[matrix, to], device)

    def answered(matrix, target):
        span = matrix_span(matrix)
        return remote(
            span, span, out_send.at[target], out_recv.at[matrix], (place.x * 2, target)
        )

    def summed(pieces, size, store):
        step = 16
        steps = 4 if size % (4 * step) == 0 else 1

        def body(k, carry):
            for j in range(steps):
                shift = (k * steps + j) * step
                total = None
                for start in pieces:
                    value = pool[rows_at(start, shift, step), :].astype(F32)
                    total = value if total is None else total + value
                store(shift, step, total)
            return carry

        lax.fori_loop(0, size // (step * steps), body, 0)

    def rows_at(start, shift, step):
        return pl.ds(pl.multiple_of(start + shift, step), step)

    def keep(start):
        def store(shift, step, total):
            pool[rows_at(start, shift, step), :] = total.astype(BF16)

        return store

    def load_tile(k):
        _, phase, i = stages[k]
        array, _, split = PHASES[phase]
        slot = k_slot[k]
        own_index = place.shard(order[i])
        span = shard_rows(phase, own_index)

        def load(source, target):
            pltpu.make_async_copy(source, target, tile_sem.at[slot]).start()

        if split:
            for core, b, column, _ in pieces_of(phase, place.x):
                load(
                    (grads, lands)[core][array].at[span, columns(column)],
                    in_block(at["own"][slot], core, b),
                )
            return
        for core in range(2):

            @pl.when(own_index // top == core)
            def _():
                load((grads, lands)[core][array].at[span], block(at["own"][slot], height[phase]))

    tiled = [k for k, stage in enumerate(stages) if stage[0] == "ring"]
    k_slot = {k: index % TILE_SLOTS for index, k in enumerate(tiled)}
    seen = set()

    def landed(phase, i):
        if (phase, i) not in seen:
            seen.add((phase, i))
            land_copy(phase, i, "wait_recv")

    def prefetch(index):
        if index >= len(tiled):
            return
        k = tiled[index]
        landed(*stages[k][1:])
        load_tile(k)

    def wait_tile(k):
        span = block(at["own"][k_slot[k]], height[stages[k][1]])
        pltpu.make_async_copy(span, span, tile_sem.at[k_slot[k]]).wait()

    def moment_copies(phase, act):
        array, units, split = PHASES[phase]
        if not split:
            act(moments[3 if array == OUT else 6], moment.at[pl.ds(moment_at[phase], height[phase])])
            return
        half = unit // 2
        for x in range(2):

            @pl.when(place.x == x)
            def _():
                for core, b, _, column in pieces_of(phase, x):
                    if array == GU:
                        source, first = 4 + x, x * 3 * unit
                    elif x == 0:
                        source, first = 0, 0
                    else:
                        source, first = 1 + b, (2 + b) * unit
                    act(
                        moments[source].at[:, pl.ds(column - first, half)],
                        moment.at[pl.ds(moment_at[phase] + b * base, base), pl.ds(core * half, half)],
                    )

    def load_moment(phase):
        moment_copies(
            phase, lambda src, dst: pltpu.make_async_copy(src, dst, moment_sem.at[phase]).start()
        )

    def finish(phase, pieces):
        span = moment.at[pl.ds(moment_at[phase], height[phase])]
        pltpu.make_async_copy(span, span, moment_sem.at[phase]).wait()

        if phase == 2:
            settle(0)

        def store(shift, step, total):
            pool[rows_at(at["grad"][phase], shift, step), :] = total.astype(BF16)
            ahead = (1.0 + MOMENTUM) * total + MOMENTUM**2 * moment[
                rows_at(moment_at[phase], shift, step), :
            ]
            pool[rows_at(at["ahead"][phase], shift, step), :] = ahead.astype(BF16)

        summed(pieces, height[phase], store)
        for matrix, (its_phase, _, _, _, xs, _) in enumerate(OWNERS):
            if its_phase != phase:
                continue

            @pl.when(place.x == xs)
            def _():
                for source, target, size in matrix_rows(matrix, place.own):
                    remote(
                        block(at["ahead"][phase] + source, size), block(at["high"][1] + target, size),
                        in_send.at[matrix], in_recv.at[place.own], owners[matrix],
                    ).start()

        for target, source in grad_place(phase, place.x):
            pltpu.make_async_copy(source, target, grad_local.at[phase]).start()
            remote(
                source, target, grad_send.at[phase, 0], grad_recv.at[phase, 0], place.core_partner
            ).start()
            if PHASES[phase][2]:
                remote(
                    source, target, grad_send.at[phase, 1], grad_recv.at[phase, 1], place.x_partner
                ).start()

    def settle(phase):
        span = block(at["grad"][phase], height[phase])
        pltpu.make_async_copy(span, span, grad_local.at[phase]).wait()
        remote(
            span, span, grad_send.at[phase, 0], grad_recv.at[phase, 0], place.core_partner
        ).wait_send()
        if PHASES[phase][2]:
            remote(
                span, span, grad_send.at[phase, 1], grad_recv.at[phase, 1], place.x_partner
            ).wait_send()
        for matrix, (its_phase, _, units, _, xs, _) in enumerate(OWNERS):
            if its_phase != phase:
                continue

            @pl.when(place.x == xs)
            def _():
                span = block(at["high"][1], units * base)
                remote(
                    span, span, in_send.at[matrix], in_recv.at[0], place.core_partner
                ).wait_send()

    def stage_x(phase, i):
        landed(phase, i)
        index = x_index(phase, i)
        if index >= X_AHEAD:
            before = index - X_AHEAD
            x_copy(1 if before < n else 3, before % n).wait_send()
        if index >= slots:
            pl.semaphore_wait(x_free, 1)
        x_copy(phase, i).start()

    def stage_ring(k, phase, i):
        distance = order[i]
        wait_tile(k)
        pieces = [at["own"][k_slot[k]]]
        if PHASES[phase][2]:
            x_copy(phase, i).wait_recv()
            pieces.append(at["x_in"][x_index(phase, i) % slots])
        size = height[phase]
        mid = size // 2
        if abs(distance) == 1 and phase == 1:
            ring_sent(0)
        if distance == 0:
            for way in range(2):
                held = at["ring"][phase][way][0]
                for part in range(2):
                    ring_copy(phase, way, 1, held, part).wait_recv()
                pieces.append(held)
            if PHASES[phase][2]:
                finish(phase, pieces)
            else:
                summed(pieces, size, keep(at["part"][phase]))
                part_copy(phase).start()
        else:
            way = 0 if distance > 0 else 1
            far = abs(distance)
            held = at["far"][phase] if far == top else at["ring"][phase][way][far]
            for part in (1 - way, way):
                starts = [start + part * mid for start in pieces]
                if far + 1 < top or (far + 1 == top and part == way):
                    ring_copy(phase, way, far + 1, held, part).wait_recv()
                    starts.append(held + part * mid)
                summed(starts, mid, keep(held + part * mid))
                for copy in ring_out(phase, distance, part):
                    copy.start()
        if PHASES[phase][2] and x_index(phase, i) < 2 * n - slots:
            pl.semaphore_signal(x_free, inc=1, device_id=place.x_partner, device_id_type=MESH)

    def ring_sent(phase):
        if phase not in ring_waited:
            ring_waited.add(phase)
            for distance in order:
                for part in range(2):
                    for copy in ring_out(phase, distance, part):
                        copy.wait_send()

    ring_waited = set()

    def gain_stage(hop):
        if hop == 0:
            gain_core_copy().wait_recv()
            gain_core[...] = gain_mine[...] + gain_core[...]
            gain_x_copy().start()
            return
        if hop == 1:
            gain_x_copy().wait_recv()
            gain_all[place.own] = gain_core[...] + gain_x[...]
            for way in range(2):
                gain_ring(way, 1, 0).start()
        for way in range(2):
            if 1 < hop <= hops(n, way, 0) + 1:
                distance = -ways[way][0] * (hop - 1)
                gain_ring(way, hop - 1, distance).wait_recv()
                if hop <= hops(n, way, 0):
                    gain_ring(way, hop, distance).start()

    gain_mine[...] = gains_in[...]

    @pl.when(place.core == 0)
    def _():
        for phase in range(4):
            load_moment(phase)
        for index in range(TILE_SLOTS - 1):
            prefetch(index)
        done = 0
        hop = 0
        for k, (kind, phase, i) in enumerate(stages):
            if kind == "final":
                part_copy(phase).wait_recv()
                finish(phase, [at["part"][phase], at["other"][phase]])
                continue
            if kind == "x":
                stage_x(phase, i)
                continue
            prefetch(done + TILE_SLOTS - 1)
            done += 1
            stage_ring(k, phase, i)
            if done % 2 == 0 and hop <= top + 1:
                gain_stage(hop)
                hop += 1

        total = gain_all[0]
        for k in range(1, n):
            total = total + gain_all[k]
        gains_out[...] = total
        gain_mine[...] = total
        gain_back_copy().start()

        for phase in (1, 3):
            grad_sent(phase, 1, place.x_partner, 1 - place.x).wait_recv()
            grad_sent(phase, 2, place.core_partner, 1 - place.x).start()

        for matrix in RETURNS:
            xs = OWNERS[matrix][4]

            @pl.when(place.x == xs)
            def _():
                answered(matrix, place.own).wait_recv()
                handed(matrix, 0, place.x_partner).start()
                handed(matrix, 1, place.core_partner).start()

            @pl.when(place.x != xs)
            def _():
                handed(matrix, 0, place.x_partner).wait_recv()
                handed(matrix, 1, place.core_partner).start()

        for matrix, (phase, _, units, _, xs, _) in enumerate(OWNERS):
            handed(matrix, 1, place.core_partner).wait_send()

            @pl.when(place.x == xs)
            def _():
                handed(matrix, 0, place.x_partner).wait_send()

        for phase, (_, _, split) in enumerate(PHASES):
            if phase != 0:
                settle(phase)
            if split:
                grad_sent(phase, 2, place.core_partner, 1 - place.x).wait_send()
            else:
                part_copy(phase).wait_send()
            ring_sent(phase)
        for index in range(2 * n - X_AHEAD, 2 * n):
            x_copy(1 if index < n else 3, index % n).wait_send()
        gain_x_copy().wait_send()
        gain_back_copy().wait_send()
        for way in range(2):
            for h in range(1, hops(n, way, 0) + 1):
                gain_ring(way, h, -ways[way][0] * (h - 1)).wait_send()

    @pl.when(place.core == 1)
    def _():
        gain_core_copy().start()
        needed = []
        for kind, phase, i in stages:
            if kind != "final" and (phase, i) not in needed:
                needed.append((phase, i))
        ahead = 8
        for index, (phase, i) in enumerate(needed):
            if index >= ahead:
                land_copy(*needed[index - ahead], "wait_send")
            land_copy(phase, i, "start")
        for phase, i in needed[-ahead:]:
            land_copy(phase, i, "wait_send")
        newton_part(n, unit, place, pool, exact, gram, squares, at, is_owner, in_recv)
        for matrix, (_, _, units, tall, _, _) in enumerate(OWNERS):

            @pl.when(is_owner[matrix])
            def _():
                final = at["high"][1 - NS_STEPS % 2 if tall else NS_STEPS % 2]

                def send(k, carry):
                    target = lax.rem(place.own + k, n)
                    for source, part in answer_parts(matrix, final, target):
                        remote(
                            source, part, out_send.at[target], out_recv.at[matrix],
                            (place.x * 2, target),
                        ).start()
                    return carry

                lax.fori_loop(0, n, send, 0)

                def sent(k, carry):
                    answered(matrix, lax.rem(place.own + k, n)).wait_send()
                    return carry

                lax.fori_loop(0, n, sent, 0)

        gain_core_copy().wait_send()
        gain_back_copy().wait_recv()
        gains_out[...] = gain_x[...]
        for phase, (_, _, split) in enumerate(PHASES):
            grad_sent(phase, 0, place.core_partner, place.x).wait_recv()
            if split:
                grad_sent(phase, 2, place.core_partner, 1 - place.x).wait_recv()
        for matrix in RETURNS:
            handed(matrix, 1, place.core_partner).wait_recv()


def newton_part(n, unit, place, pool, exact, gram, squares, at, is_owner, in_recv):
    base = unit // n
    small = min(256, unit // 2)
    per = unit // small
    wide = unit // 2
    few = 32
    count, tall = 0, 0
    for mine, (_, _, units, lies_tall, _, _) in zip(is_owner, OWNERS):
        count = count + units * mine.astype(jnp.int32)
        tall = tall + int(lies_tall) * mine.astype(jnp.int32)
    high, poly = at["high"], at["poly"]

    def rows(start, size):
        return pl.ds(pl.multiple_of(start, size), size)

    for matrix, (_, _, units, *_) in enumerate(OWNERS):

        @pl.when(is_owner[matrix])
        def _():
            span = pool.at[pl.ds(high[1], units * base)]
            for own_index in range(n):
                remote(
                    span, span, in_recv.at[own_index], in_recv.at[own_index], place.core_partner
                ).wait_recv()

    @pl.when(count > 0)
    def _():
        squares[...] = jnp.zeros_like(squares)

        def square(k, carry):
            part = pool[rows(high[1] + k * few, few), :].astype(F32)
            squares[...] += jnp.sum((part * part).reshape(few // 8, 8, unit), 0)
            return carry

        lax.fori_loop(0, count * (unit // few), square, 0)
        total = jnp.sum(jnp.sum(squares[...], 1, keepdims=True), 0, keepdims=True)
        inverse = 1.0 / (jnp.sqrt(total) + 1e-07)

        @pl.when(tall == 0)
        def _():
            def scale(k, carry):
                value = pool[rows(high[1] + k * few, few), :].astype(F32) * inverse
                exact[rows(k * few, few), :] = value
                pool[rows(high[0] + k * few, few), :] = value.astype(BF16)
                return carry

            lax.fori_loop(0, count * (unit // few), scale, 0)

        @pl.when(tall == 1)
        def _():
            def scale(k, carry):
                block, row = k // per, k % per
                for column in range(per):
                    part = pool[
                        rows(high[1] + k * small, small), pl.ds(column * small, small)
                    ].astype(F32)
                    value = (part * inverse).T
                    shift = block * unit + column * small
                    columns = rows(row * small, small)
                    exact[rows(shift, small), columns] = value
                    pool[rows(high[0] + shift, small), columns] = value.astype(BF16)
                return carry

            lax.fori_loop(0, count * per, scale, 0)

        def newton(step, carry):
            even = step % 2
            now = high[0] + even * (high[1] - high[0])
            later = high[1] - even * (high[1] - high[0])

            def grams(i, carry):
                def product(block):
                    left = pool[rows(now + block * unit + i * wide, wide), :]
                    right = pool[rows(now + block * unit, unit), :]
                    return lax.dot_general(
                        left, right, (((1,), (1,)), ((), ())), preferred_element_type=F32
                    )

                gram[...] = product(0)

                def more(block, carry):
                    gram[...] += product(block)
                    return carry

                lax.fori_loop(1, count, more, 0)
                pool[rows(poly[0] + i * wide, wide), :] = gram[...].astype(BF16)
                return carry

            lax.fori_loop(0, 2, grams, 0)

            def polynomial(i, carry):
                part = pool[rows(poly[0] + i * wide, wide), :]
                squared = jnp.dot(part, pool[pl.ds(poly[0], unit), :], preferred_element_type=F32)
                value = NEWTON_B * part.astype(F32) + NEWTON_C * squared
                pool[rows(poly[1] + i * wide, wide), :] = value.astype(BF16)
                return carry

            lax.fori_loop(0, 2, polynomial, 0)

            def advance(k, carry):
                block, i = k // 2, k % 2
                value = NEWTON_A * exact[rows(k * wide, wide), :] + jnp.dot(
                    pool[rows(poly[1] + i * wide, wide), :],
                    pool[rows(now + block * unit, unit), :],
                    preferred_element_type=F32,
                )
                exact[rows(k * wide, wide), :] = value
                pool[rows(later + k * wide, wide), :] = value.astype(BF16)
                return carry

            lax.fori_loop(0, 2 * count, advance, 0)
            return carry

        lax.fori_loop(0, NS_STEPS, newton, 0)

        @pl.when(tall == 1)
        def _():
            free = high[1 - NS_STEPS % 2]
            factor = jnp.sqrt(jnp.full((1, 1), count, jnp.int32).astype(F32))

            def lay(k, carry):
                block, row = k // per, k % per
                for column in range(per):
                    columns = pl.ds(column * small, small)
                    part = exact[rows(k * small, small), columns]
                    pool[
                        rows(free + block * unit + column * small, small), rows(row * small, small)
                    ] = (part * factor).T.astype(BF16)
                return carry

            lax.fori_loop(0, count * per, lay, 0)


def update_all(grads, moments, gains, n, unit):
    top = n // 2
    dma = pltpu.SemaphoreType.DMA
    vmem = pltpu.VMEM
    _, pool_rows = layout(n, unit)
    shapes = [(unit // n, 4 * unit), (2 * unit // n, unit), (unit // n, 6 * unit), (3 * unit // n, unit)]
    own = [jax.ShapeDtypeStruct(shape, BF16) for shape in shapes]
    whole = [jax.ShapeDtypeStruct(grad.shape, BF16) for grad in grads]
    in_vmem = pl.BlockSpec(memory_space=pltpu.VMEM)
    results = pl.pallas_call(
        functools.partial(update_kernel, n, unit),
        out_shape=own + own + whole + [jax.ShapeDtypeStruct(gains.shape, F32)],
        in_specs=[ANY] * 11 + [in_vmem],
        out_specs=[ANY] * 12 + [in_vmem],
        scratch_shapes=[
            vmem((pool_rows, unit), BF16),
            vmem((3 * unit, unit), F32),
            vmem((unit // 2, unit), F32),
            vmem((8, unit), F32),
            vmem(gains.shape, F32),
            vmem(gains.shape, F32),
            vmem(gains.shape, F32),
            vmem((n,) + gains.shape, F32),
            dma((4 * n,)),
            dma((4 * n,)),
            dma((TILE_SLOTS,)),
            dma((2 * n,)),
            dma((2 * n,)),
            pltpu.SemaphoreType.REGULAR,
            dma((16 * top,)),
            dma((16 * top,)),
            dma((2,)),
            dma((2,)),
            dma((4,)),
            dma((4,)),
            dma((4, 3)),
            dma((4, 3)),
            dma((7,)),
            dma((n,)),
            dma((n,)),
            dma((7,)),
            dma((7, 2)),
            dma((7, 2)),
            dma((3 + 2 * top,)),
            dma((3 + 2 * top,)),
        ],
        compiler_params=pltpu.CompilerParams(
            collective_id=1, has_side_effects=True, vmem_limit_bytes=56 * 2**20
        ),
    )(*grads, *moments, gains)
    return results[:4], results[4:8], results[12]


def unpacked(arrays, unit):
    qkv, out, gate_up, down = arrays
    return (
        qkv[:, : 2 * unit],
        qkv[:, 2 * unit : 3 * unit],
        qkv[:, 3 * unit :],
        out,
        gate_up[:, : 3 * unit],
        gate_up[:, 3 * unit :],
        down,
    )


def body(
    layer_input,
    output_grad,
    lengths,
    attention_gain,
    feed_gain,
    query_gain,
    key_gain,
    query_weight,
    key_weight,
    value_weight,
    out_weight,
    gate_weight,
    up_weight,
    down_weight,
    query_moment,
    key_moment,
    value_moment,
    out_moment,
    gate_moment,
    up_moment,
    down_moment,
):
    owned = (
        query_weight, key_weight, value_weight, out_weight, gate_weight, up_weight, down_weight,
    )
    moments = (
        query_moment, key_moment, value_moment, out_moment, gate_moment, up_moment, down_moment,
    )
    n = lax.axis_size("own")
    unit = layer_input.shape[1]
    core = lax.axis_index("rep") % 2

    def halves(*matrices):
        parts = []
        for matrix in matrices:
            width = matrix.shape[1] // 2
            parts.append(lax.dynamic_slice_in_dim(matrix, core * width, width, 1))
        return jnp.concatenate(parts, 1).astype(BF16)

    step = unit // 2
    gate_half, up_half = halves(gate_weight), halves(up_weight)
    shards = (
        halves(query_weight, key_weight, value_weight),
        out_weight.astype(BF16),
        jnp.concatenate(
            [part[:, k * step : (k + 1) * step] for k in range(3) for part in (gate_half, up_half)], 1
        ),
        down_weight.astype(BF16),
    )
    row_count = layer_input.shape[0]
    _, positions = segments(lengths[0], row_count)
    cosine_table, sine_table = rope_tables(positions)
    starts = (jnp.arange(row_count, dtype=jnp.int32) - positions).astype(F32)
    table = jnp.concatenate(
        [
            cosine_table[:, 0], cosine_table[:, 0], -sine_table[:, 0], sine_table[:, 0],
            jnp.broadcast_to(starts[:, None], (row_count, HEAD_DIM)),
        ],
        1,
    )
    gain_rows = [gain[None, :] for gain in (attention_gain, feed_gain, query_gain, key_gain)]
    (block_output, input_grad), gain_grads, grads = layer_pass(
        layer_input, output_grad, table, gain_rows, shards, n
    )
    gains = jnp.concatenate([grad[0] for grad in gain_grads])
    gains = jnp.pad(gains, (0, 24 * 128 - gains.shape[0])).reshape(24, 128)
    reduced, orth, gain_sums = update_all(grads, moments, gains, n, unit)
    moments_next = [
        MOMENTUM * moment + part.astype(F32) for moment, part in zip(moments, unpacked(reduced, unit))
    ]
    new_weights = [
        matrix * (1.0 - LEARN_RATE * WEIGHT_DECAY) - LEARN_RATE * part.astype(F32)
        for matrix, part in zip(owned, unpacked(orth, unit))
    ]
    gain_sums = gain_sums.reshape(-1)
    norm_grads = gain_sums[: 2 * unit].reshape(2, unit)
    head_grads = gain_sums[2 * unit : 2 * unit + 2 * HEAD_DIM].reshape(2, HEAD_DIM)
    return (block_output, input_grad, norm_grads, head_grads, *new_weights, *moments_next)


def solution(mesh):
    tokens, owned = P(("rep", "own"), None), P("own", None)
    return jax.shard_map(
        body,
        mesh=mesh,
        in_specs=(tokens,) * 3 + (P(),) * 4 + (owned,) * 14,
        out_specs=(tokens,) * 2 + (P(),) * 2 + (owned,) * 14,
        check_vma=False,
    )
```

```python
import functools

import jax
import jax.numpy as jnp
from jax import lax
from jax.experimental import pallas as pl
from jax.experimental.pallas import tpu as pltpu
from jax.sharding import PartitionSpec as P

HEADS = 16
KV_HEADS = 8
HEAD_DIM = 128
NS_STEPS = 5

EPSILON = 1e-06
ROPE_BASE = 1000000.0
MOMENTUM = 0.95
LEARN_RATE = 0.8
WEIGHT_DECAY = 0.01
NEWTON_A = 3.4445
NEWTON_B = -4.775
NEWTON_C = 2.0315

BF16 = jnp.bfloat16
F32 = jnp.float32
MESH = pl.DeviceIdType.MESH
ANY = pl.BlockSpec(memory_space=pltpu.HBM)

QKV, OUT, GU, DOWN = range(4)


def segments(lengths, row_count):
    seq_ends = jnp.cumsum(lengths)
    seq_starts = seq_ends - lengths
    row_ids = jnp.arange(row_count, dtype=jnp.int32)
    segment_ids = jnp.sum((row_ids[:, None] >= seq_ends[None, :]).astype(jnp.int32), 1)
    slot_ids = jnp.arange(lengths.shape[0], dtype=jnp.int32)
    row_starts = jnp.sum(
        jnp.where(segment_ids[:, None] == slot_ids[None, :], seq_starts[None, :], 0), 1
    )
    return (segment_ids, row_ids - row_starts)


def rope_tables(positions):
    inverse = ROPE_BASE ** (-jnp.arange(0, HEAD_DIM, 2, dtype=jnp.float32) / HEAD_DIM)
    angles = positions.astype(jnp.float32)[:, None] * inverse[None, :]
    return (jnp.cos(angles)[:, None, :], jnp.sin(angles)[:, None, :])


class Place:
    def __init__(self, n):
        self.n = n
        self.rep = lax.axis_index("rep")
        self.own = lax.axis_index("own")
        self.x = self.rep // 2
        self.core = self.rep % 2
        odd, pair = self.own % 2, self.own // 2
        self.ring = pair * (1 - odd) + odd * (n - 1 - pair)

    def own_at(self, ring):
        odd = ring // (self.n // 2)
        return 2 * (ring * (1 - odd) + odd * (self.n - 1 - ring)) + odd

    def shard(self, distance):
        return self.own_at(lax.rem(self.ring + distance + self.n, self.n))

    def ring_neighbour(self, way):
        return (self.rep, self.shard(way))

    @property
    def core_partner(self):
        return (self.x * 2 + 1 - self.core, self.own)

    @property
    def x_partner(self):
        return ((1 - self.x) * 2 + self.core, self.own)


def greet(devices):
    barrier = pltpu.get_barrier_semaphore()
    for device in devices:
        pl.semaphore_signal(barrier, inc=1, device_id=device, device_id_type=MESH)
    pl.semaphore_wait(barrier, len(devices))


class Several:
    def __init__(self, whole, copies):
        self.whole = whole
        self.copies = copies

    def start(self):
        for copy in self.copies:
            copy().start()

    def wait_send(self):
        self.whole().wait_send()

    def wait_recv(self):
        self.whole().wait_recv()


def remote(src, dst, send, recv, device):
    return pltpu.make_async_remote_copy(
        src_ref=src, dst_ref=dst, send_sem=send, recv_sem=recv, device_id=device, device_id_type=MESH
    )


def hops(n, way, kind):
    return n // 2 if (way == 0) == (kind == 0) else n // 2 - 1


SPREADS = ((QKV, True), (OUT, False), (GU, True), (DOWN, False))


def layer_kernel(n, tokens, unit, *refs):
    (
        x_ref, back_ref, table_ref, attention_gain, feed_gain, query_gain, key_gain,
    ) = refs[:7]
    shards = refs[7:11]
    output, input_grad, grad_attention, grad_feed, grad_query_gain, grad_key_gain = refs[11:17]
    grads = refs[17:21]
    (
        w_qkv, w_out, w_gu, w_down, normed, raw, low, probs, context, hidden, out_low, attended,
        grad_context, activated, gu_back, part, sent, got, middle, tables, stage, turned_left, gain_sums,
        local, ring_send, ring_recv, x_send, x_recv, swap_send, swap_recv, stage_sem,
    ) = refs[21:]
    weights = (w_qkv, w_out, w_gu, w_down)
    place = Place(n)
    top = n // 2
    cw, ccw = place.ring_neighbour(1), place.ring_neighbour(-1)
    ways = ((1, cw), (-1, ccw))
    greet([cw, ccw, place.core_partner, place.x_partner])
    both = 2 * tokens
    mine = pl.multiple_of(place.core * tokens, tokens)
    theirs = pl.multiple_of((1 - place.core) * tokens, tokens)
    my_rows, their_rows = pl.ds(mine, tokens), pl.ds(theirs, tokens)
    chunk = unit // 2
    ff = 3 * unit // 2
    few = 32
    base = unit // n
    heads = unit // HEAD_DIM
    kv_heads = heads // 2
    scale = HEAD_DIM ** (-0.5)

    def holds(which, own_index, act):
        if SPREADS[which][1]:
            act()
        else:
            pl.when(own_index // top == place.core)(act)

    def region(which, own_index, x):
        array, split = SPREADS[which]
        height = shards[which].shape[0]
        if split:
            width = weights[which].shape[1] // 2
            start = pl.multiple_of(own_index * height, height)
            return weights[which].at[pl.ds(start, height), pl.ds(pl.multiple_of(x * width, width), width)]
        start = pl.multiple_of(lax.rem(own_index, top) * height, height)
        return weights[which].at[pl.ds(start, height)]

    def own_copy(which):
        height = shards[which].shape[0]
        index = place.own if SPREADS[which][1] else lax.rem(place.own, top)
        start = pl.multiple_of(index * height, height)
        return pltpu.make_async_copy(
            shards[which], weights[which].at[pl.ds(start, height)], local.at[which]
        )

    def reach(which, way):
        return hops(n, way, 0 if SPREADS[which][1] else 1)

    def ring_copy(which, way, hop, act):
        step, target = ways[way]
        own_index = place.shard(-step * (hop if act == "wait_recv" else hop - 1))
        spot = region(which, own_index, place.x)
        index = (which * 2 + way) * top + hop - 1

        def do():
            copy = remote(spot, spot, ring_send.at[index], ring_recv.at[index], target)
            getattr(copy, act)()

        holds(which, own_index, do)

    def send_on(which, way, hop):
        ring_copy(which, way, hop, "start")

    def x_copy(which, way, hop, x):
        spot = region(which, place.shard(-ways[way][0] * hop), x)
        index = (which // 2 * 2 + way) * top + hop - 1
        return remote(spot, spot, x_send.at[index], x_recv.at[index], place.x_partner)

    def serve(which, hop):
        for way in range(2):
            if hop > reach(which, way):
                continue
            ring_copy(which, way, hop, "wait_recv")
            if hop < reach(which, way):
                send_on(which, way, hop + 1)
            if SPREADS[which][1]:
                x_copy(which, way, hop, place.x).start()

    def begin(which):
        def act():
            own_copy(which).wait()

        holds(which, place.own, act)
        for way in range(2):
            if reach(which, way) > 0:
                send_on(which, way, 1)

    def take_x(which):
        for way in range(2):
            for hop in range(1, reach(which, way) + 1):
                x_copy(which, way, hop, 1 - place.x).wait_recv()

    def swap(index, src, dst):
        return remote(src, dst, swap_send.at[index], swap_recv.at[index], place.core_partner)

    def rows_swap(index, ref):
        return swap(index, ref.at[my_rows], ref.at[my_rows])

    def part_swap(index, slot):
        return swap(index, sent.at[slot], got.at[slot])

    def loop(size, step, act):
        def body(k, carry):
            act(pl.multiple_of(k * step, step))
            return carry

        lax.fori_loop(0, size // step, body, 0)

    def normalize(source, gain, target):
        def act(k):
            value = source[pl.ds(k, few), :]
            value = value * lax.rsqrt(jnp.mean(value * value, -1, keepdims=True) + EPSILON)
            target[pl.ds(pl.multiple_of(mine + k, few), few), :] = (value * gain[...]).astype(BF16)

        loop(tokens, few, act)

    def normalize_back(k, source, gain, grad):
        value = source[pl.ds(k, few), :]
        inverse = lax.rsqrt(jnp.mean(value * value, -1, keepdims=True) + EPSILON)
        unscaled = value * inverse
        inner = grad * gain[...]
        back = inverse * (inner - unscaled * jnp.mean(inner * unscaled, -1, keepdims=True))
        return back, jnp.sum((grad * unscaled).reshape(few // 8, 8, unit), 0)

    def dot(left, right, across):
        return lax.dot_general(left, right, ((across[0], across[1]), ((), ())), preferred_element_type=F32)

    NN, NT, TN = ((1,), (0,)), ((1,), (1,)), ((0,), (0,))

    def partial_product(index, slot, left, right, across):
        part[...] = dot(left[...], right[...], across)

        def pack(k):
            sent[slot, pl.ds(k, few), :] = part[
                pl.ds(pl.multiple_of(theirs + k, few), few), :
            ].astype(BF16)

        loop(tokens, few, pack)
        part_swap(index, slot).start()

    def whole_rows(k, slot):
        own = part[pl.ds(pl.multiple_of(mine + k, few), few), :]
        return own + got[slot, pl.ds(k, few), :].astype(F32)

    def weight_grad(which, left, right):
        columns = right.shape[1] // unit

        def by_rows(r, carry):
            row = pl.multiple_of(r * chunk, chunk)
            turned_left[...] = left[:, pl.ds(row, chunk)].T

            def by_columns(c, carry):
                column = pl.multiple_of(c * unit, unit)
                index = r * columns + c
                slot = lax.rem(index, 2)

                @pl.when(index >= 2)
                def _():
                    stage_copy(which, slot, row, column, chunk, unit).wait()

                value = dot(turned_left[...], right[:, pl.ds(column, unit)], NN)
                stage[slot] = value.astype(BF16)
                stage_copy(which, slot, row, column, chunk, unit).start()
                return carry

            lax.fori_loop(0, columns, by_columns, 0)
            return carry

        lax.fori_loop(0, left.shape[1] // chunk, by_rows, 0)
        for slot in range(2):
            stage_copy(which, slot, 0, 0, chunk, unit).wait()

    def stage_copy(which, slot, row, column, height, width):
        return pltpu.make_async_copy(
            stage.at[slot], grads[which].at[pl.ds(row, height), pl.ds(column, width)],
            stage_sem.at[slot],
        )

    for which in range(4):
        holds(which, place.own, lambda: own_copy(which).start())
    tables[my_rows, :] = table_ref[...]
    normalize(x_ref, attention_gain, normed)
    rows_swap(0, normed).start()
    rows_swap(1, tables).start()
    begin(0)
    begin(1)

    def round_back(k):
        out_low[pl.ds(pl.multiple_of(mine + k, few), few), :] = back_ref[pl.ds(k, few), :].astype(BF16)

    loop(tokens, few, round_back)
    rows_swap(2, out_low).start()
    gain_sums[...] = jnp.zeros_like(gain_sums)

    late = [(1, top)] if top < 3 else [(1, h) for h in range(3, top + 1)]
    serve(0, 1)
    serve(1, 1)
    begin(2)
    for hop in range(2, top + 1):
        serve(0, hop)
        if (1, hop) not in late:
            serve(1, hop)
        if hop == 2:
            serve(2, 1)
    take_x(0)
    begin(3)
    pending = late + [(2, h) for h in range(2, top)] + [(3, 1), (2, top)]
    pending += [(3, h) for h in range(2, top + 1)]
    for name in (0, 1):
        rows_swap(name, (normed, tables)[name]).wait_recv()

    raw[:, pl.ds(0, unit)] = dot(normed[...], w_qkv[:, pl.ds(0, unit)], NN)
    keys_values = dot(normed[...], w_qkv[:, pl.ds(unit, unit)], NN)
    raw[:, pl.ds(unit, chunk)] = keys_values[:, :chunk]
    low[:, pl.ds(unit + chunk, chunk)] = keys_values[:, chunk:].astype(BF16)
    serve(*pending.pop(0))

    def turned(value, rows):
        return value * tables[rows, pl.ds(0, HEAD_DIM)] + pltpu.roll(
            value, HEAD_DIM // 2, 1
        ) * tables[rows, pl.ds(HEAD_DIM, HEAD_DIM)]

    def turned_back(value, rows):
        return value * tables[rows, pl.ds(0, HEAD_DIM)] - pltpu.roll(
            value, HEAD_DIM // 2, 1
        ) * tables[rows, pl.ds(HEAD_DIM, HEAD_DIM)]

    def head_norm(first, count, gain):
        def act(k):
            for half in range(2):
                rows = pl.ds(half * tokens, tokens)
                columns = pl.ds(pl.multiple_of(first + k, HEAD_DIM), HEAD_DIM)
                value = raw[rows, columns]
                inverse = lax.rsqrt(jnp.mean(value * value, -1, keepdims=True) + EPSILON)
                low[rows, columns] = turned(value * inverse * gain[...], rows).astype(BF16)

        loop(count * HEAD_DIM, HEAD_DIM, act)

    head_norm(0, heads, query_gain)
    if pending:
        serve(*pending.pop(0))
    head_norm(unit, kv_heads, key_gain)

    def spans(k, half):
        queries = [pl.ds(pl.multiple_of((2 * k + g) * HEAD_DIM, HEAD_DIM), HEAD_DIM) for g in range(2)]
        keys = pl.ds(pl.multiple_of(unit + k * HEAD_DIM, HEAD_DIM), HEAD_DIM)
        values = pl.ds(pl.multiple_of(unit + unit // 2 + k * HEAD_DIM, HEAD_DIM), HEAD_DIM)
        return queries, keys, values, pl.ds(half * tokens, tokens)

    def stacked(ref, rows, columns):
        return jnp.concatenate([ref[rows, columns[0]], ref[rows, columns[1]]], 0)

    def attend(k, half):
        queries, keys, values, rows = spans(k, half)
        row_id = lax.broadcasted_iota(jnp.int32, (tokens, tokens), 0)
        column_id = lax.broadcasted_iota(jnp.int32, (tokens, tokens), 1)
        start = tables[rows, pl.ds(2 * HEAD_DIM, HEAD_DIM)][:, :1]
        allowed = (column_id <= row_id) & (column_id.astype(F32) >= start)
        masks = jnp.where(allowed, 0.0, -1e30)
        scores = dot(stacked(low, rows, queries), low[rows, keys], NT) * scale
        scores = scores + jnp.concatenate([masks, masks], 0)
        exponent = jnp.exp(scores - jnp.max(scores, -1, keepdims=True))
        value = exponent / jnp.sum(exponent, -1, keepdims=True)
        probs[k * 2 + half] = value
        result = dot(value.astype(BF16), low[rows, values], NN).astype(BF16)
        for g in range(2):
            context[rows, queries[g]] = result[g * tokens : (g + 1) * tokens]

    for k in range(kv_heads):
        for half in range(2):
            attend(k, half)
        if pending and k % 2 == 0:
            serve(*pending.pop(0))

    while pending and pending[0][0] == 1:
        serve(*pending.pop(0))
    partial_product(3, 0, context, w_out, NN)
    if pending and pending[0][0] == 2:
        serve(*pending.pop(0))
    part_swap(3, 0).wait_recv()

    def add_middle(k):
        middle[pl.ds(k, few), :] = x_ref[pl.ds(k, few), :] + whole_rows(k, 0)

    loop(tokens, few, add_middle)
    normalize(middle, feed_gain, hidden)
    rows_swap(4, hidden).start()
    while pending:
        serve(*pending.pop(0))
    take_x(2)
    rows_swap(4, hidden).wait_recv()
    rows_swap(2, out_low).wait_recv()

    def feed(k):
        span = pl.ds(k, chunk)
        pair = pl.ds(pl.multiple_of(2 * k, unit), unit)
        gate_up = dot(hidden[...], w_gu[:, pair], NN)
        gate, up = gate_up[:, :chunk], gate_up[:, chunk:]
        grad = dot(out_low[...], w_down[span, :], NT)
        sigmoid = 1.0 / (1.0 + jnp.exp(-gate))
        swish = gate * sigmoid
        activated[:, span] = (swish * up).astype(BF16)
        gu_back[:, pl.ds(pl.multiple_of(2 * k, chunk), chunk)] = (
            grad * up * (sigmoid + swish * (1.0 - sigmoid))
        ).astype(BF16)
        gu_back[:, pl.ds(pl.multiple_of(2 * k + chunk, chunk), chunk)] = (grad * swish).astype(BF16)

    loop(ff, chunk, feed)
    part_swap(3, 0).wait_send()
    partial_product(6, 0, gu_back, w_gu, NT)
    weight_grad(3, activated, out_low)
    part_swap(6, 0).wait_recv()

    def middle_back(k):
        back, gain_part = normalize_back(k, middle, feed_gain, whole_rows(k, 0))
        back = back_ref[pl.ds(k, few), :] + back
        input_grad[pl.ds(k, few), :] = back
        attended[pl.ds(pl.multiple_of(mine + k, few), few), :] = back.astype(BF16)
        gain_sums[1] += gain_part

    loop(tokens, few, middle_back)
    rows_swap(7, attended).start()
    partial_product(5, 1, activated, w_down, NN)
    weight_grad(2, hidden, gu_back)
    part_swap(5, 1).wait_recv()

    def add_output(k):
        output[pl.ds(k, few), :] = middle[pl.ds(k, few), :] + whole_rows(k, 1)

    loop(tokens, few, add_output)
    rows_swap(7, attended).wait_recv()

    grad_context[...] = dot(attended[...], w_out[...], NT).astype(BF16)
    weight_grad(1, context, attended)

    def head_back(rows, columns, gain, grad, index):
        value = raw[rows, columns]
        inverse = lax.rsqrt(jnp.mean(value * value, -1, keepdims=True) + EPSILON)
        unscaled = value * inverse
        grad = turned_back(grad, rows)
        gain_sums[index, :, pl.ds(0, HEAD_DIM)] += jnp.sum(
            (grad * unscaled).reshape(tokens // 8, 8, HEAD_DIM), 0
        )
        inner = grad * gain[...]
        back = inverse * (inner - unscaled * jnp.mean(inner * unscaled, -1, keepdims=True))
        low[rows, columns] = back.astype(BF16)

    def attend_back(k, half):
        queries, keys, values, rows = spans(k, half)
        prob = probs[k * 2 + half]
        above = stacked(grad_context, rows, queries)
        query_pair = stacked(low, rows, queries)
        grad_values = dot(prob.astype(BF16), above, TN)
        grad_probs = dot(above, low[rows, values], NT)
        grad_scores = prob * (grad_probs - jnp.sum(prob * grad_probs, -1, keepdims=True))
        grad_scores = grad_scores.astype(BF16)
        grad_queries = dot(grad_scores, low[rows, keys], NN) * scale
        grad_keys = dot(grad_scores, query_pair, TN) * scale
        for g in range(2):
            head_back(rows, queries[g], query_gain, grad_queries[g * tokens : (g + 1) * tokens], 2)
        head_back(rows, keys, key_gain, grad_keys, 3)
        low[rows, values] = grad_values.astype(BF16)

    def back_body(k, carry):
        for half in range(2):
            attend_back(k, half)
        return carry

    lax.fori_loop(0, kv_heads, back_body, 0)

    part_swap(6, 0).wait_send()
    partial_product(8, 0, low, w_qkv, NT)
    weight_grad(0, normed, low)
    part_swap(8, 0).wait_recv()

    def input_back(k):
        back, gain_part = normalize_back(k, x_ref, attention_gain, whole_rows(k, 0))
        input_grad[pl.ds(k, few), :] += back
        gain_sums[0] += gain_part

    loop(tokens, few, input_back)
    grad_attention[...] = jnp.sum(gain_sums[0], 0, keepdims=True)
    grad_feed[...] = jnp.sum(gain_sums[1], 0, keepdims=True)
    grad_query_gain[...] = jnp.sum(gain_sums[2, :, pl.ds(0, HEAD_DIM)], 0, keepdims=True)
    grad_key_gain[...] = jnp.sum(gain_sums[3, :, pl.ds(0, HEAD_DIM)], 0, keepdims=True)

    for index, ref in ((0, normed), (1, tables), (2, out_low), (4, hidden), (7, attended)):
        rows_swap(index, ref).wait_send()
    part_swap(5, 1).wait_send()
    part_swap(8, 0).wait_send()
    for which in range(4):
        for way in range(2):
            for hop in range(1, reach(which, way) + 1):
                ring_copy(which, way, hop, "wait_send")
                if SPREADS[which][1]:
                    x_copy(which, way, hop, place.x).wait_send()


def layer_pass(values, back, table, gains, shards, n):
    tokens, unit = values.shape
    top = n // 2
    dma = pltpu.SemaphoreType.DMA
    vmem = pltpu.VMEM
    both = 2 * tokens
    heads = unit // HEAD_DIM
    in_vmem = pl.BlockSpec(memory_space=pltpu.VMEM)
    row = lambda width: jax.ShapeDtypeStruct((1, width), F32)
    shapes = [(unit, 2 * unit), (unit, unit), (unit, 3 * unit), (3 * unit // 2, unit)]
    results = pl.pallas_call(
        functools.partial(layer_kernel, n, tokens, unit),
        out_shape=[jax.ShapeDtypeStruct((tokens, unit), F32)] * 2
        + [row(unit), row(unit), row(HEAD_DIM), row(HEAD_DIM)]
        + [jax.ShapeDtypeStruct(shape, BF16) for shape in shapes],
        in_specs=[in_vmem] * 7 + [ANY] * 4,
        out_specs=[in_vmem] * 6 + [ANY] * 4,
        scratch_shapes=[vmem(shape, BF16) for shape in shapes]
        + [
            vmem((both, unit), BF16),
            vmem((both, 3 * unit // 2), F32),
            vmem((both, 2 * unit), BF16),
            vmem((heads, both, tokens), F32),
            vmem((both, unit), BF16),
            vmem((both, unit), BF16),
            vmem((both, unit), BF16),
            vmem((both, unit), BF16),
            vmem((both, unit), BF16),
            vmem((both, 3 * unit // 2), BF16),
            vmem((both, 3 * unit), BF16),
            vmem((both, unit), F32),
            vmem((2, tokens, unit), BF16),
            vmem((2, tokens, unit), BF16),
            vmem((tokens, unit), F32),
            vmem((both, 3 * HEAD_DIM), F32),
            vmem((2, unit // 2, unit), BF16),
            vmem((unit // 2, both), BF16),
            vmem((4, 8, unit), F32),
            dma((4,)),
            dma((8 * top,)),
            dma((8 * top,)),
            dma((4 * top,)),
            dma((4 * top,)),
            dma((9,)),
            dma((9,)),
            dma((2,)),
        ],
        compiler_params=pltpu.CompilerParams(
            collective_id=0, has_side_effects=True, vmem_limit_bytes=56 * 2**20
        ),
    )(values, back, table, *gains, *shards)
    return results[:2], results[2:6], results[6:]


PHASES = ((DOWN, 3, False), (GU, 3, True), (OUT, 2, False), (QKV, 2, True))

OWNERS = (
    (3, 0, 1, False, 1, 2),
    (3, 1, 1, False, 1, 6),
    (3, 0, 2, False, 0, 2),
    (2, 0, 2, True, 1, 5),
    (1, 0, 3, False, 0, 5),
    (1, 0, 3, False, 1, 1),
    (0, 0, 3, True, 0, 1),
)
KEY, VALUE, QUERY, OUTM, GATE, UP, DOWNM = range(7)
RETURNS = (OUTM, KEY, VALUE, DOWNM, GATE, UP, QUERY)
TILE_SLOTS = 4
X_AHEAD = 4
LAND_AHEAD = 6


def summing_core(phase):
    return 0 if PHASES[phase][2] else 1


def stage_order(n, core):
    rings = ((1.0, 1.5), (4.0, 2.7), (13.0, 1.1), (26.6, 1.7))
    crossings = {1: (-6.0, 2.5), 3: (16.0, 1.5)}
    keys, needs = {}, {}
    for phase in range(4):
        first, step = rings[phase]
        for i in range(n):
            key = first + step * i * 8 / n
            if summing_core(phase) == core:
                keys["ring", phase, i] = key
                needs["ring", phase, i] = [("ring", phase, i - 1)] if i else []
                if phase in crossings:
                    needs["ring", phase, i].append(("x", phase, i))
            else:
                keys["land", phase, i] = key - 6.0
                needs["land", phase, i] = [("land", phase, i - 1)] if i else []
        if phase in crossings:
            first, step = crossings[phase]
            for i in range(n):
                keys["x", phase, i] = first + step * i * 8 / n
                needs["x", phase, i] = [("x", phase, i - 1)] if i else [("x", 1, n - 1)] * (phase == 3)
                if core == 0 and phase == 3:
                    needs["x", phase, i].append(("ring", 1, i))
        elif core == 1:
            keys["final", phase, 0] = {0: 16.0, 2: 27.0}[phase]
            needs["final", phase, 0] = [("ring", phase, n - 1)]
    left, found = sorted(keys, key=lambda stage: (keys[stage], stage)), []
    while left:
        stage = next(stage for stage in left if all(need in found for need in needs[stage]))
        left.remove(stage)
        found.append(stage)
    return found


class Rows:
    def __init__(self):
        self.next = 0

    def take(self, rows):
        start = self.next
        self.next += rows
        return start


def layout(n, unit):
    base = unit // n
    top = n // 2
    place = {}
    rows = (Rows(), Rows())
    place["high"] = [None, rows[1].take(3 * unit)]
    for name in ("grad", "ahead"):
        place[name] = [rows[summing_core(p)].take(PHASES[p][1] * base) for p in range(4)]
    for name in ("part", "other"):
        place[name] = [0 if split else rows[1].take(units * base) for _, units, split in PHASES]
    newton = Rows()
    newton.next = -(-rows[1].next // unit) * unit
    place["high"][0] = newton.take(3 * unit)
    place["poly"] = [newton.take(unit) for _ in range(2)]
    place["x_in"] = [rows[0].take(3 * base) for _ in range(n)]
    place["own"] = [[rows[core].take(3 * base) for _ in range(TILE_SLOTS)] for core in range(2)]
    place["ring"], place["far"] = [], []
    for phase, (_, units, _) in enumerate(PHASES):
        take = rows[summing_core(phase)].take
        place["ring"].append([[take(units * base) for _ in range(top)] for _ in range(2)])
        place["far"].append(take(units * base))
    return place, max(rows[0].next, rows[1].next, newton.next)


def update_kernel(n, unit, *refs):
    grads, moments, gains_in = refs[:4], refs[4:11], refs[11]
    outs, orths, lands, gains_out = refs[12:16], refs[16:20], refs[20:24], refs[24]
    (
        pool, exact, gram, squares, gain_mine, gain_core, gain_x, gain_all,
        land_send, land_recv, tile_sem, x_send, x_recv, x_free, ring_send, ring_recv, part_send, part_recv,
        moment_sem, grad_local, grad_send, grad_recv, in_send, in_recv, in_local,
        out_send, out_recv, pass_send, pass_recv, gain_send, gain_recv,
    ) = refs[25:]
    place = Place(n)
    base = unit // n
    top = n // 2
    at, _ = layout(n, unit)
    cw, ccw = place.ring_neighbour(1), place.ring_neighbour(-1)
    ways = ((1, cw), (-1, ccw))
    side = [(place.x * 2 + core, lax.rem(place.own + k, n)) for k in range(1, n) for core in range(2)]
    across = [((1 - place.x) * 2 + core, place.own) for core in range(2)]
    greet(side + [place.core_partner] + across)
    order = [top]
    for distance in range(top - 1, 0, -1):
        order += [distance, -distance]
    order.append(0)
    moment = exact
    height = [units * base for _, units, _ in PHASES]
    moment_at = [sum(height[:phase]) for phase in range(4)]
    owners = [
        (xs * 2 + 1, place.own_at(spot * n // 8)) for _, _, _, _, xs, spot in OWNERS
    ]
    here = place.rep * n + place.own
    is_owner = [here == rep * n + own for rep, own in owners]

    def rows(start, size):
        if isinstance(start, int):
            return pl.ds(start, size)
        return pl.ds(pl.multiple_of(start, size), size)

    def block(start, size):
        return pool.at[rows(start, size)]

    def pieces_of(phase, x):
        array, units, _ = PHASES[phase]
        half = unit // 2
        found = []
        for core in range(2):
            for b in range(units):
                if array == GU:
                    own_column = b * unit + x * half
                    column = x * 3 * unit + core * (3 * half) + b * half
                else:
                    own_column = x * units * half + b * half
                    column = x * 2 * unit + core * (unit - x * half) + b * (half + x * half)
                found.append((core, b, own_column, column))
        return found

    def columns(start):
        return pl.ds(pl.multiple_of(start, unit // 2), unit // 2)

    def in_block(start, core, b):
        return pool.at[pl.ds(start + b * base, base), pl.ds(core * (unit // 2), unit // 2)]

    def shard_rows(phase, own_index):
        if PHASES[phase][2]:
            return rows(own_index * base, base)
        return rows(lax.rem(own_index, top) * height[phase], height[phase])

    def landing(phase, own_index, act):
        if PHASES[phase][2]:
            act()
        else:
            pl.when(own_index // top != summing_core(phase))(act)

    def spread(source, target, size, send, recv, device):
        step = size

        def copy(k, count):
            return remote(block(source + k, count), block(target + k, count), send, recv, device)

        return Several(
            functools.partial(copy, 0, size),
            [functools.partial(copy, k, step) for k in range(0, size, step)],
        )

    def land_copy(phase, i, act):
        array, units, split = PHASES[phase]
        own_index = place.shard(order[i])
        span = shard_rows(phase, own_index)

        def copy(at_columns):
            return remote(
                grads[array].at[span, at_columns], lands[array].at[span, at_columns],
                land_send.at[phase * n + i], land_recv.at[phase * n + i], place.core_partner,
            )

        def do():
            if not split:
                getattr(copy(pl.ds(0, unit)), act)()
            elif act == "start":
                for core, _, column, _ in pieces_of(phase, place.x):
                    if core == 1:
                        copy(columns(column)).start()
            else:
                getattr(copy(pl.ds(0, units * unit // 2)), act)()

        landing(phase, own_index, do)

    def x_index(phase, i):
        return (phase // 2) * n + i

    def x_copies(phase, i, core, act):
        index = x_index(phase, i)
        array, units, _ = PHASES[phase]
        span = shard_rows(phase, place.shard(order[i]))
        target = at["x_in"][i]

        def copy(source, spot):
            return remote(
                source, spot, x_send.at[index], x_recv.at[core, index], ((1 - place.x) * 2, place.own)
            )

        if act == "start":
            for its_core, b, column, _ in pieces_of(phase, 1 - place.x):
                if its_core == core:
                    copy(grads[array].at[span, columns(column)], in_block(target, core, b)).start()
        else:
            spot = pool.at[pl.ds(target, height[phase]), pl.ds(core * (unit // 2), unit // 2)]
            getattr(copy(spot, spot), act)()

    def ring_copy(phase, way, distance, source, part):
        size = height[phase] // 2
        target = at["ring"][phase][way][distance - 1] + part * size
        index = ((phase * 2 + way) * top + distance - 1) * 2 + part
        return spread(
            source + part * size, target, size,
            ring_send.at[index], ring_recv.at[index], ways[way][1],
        )

    def ring_out(phase, distance, part):
        if distance == 0:
            return []
        if distance == top:
            return [ring_copy(phase, part, top, at["far"][phase], part)]
        way = 0 if distance > 0 else 1
        far = abs(distance)
        return [ring_copy(phase, way, far, at["ring"][phase][way][far], part)]

    def part_copy(phase):
        return spread(
            at["part"][phase], at["other"][phase], height[phase],
            part_send.at[phase // 2], part_recv.at[phase // 2], place.x_partner,
        )

    def gain_copy(src, dst, slot, device):
        return remote(src, dst, gain_send.at[slot], gain_recv.at[slot], device)

    def gain_core_copy():
        return gain_copy(gain_mine, gain_core, 0, place.core_partner)

    def gain_x_copy():
        return gain_copy(gain_core, gain_x, 1, place.x_partner)

    def gain_back_copy():
        return gain_copy(gain_mine, gain_x, 2, place.core_partner)

    def gain_ring(way, hop, distance):
        spot = gain_all.at[place.shard(distance)]
        return gain_copy(spot, spot, 3 + way * top + hop - 1, ways[way][1])

    def grad_place(phase, x):
        array = PHASES[phase][0]
        start = at["grad"][phase]
        if not PHASES[phase][2]:
            return [(outs[array], block(start, height[phase]))]
        return [
            (outs[array].at[:, columns(column)], in_block(start, core, b))
            for core, b, _, column in pieces_of(phase, x)
        ]

    def grad_span(phase, x):
        array, units, split = PHASES[phase]
        if not split:
            return outs[array]
        first = pl.multiple_of(x * units * unit, unit)
        return outs[array].at[:, pl.ds(first, units * unit)]

    def grad_sent(phase, to, device, x):
        span = grad_span(phase, x)
        return remote(span, span, grad_send.at[phase, to], grad_recv.at[phase, to], device)

    def matrix_rows(matrix, own_index):
        phase, first, units, tall, _, _ = OWNERS[matrix]
        if tall:
            return [(0, own_index * units * base, units * base)]
        return [
            ((first + k) * base, k * unit + own_index * base, base) for k in range(units)
        ]

    def matrix_span(matrix):
        phase, first, units, tall, xs, _ = OWNERS[matrix]
        array = PHASES[phase][0]
        if tall:
            return orths[array]
        start = (xs * PHASES[phase][1] + first) * unit
        return orths[array].at[:, pl.ds(start, units * unit)]

    def answer_parts(matrix, final, own_index):
        phase, first, units, tall, xs, _ = OWNERS[matrix]
        array = PHASES[phase][0]
        if tall:
            return [(block(final + own_index * units * base, units * base), orths[array])]
        return [
            (
                pool.at[
                    rows(final + (b - first) * unit + own_index * base, base),
                    pl.ds(core * (unit // 2), unit // 2),
                ],
                orths[array].at[:, columns(column)],
            )
            for core, b, _, column in pieces_of(phase, xs)
            if first <= b < first + units
        ]

    def handed(matrix, to, device):
        span = matrix_span(matrix)
        return remote(span, span, pass_send.at[matrix, to], pass_recv.at[matrix, to], device)

    def answered(matrix, target):
        span = matrix_span(matrix)
        return remote(
            span, span, out_send.at[target], out_recv.at[matrix], (place.x * 2, target)
        )

    def summed(pieces, size, store):
        step = 16
        steps = 4 if size % (4 * step) == 0 else 1

        def body(k, carry):
            for j in range(steps):
                shift = (k * steps + j) * step
                total = None
                for start in pieces:
                    value = pool[rows_at(start, shift, step), :].astype(F32)
                    total = value if total is None else total + value
                store(shift, step, total)
            return carry

        lax.fori_loop(0, size // (step * steps), body, 0)

    def rows_at(start, shift, step):
        return pl.ds(pl.multiple_of(start + shift, step), step)

    def keep(start):
        def store(shift, step, total):
            pool[rows_at(start, shift, step), :] = total.astype(BF16)

        return store

    def load_tile(phase, i, slot):
        array, _, split = PHASES[phase]
        own_index = place.shard(order[i])
        span = shard_rows(phase, own_index)
        summing = summing_core(phase)

        def load(source, target):
            pltpu.make_async_copy(source, target, tile_sem.at[slot]).start()

        if split:
            for core, b, column, _ in pieces_of(phase, place.x):
                load(
                    (grads, lands)[core][array].at[span, columns(column)],
                    in_block(at["own"][summing][slot], core, b),
                )
            return
        for core in range(2):

            @pl.when(own_index // top == core)
            def _():
                load(
                    (lands, grads)[core == summing][array].at[span],
                    block(at["own"][summing][slot], height[phase]),
                )

    def prefetch(rings, index):
        if index < len(rings):
            _, phase, i = rings[index]
            land_copy(phase, i, "wait_recv")
            load_tile(phase, i, index % TILE_SLOTS)

    def moment_copies(phase, act):
        array, units, split = PHASES[phase]
        if not split:
            act(moments[3 if array == OUT else 6], moment.at[pl.ds(moment_at[phase], height[phase])])
            return
        half = unit // 2
        for x in range(2):

            @pl.when(place.x == x)
            def _():
                for core, b, _, column in pieces_of(phase, x):
                    if array == GU:
                        source, first = 4 + x, x * 3 * unit
                    elif x == 0:
                        source, first = 0, 0
                    else:
                        source, first = 1 + b, (2 + b) * unit
                    act(
                        moments[source].at[:, pl.ds(column - first, half)],
                        moment.at[pl.ds(moment_at[phase] + b * base, base), pl.ds(core * half, half)],
                    )

    def load_moment(phase):
        moment_copies(
            phase, lambda src, dst: pltpu.make_async_copy(src, dst, moment_sem.at[phase]).start()
        )

    def finish(phase, pieces):
        span = moment.at[pl.ds(moment_at[phase], height[phase])]
        pltpu.make_async_copy(span, span, moment_sem.at[phase]).wait()

        def store(shift, step, total):
            pool[rows_at(at["grad"][phase], shift, step), :] = total.astype(BF16)
            ahead = (1.0 + MOMENTUM) * total + MOMENTUM**2 * moment[
                rows_at(moment_at[phase], shift, step), :
            ]
            pool[rows_at(at["ahead"][phase], shift, step), :] = ahead.astype(BF16)

        summed(pieces, height[phase], store)
        for matrix, (its_phase, _, _, _, xs, _) in enumerate(OWNERS):
            if its_phase != phase:
                continue

            def hand_in(local):
                for source, target, size in matrix_rows(matrix, place.own):
                    source = block(at["ahead"][phase] + source, size)
                    target = block(at["high"][1] + target, size)
                    if local:
                        pltpu.make_async_copy(source, target, in_local).start()
                    else:
                        remote(
                            source, target, in_send.at[matrix], in_recv.at[place.own], owners[matrix]
                        ).start()

            if summing_core(phase) == 0:
                pl.when(place.x == xs)(functools.partial(hand_in, False))
            else:
                pl.when(is_owner[matrix])(functools.partial(hand_in, True))
                pl.when((place.x == xs) & (here != owners[matrix][0] * n + owners[matrix][1]))(
                    functools.partial(hand_in, False)
                )

        for target, source in grad_place(phase, place.x):
            pltpu.make_async_copy(source, target, grad_local.at[phase]).start()
            remote(
                source, target, grad_send.at[phase, 0], grad_recv.at[phase, 0], place.core_partner
            ).start()
            if PHASES[phase][2]:
                remote(
                    source, target, grad_send.at[phase, 1], grad_recv.at[phase, 1], place.x_partner
                ).start()

    def settle(phase):
        span = block(at["grad"][phase], height[phase])
        pltpu.make_async_copy(span, span, grad_local.at[phase]).wait()
        remote(
            span, span, grad_send.at[phase, 0], grad_recv.at[phase, 0], place.core_partner
        ).wait_send()
        if PHASES[phase][2]:
            remote(
                span, span, grad_send.at[phase, 1], grad_recv.at[phase, 1], place.x_partner
            ).wait_send()
        for matrix, (its_phase, _, units, _, xs, _) in enumerate(OWNERS):
            if its_phase != phase:
                continue

            sends = place.x == xs
            if summing_core(phase) == 1:
                sends = sends & (here != owners[matrix][0] * n + owners[matrix][1])

            @pl.when(sends)
            def _():
                span = block(at["high"][1], units * base)
                remote(
                    span, span, in_send.at[matrix], in_recv.at[0], place.core_partner
                ).wait_send()

    def stage_x(phase, i, core):
        index = x_index(phase, i)
        if index >= X_AHEAD:
            before = index - X_AHEAD
            x_copies(1 if before < n else 3, before % n, core, "wait_send")
        if phase == 3:
            pl.semaphore_wait(x_free, 1)
        x_copies(phase, i, core, "start")

    def stage_ring(phase, i, slot):
        distance = order[i]
        start = at["own"][summing_core(phase)][slot]
        span = block(start, height[phase])
        pltpu.make_async_copy(span, span, tile_sem.at[slot]).wait()
        pieces = [start]
        if PHASES[phase][2]:
            for core in range(2):
                x_copies(phase, i, core, "wait_recv")
            pieces.append(at["x_in"][i])
        size = height[phase]
        mid = size // 2
        if distance == 0:
            for way in range(2):
                held = at["ring"][phase][way][0]
                for part in range(2):
                    ring_copy(phase, way, 1, held, part).wait_recv()
                pieces.append(held)
            if PHASES[phase][2]:
                finish(phase, pieces)
            else:
                summed(pieces, size, keep(at["part"][phase]))
                part_copy(phase).start()
        else:
            way = 0 if distance > 0 else 1
            far = abs(distance)
            held = at["far"][phase] if far == top else at["ring"][phase][way][far]
            for part in (1 - way, way):
                starts = [start + part * mid for start in pieces]
                if far + 1 < top or (far + 1 == top and part == way):
                    ring_copy(phase, way, far + 1, held, part).wait_recv()
                    starts.append(held + part * mid)
                summed(starts, mid, keep(held + part * mid))
                for copy in ring_out(phase, distance, part):
                    copy.start()
        if phase == 1:
            for device in across:
                pl.semaphore_signal(x_free, inc=1, device_id=device, device_id_type=MESH)

    def ring_sent(phase):
        for distance in order:
            for part in range(2):
                for copy in ring_out(phase, distance, part):
                    copy.wait_send()

    def run(core):
        stages = stage_order(n, core)
        rings = [stage for stage in stages if stage[0] == "ring"]
        landed = [stage for stage in stages if stage[0] == "land"]
        for phase in range(4):
            if summing_core(phase) == core:
                load_moment(phase)
        done, sent, hop = 0, 0, 0
        for index in range(LAND_AHEAD):
            land_copy(*landed[index][1:], "start")
        for index in range(TILE_SLOTS - 1):
            prefetch(rings, index)
        for kind, phase, i in stages:
            if kind == "x":
                stage_x(phase, i, core)
            elif kind == "land":
                land_copy(phase, i, "wait_send")
                if sent + LAND_AHEAD < len(landed):
                    land_copy(*landed[sent + LAND_AHEAD][1:], "start")
                sent += 1
            elif kind == "final":
                part_copy(phase).wait_recv()
                finish(phase, [at["part"][phase], at["other"][phase]])
            else:
                prefetch(rings, done + TILE_SLOTS - 1)
                stage_ring(phase, i, done % TILE_SLOTS)
                done += 1
                if core == 0 and hop <= top + 1:
                    gain_stage(hop)
                    hop += 1

    def settle_all(core):
        for phase, (_, _, split) in enumerate(PHASES):
            if summing_core(phase) == core:
                settle(phase)
                if not split:
                    part_copy(phase).wait_send()
        for index in range(2 * n - X_AHEAD, 2 * n):
            x_copies(1 if index < n else 3, index % n, core, "wait_send")

    def take_sums(core):
        for phase, (_, _, split) in enumerate(PHASES):
            if summing_core(phase) != core:
                grad_sent(phase, 0, place.core_partner, place.x).wait_recv()
                if split:
                    grad_sent(phase, 2, place.core_partner, 1 - place.x).wait_recv()

    def gain_stage(hop):
        if hop == 0:
            gain_core_copy().wait_recv()
            gain_core[...] = gain_mine[...] + gain_core[...]
            gain_x_copy().start()
            return
        if hop == 1:
            gain_x_copy().wait_recv()
            gain_all[place.own] = gain_core[...] + gain_x[...]
            for way in range(2):
                gain_ring(way, 1, 0).start()
        for way in range(2):
            if 1 < hop <= hops(n, way, 0) + 1:
                distance = -ways[way][0] * (hop - 1)
                gain_ring(way, hop - 1, distance).wait_recv()
                if hop <= hops(n, way, 0):
                    gain_ring(way, hop, distance).start()

    gain_mine[...] = gains_in[...]

    @pl.when(place.core == 0)
    def _():
        run(0)
        total = gain_all[0]
        for k in range(1, n):
            total = total + gain_all[k]
        gains_out[...] = total
        gain_mine[...] = total
        gain_back_copy().start()

        for phase in (1, 3):
            grad_sent(phase, 1, place.x_partner, 1 - place.x).wait_recv()
            grad_sent(phase, 2, place.core_partner, 1 - place.x).start()

        for matrix in RETURNS:
            xs = OWNERS[matrix][4]

            @pl.when(place.x == xs)
            def _():
                answered(matrix, place.own).wait_recv()
                handed(matrix, 0, place.x_partner).start()
                handed(matrix, 1, place.core_partner).start()

            @pl.when(place.x != xs)
            def _():
                handed(matrix, 0, place.x_partner).wait_recv()
                handed(matrix, 1, place.core_partner).start()

        for matrix, (phase, _, units, _, xs, _) in enumerate(OWNERS):
            handed(matrix, 1, place.core_partner).wait_send()

            @pl.when(place.x == xs)
            def _():
                handed(matrix, 0, place.x_partner).wait_send()

        take_sums(0)
        settle_all(0)
        for phase in (1, 3):
            ring_sent(phase)
            grad_sent(phase, 2, place.core_partner, 1 - place.x).wait_send()
        gain_x_copy().wait_send()
        gain_back_copy().wait_send()
        for way in range(2):
            for h in range(1, hops(n, way, 0) + 1):
                gain_ring(way, h, -ways[way][0] * (h - 1)).wait_send()

    @pl.when(place.core == 1)
    def _():
        gain_core_copy().start()
        run(1)
        for phase in (0, 2):
            ring_sent(phase)
        newton_part(n, unit, place, pool, exact, gram, squares, at, is_owner, in_recv, in_local)
        for matrix, (_, _, units, tall, _, _) in enumerate(OWNERS):

            @pl.when(is_owner[matrix])
            def _():
                final = at["high"][1 - NS_STEPS % 2 if tall else NS_STEPS % 2]

                def send(k, carry):
                    target = lax.rem(place.own + k, n)
                    for source, part in answer_parts(matrix, final, target):
                        remote(
                            source, part, out_send.at[target], out_recv.at[matrix],
                            (place.x * 2, target),
                        ).start()
                    return carry

                lax.fori_loop(0, n, send, 0)

                def sent(k, carry):
                    answered(matrix, lax.rem(place.own + k, n)).wait_send()
                    return carry

                lax.fori_loop(0, n, sent, 0)

        gain_core_copy().wait_send()
        gain_back_copy().wait_recv()
        gains_out[...] = gain_x[...]
        take_sums(1)
        settle_all(1)
        for matrix in RETURNS:
            handed(matrix, 1, place.core_partner).wait_recv()


def newton_part(n, unit, place, pool, exact, gram, squares, at, is_owner, in_recv, in_local):
    base = unit // n
    small = min(256, unit // 2)
    per = unit // small
    wide = unit // 2
    few = 32
    count, tall = 0, 0
    for mine, (_, _, units, lies_tall, _, _) in zip(is_owner, OWNERS):
        count = count + units * mine.astype(jnp.int32)
        tall = tall + int(lies_tall) * mine.astype(jnp.int32)
    high, poly = at["high"], at["poly"]

    def rows(start, size):
        return pl.ds(pl.multiple_of(start, size), size)

    for matrix, (phase, _, units, *_) in enumerate(OWNERS):

        @pl.when(is_owner[matrix])
        def _():
            span = pool.at[pl.ds(high[1], units * base)]
            inside = summing_core(phase) == 1
            if inside:
                pltpu.make_async_copy(span, span, in_local).wait()
            for k in range(1 if inside else 0, n):
                own_index = lax.rem(place.own + k, n)
                remote(
                    span, span, in_recv.at[own_index], in_recv.at[own_index], place.core_partner
                ).wait_recv()

    @pl.when(count > 0)
    def _():
        squares[...] = jnp.zeros_like(squares)

        def square(k, carry):
            part = pool[rows(high[1] + k * few, few), :].astype(F32)
            squares[...] += jnp.sum((part * part).reshape(few // 8, 8, unit), 0)
            return carry

        lax.fori_loop(0, count * (unit // few), square, 0)
        total = jnp.sum(jnp.sum(squares[...], 1, keepdims=True), 0, keepdims=True)
        inverse = 1.0 / (jnp.sqrt(total) + 1e-07)

        @pl.when(tall == 0)
        def _():
            def scale(k, carry):
                value = pool[rows(high[1] + k * few, few), :].astype(F32) * inverse
                exact[rows(k * few, few), :] = value
                pool[rows(high[0] + k * few, few), :] = value.astype(BF16)
                return carry

            lax.fori_loop(0, count * (unit // few), scale, 0)

        @pl.when(tall == 1)
        def _():
            def scale(k, carry):
                block, row = k // per, k % per
                for column in range(per):
                    part = pool[
                        rows(high[1] + k * small, small), pl.ds(column * small, small)
                    ].astype(F32)
                    value = (part * inverse).T
                    shift = block * unit + column * small
                    columns = rows(row * small, small)
                    exact[rows(shift, small), columns] = value
                    pool[rows(high[0] + shift, small), columns] = value.astype(BF16)
                return carry

            lax.fori_loop(0, count * per, scale, 0)

        def newton(step, carry):
            even = step % 2
            now = high[0] + even * (high[1] - high[0])
            later = high[1] - even * (high[1] - high[0])

            def keep_symmetric(to, chunk, value):
                pool[pl.ds(to, (chunk + 1) * wide), pl.ds(chunk * wide, wide)] = value.astype(BF16)
                if chunk == 1:
                    pool[pl.ds(to + wide, wide), pl.ds(0, wide)] = value[:wide].T.astype(BF16)

            for chunk in range(2):
                down = (chunk + 1) * wide

                def product(block):
                    left = pool[pl.ds(pl.multiple_of(now + block * unit, unit), down), :]
                    right = pool[rows(now + block * unit + chunk * wide, wide), :]
                    return lax.dot_general(
                        left, right, (((1,), (1,)), ((), ())), preferred_element_type=F32
                    )

                gram[:down, :] = product(0)

                def more(block, carry):
                    gram[:down, :] += product(block)
                    return carry

                lax.fori_loop(1, count, more, 0)
                keep_symmetric(poly[0], chunk, gram[:down, :])

            for chunk in range(2):
                down = (chunk + 1) * wide
                columns = pl.ds(chunk * wide, wide)
                squared = jnp.dot(
                    pool[pl.ds(poly[0], down), :], pool[pl.ds(poly[0], unit), columns],
                    preferred_element_type=F32,
                )
                plain = pool[pl.ds(poly[0], down), columns].astype(F32)
                keep_symmetric(poly[1], chunk, NEWTON_B * plain + NEWTON_C * squared)

            def advance(block, carry):
                for chunk in range(2):
                    columns = pl.ds(chunk * wide, wide)
                    value = NEWTON_A * exact[rows(block * unit, unit), columns] + jnp.dot(
                        pool[pl.ds(poly[1], unit), :],
                        pool[rows(now + block * unit, unit), columns],
                        preferred_element_type=F32,
                    )
                    exact[rows(block * unit, unit), columns] = value
                    pool[rows(later + block * unit, unit), columns] = value.astype(BF16)
                return carry

            lax.fori_loop(0, count, advance, 0)
            return carry

        lax.fori_loop(0, NS_STEPS, newton, 0)

        @pl.when(tall == 1)
        def _():
            free = high[1 - NS_STEPS % 2]
            factor = jnp.sqrt(jnp.full((1, 1), count, jnp.int32).astype(F32))

            def lay(k, carry):
                block, row = k // per, k % per
                for column in range(per):
                    columns = pl.ds(column * small, small)
                    part = exact[rows(k * small, small), columns]
                    pool[
                        rows(free + block * unit + column * small, small), rows(row * small, small)
                    ] = (part * factor).T.astype(BF16)
                return carry

            lax.fori_loop(0, count * per, lay, 0)


def update_all(grads, moments, gains, n, unit):
    top = n // 2
    dma = pltpu.SemaphoreType.DMA
    vmem = pltpu.VMEM
    _, pool_rows = layout(n, unit)
    shapes = [(unit // n, 4 * unit), (2 * unit // n, unit), (unit // n, 6 * unit), (3 * unit // n, unit)]
    own = [jax.ShapeDtypeStruct(shape, BF16) for shape in shapes]
    whole = [jax.ShapeDtypeStruct(grad.shape, BF16) for grad in grads]
    in_vmem = pl.BlockSpec(memory_space=pltpu.VMEM)
    results = pl.pallas_call(
        functools.partial(update_kernel, n, unit),
        out_shape=own + own + whole + [jax.ShapeDtypeStruct(gains.shape, F32)],
        in_specs=[ANY] * 11 + [in_vmem],
        out_specs=[ANY] * 12 + [in_vmem],
        scratch_shapes=[
            vmem((pool_rows, unit), BF16),
            vmem((3 * unit, unit), F32),
            vmem((unit, unit // 2), F32),
            vmem((8, unit), F32),
            vmem(gains.shape, F32),
            vmem(gains.shape, F32),
            vmem(gains.shape, F32),
            vmem((n,) + gains.shape, F32),
            dma((4 * n,)),
            dma((4 * n,)),
            dma((TILE_SLOTS,)),
            dma((2 * n,)),
            dma((2, 2 * n)),
            pltpu.SemaphoreType.REGULAR,
            dma((16 * top,)),
            dma((16 * top,)),
            dma((2,)),
            dma((2,)),
            dma((4,)),
            dma((4,)),
            dma((4, 3)),
            dma((4, 3)),
            dma((7,)),
            dma((n,)),
            dma,
            dma((n,)),
            dma((7,)),
            dma((7, 2)),
            dma((7, 2)),
            dma((3 + 2 * top,)),
            dma((3 + 2 * top,)),
        ],
        compiler_params=pltpu.CompilerParams(
            collective_id=1, has_side_effects=True, vmem_limit_bytes=56 * 2**20
        ),
    )(*grads, *moments, gains)
    return results[:4], results[4:8], results[12]


def unpacked(arrays, unit):
    qkv, out, gate_up, down = arrays
    return (
        qkv[:, : 2 * unit],
        qkv[:, 2 * unit : 3 * unit],
        qkv[:, 3 * unit :],
        out,
        gate_up[:, : 3 * unit],
        gate_up[:, 3 * unit :],
        down,
    )


def body(
    layer_input,
    output_grad,
    lengths,
    attention_gain,
    feed_gain,
    query_gain,
    key_gain,
    query_weight,
    key_weight,
    value_weight,
    out_weight,
    gate_weight,
    up_weight,
    down_weight,
    query_moment,
    key_moment,
    value_moment,
    out_moment,
    gate_moment,
    up_moment,
    down_moment,
):
    owned = (
        query_weight, key_weight, value_weight, out_weight, gate_weight, up_weight, down_weight,
    )
    moments = (
        query_moment, key_moment, value_moment, out_moment, gate_moment, up_moment, down_moment,
    )
    n = lax.axis_size("own")
    unit = layer_input.shape[1]
    core = lax.axis_index("rep") % 2

    def halves(*matrices):
        parts = []
        for matrix in matrices:
            width = matrix.shape[1] // 2
            parts.append(lax.dynamic_slice_in_dim(matrix, core * width, width, 1))
        return jnp.concatenate(parts, 1).astype(BF16)

    step = unit // 2
    gate_half, up_half = halves(gate_weight), halves(up_weight)
    shards = (
        halves(query_weight, key_weight, value_weight),
        out_weight.astype(BF16),
        jnp.concatenate(
            [part[:, k * step : (k + 1) * step] for k in range(3) for part in (gate_half, up_half)], 1
        ),
        down_weight.astype(BF16),
    )
    row_count = layer_input.shape[0]
    _, positions = segments(lengths[0], row_count)
    cosine_table, sine_table = rope_tables(positions)
    starts = (jnp.arange(row_count, dtype=jnp.int32) - positions).astype(F32)
    table = jnp.concatenate(
        [
            cosine_table[:, 0], cosine_table[:, 0], -sine_table[:, 0], sine_table[:, 0],
            jnp.broadcast_to(starts[:, None], (row_count, HEAD_DIM)),
        ],
        1,
    )
    gain_rows = [gain[None, :] for gain in (attention_gain, feed_gain, query_gain, key_gain)]
    (block_output, input_grad), gain_grads, grads = layer_pass(
        layer_input, output_grad, table, gain_rows, shards, n
    )
    gains = jnp.concatenate([grad[0] for grad in gain_grads])
    gains = jnp.pad(gains, (0, 24 * 128 - gains.shape[0])).reshape(24, 128)
    reduced, orth, gain_sums = update_all(grads, moments, gains, n, unit)
    moments_next = [
        MOMENTUM * moment + part.astype(F32) for moment, part in zip(moments, unpacked(reduced, unit))
    ]
    new_weights = [
        matrix * (1.0 - LEARN_RATE * WEIGHT_DECAY) - LEARN_RATE * part.astype(F32)
        for matrix, part in zip(owned, unpacked(orth, unit))
    ]
    gain_sums = gain_sums.reshape(-1)
    norm_grads = gain_sums[: 2 * unit].reshape(2, unit)
    head_grads = gain_sums[2 * unit : 2 * unit + 2 * HEAD_DIM].reshape(2, HEAD_DIM)
    return (block_output, input_grad, norm_grads, head_grads, *new_weights, *moments_next)


def solution(mesh):
    tokens, owned = P(("rep", "own"), None), P("own", None)
    return jax.shard_map(
        body,
        mesh=mesh,
        in_specs=(tokens,) * 3 + (P(),) * 4 + (owned,) * 14,
        out_specs=(tokens,) * 2 + (P(),) * 2 + (owned,) * 14,
        check_vma=False,
    )
```

```python
import functools

import jax
import jax.numpy as jnp
from jax import lax
from jax.experimental import pallas as pl
from jax.experimental.pallas import tpu as pltpu
from jax.sharding import PartitionSpec as P

HEADS = 16
KV_HEADS = 8
HEAD_DIM = 128
NS_STEPS = 5

EPSILON = 1e-06
ROPE_BASE = 1000000.0
MOMENTUM = 0.95
LEARN_RATE = 0.8
WEIGHT_DECAY = 0.01
NEWTON_A = 3.4445
NEWTON_B = -4.775
NEWTON_C = 2.0315

BF16 = jnp.bfloat16
F32 = jnp.float32
MESH = pl.DeviceIdType.MESH
ANY = pl.BlockSpec(memory_space=pltpu.HBM)

QKV, OUT, GU, DOWN = range(4)


def segments(lengths, row_count):
    seq_ends = jnp.cumsum(lengths)
    seq_starts = seq_ends - lengths
    row_ids = jnp.arange(row_count, dtype=jnp.int32)
    segment_ids = jnp.sum((row_ids[:, None] >= seq_ends[None, :]).astype(jnp.int32), 1)
    slot_ids = jnp.arange(lengths.shape[0], dtype=jnp.int32)
    row_starts = jnp.sum(
        jnp.where(segment_ids[:, None] == slot_ids[None, :], seq_starts[None, :], 0), 1
    )
    return (segment_ids, row_ids - row_starts)


def rope_tables(positions):
    inverse = ROPE_BASE ** (-jnp.arange(0, HEAD_DIM, 2, dtype=jnp.float32) / HEAD_DIM)
    angles = positions.astype(jnp.float32)[:, None] * inverse[None, :]
    return (jnp.cos(angles)[:, None, :], jnp.sin(angles)[:, None, :])


class Place:
    def __init__(self, n):
        self.n = n
        self.rep = lax.axis_index("rep")
        self.own = lax.axis_index("own")
        self.x = self.rep // 2
        self.core = self.rep % 2
        odd, pair = self.own % 2, self.own // 2
        self.ring = pair * (1 - odd) + odd * (n - 1 - pair)

    def own_at(self, ring):
        odd = ring // (self.n // 2)
        return 2 * (ring * (1 - odd) + odd * (self.n - 1 - ring)) + odd

    def shard(self, distance):
        return self.own_at(lax.rem(self.ring + distance + self.n, self.n))

    def ring_neighbour(self, way):
        return (self.rep, self.shard(way))

    @property
    def core_partner(self):
        return (self.x * 2 + 1 - self.core, self.own)

    @property
    def x_partner(self):
        return ((1 - self.x) * 2 + self.core, self.own)


def greet(devices):
    barrier = pltpu.get_barrier_semaphore()
    for device in devices:
        pl.semaphore_signal(barrier, inc=1, device_id=device, device_id_type=MESH)
    pl.semaphore_wait(barrier, len(devices))


class Several:
    def __init__(self, whole, copies):
        self.whole = whole
        self.copies = copies

    def start(self):
        for copy in self.copies:
            copy().start()

    def wait_send(self):
        self.whole().wait_send()

    def wait_recv(self):
        self.whole().wait_recv()


def remote(src, dst, send, recv, device):
    return pltpu.make_async_remote_copy(
        src_ref=src, dst_ref=dst, send_sem=send, recv_sem=recv, device_id=device, device_id_type=MESH
    )


def hops(n, way, kind):
    return n // 2 if (way == 0) == (kind == 0) else n // 2 - 1


SPREADS = ((QKV, True), (OUT, False), (GU, True), (DOWN, False))


def layer_kernel(n, tokens, unit, *refs):
    (
        x_ref, back_ref, table_ref, attention_gain, feed_gain, query_gain, key_gain,
    ) = refs[:7]
    shards = refs[7:11]
    output, input_grad, grad_attention, grad_feed, grad_query_gain, grad_key_gain = refs[11:17]
    grads = refs[17:21]
    (
        w_qkv, w_out, w_gu, w_down, normed, raw, low, probs, context, hidden, out_low, attended,
        grad_context, activated, gu_back, part, sent, got, middle, tables, stage, turned_left, gain_sums,
        local, ring_send, ring_recv, x_send, x_recv, swap_send, swap_recv, stage_sem,
    ) = refs[21:]
    weights = (w_qkv, w_out, w_gu, w_down)
    place = Place(n)
    top = n // 2
    cw, ccw = place.ring_neighbour(1), place.ring_neighbour(-1)
    ways = ((1, cw), (-1, ccw))
    greet([cw, ccw, place.core_partner, place.x_partner])
    both = 2 * tokens
    mine = pl.multiple_of(place.core * tokens, tokens)
    theirs = pl.multiple_of((1 - place.core) * tokens, tokens)
    my_rows, their_rows = pl.ds(mine, tokens), pl.ds(theirs, tokens)
    chunk = unit // 2
    ff = 3 * unit // 2
    few = 32
    base = unit // n
    heads = unit // HEAD_DIM
    kv_heads = heads // 2
    scale = HEAD_DIM ** (-0.5)

    def holds(which, own_index, act):
        if SPREADS[which][1]:
            act()
        else:
            pl.when(own_index // top == place.core)(act)

    def region(which, own_index, x):
        array, split = SPREADS[which]
        height = shards[which].shape[0]
        if split:
            width = weights[which].shape[1] // 2
            start = pl.multiple_of(own_index * height, height)
            return weights[which].at[pl.ds(start, height), pl.ds(pl.multiple_of(x * width, width), width)]
        start = pl.multiple_of(lax.rem(own_index, top) * height, height)
        return weights[which].at[pl.ds(start, height)]

    def own_copy(which):
        height = shards[which].shape[0]
        index = place.own if SPREADS[which][1] else lax.rem(place.own, top)
        start = pl.multiple_of(index * height, height)
        return pltpu.make_async_copy(
            shards[which], weights[which].at[pl.ds(start, height)], local.at[which]
        )

    def reach(which, way):
        return hops(n, way, 0 if SPREADS[which][1] else 1)

    def ring_copy(which, way, hop, act):
        step, target = ways[way]
        own_index = place.shard(-step * (hop if act == "wait_recv" else hop - 1))
        spot = region(which, own_index, place.x)
        index = (which * 2 + way) * top + hop - 1

        def do():
            copy = remote(spot, spot, ring_send.at[index], ring_recv.at[index], target)
            getattr(copy, act)()

        holds(which, own_index, do)

    def send_on(which, way, hop):
        ring_copy(which, way, hop, "start")

    def x_copy(which, way, hop, x):
        spot = region(which, place.shard(-ways[way][0] * hop), x)
        index = (which // 2 * 2 + way) * top + hop - 1
        return remote(spot, spot, x_send.at[index], x_recv.at[index], place.x_partner)

    def serve(which, hop):
        for way in range(2):
            if hop > reach(which, way):
                continue
            ring_copy(which, way, hop, "wait_recv")
            if hop < reach(which, way):
                send_on(which, way, hop + 1)
            if SPREADS[which][1]:
                x_copy(which, way, hop, place.x).start()

    def begin(which):
        def act():
            own_copy(which).wait()

        holds(which, place.own, act)
        for way in range(2):
            if reach(which, way) > 0:
                send_on(which, way, 1)

    def take_x(which):
        for way in range(2):
            for hop in range(1, reach(which, way) + 1):
                x_copy(which, way, hop, 1 - place.x).wait_recv()

    def swap(index, src, dst):
        return remote(src, dst, swap_send.at[index], swap_recv.at[index], place.core_partner)

    def rows_swap(index, ref):
        return swap(index, ref.at[my_rows], ref.at[my_rows])

    def part_swap(index, slot):
        return swap(index, sent.at[slot], got.at[slot])

    def loop(size, step, act):
        def body(k, carry):
            act(pl.multiple_of(k * step, step))
            return carry

        lax.fori_loop(0, size // step, body, 0)

    def normalize(source, gain, target):
        def act(k):
            value = source[pl.ds(k, few), :]
            value = value * lax.rsqrt(jnp.mean(value * value, -1, keepdims=True) + EPSILON)
            target[pl.ds(pl.multiple_of(mine + k, few), few), :] = (value * gain[...]).astype(BF16)

        loop(tokens, few, act)

    def normalize_back(k, source, gain, grad):
        value = source[pl.ds(k, few), :]
        inverse = lax.rsqrt(jnp.mean(value * value, -1, keepdims=True) + EPSILON)
        unscaled = value * inverse
        inner = grad * gain[...]
        back = inverse * (inner - unscaled * jnp.mean(inner * unscaled, -1, keepdims=True))
        return back, jnp.sum((grad * unscaled).reshape(few // 8, 8, unit), 0)

    def dot(left, right, across):
        return lax.dot_general(left, right, ((across[0], across[1]), ((), ())), preferred_element_type=F32)

    NN, NT, TN = ((1,), (0,)), ((1,), (1,)), ((0,), (0,))

    def partial_product(index, slot, left, right, across):
        part[...] = dot(left[...], right[...], across)

        def pack(k):
            sent[slot, pl.ds(k, few), :] = part[
                pl.ds(pl.multiple_of(theirs + k, few), few), :
            ].astype(BF16)

        loop(tokens, few, pack)
        part_swap(index, slot).start()

    def whole_rows(k, slot):
        own = part[pl.ds(pl.multiple_of(mine + k, few), few), :]
        return own + got[slot, pl.ds(k, few), :].astype(F32)

    def weight_grad(which, left, right):
        columns = right.shape[1] // unit

        def by_rows(r, carry):
            row = pl.multiple_of(r * chunk, chunk)
            turned_left[...] = left[:, pl.ds(row, chunk)].T

            def by_columns(c, carry):
                column = pl.multiple_of(c * unit, unit)
                index = r * columns + c
                slot = lax.rem(index, 2)

                @pl.when(index >= 2)
                def _():
                    stage_copy(which, slot, row, column, chunk, unit).wait()

                value = dot(turned_left[...], right[:, pl.ds(column, unit)], NN)
                stage[slot] = value.astype(BF16)
                stage_copy(which, slot, row, column, chunk, unit).start()
                return carry

            lax.fori_loop(0, columns, by_columns, 0)
            return carry

        lax.fori_loop(0, left.shape[1] // chunk, by_rows, 0)
        for slot in range(2):
            stage_copy(which, slot, 0, 0, chunk, unit).wait()

    def stage_copy(which, slot, row, column, height, width):
        return pltpu.make_async_copy(
            stage.at[slot], grads[which].at[pl.ds(row, height), pl.ds(column, width)],
            stage_sem.at[slot],
        )

    for which in range(4):
        holds(which, place.own, lambda: own_copy(which).start())
    tables[my_rows, :] = table_ref[...]
    normalize(x_ref, attention_gain, normed)
    rows_swap(0, normed).start()
    rows_swap(1, tables).start()
    begin(0)
    begin(1)

    def round_back(k):
        out_low[pl.ds(pl.multiple_of(mine + k, few), few), :] = back_ref[pl.ds(k, few), :].astype(BF16)

    loop(tokens, few, round_back)
    rows_swap(2, out_low).start()
    gain_sums[...] = jnp.zeros_like(gain_sums)

    late = [(1, top)] if top < 3 else [(1, h) for h in range(3, top + 1)]
    serve(0, 1)
    serve(1, 1)
    begin(2)
    for hop in range(2, top + 1):
        serve(0, hop)
        if (1, hop) not in late:
            serve(1, hop)
        if hop == 2:
            serve(2, 1)
    take_x(0)
    begin(3)
    pending = late + [(2 + w, h - w) for h in range(2, top + 1) for w in range(2)] + [(3, top)]
    for name in (0, 1):
        rows_swap(name, (normed, tables)[name]).wait_recv()

    raw[:, pl.ds(0, unit)] = dot(normed[...], w_qkv[:, pl.ds(0, unit)], NN)
    keys_values = dot(normed[...], w_qkv[:, pl.ds(unit, unit)], NN)
    raw[:, pl.ds(unit, chunk)] = keys_values[:, :chunk]
    low[:, pl.ds(unit + chunk, chunk)] = keys_values[:, chunk:].astype(BF16)
    serve(*pending.pop(0))

    def turned(value, rows):
        return value * tables[rows, pl.ds(0, HEAD_DIM)] + pltpu.roll(
            value, HEAD_DIM // 2, 1
        ) * tables[rows, pl.ds(HEAD_DIM, HEAD_DIM)]

    def turned_back(value, rows):
        return value * tables[rows, pl.ds(0, HEAD_DIM)] - pltpu.roll(
            value, HEAD_DIM // 2, 1
        ) * tables[rows, pl.ds(HEAD_DIM, HEAD_DIM)]

    def head_norm(first, count, gain):
        def act(k):
            for half in range(2):
                rows = pl.ds(half * tokens, tokens)
                columns = pl.ds(pl.multiple_of(first + k, HEAD_DIM), HEAD_DIM)
                value = raw[rows, columns]
                inverse = lax.rsqrt(jnp.mean(value * value, -1, keepdims=True) + EPSILON)
                low[rows, columns] = turned(value * inverse * gain[...], rows).astype(BF16)

        loop(count * HEAD_DIM, HEAD_DIM, act)

    head_norm(0, heads, query_gain)
    if pending:
        serve(*pending.pop(0))
    head_norm(unit, kv_heads, key_gain)

    def spans(k, half):
        queries = [pl.ds(pl.multiple_of((2 * k + g) * HEAD_DIM, HEAD_DIM), HEAD_DIM) for g in range(2)]
        keys = pl.ds(pl.multiple_of(unit + k * HEAD_DIM, HEAD_DIM), HEAD_DIM)
        values = pl.ds(pl.multiple_of(unit + unit // 2 + k * HEAD_DIM, HEAD_DIM), HEAD_DIM)
        return queries, keys, values, pl.ds(half * tokens, tokens)

    def stacked(ref, rows, columns):
        return jnp.concatenate([ref[rows, columns[0]], ref[rows, columns[1]]], 0)

    def attend(k, half):
        queries, keys, values, rows = spans(k, half)
        row_id = lax.broadcasted_iota(jnp.int32, (tokens, tokens), 0)
        column_id = lax.broadcasted_iota(jnp.int32, (tokens, tokens), 1)
        start = tables[rows, pl.ds(2 * HEAD_DIM, HEAD_DIM)][:, :1]
        allowed = (column_id <= row_id) & (column_id.astype(F32) >= start)
        masks = jnp.where(allowed, 0.0, -1e30)
        scores = dot(stacked(low, rows, queries), low[rows, keys], NT) * scale
        scores = scores + jnp.concatenate([masks, masks], 0)
        exponent = jnp.exp(scores - jnp.max(scores, -1, keepdims=True))
        value = exponent / jnp.sum(exponent, -1, keepdims=True)
        probs[k * 2 + half] = value
        result = dot(value.astype(BF16), low[rows, values], NN).astype(BF16)
        for g in range(2):
            context[rows, queries[g]] = result[g * tokens : (g + 1) * tokens]

    slots = 2 * kv_heads
    for k in range(kv_heads):
        for half in range(2):
            attend(k, half)
            slots -= 1
            for _ in range(-(-len(pending) // (slots + 1))):
                serve(*pending.pop(0))

    partial_product(3, 0, context, w_out, NN)
    part_swap(3, 0).wait_recv()

    def add_middle(k):
        middle[pl.ds(k, few), :] = x_ref[pl.ds(k, few), :] + whole_rows(k, 0)

    loop(tokens, few, add_middle)
    normalize(middle, feed_gain, hidden)
    rows_swap(4, hidden).start()
    while pending:
        serve(*pending.pop(0))
    take_x(2)
    rows_swap(4, hidden).wait_recv()
    rows_swap(2, out_low).wait_recv()

    def feed(k):
        span = pl.ds(k, chunk)
        pair = pl.ds(pl.multiple_of(2 * k, unit), unit)
        gate_up = dot(hidden[...], w_gu[:, pair], NN)
        gate, up = gate_up[:, :chunk], gate_up[:, chunk:]
        grad = dot(out_low[...], w_down[span, :], NT)
        sigmoid = 1.0 / (1.0 + jnp.exp(-gate))
        swish = gate * sigmoid
        activated[:, span] = (swish * up).astype(BF16)
        gu_back[:, pl.ds(pl.multiple_of(2 * k, chunk), chunk)] = (
            grad * up * (sigmoid + swish * (1.0 - sigmoid))
        ).astype(BF16)
        gu_back[:, pl.ds(pl.multiple_of(2 * k + chunk, chunk), chunk)] = (grad * swish).astype(BF16)

    loop(ff, chunk, feed)
    part_swap(3, 0).wait_send()
    partial_product(6, 0, gu_back, w_gu, NT)
    weight_grad(3, activated, out_low)
    part_swap(6, 0).wait_recv()

    def middle_back(k):
        back, gain_part = normalize_back(k, middle, feed_gain, whole_rows(k, 0))
        back = back_ref[pl.ds(k, few), :] + back
        input_grad[pl.ds(k, few), :] = back
        attended[pl.ds(pl.multiple_of(mine + k, few), few), :] = back.astype(BF16)
        gain_sums[1] += gain_part

    loop(tokens, few, middle_back)
    rows_swap(7, attended).start()
    partial_product(5, 1, activated, w_down, NN)
    weight_grad(2, hidden, gu_back)
    part_swap(5, 1).wait_recv()

    def add_output(k):
        output[pl.ds(k, few), :] = middle[pl.ds(k, few), :] + whole_rows(k, 1)

    loop(tokens, few, add_output)
    rows_swap(7, attended).wait_recv()

    grad_context[...] = dot(attended[...], w_out[...], NT).astype(BF16)
    weight_grad(1, context, attended)

    def head_back(rows, columns, gain, grad, index):
        value = raw[rows, columns]
        inverse = lax.rsqrt(jnp.mean(value * value, -1, keepdims=True) + EPSILON)
        unscaled = value * inverse
        grad = turned_back(grad, rows)
        gain_sums[index, :, pl.ds(0, HEAD_DIM)] += jnp.sum(
            (grad * unscaled).reshape(tokens // 8, 8, HEAD_DIM), 0
        )
        inner = grad * gain[...]
        back = inverse * (inner - unscaled * jnp.mean(inner * unscaled, -1, keepdims=True))
        low[rows, columns] = back.astype(BF16)

    def attend_back(k, half):
        queries, keys, values, rows = spans(k, half)
        prob = probs[k * 2 + half]
        above = stacked(grad_context, rows, queries)
        query_pair = stacked(low, rows, queries)
        grad_values = dot(prob.astype(BF16), above, TN)
        grad_probs = dot(above, low[rows, values], NT)
        grad_scores = prob * (grad_probs - jnp.sum(prob * grad_probs, -1, keepdims=True))
        grad_scores = grad_scores.astype(BF16)
        grad_queries = dot(grad_scores, low[rows, keys], NN) * scale
        grad_keys = dot(grad_scores, query_pair, TN) * scale
        for g in range(2):
            head_back(rows, queries[g], query_gain, grad_queries[g * tokens : (g + 1) * tokens], 2)
        head_back(rows, keys, key_gain, grad_keys, 3)
        low[rows, values] = grad_values.astype(BF16)

    def back_body(k, carry):
        for half in range(2):
            attend_back(k, half)
        return carry

    lax.fori_loop(0, kv_heads, back_body, 0)

    part_swap(6, 0).wait_send()
    partial_product(8, 0, low, w_qkv, NT)
    weight_grad(0, normed, low)
    part_swap(8, 0).wait_recv()

    def input_back(k):
        back, gain_part = normalize_back(k, x_ref, attention_gain, whole_rows(k, 0))
        input_grad[pl.ds(k, few), :] += back
        gain_sums[0] += gain_part

    loop(tokens, few, input_back)
    grad_attention[...] = jnp.sum(gain_sums[0], 0, keepdims=True)
    grad_feed[...] = jnp.sum(gain_sums[1], 0, keepdims=True)
    grad_query_gain[...] = jnp.sum(gain_sums[2, :, pl.ds(0, HEAD_DIM)], 0, keepdims=True)
    grad_key_gain[...] = jnp.sum(gain_sums[3, :, pl.ds(0, HEAD_DIM)], 0, keepdims=True)

    for index, ref in ((0, normed), (1, tables), (2, out_low), (4, hidden), (7, attended)):
        rows_swap(index, ref).wait_send()
    part_swap(5, 1).wait_send()
    part_swap(8, 0).wait_send()
    for which in range(4):
        for way in range(2):
            for hop in range(1, reach(which, way) + 1):
                ring_copy(which, way, hop, "wait_send")
                if SPREADS[which][1]:
                    x_copy(which, way, hop, place.x).wait_send()


def layer_pass(values, back, table, gains, shards, n):
    tokens, unit = values.shape
    top = n // 2
    dma = pltpu.SemaphoreType.DMA
    vmem = pltpu.VMEM
    both = 2 * tokens
    heads = unit // HEAD_DIM
    in_vmem = pl.BlockSpec(memory_space=pltpu.VMEM)
    row = lambda width: jax.ShapeDtypeStruct((1, width), F32)
    shapes = [(unit, 2 * unit), (unit, unit), (unit, 3 * unit), (3 * unit // 2, unit)]
    results = pl.pallas_call(
        functools.partial(layer_kernel, n, tokens, unit),
        out_shape=[jax.ShapeDtypeStruct((tokens, unit), F32)] * 2
        + [row(unit), row(unit), row(HEAD_DIM), row(HEAD_DIM)]
        + [jax.ShapeDtypeStruct(shape, BF16) for shape in shapes],
        in_specs=[in_vmem] * 7 + [ANY] * 4,
        out_specs=[in_vmem] * 6 + [ANY] * 4,
        scratch_shapes=[vmem(shape, BF16) for shape in shapes]
        + [
            vmem((both, unit), BF16),
            vmem((both, 3 * unit // 2), F32),
            vmem((both, 2 * unit), BF16),
            vmem((heads, both, tokens), F32),
            vmem((both, unit), BF16),
            vmem((both, unit), BF16),
            vmem((both, unit), BF16),
            vmem((both, unit), BF16),
            vmem((both, unit), BF16),
            vmem((both, 3 * unit // 2), BF16),
            vmem((both, 3 * unit), BF16),
            vmem((both, unit), F32),
            vmem((2, tokens, unit), BF16),
            vmem((2, tokens, unit), BF16),
            vmem((tokens, unit), F32),
            vmem((both, 3 * HEAD_DIM), F32),
            vmem((2, unit // 2, unit), BF16),
            vmem((unit // 2, both), BF16),
            vmem((4, 8, unit), F32),
            dma((4,)),
            dma((8 * top,)),
            dma((8 * top,)),
            dma((4 * top,)),
            dma((4 * top,)),
            dma((9,)),
            dma((9,)),
            dma((2,)),
        ],
        compiler_params=pltpu.CompilerParams(
            collective_id=0, has_side_effects=True, vmem_limit_bytes=56 * 2**20
        ),
    )(values, back, table, *gains, *shards)
    return results[:2], results[2:6], results[6:]


PHASES = ((DOWN, 3, False), (GU, 3, True), (OUT, 2, False), (QKV, 2, True))

OWNERS = (
    (3, 0, 1, False, 1, 2),
    (3, 1, 1, False, 1, 6),
    (3, 0, 2, False, 0, 2),
    (2, 0, 2, True, 1, 5),
    (1, 0, 3, False, 0, 5),
    (1, 0, 3, False, 1, 1),
    (0, 0, 3, True, 0, 1),
)
KEY, VALUE, QUERY, OUTM, GATE, UP, DOWNM = range(7)
RETURNS = (OUTM, KEY, VALUE, DOWNM, GATE, UP, QUERY)
TILE_SLOTS = 4
X_AHEAD = 4
LAND_AHEAD = 6


def summing_core(phase):
    return 0 if PHASES[phase][2] else 1


def stage_order(n, core):
    rings = ((1.0, 1.5), (4.0, 2.7), (13.0, 1.1), (26.6, 1.7))
    crossings = {1: (-6.0, 2.2), 3: (16.0 + 12.0 * core, 1.5 - 1.4 * core)}
    keys, needs = {}, {}
    for phase in range(4):
        first, step = rings[phase]
        for i in range(n):
            key = first + step * i * 8 / n
            if summing_core(phase) == core:
                keys["ring", phase, i] = key
                needs["ring", phase, i] = [("ring", phase, i - 1)] if i else []
                if phase in crossings:
                    needs["ring", phase, i].append(("x", phase, i))
            else:
                keys["land", phase, i] = key - 6.0
                needs["land", phase, i] = [("land", phase, i - 1)] if i else []
        if phase in crossings:
            first, step = crossings[phase]
            for i in range(n):
                keys["x", phase, i] = first + step * i * 8 / n
                needs["x", phase, i] = [("x", phase, i - 1)] if i else [("x", 1, n - 1)] * (phase == 3)
        elif core == 1:
            keys["final", phase, 0] = {0: 16.0, 2: 25.0}[phase]
            needs["final", phase, 0] = [("ring", phase, n - 1)]
    left, found = sorted(keys, key=lambda stage: (keys[stage], stage)), []
    while left:
        stage = next(stage for stage in left if all(need in found for need in needs[stage]))
        left.remove(stage)
        found.append(stage)
    return found


class Rows:
    def __init__(self):
        self.next = 0

    def take(self, rows):
        start = self.next
        self.next += rows
        return start


def layout(n, unit):
    base = unit // n
    top = n // 2
    place = {}
    rows = (Rows(), Rows())
    place["high"] = [None, rows[1].take(3 * unit)]
    for name in ("grad", "ahead"):
        place[name] = [rows[summing_core(p)].take(PHASES[p][1] * base) for p in range(4)]
    for name in ("part", "other"):
        place[name] = [0 if split else rows[1].take(units * base) for _, units, split in PHASES]
    newton = Rows()
    newton.next = -(-rows[1].next // unit) * unit
    place["high"][0] = newton.take(3 * unit)
    place["poly"] = [newton.take(unit) for _ in range(2)]
    place["x_in"] = {p: [rows[0].take(PHASES[p][1] * base) for _ in range(n)] for p in (1, 3)}
    place["own"] = [[rows[core].take(3 * base) for _ in range(TILE_SLOTS)] for core in range(2)]
    place["ring"], place["far"] = [], []
    for phase, (_, units, _) in enumerate(PHASES):
        take = rows[summing_core(phase)].take
        place["ring"].append([[take(units * base) for _ in range(top)] for _ in range(2)])
        place["far"].append(take(units * base))
    return place, max(rows[0].next, rows[1].next, newton.next)


def update_kernel(n, unit, *refs):
    grads, moments, gains_in = refs[:4], refs[4:11], refs[11]
    outs, orths, lands, gains_out = refs[12:16], refs[16:20], refs[20:24], refs[24]
    (
        pool, exact, gram, squares, gain_mine, gain_core, gain_x, gain_all,
        land_send, land_recv, tile_sem, x_send, x_recv, ring_send, ring_recv, part_send, part_recv,
        moment_sem, grad_local, grad_send, grad_recv, in_send, in_recv, in_local,
        out_send, out_recv, pass_send, pass_recv, gain_send, gain_recv,
    ) = refs[25:]
    place = Place(n)
    base = unit // n
    top = n // 2
    at, _ = layout(n, unit)
    cw, ccw = place.ring_neighbour(1), place.ring_neighbour(-1)
    ways = ((1, cw), (-1, ccw))
    side = [(place.x * 2 + core, lax.rem(place.own + k, n)) for k in range(1, n) for core in range(2)]
    across = [((1 - place.x) * 2 + core, place.own) for core in range(2)]
    greet(side + [place.core_partner] + across)
    order = [top]
    for distance in range(top - 1, 0, -1):
        order += [distance, -distance]
    order.append(0)
    moment = exact
    height = [units * base for _, units, _ in PHASES]
    moment_at = [sum(height[:phase]) for phase in range(4)]
    owners = [
        (xs * 2 + 1, place.own_at(spot * n // 8)) for _, _, _, _, xs, spot in OWNERS
    ]
    here = place.rep * n + place.own
    is_owner = [here == rep * n + own for rep, own in owners]

    def rows(start, size):
        if isinstance(start, int):
            return pl.ds(start, size)
        return pl.ds(pl.multiple_of(start, size), size)

    def block(start, size):
        return pool.at[rows(start, size)]

    def pieces_of(phase, x):
        array, units, _ = PHASES[phase]
        half = unit // 2
        found = []
        for core in range(2):
            for b in range(units):
                if array == GU:
                    own_column = b * unit + x * half
                    column = x * 3 * unit + core * (3 * half) + b * half
                else:
                    own_column = x * units * half + b * half
                    column = x * 2 * unit + core * (unit - x * half) + b * (half + x * half)
                found.append((core, b, own_column, column))
        return found

    def columns(start):
        return pl.ds(pl.multiple_of(start, unit // 2), unit // 2)

    def in_block(start, core, b):
        return pool.at[pl.ds(start + b * base, base), pl.ds(core * (unit // 2), unit // 2)]

    def shard_rows(phase, own_index):
        if PHASES[phase][2]:
            return rows(own_index * base, base)
        return rows(lax.rem(own_index, top) * height[phase], height[phase])

    def landing(phase, own_index, act):
        if PHASES[phase][2]:
            act()
        else:
            pl.when(own_index // top != summing_core(phase))(act)

    def spread(source, target, size, send, recv, device):
        step = size

        def copy(k, count):
            return remote(block(source + k, count), block(target + k, count), send, recv, device)

        return Several(
            functools.partial(copy, 0, size),
            [functools.partial(copy, k, step) for k in range(0, size, step)],
        )

    def land_copy(phase, i, act):
        array, units, split = PHASES[phase]
        own_index = place.shard(order[i])
        span = shard_rows(phase, own_index)

        def copy(at_columns):
            return remote(
                grads[array].at[span, at_columns], lands[array].at[span, at_columns],
                land_send.at[phase * n + i], land_recv.at[phase * n + i], place.core_partner,
            )

        def do():
            if not split:
                getattr(copy(pl.ds(0, unit)), act)()
            elif act == "start":
                for core, _, column, _ in pieces_of(phase, place.x):
                    if core == 1:
                        copy(columns(column)).start()
            else:
                getattr(copy(pl.ds(0, units * unit // 2)), act)()

        landing(phase, own_index, do)

    def x_index(phase, i):
        return (phase // 2) * n + i

    def x_copies(phase, i, core, act):
        index = x_index(phase, i)
        array, units, _ = PHASES[phase]
        span = shard_rows(phase, place.shard(order[i]))
        target = at["x_in"][phase][i]

        def copy(source, spot):
            return remote(
                source, spot, x_send.at[index], x_recv.at[core, index], ((1 - place.x) * 2, place.own)
            )

        if act == "start":
            for its_core, b, column, _ in pieces_of(phase, 1 - place.x):
                if its_core == core:
                    copy(grads[array].at[span, columns(column)], in_block(target, core, b)).start()
        else:
            spot = pool.at[pl.ds(target, height[phase]), pl.ds(core * (unit // 2), unit // 2)]
            getattr(copy(spot, spot), act)()

    def ring_copy(phase, way, distance, source, part):
        size = height[phase] // 2
        target = at["ring"][phase][way][distance - 1] + part * size
        index = ((phase * 2 + way) * top + distance - 1) * 2 + part
        return spread(
            source + part * size, target, size,
            ring_send.at[index], ring_recv.at[index], ways[way][1],
        )

    def ring_out(phase, distance, part):
        if distance == 0:
            return []
        if distance == top:
            return [ring_copy(phase, part, top, at["far"][phase], part)]
        way = 0 if distance > 0 else 1
        far = abs(distance)
        return [ring_copy(phase, way, far, at["ring"][phase][way][far], part)]

    def part_copy(phase):
        return spread(
            at["part"][phase], at["other"][phase], height[phase],
            part_send.at[phase // 2], part_recv.at[phase // 2], place.x_partner,
        )

    def gain_copy(src, dst, slot, device):
        return remote(src, dst, gain_send.at[slot], gain_recv.at[slot], device)

    def gain_core_copy():
        return gain_copy(gain_mine, gain_core, 0, place.core_partner)

    def gain_x_copy():
        return gain_copy(gain_core, gain_x, 1, place.x_partner)

    def gain_back_copy():
        return gain_copy(gain_mine, gain_x, 2, place.core_partner)

    def gain_ring(way, hop, distance):
        spot = gain_all.at[place.shard(distance)]
        return gain_copy(spot, spot, 3 + way * top + hop - 1, ways[way][1])

    def grad_place(phase, x):
        array = PHASES[phase][0]
        start = at["grad"][phase]
        if not PHASES[phase][2]:
            return [(outs[array], block(start, height[phase]))]
        return [
            (outs[array].at[:, columns(column)], in_block(start, core, b))
            for core, b, _, column in pieces_of(phase, x)
        ]

    def grad_span(phase, x):
        array, units, split = PHASES[phase]
        if not split:
            return outs[array]
        first = pl.multiple_of(x * units * unit, unit)
        return outs[array].at[:, pl.ds(first, units * unit)]

    def grad_sent(phase, to, device, x):
        span = grad_span(phase, x)
        return remote(span, span, grad_send.at[phase, to], grad_recv.at[phase, to], device)

    def matrix_rows(matrix, own_index):
        phase, first, units, tall, _, _ = OWNERS[matrix]
        if tall:
            return [(0, own_index * units * base, units * base)]
        return [
            ((first + k) * base, k * unit + own_index * base, base) for k in range(units)
        ]

    def matrix_span(matrix):
        phase, first, units, tall, xs, _ = OWNERS[matrix]
        array = PHASES[phase][0]
        if tall:
            return orths[array]
        start = (xs * PHASES[phase][1] + first) * unit
        return orths[array].at[:, pl.ds(start, units * unit)]

    def answer_parts(matrix, final, own_index):
        phase, first, units, tall, xs, _ = OWNERS[matrix]
        array = PHASES[phase][0]
        if tall:
            return [(block(final + own_index * units * base, units * base), orths[array])]
        return [
            (
                pool.at[
                    rows(final + (b - first) * unit + own_index * base, base),
                    pl.ds(core * (unit // 2), unit // 2),
                ],
                orths[array].at[:, columns(column)],
            )
            for core, b, _, column in pieces_of(phase, xs)
            if first <= b < first + units
        ]

    def handed(matrix, to, device):
        span = matrix_span(matrix)
        return remote(span, span, pass_send.at[matrix, to], pass_recv.at[matrix, to], device)

    def answered(matrix, target):
        span = matrix_span(matrix)
        return remote(
            span, span, out_send.at[target], out_recv.at[matrix], (place.x * 2, target)
        )

    def summed(pieces, size, store):
        step = 16
        steps = 4 if size % (4 * step) == 0 else 1

        def body(k, carry):
            for j in range(steps):
                shift = (k * steps + j) * step
                total = None
                for start in pieces:
                    value = pool[rows_at(start, shift, step), :].astype(F32)
                    total = value if total is None else total + value
                store(shift, step, total)
            return carry

        lax.fori_loop(0, size // (step * steps), body, 0)

    def rows_at(start, shift, step):
        return pl.ds(pl.multiple_of(start + shift, step), step)

    def keep(start):
        def store(shift, step, total):
            pool[rows_at(start, shift, step), :] = total.astype(BF16)

        return store

    def load_tile(phase, i, slot):
        array, _, split = PHASES[phase]
        own_index = place.shard(order[i])
        span = shard_rows(phase, own_index)
        summing = summing_core(phase)

        def load(source, target):
            pltpu.make_async_copy(source, target, tile_sem.at[slot]).start()

        if split:
            for core, b, column, _ in pieces_of(phase, place.x):
                load(
                    (grads, lands)[core][array].at[span, columns(column)],
                    in_block(at["own"][summing][slot], core, b),
                )
            return
        for core in range(2):

            @pl.when(own_index // top == core)
            def _():
                load(
                    (lands, grads)[core == summing][array].at[span],
                    block(at["own"][summing][slot], height[phase]),
                )

    def prefetch(rings, index):
        if index < len(rings):
            _, phase, i = rings[index]
            land_copy(phase, i, "wait_recv")
            load_tile(phase, i, index % TILE_SLOTS)

    def moment_copies(phase, act):
        array, units, split = PHASES[phase]
        if not split:
            act(moments[3 if array == OUT else 6], moment.at[pl.ds(moment_at[phase], height[phase])])
            return
        half = unit // 2
        for x in range(2):

            @pl.when(place.x == x)
            def _():
                for core, b, _, column in pieces_of(phase, x):
                    if array == GU:
                        source, first = 4 + x, x * 3 * unit
                    elif x == 0:
                        source, first = 0, 0
                    else:
                        source, first = 1 + b, (2 + b) * unit
                    act(
                        moments[source].at[:, pl.ds(column - first, half)],
                        moment.at[pl.ds(moment_at[phase] + b * base, base), pl.ds(core * half, half)],
                    )

    def load_moment(phase):
        moment_copies(
            phase, lambda src, dst: pltpu.make_async_copy(src, dst, moment_sem.at[phase]).start()
        )

    def finish(phase, pieces):
        span = moment.at[pl.ds(moment_at[phase], height[phase])]
        pltpu.make_async_copy(span, span, moment_sem.at[phase]).wait()

        def store(shift, step, total):
            pool[rows_at(at["grad"][phase], shift, step), :] = total.astype(BF16)
            ahead = (1.0 + MOMENTUM) * total + MOMENTUM**2 * moment[
                rows_at(moment_at[phase], shift, step), :
            ]
            pool[rows_at(at["ahead"][phase], shift, step), :] = ahead.astype(BF16)

        summed(pieces, height[phase], store)
        for matrix, (its_phase, _, _, _, xs, _) in enumerate(OWNERS):
            if its_phase != phase:
                continue

            def hand_in(local):
                for source, target, size in matrix_rows(matrix, place.own):
                    source = block(at["ahead"][phase] + source, size)
                    target = block(at["high"][1] + target, size)
                    if local:
                        pltpu.make_async_copy(source, target, in_local).start()
                    else:
                        remote(
                            source, target, in_send.at[matrix], in_recv.at[place.own], owners[matrix]
                        ).start()

            if summing_core(phase) == 0:
                pl.when(place.x == xs)(functools.partial(hand_in, False))
            else:
                pl.when(is_owner[matrix])(functools.partial(hand_in, True))
                pl.when((place.x == xs) & (here != owners[matrix][0] * n + owners[matrix][1]))(
                    functools.partial(hand_in, False)
                )

        for target, source in grad_place(phase, place.x):
            pltpu.make_async_copy(source, target, grad_local.at[phase]).start()
            remote(
                source, target, grad_send.at[phase, 0], grad_recv.at[phase, 0], place.core_partner
            ).start()
            if PHASES[phase][2]:
                remote(
                    source, target, grad_send.at[phase, 1], grad_recv.at[phase, 1], place.x_partner
                ).start()

    def settle(phase):
        span = block(at["grad"][phase], height[phase])
        pltpu.make_async_copy(span, span, grad_local.at[phase]).wait()
        remote(
            span, span, grad_send.at[phase, 0], grad_recv.at[phase, 0], place.core_partner
        ).wait_send()
        if PHASES[phase][2]:
            remote(
                span, span, grad_send.at[phase, 1], grad_recv.at[phase, 1], place.x_partner
            ).wait_send()
        for matrix, (its_phase, _, units, _, xs, _) in enumerate(OWNERS):
            if its_phase != phase:
                continue

            sends = place.x == xs
            if summing_core(phase) == 1:
                sends = sends & (here != owners[matrix][0] * n + owners[matrix][1])

            @pl.when(sends)
            def _():
                span = block(at["high"][1], units * base)
                remote(
                    span, span, in_send.at[matrix], in_recv.at[0], place.core_partner
                ).wait_send()

    def stage_x(phase, i, core, paced):
        before = x_index(phase, i) - X_AHEAD
        if paced and before >= 0:
            x_copies(1 if before < n else 3, before % n, core, "wait_send")
        x_copies(phase, i, core, "start")

    def stage_ring(phase, i, slot):
        distance = order[i]
        start = at["own"][summing_core(phase)][slot]
        span = block(start, height[phase])
        pltpu.make_async_copy(span, span, tile_sem.at[slot]).wait()
        pieces = [start]
        if PHASES[phase][2]:
            for core in range(2):
                x_copies(phase, i, core, "wait_recv")
            pieces.append(at["x_in"][phase][i])
        size = height[phase]
        mid = size // 2
        if distance == 0:
            for way in range(2):
                held = at["ring"][phase][way][0]
                for part in range(2):
                    ring_copy(phase, way, 1, held, part).wait_recv()
                pieces.append(held)
            if PHASES[phase][2]:
                finish(phase, pieces)
            else:
                summed(pieces, size, keep(at["part"][phase]))
                part_copy(phase).start()
        else:
            way = 0 if distance > 0 else 1
            far = abs(distance)
            held = at["far"][phase] if far == top else at["ring"][phase][way][far]
            for part in (1 - way, way):
                starts = [start + part * mid for start in pieces]
                if far + 1 < top or (far + 1 == top and part == way):
                    ring_copy(phase, way, far + 1, held, part).wait_recv()
                    starts.append(held + part * mid)
                summed(starts, mid, keep(held + part * mid))
                for copy in ring_out(phase, distance, part):
                    copy.start()
    def ring_sent(phase):
        for distance in order:
            for part in range(2):
                for copy in ring_out(phase, distance, part):
                    copy.wait_send()

    unsent, x_left = [], {}

    def run(core):
        crossed = []
        stages = stage_order(n, core)
        rings = [stage for stage in stages if stage[0] == "ring"]
        landed = [stage for stage in stages if stage[0] == "land"]
        for phase in range(4):
            if summing_core(phase) == core:
                load_moment(phase)
        done, sent, hop = 0, 0, 0
        sums_left = len([stage for stage in stages if stage[0] in ("ring", "final")])
        for index in range(LAND_AHEAD):
            land_copy(*landed[index][1:], "start")
        for index in range(TILE_SLOTS - 1):
            prefetch(rings, index)
        for kind, phase, i in stages:
            paced = core == 0 or sums_left > 0
            sums_left -= kind in ("ring", "final")
            if kind == "x":
                stage_x(phase, i, core, paced)
                crossed.append((phase, i, paced))
            elif kind == "land":
                if paced:
                    land_copy(phase, i, "wait_send")
                else:
                    unsent.append((phase, i))
                if sent + LAND_AHEAD < len(landed):
                    land_copy(*landed[sent + LAND_AHEAD][1:], "start")
                sent += 1
            elif kind == "final":
                part_copy(phase).wait_recv()
                finish(phase, [at["part"][phase], at["other"][phase]])
            else:
                prefetch(rings, done + TILE_SLOTS - 1)
                stage_ring(phase, i, done % TILE_SLOTS)
                done += 1
                if core == 0 and hop <= top + 1:
                    gain_stage(hop)
                    hop += 1
        waited = {x_index(p, i) - X_AHEAD for p, i, paced in crossed if paced}
        x_left[core] = [(p, i) for p, i, _ in crossed if x_index(p, i) not in waited]

    def settle_all(core):
        for phase, (_, _, split) in enumerate(PHASES):
            if summing_core(phase) == core:
                settle(phase)
                if not split:
                    part_copy(phase).wait_send()
        for phase, i in x_left[core]:
            x_copies(phase, i, core, "wait_send")
        if core == 1:
            for phase, i in unsent:
                land_copy(phase, i, "wait_send")

    def take_sums(core):
        for phase, (_, _, split) in enumerate(PHASES):
            if summing_core(phase) != core:
                grad_sent(phase, 0, place.core_partner, place.x).wait_recv()
                if split:
                    grad_sent(phase, 2, place.core_partner, 1 - place.x).wait_recv()

    def gain_stage(hop):
        if hop == 0:
            gain_core_copy().wait_recv()
            gain_core[...] = gain_mine[...] + gain_core[...]
            gain_x_copy().start()
            return
        if hop == 1:
            gain_x_copy().wait_recv()
            gain_all[place.own] = gain_core[...] + gain_x[...]
            for way in range(2):
                gain_ring(way, 1, 0).start()
        for way in range(2):
            if 1 < hop <= hops(n, way, 0) + 1:
                distance = -ways[way][0] * (hop - 1)
                gain_ring(way, hop - 1, distance).wait_recv()
                if hop <= hops(n, way, 0):
                    gain_ring(way, hop, distance).start()

    gain_mine[...] = gains_in[...]

    @pl.when(place.core == 0)
    def _():
        run(0)
        total = gain_all[0]
        for k in range(1, n):
            total = total + gain_all[k]
        gains_out[...] = total
        gain_mine[...] = total
        gain_back_copy().start()

        for phase in (1, 3):
            grad_sent(phase, 1, place.x_partner, 1 - place.x).wait_recv()
            grad_sent(phase, 2, place.core_partner, 1 - place.x).start()

        for matrix in RETURNS:
            xs = OWNERS[matrix][4]

            @pl.when(place.x == xs)
            def _():
                answered(matrix, place.own).wait_recv()
                handed(matrix, 0, place.x_partner).start()
                handed(matrix, 1, place.core_partner).start()

            @pl.when(place.x != xs)
            def _():
                handed(matrix, 0, place.x_partner).wait_recv()
                handed(matrix, 1, place.core_partner).start()

        for matrix, (phase, _, units, _, xs, _) in enumerate(OWNERS):
            handed(matrix, 1, place.core_partner).wait_send()

            @pl.when(place.x == xs)
            def _():
                handed(matrix, 0, place.x_partner).wait_send()

        take_sums(0)
        settle_all(0)
        for phase in (1, 3):
            ring_sent(phase)
            grad_sent(phase, 2, place.core_partner, 1 - place.x).wait_send()
        gain_x_copy().wait_send()
        gain_back_copy().wait_send()
        for way in range(2):
            for h in range(1, hops(n, way, 0) + 1):
                gain_ring(way, h, -ways[way][0] * (h - 1)).wait_send()

    @pl.when(place.core == 1)
    def _():
        gain_core_copy().start()
        run(1)
        for phase in (0, 2):
            ring_sent(phase)
        newton_part(n, unit, place, pool, exact, gram, squares, at, is_owner, in_recv, in_local)
        for matrix, (_, _, units, tall, _, _) in enumerate(OWNERS):

            @pl.when(is_owner[matrix])
            def _():
                final = at["high"][1 - NS_STEPS % 2 if tall else NS_STEPS % 2]

                def send(k, carry):
                    target = lax.rem(place.own + k, n)
                    for source, part in answer_parts(matrix, final, target):
                        remote(
                            source, part, out_send.at[target], out_recv.at[matrix],
                            (place.x * 2, target),
                        ).start()
                    return carry

                lax.fori_loop(0, n, send, 0)

                def sent(k, carry):
                    answered(matrix, lax.rem(place.own + k, n)).wait_send()
                    return carry

                lax.fori_loop(0, n, sent, 0)

        gain_core_copy().wait_send()
        gain_back_copy().wait_recv()
        gains_out[...] = gain_x[...]
        take_sums(1)
        settle_all(1)
        for matrix in RETURNS:
            handed(matrix, 1, place.core_partner).wait_recv()


def newton_part(n, unit, place, pool, exact, gram, squares, at, is_owner, in_recv, in_local):
    base = unit // n
    small = min(256, unit // 2)
    per = unit // small
    wide = unit // 2
    few = 32
    count, tall = 0, 0
    for mine, (_, _, units, lies_tall, _, _) in zip(is_owner, OWNERS):
        count = count + units * mine.astype(jnp.int32)
        tall = tall + int(lies_tall) * mine.astype(jnp.int32)
    high, poly = at["high"], at["poly"]

    def rows(start, size):
        return pl.ds(pl.multiple_of(start, size), size)

    for matrix, (phase, _, units, *_) in enumerate(OWNERS):

        @pl.when(is_owner[matrix])
        def _():
            span = pool.at[pl.ds(high[1], units * base)]
            inside = summing_core(phase) == 1
            if inside:
                pltpu.make_async_copy(span, span, in_local).wait()
            for k in range(1 if inside else 0, n):
                own_index = lax.rem(place.own + k, n)
                remote(
                    span, span, in_recv.at[own_index], in_recv.at[own_index], place.core_partner
                ).wait_recv()

    @pl.when(count > 0)
    def _():
        squares[...] = jnp.zeros_like(squares)

        def square(k, carry):
            part = pool[rows(high[1] + k * few, few), :].astype(F32)
            squares[...] += jnp.sum((part * part).reshape(few // 8, 8, unit), 0)
            return carry

        lax.fori_loop(0, count * (unit // few), square, 0)
        total = jnp.sum(jnp.sum(squares[...], 1, keepdims=True), 0, keepdims=True)
        inverse = 1.0 / (jnp.sqrt(total) + 1e-07)

        @pl.when(tall == 0)
        def _():
            def scale(k, carry):
                value = pool[rows(high[1] + k * few, few), :].astype(F32) * inverse
                exact[rows(k * few, few), :] = value
                pool[rows(high[0] + k * few, few), :] = value.astype(BF16)
                return carry

            lax.fori_loop(0, count * (unit // few), scale, 0)

        @pl.when(tall == 1)
        def _():
            def scale(k, carry):
                block, row = k // per, k % per
                for column in range(per):
                    part = pool[
                        rows(high[1] + k * small, small), pl.ds(column * small, small)
                    ].astype(F32)
                    value = (part * inverse).T
                    shift = block * unit + column * small
                    columns = rows(row * small, small)
                    exact[rows(shift, small), columns] = value
                    pool[rows(high[0] + shift, small), columns] = value.astype(BF16)
                return carry

            lax.fori_loop(0, count * per, scale, 0)

        def newton(step, carry):
            even = step % 2
            now = high[0] + even * (high[1] - high[0])
            later = high[1] - even * (high[1] - high[0])

            def keep_symmetric(to, chunk, value):
                pool[pl.ds(to, (chunk + 1) * wide), pl.ds(chunk * wide, wide)] = value.astype(BF16)
                if chunk == 1:
                    pool[pl.ds(to + wide, wide), pl.ds(0, wide)] = value[:wide].T.astype(BF16)

            for chunk in range(2):
                down = (chunk + 1) * wide

                def product(block):
                    left = pool[pl.ds(pl.multiple_of(now + block * unit, unit), down), :]
                    right = pool[rows(now + block * unit + chunk * wide, wide), :]
                    return lax.dot_general(
                        left, right, (((1,), (1,)), ((), ())), preferred_element_type=F32
                    )

                gram[:down, :] = product(0)

                def more(block, carry):
                    gram[:down, :] += product(block)
                    return carry

                lax.fori_loop(1, count, more, 0)
                keep_symmetric(poly[0], chunk, gram[:down, :])

            for chunk in range(2):
                down = (chunk + 1) * wide
                columns = pl.ds(chunk * wide, wide)
                squared = jnp.dot(
                    pool[pl.ds(poly[0], down), :], pool[pl.ds(poly[0], unit), columns],
                    preferred_element_type=F32,
                )
                plain = pool[pl.ds(poly[0], down), columns].astype(F32)
                keep_symmetric(poly[1], chunk, NEWTON_B * plain + NEWTON_C * squared)

            def advance(block, carry):
                for chunk in range(2):
                    columns = pl.ds(chunk * wide, wide)
                    value = NEWTON_A * exact[rows(block * unit, unit), columns] + jnp.dot(
                        pool[pl.ds(poly[1], unit), :],
                        pool[rows(now + block * unit, unit), columns],
                        preferred_element_type=F32,
                    )
                    exact[rows(block * unit, unit), columns] = value
                    pool[rows(later + block * unit, unit), columns] = value.astype(BF16)
                return carry

            lax.fori_loop(0, count, advance, 0)
            return carry

        lax.fori_loop(0, NS_STEPS, newton, 0)

        @pl.when(tall == 1)
        def _():
            free = high[1 - NS_STEPS % 2]
            factor = jnp.sqrt(jnp.full((1, 1), count, jnp.int32).astype(F32))

            def lay(k, carry):
                block, row = k // per, k % per
                for column in range(per):
                    columns = pl.ds(column * small, small)
                    part = exact[rows(k * small, small), columns]
                    pool[
                        rows(free + block * unit + column * small, small), rows(row * small, small)
                    ] = (part * factor).T.astype(BF16)
                return carry

            lax.fori_loop(0, count * per, lay, 0)


def update_all(grads, moments, gains, n, unit):
    top = n // 2
    dma = pltpu.SemaphoreType.DMA
    vmem = pltpu.VMEM
    _, pool_rows = layout(n, unit)
    shapes = [(unit // n, 4 * unit), (2 * unit // n, unit), (unit // n, 6 * unit), (3 * unit // n, unit)]
    own = [jax.ShapeDtypeStruct(shape, BF16) for shape in shapes]
    whole = [jax.ShapeDtypeStruct(grad.shape, BF16) for grad in grads]
    in_vmem = pl.BlockSpec(memory_space=pltpu.VMEM)
    results = pl.pallas_call(
        functools.partial(update_kernel, n, unit),
        out_shape=own + own + whole + [jax.ShapeDtypeStruct(gains.shape, F32)],
        in_specs=[ANY] * 11 + [in_vmem],
        out_specs=[ANY] * 12 + [in_vmem],
        scratch_shapes=[
            vmem((pool_rows, unit), BF16),
            vmem((3 * unit, unit), F32),
            vmem((unit, unit // 2), F32),
            vmem((8, unit), F32),
            vmem(gains.shape, F32),
            vmem(gains.shape, F32),
            vmem(gains.shape, F32),
            vmem((n,) + gains.shape, F32),
            dma((4 * n,)),
            dma((4 * n,)),
            dma((TILE_SLOTS,)),
            dma((2 * n,)),
            dma((2, 2 * n)),
            dma((16 * top,)),
            dma((16 * top,)),
            dma((2,)),
            dma((2,)),
            dma((4,)),
            dma((4,)),
            dma((4, 3)),
            dma((4, 3)),
            dma((7,)),
            dma((n,)),
            dma,
            dma((n,)),
            dma((7,)),
            dma((7, 2)),
            dma((7, 2)),
            dma((3 + 2 * top,)),
            dma((3 + 2 * top,)),
        ],
        compiler_params=pltpu.CompilerParams(
            collective_id=1, has_side_effects=True, vmem_limit_bytes=56 * 2**20
        ),
    )(*grads, *moments, gains)
    return results[:4], results[4:8], results[12]


def apply_kernel(unit, *refs):
    weights, moments, sums, orths = refs[:7], refs[7:14], refs[14:18], refs[18:22]
    new_weights, new_moments = refs[22:29], refs[29:36]
    weight, moment, grad, orth, weight_out, moment_out, load_sem, store_sem = refs[36:]
    slots, base = weight.shape[0], weight.shape[1]
    arrays = ((QKV, 0), (QKV, 2), (QKV, 3), (OUT, 0), (GU, 0), (GU, 3), (DOWN, 0))
    tiles = []
    for matrix, (array, first) in enumerate(arrays):
        for row in range(weights[matrix].shape[0] // base):
            for column in range(weights[matrix].shape[1] // unit):
                tiles.append((matrix, array, row * base, column * unit, (first + column) * unit))

    def loads(t):
        matrix, array, row, column, array_column = tiles[t]
        here = (pl.ds(row, base), pl.ds(column, unit))
        there = (pl.ds(row, base), pl.ds(array_column, unit))
        slot = t % slots
        return [
            pltpu.make_async_copy(source, target.at[slot], load_sem.at[slot, k])
            for k, (source, target) in enumerate(
                (
                    (weights[matrix].at[here], weight), (moments[matrix].at[here], moment),
                    (sums[array].at[there], grad), (orths[array].at[there], orth),
                )
            )
        ]

    def stores(t):
        matrix, _, row, column, _ = tiles[t]
        here = (pl.ds(row, base), pl.ds(column, unit))
        slot = t % slots
        return [
            pltpu.make_async_copy(weight_out.at[slot], new_weights[matrix].at[here], store_sem.at[slot, 0]),
            pltpu.make_async_copy(moment_out.at[slot], new_moments[matrix].at[here], store_sem.at[slot, 1]),
        ]

    for t in range(slots - 1):
        for copy in loads(t):
            copy.start()
    few = 16
    for t in range(len(tiles)):
        slot = t % slots
        if t + slots - 1 < len(tiles):
            for copy in loads(t + slots - 1):
                copy.start()
        for copy in loads(t):
            copy.wait()
        if t >= slots:
            for copy in stores(t - slots):
                copy.wait()

        def act(k, carry):
            rows = pl.ds(pl.multiple_of(k * few, few), few)
            weight_out[slot, rows, :] = weight[slot, rows, :] * (
                1.0 - LEARN_RATE * WEIGHT_DECAY
            ) - LEARN_RATE * orth[slot, rows, :].astype(F32)
            moment_out[slot, rows, :] = MOMENTUM * moment[slot, rows, :] + grad[
                slot, rows, :
            ].astype(F32)
            return carry

        lax.fori_loop(0, base // few, act, 0)
        for copy in stores(t):
            copy.start()
    for t in range(len(tiles) - slots, len(tiles)):
        for copy in stores(t):
            copy.wait()


def apply_all(weights, moments, sums, orths, n, unit):
    slots, base = 4, unit // n
    dma = pltpu.SemaphoreType.DMA
    vmem = pltpu.VMEM
    results = pl.pallas_call(
        functools.partial(apply_kernel, unit),
        out_shape=[jax.ShapeDtypeStruct(matrix.shape, F32) for matrix in weights] * 2,
        in_specs=[ANY] * 22,
        out_specs=[ANY] * 14,
        scratch_shapes=[
            vmem((slots, base, unit), F32),
            vmem((slots, base, unit), F32),
            vmem((slots, base, unit), BF16),
            vmem((slots, base, unit), BF16),
            vmem((slots, base, unit), F32),
            vmem((slots, base, unit), F32),
            dma((slots, 4)),
            dma((slots, 2)),
        ],
        compiler_params=pltpu.CompilerParams(vmem_limit_bytes=32 * 2**20),
    )(*weights, *moments, *sums, *orths)
    return results[:7], results[7:]


def body(
    layer_input,
    output_grad,
    lengths,
    attention_gain,
    feed_gain,
    query_gain,
    key_gain,
    query_weight,
    key_weight,
    value_weight,
    out_weight,
    gate_weight,
    up_weight,
    down_weight,
    query_moment,
    key_moment,
    value_moment,
    out_moment,
    gate_moment,
    up_moment,
    down_moment,
):
    owned = (
        query_weight, key_weight, value_weight, out_weight, gate_weight, up_weight, down_weight,
    )
    moments = (
        query_moment, key_moment, value_moment, out_moment, gate_moment, up_moment, down_moment,
    )
    n = lax.axis_size("own")
    unit = layer_input.shape[1]
    core = lax.axis_index("rep") % 2

    def halves(*matrices):
        parts = []
        for matrix in matrices:
            width = matrix.shape[1] // 2
            parts.append(lax.dynamic_slice_in_dim(matrix, core * width, width, 1))
        return jnp.concatenate(parts, 1).astype(BF16)

    step = unit // 2
    gate_half, up_half = halves(gate_weight), halves(up_weight)
    shards = (
        halves(query_weight, key_weight, value_weight),
        out_weight.astype(BF16),
        jnp.concatenate(
            [part[:, k * step : (k + 1) * step] for k in range(3) for part in (gate_half, up_half)], 1
        ),
        down_weight.astype(BF16),
    )
    row_count = layer_input.shape[0]
    _, positions = segments(lengths[0], row_count)
    cosine_table, sine_table = rope_tables(positions)
    starts = (jnp.arange(row_count, dtype=jnp.int32) - positions).astype(F32)
    table = jnp.concatenate(
        [
            cosine_table[:, 0], cosine_table[:, 0], -sine_table[:, 0], sine_table[:, 0],
            jnp.broadcast_to(starts[:, None], (row_count, HEAD_DIM)),
        ],
        1,
    )
    gain_rows = [gain[None, :] for gain in (attention_gain, feed_gain, query_gain, key_gain)]
    (block_output, input_grad), gain_grads, grads = layer_pass(
        layer_input, output_grad, table, gain_rows, shards, n
    )
    gains = jnp.concatenate([grad[0] for grad in gain_grads])
    gains = jnp.pad(gains, (0, 24 * 128 - gains.shape[0])).reshape(24, 128)
    reduced, orth, gain_sums = update_all(grads, moments, gains, n, unit)
    new_weights, moments_next = apply_all(owned, moments, reduced, orth, n, unit)
    gain_sums = gain_sums.reshape(-1)
    norm_grads = gain_sums[: 2 * unit].reshape(2, unit)
    head_grads = gain_sums[2 * unit : 2 * unit + 2 * HEAD_DIM].reshape(2, HEAD_DIM)
    return (block_output, input_grad, norm_grads, head_grads, *new_weights, *moments_next)


def solution(mesh):
    tokens, owned = P(("rep", "own"), None), P("own", None)
    return jax.shard_map(
        body,
        mesh=mesh,
        in_specs=(tokens,) * 3 + (P(),) * 4 + (owned,) * 14,
        out_specs=(tokens,) * 2 + (P(),) * 2 + (owned,) * 14,
        check_vma=False,
    )
```

```python
import functools

import jax
import jax.numpy as jnp
from jax import lax
from jax.experimental import pallas as pl
from jax.experimental.pallas import tpu as pltpu
from jax.sharding import PartitionSpec as P

HEADS = 16
KV_HEADS = 8
HEAD_DIM = 128
NS_STEPS = 5

EPSILON = 1e-06
ROPE_BASE = 1000000.0
MOMENTUM = 0.95
LEARN_RATE = 0.8
WEIGHT_DECAY = 0.01
NEWTON_A = 3.4445
NEWTON_B = -4.775
NEWTON_C = 2.0315

BF16 = jnp.bfloat16
F32 = jnp.float32
MESH = pl.DeviceIdType.MESH
ANY = pl.BlockSpec(memory_space=pltpu.HBM)

QKV, OUT, GU, DOWN = range(4)


def segments(lengths, row_count):
    seq_ends = jnp.cumsum(lengths)
    seq_starts = seq_ends - lengths
    row_ids = jnp.arange(row_count, dtype=jnp.int32)
    segment_ids = jnp.sum((row_ids[:, None] >= seq_ends[None, :]).astype(jnp.int32), 1)
    slot_ids = jnp.arange(lengths.shape[0], dtype=jnp.int32)
    row_starts = jnp.sum(
        jnp.where(segment_ids[:, None] == slot_ids[None, :], seq_starts[None, :], 0), 1
    )
    return (segment_ids, row_ids - row_starts)


def rope_tables(positions):
    inverse = ROPE_BASE ** (-jnp.arange(0, HEAD_DIM, 2, dtype=jnp.float32) / HEAD_DIM)
    angles = positions.astype(jnp.float32)[:, None] * inverse[None, :]
    return (jnp.cos(angles)[:, None, :], jnp.sin(angles)[:, None, :])


class Place:
    def __init__(self, n):
        self.n = n
        self.rep = lax.axis_index("rep")
        self.own = lax.axis_index("own")
        self.x = self.rep // 2
        self.core = self.rep % 2
        odd, pair = self.own % 2, self.own // 2
        self.ring = pair * (1 - odd) + odd * (n - 1 - pair)

    def own_at(self, ring):
        odd = ring // (self.n // 2)
        return 2 * (ring * (1 - odd) + odd * (self.n - 1 - ring)) + odd

    def shard(self, distance):
        return self.own_at(lax.rem(self.ring + distance + self.n, self.n))

    def ring_neighbour(self, way):
        return (self.rep, self.shard(way))

    @property
    def core_partner(self):
        return (self.x * 2 + 1 - self.core, self.own)

    @property
    def x_partner(self):
        return ((1 - self.x) * 2 + self.core, self.own)


def greet(devices):
    barrier = pltpu.get_barrier_semaphore()
    for device in devices:
        pl.semaphore_signal(barrier, inc=1, device_id=device, device_id_type=MESH)
    pl.semaphore_wait(barrier, len(devices))


class Several:
    def __init__(self, whole, copies):
        self.whole = whole
        self.copies = copies

    def start(self):
        for copy in self.copies:
            copy().start()

    def wait_send(self):
        self.whole().wait_send()

    def wait_recv(self):
        self.whole().wait_recv()


def remote(src, dst, send, recv, device):
    return pltpu.make_async_remote_copy(
        src_ref=src, dst_ref=dst, send_sem=send, recv_sem=recv, device_id=device, device_id_type=MESH
    )


def hops(n, way, kind):
    return n // 2 if (way == 0) == (kind == 0) else n // 2 - 1


SPREADS = ((QKV, True), (OUT, False), (GU, True), (DOWN, False))


def layer_kernel(n, tokens, unit, *refs):
    (
        x_ref, back_ref, table_ref, attention_gain, feed_gain, query_gain, key_gain,
    ) = refs[:7]
    shards = refs[7:11]
    output, input_grad, grad_attention, grad_feed, grad_query_gain, grad_key_gain = refs[11:17]
    grads = refs[17:21]
    (
        w_qkv, w_out, w_gu, w_down, normed, raw, low, probs, context, hidden, out_low, attended,
        grad_context, activated, gu_back, part, sent, got, middle, tables, stage, turned_left, gain_sums,
        local, ring_send, ring_recv, x_send, x_recv, swap_send, swap_recv, stage_sem,
    ) = refs[21:]
    weights = (w_qkv, w_out, w_gu, w_down)
    place = Place(n)
    top = n // 2
    cw, ccw = place.ring_neighbour(1), place.ring_neighbour(-1)
    ways = ((1, cw), (-1, ccw))
    greet([cw, ccw, place.core_partner, place.x_partner])
    both = 2 * tokens
    mine = pl.multiple_of(place.core * tokens, tokens)
    theirs = pl.multiple_of((1 - place.core) * tokens, tokens)
    my_rows, their_rows = pl.ds(mine, tokens), pl.ds(theirs, tokens)
    chunk = unit // 2
    ff = 3 * unit // 2
    few = 32
    base = unit // n
    heads = unit // HEAD_DIM
    kv_heads = heads // 2
    scale = HEAD_DIM ** (-0.5)

    def holds(which, own_index, act):
        if SPREADS[which][1]:
            act()
        else:
            pl.when(own_index // top == place.core)(act)

    def region(which, own_index, x):
        array, split = SPREADS[which]
        height = shards[which].shape[0]
        if split:
            width = weights[which].shape[1] // 2
            start = pl.multiple_of(own_index * height, height)
            return weights[which].at[pl.ds(start, height), pl.ds(pl.multiple_of(x * width, width), width)]
        start = pl.multiple_of(lax.rem(own_index, top) * height, height)
        return weights[which].at[pl.ds(start, height)]

    def own_copy(which):
        height = shards[which].shape[0]
        index = place.own if SPREADS[which][1] else lax.rem(place.own, top)
        start = pl.multiple_of(index * height, height)
        return pltpu.make_async_copy(
            shards[which], weights[which].at[pl.ds(start, height)], local.at[which]
        )

    def reach(which, way):
        return hops(n, way, 0 if SPREADS[which][1] else 1)

    def ring_copy(which, way, hop, act):
        step, target = ways[way]
        own_index = place.shard(-step * (hop if act == "wait_recv" else hop - 1))
        spot = region(which, own_index, place.x)
        index = (which * 2 + way) * top + hop - 1

        def do():
            copy = remote(spot, spot, ring_send.at[index], ring_recv.at[index], target)
            getattr(copy, act)()

        holds(which, own_index, do)

    def send_on(which, way, hop):
        ring_copy(which, way, hop, "start")

    def x_copy(which, way, hop, x):
        spot = region(which, place.shard(-ways[way][0] * hop), x)
        index = (which // 2 * 2 + way) * top + hop - 1
        return remote(spot, spot, x_send.at[index], x_recv.at[index], place.x_partner)

    def serve(which, hop):
        for way in range(2):
            if hop > reach(which, way):
                continue
            ring_copy(which, way, hop, "wait_recv")
            if hop < reach(which, way):
                send_on(which, way, hop + 1)
            if SPREADS[which][1]:
                x_copy(which, way, hop, place.x).start()

    def begin(which):
        def act():
            own_copy(which).wait()

        holds(which, place.own, act)
        for way in range(2):
            if reach(which, way) > 0:
                send_on(which, way, 1)

    def take_x(which):
        for way in range(2):
            for hop in range(1, reach(which, way) + 1):
                x_copy(which, way, hop, 1 - place.x).wait_recv()

    def swap(index, src, dst):
        return remote(src, dst, swap_send.at[index], swap_recv.at[index], place.core_partner)

    def rows_swap(index, ref):
        return swap(index, ref.at[my_rows], ref.at[my_rows])

    def part_swap(index, slot):
        return swap(index, sent.at[slot], got.at[slot])

    def loop(size, step, act):
        def body(k, carry):
            act(pl.multiple_of(k * step, step))
            return carry

        lax.fori_loop(0, size // step, body, 0)

    def normalize(source, gain, target):
        def act(k):
            value = source[pl.ds(k, few), :]
            value = value * lax.rsqrt(jnp.mean(value * value, -1, keepdims=True) + EPSILON)
            target[pl.ds(pl.multiple_of(mine + k, few), few), :] = (value * gain[...]).astype(BF16)

        loop(tokens, few, act)

    def normalize_back(k, source, gain, grad):
        value = source[pl.ds(k, few), :]
        inverse = lax.rsqrt(jnp.mean(value * value, -1, keepdims=True) + EPSILON)
        unscaled = value * inverse
        inner = grad * gain[...]
        back = inverse * (inner - unscaled * jnp.mean(inner * unscaled, -1, keepdims=True))
        return back, jnp.sum((grad * unscaled).reshape(few // 8, 8, unit), 0)

    def dot(left, right, across):
        return lax.dot_general(left, right, ((across[0], across[1]), ((), ())), preferred_element_type=F32)

    NN, NT, TN = ((1,), (0,)), ((1,), (1,)), ((0,), (0,))

    def partial_product(index, slot, left, right, across):
        part[...] = dot(left[...], right[...], across)

        def pack(k):
            sent[slot, pl.ds(k, few), :] = part[
                pl.ds(pl.multiple_of(theirs + k, few), few), :
            ].astype(BF16)

        loop(tokens, few, pack)
        part_swap(index, slot).start()

    def whole_rows(k, slot):
        own = part[pl.ds(pl.multiple_of(mine + k, few), few), :]
        return own + got[slot, pl.ds(k, few), :].astype(F32)

    def weight_grad(which, left, right):
        columns = right.shape[1] // unit

        def by_rows(r, carry):
            row = pl.multiple_of(r * chunk, chunk)
            turned_left[...] = left[:, pl.ds(row, chunk)].T

            def by_columns(c, carry):
                column = pl.multiple_of(c * unit, unit)
                index = r * columns + c
                slot = lax.rem(index, 2)

                @pl.when(index >= 2)
                def _():
                    stage_copy(which, slot, row, column, chunk, unit).wait()

                value = dot(turned_left[...], right[:, pl.ds(column, unit)], NN)
                stage[slot] = value.astype(BF16)
                stage_copy(which, slot, row, column, chunk, unit).start()
                return carry

            lax.fori_loop(0, columns, by_columns, 0)
            return carry

        lax.fori_loop(0, left.shape[1] // chunk, by_rows, 0)
        for slot in range(2):
            stage_copy(which, slot, 0, 0, chunk, unit).wait()

    def stage_copy(which, slot, row, column, height, width):
        return pltpu.make_async_copy(
            stage.at[slot], grads[which].at[pl.ds(row, height), pl.ds(column, width)],
            stage_sem.at[slot],
        )

    for which in range(4):
        holds(which, place.own, lambda: own_copy(which).start())
    tables[my_rows, :] = table_ref[...]
    normalize(x_ref, attention_gain, normed)
    rows_swap(0, normed).start()
    rows_swap(1, tables).start()
    begin(0)
    begin(1)

    def round_back(k):
        out_low[pl.ds(pl.multiple_of(mine + k, few), few), :] = back_ref[pl.ds(k, few), :].astype(BF16)

    loop(tokens, few, round_back)
    rows_swap(2, out_low).start()
    gain_sums[...] = jnp.zeros_like(gain_sums)

    late = [(1, top)] if top < 3 else [(1, h) for h in range(3, top + 1)]
    serve(0, 1)
    serve(1, 1)
    begin(2)
    for hop in range(2, top + 1):
        serve(0, hop)
        if (1, hop) not in late:
            serve(1, hop)
        if hop == 2:
            serve(2, 1)
    take_x(0)
    begin(3)
    pending = late + [(2 + w, h - w) for h in range(2, top + 1) for w in range(2)] + [(3, top)]
    for name in (0, 1):
        rows_swap(name, (normed, tables)[name]).wait_recv()

    raw[:, pl.ds(0, unit)] = dot(normed[...], w_qkv[:, pl.ds(0, unit)], NN)
    keys_values = dot(normed[...], w_qkv[:, pl.ds(unit, unit)], NN)
    raw[:, pl.ds(unit, chunk)] = keys_values[:, :chunk]
    low[:, pl.ds(unit + chunk, chunk)] = keys_values[:, chunk:].astype(BF16)
    serve(*pending.pop(0))

    def turned(value, rows):
        return value * tables[rows, pl.ds(0, HEAD_DIM)] + pltpu.roll(
            value, HEAD_DIM // 2, 1
        ) * tables[rows, pl.ds(HEAD_DIM, HEAD_DIM)]

    def turned_back(value, rows):
        return value * tables[rows, pl.ds(0, HEAD_DIM)] - pltpu.roll(
            value, HEAD_DIM // 2, 1
        ) * tables[rows, pl.ds(HEAD_DIM, HEAD_DIM)]

    def head_norm(first, count, gain):
        def act(k):
            for half in range(2):
                rows = pl.ds(half * tokens, tokens)
                columns = pl.ds(pl.multiple_of(first + k, HEAD_DIM), HEAD_DIM)
                value = raw[rows, columns]
                inverse = lax.rsqrt(jnp.mean(value * value, -1, keepdims=True) + EPSILON)
                low[rows, columns] = turned(value * inverse * gain[...], rows).astype(BF16)

        loop(count * HEAD_DIM, HEAD_DIM, act)

    head_norm(0, heads, query_gain)
    if pending:
        serve(*pending.pop(0))
    head_norm(unit, kv_heads, key_gain)

    def spans(k, half):
        queries = [pl.ds(pl.multiple_of((2 * k + g) * HEAD_DIM, HEAD_DIM), HEAD_DIM) for g in range(2)]
        keys = pl.ds(pl.multiple_of(unit + k * HEAD_DIM, HEAD_DIM), HEAD_DIM)
        values = pl.ds(pl.multiple_of(unit + unit // 2 + k * HEAD_DIM, HEAD_DIM), HEAD_DIM)
        return queries, keys, values, pl.ds(half * tokens, tokens)

    def stacked(ref, rows, columns):
        return jnp.concatenate([ref[rows, columns[0]], ref[rows, columns[1]]], 0)

    def attend(k, half):
        queries, keys, values, rows = spans(k, half)
        row_id = lax.broadcasted_iota(jnp.int32, (tokens, tokens), 0)
        column_id = lax.broadcasted_iota(jnp.int32, (tokens, tokens), 1)
        start = tables[rows, pl.ds(2 * HEAD_DIM, HEAD_DIM)][:, :1]
        allowed = (column_id <= row_id) & (column_id.astype(F32) >= start)
        masks = jnp.where(allowed, 0.0, -1e30)
        scores = dot(stacked(low, rows, queries), low[rows, keys], NT) * scale
        scores = scores + jnp.concatenate([masks, masks], 0)
        exponent = jnp.exp(scores - jnp.max(scores, -1, keepdims=True))
        value = exponent / jnp.sum(exponent, -1, keepdims=True)
        probs[k * 2 + half] = value
        result = dot(value.astype(BF16), low[rows, values], NN).astype(BF16)
        for g in range(2):
            context[rows, queries[g]] = result[g * tokens : (g + 1) * tokens]

    slots = 2 * kv_heads
    for k in range(kv_heads):
        for half in range(2):
            attend(k, half)
            slots -= 1
            for _ in range(-(-len(pending) // (slots + 1))):
                serve(*pending.pop(0))

    partial_product(3, 0, context, w_out, NN)
    part_swap(3, 0).wait_recv()

    def add_middle(k):
        middle[pl.ds(k, few), :] = x_ref[pl.ds(k, few), :] + whole_rows(k, 0)

    loop(tokens, few, add_middle)
    normalize(middle, feed_gain, hidden)
    rows_swap(4, hidden).start()
    while pending:
        serve(*pending.pop(0))
    take_x(2)
    rows_swap(4, hidden).wait_recv()
    rows_swap(2, out_low).wait_recv()

    def feed(k):
        span = pl.ds(k, chunk)
        pair = pl.ds(pl.multiple_of(2 * k, unit), unit)
        gate_up = dot(hidden[...], w_gu[:, pair], NN)
        gate, up = gate_up[:, :chunk], gate_up[:, chunk:]
        grad = dot(out_low[...], w_down[span, :], NT)
        sigmoid = 1.0 / (1.0 + jnp.exp(-gate))
        swish = gate * sigmoid
        activated[:, span] = (swish * up).astype(BF16)
        gu_back[:, pl.ds(pl.multiple_of(2 * k, chunk), chunk)] = (
            grad * up * (sigmoid + swish * (1.0 - sigmoid))
        ).astype(BF16)
        gu_back[:, pl.ds(pl.multiple_of(2 * k + chunk, chunk), chunk)] = (grad * swish).astype(BF16)

    loop(ff, chunk, feed)
    part_swap(3, 0).wait_send()
    partial_product(6, 0, gu_back, w_gu, NT)
    weight_grad(3, activated, out_low)
    part_swap(6, 0).wait_recv()

    def middle_back(k):
        back, gain_part = normalize_back(k, middle, feed_gain, whole_rows(k, 0))
        back = back_ref[pl.ds(k, few), :] + back
        input_grad[pl.ds(k, few), :] = back
        attended[pl.ds(pl.multiple_of(mine + k, few), few), :] = back.astype(BF16)
        gain_sums[1] += gain_part

    loop(tokens, few, middle_back)
    rows_swap(7, attended).start()
    partial_product(5, 1, activated, w_down, NN)
    weight_grad(2, hidden, gu_back)
    part_swap(5, 1).wait_recv()

    def add_output(k):
        output[pl.ds(k, few), :] = middle[pl.ds(k, few), :] + whole_rows(k, 1)

    loop(tokens, few, add_output)
    rows_swap(7, attended).wait_recv()

    grad_context[...] = dot(attended[...], w_out[...], NT).astype(BF16)
    weight_grad(1, context, attended)

    def head_back(rows, columns, gain, grad, index):
        value = raw[rows, columns]
        inverse = lax.rsqrt(jnp.mean(value * value, -1, keepdims=True) + EPSILON)
        unscaled = value * inverse
        grad = turned_back(grad, rows)
        gain_sums[index, :, pl.ds(0, HEAD_DIM)] += jnp.sum(
            (grad * unscaled).reshape(tokens // 8, 8, HEAD_DIM), 0
        )
        inner = grad * gain[...]
        back = inverse * (inner - unscaled * jnp.mean(inner * unscaled, -1, keepdims=True))
        low[rows, columns] = back.astype(BF16)

    def attend_back(k, half):
        queries, keys, values, rows = spans(k, half)
        prob = probs[k * 2 + half]
        above = stacked(grad_context, rows, queries)
        query_pair = stacked(low, rows, queries)
        grad_values = dot(prob.astype(BF16), above, TN)
        grad_probs = dot(above, low[rows, values], NT)
        grad_scores = prob * (grad_probs - jnp.sum(prob * grad_probs, -1, keepdims=True))
        grad_scores = grad_scores.astype(BF16)
        grad_queries = dot(grad_scores, low[rows, keys], NN) * scale
        grad_keys = dot(grad_scores, query_pair, TN) * scale
        for g in range(2):
            head_back(rows, queries[g], query_gain, grad_queries[g * tokens : (g + 1) * tokens], 2)
        head_back(rows, keys, key_gain, grad_keys, 3)
        low[rows, values] = grad_values.astype(BF16)

    def back_body(k, carry):
        for half in range(2):
            attend_back(k, half)
        return carry

    lax.fori_loop(0, kv_heads, back_body, 0)

    part_swap(6, 0).wait_send()
    partial_product(8, 0, low, w_qkv, NT)
    weight_grad(0, normed, low)
    part_swap(8, 0).wait_recv()

    def input_back(k):
        back, gain_part = normalize_back(k, x_ref, attention_gain, whole_rows(k, 0))
        input_grad[pl.ds(k, few), :] += back
        gain_sums[0] += gain_part

    loop(tokens, few, input_back)
    grad_attention[...] = jnp.sum(gain_sums[0], 0, keepdims=True)
    grad_feed[...] = jnp.sum(gain_sums[1], 0, keepdims=True)
    grad_query_gain[...] = jnp.sum(gain_sums[2, :, pl.ds(0, HEAD_DIM)], 0, keepdims=True)
    grad_key_gain[...] = jnp.sum(gain_sums[3, :, pl.ds(0, HEAD_DIM)], 0, keepdims=True)

    for index, ref in ((0, normed), (1, tables), (2, out_low), (4, hidden), (7, attended)):
        rows_swap(index, ref).wait_send()
    part_swap(5, 1).wait_send()
    part_swap(8, 0).wait_send()
    for which in range(4):
        for way in range(2):
            for hop in range(1, reach(which, way) + 1):
                ring_copy(which, way, hop, "wait_send")
                if SPREADS[which][1]:
                    x_copy(which, way, hop, place.x).wait_send()


def layer_pass(values, back, table, gains, shards, n):
    tokens, unit = values.shape
    top = n // 2
    dma = pltpu.SemaphoreType.DMA
    vmem = pltpu.VMEM
    both = 2 * tokens
    heads = unit // HEAD_DIM
    in_vmem = pl.BlockSpec(memory_space=pltpu.VMEM)
    row = lambda width: jax.ShapeDtypeStruct((1, width), F32)
    shapes = [(unit, 2 * unit), (unit, unit), (unit, 3 * unit), (3 * unit // 2, unit)]
    results = pl.pallas_call(
        functools.partial(layer_kernel, n, tokens, unit),
        out_shape=[jax.ShapeDtypeStruct((tokens, unit), F32)] * 2
        + [row(unit), row(unit), row(HEAD_DIM), row(HEAD_DIM)]
        + [jax.ShapeDtypeStruct(shape, BF16) for shape in shapes],
        in_specs=[in_vmem] * 7 + [ANY] * 4,
        out_specs=[in_vmem] * 6 + [ANY] * 4,
        scratch_shapes=[vmem(shape, BF16) for shape in shapes]
        + [
            vmem((both, unit), BF16),
            vmem((both, 3 * unit // 2), F32),
            vmem((both, 2 * unit), BF16),
            vmem((heads, both, tokens), F32),
            vmem((both, unit), BF16),
            vmem((both, unit), BF16),
            vmem((both, unit), BF16),
            vmem((both, unit), BF16),
            vmem((both, unit), BF16),
            vmem((both, 3 * unit // 2), BF16),
            vmem((both, 3 * unit), BF16),
            vmem((both, unit), F32),
            vmem((2, tokens, unit), BF16),
            vmem((2, tokens, unit), BF16),
            vmem((tokens, unit), F32),
            vmem((both, 3 * HEAD_DIM), F32),
            vmem((2, unit // 2, unit), BF16),
            vmem((unit // 2, both), BF16),
            vmem((4, 8, unit), F32),
            dma((4,)),
            dma((8 * top,)),
            dma((8 * top,)),
            dma((4 * top,)),
            dma((4 * top,)),
            dma((9,)),
            dma((9,)),
            dma((2,)),
        ],
        compiler_params=pltpu.CompilerParams(
            collective_id=0, has_side_effects=True, vmem_limit_bytes=56 * 2**20
        ),
    )(values, back, table, *gains, *shards)
    return results[:2], results[2:6], results[6:]


PHASES = ((DOWN, 3, "rows"), (GU, 3, "split"), (OUT, 2, "rows"), (QKV, 2, "wide"), (QKV, 1, "split"))
SPLIT = tuple(p for p, (_, _, how) in enumerate(PHASES) if how == "split")
WHOLE = tuple(p for p, (_, _, how) in enumerate(PHASES) if how != "split")

OWNERS = (
    (4, 1, False, 0, 3),
    (4, 1, False, 1, 3),
    (3, 2, False, 1, 6),
    (2, 2, True, 1, 5),
    (1, 3, False, 0, 5),
    (1, 3, False, 1, 1),
    (0, 3, True, 0, 1),
)
KEY, VALUE, QUERY, OUTM, GATE, UP, DOWNM = range(7)
RETURNS = (OUTM, KEY, VALUE, QUERY, DOWNM, GATE, UP)
TILE_SLOTS = 4
X_AHEAD = 4
LAND_AHEAD = 6


def summing_core(phase):
    return 1 if PHASES[phase][2] == "rows" else 0


def stage_order(n, core):
    rings = ((1.0, 1.5), (4.0, 2.7), (13.0, 1.1), (16.0, 1.8), (31.0, 0.9))
    crossings = {1: (-6.0, 2.3), 4: (15.0, 1.0)}
    finals = {0: 16.0, 2: 25.0, 3: 34.0}
    keys, needs = {}, {}
    for phase in range(len(PHASES)):
        first, step = rings[phase]
        for i in range(n):
            key = first + step * i * 8 / n
            if summing_core(phase) == core:
                keys["ring", phase, i] = key
                needs["ring", phase, i] = [("ring", phase, i - 1)] if i else []
                if phase in crossings:
                    needs["ring", phase, i].append(("x", phase, i))
            else:
                keys["land", phase, i] = key - 6.0
                needs["land", phase, i] = [("land", phase, i - 1)] if i else []
        if phase in crossings:
            first, step = crossings[phase]
            for i in range(n):
                keys["x", phase, i] = first + step * i * 8 / n
                needs["x", phase, i] = [("x", phase, i - 1)] if i else [("x", 1, n - 1)] * (phase == 4)
        elif summing_core(phase) == core:
            keys["final", phase, 0] = finals[phase]
            needs["final", phase, 0] = [("ring", phase, n - 1)]
    left, found = sorted(keys, key=lambda stage: (keys[stage], stage)), []
    while left:
        stage = next(stage for stage in left if all(need in found for need in needs[stage]))
        left.remove(stage)
        found.append(stage)
    return found


class Rows:
    def __init__(self):
        self.next = 0

    def take(self, rows):
        start = self.next
        self.next += rows
        return start


def layout(n, unit):
    base = unit // n
    top = n // 2
    place = {}
    rows = (Rows(), Rows())
    place["high"] = [None, rows[1].take(3 * unit)]
    for name in ("grad", "ahead"):
        place[name] = [rows[summing_core(p)].take(PHASES[p][1] * base) for p in range(len(PHASES))]
    for name in ("part", "other"):
        place[name] = {p: rows[summing_core(p)].take(PHASES[p][1] * base) for p in WHOLE}
    newton = Rows()
    newton.next = -(-rows[1].next // unit) * unit
    place["high"][0] = newton.take(3 * unit)
    place["poly"] = [newton.take(unit) for _ in range(2)]
    place["x_in"] = {p: [rows[0].take(PHASES[p][1] * base) for _ in range(n)] for p in SPLIT}
    place["own"] = [[rows[core].take(3 * base) for _ in range(TILE_SLOTS)] for core in range(2)]
    place["ring"], place["far"] = [], []
    for phase, (_, units, _) in enumerate(PHASES):
        take = rows[summing_core(phase)].take
        place["ring"].append([[take(units * base) for _ in range(top)] for _ in range(2)])
        place["far"].append(take(units * base))
    return place, max(rows[0].next, rows[1].next, newton.next)


def update_kernel(n, unit, *refs):
    grads, moments, gains_in = refs[:4], refs[4:11], refs[11]
    outs, orths, lands, gains_out = refs[12:16], refs[16:20], refs[20:24], refs[24]
    (
        pool, exact, gram, squares, gain_mine, gain_core, gain_x, gain_all,
        land_send, land_recv, tile_sem, x_send, x_recv, ring_send, ring_recv, part_send, part_recv,
        moment_sem, grad_local, grad_send, grad_recv, in_send, in_recv, in_local,
        out_send, out_recv, pass_send, pass_recv, gain_send, gain_recv,
    ) = refs[25:]
    place = Place(n)
    base = unit // n
    top = n // 2
    at, _ = layout(n, unit)
    cw, ccw = place.ring_neighbour(1), place.ring_neighbour(-1)
    ways = ((1, cw), (-1, ccw))
    side = [(place.x * 2 + core, lax.rem(place.own + k, n)) for k in range(1, n) for core in range(2)]
    across = [((1 - place.x) * 2 + core, place.own) for core in range(2)]
    greet(side + [place.core_partner] + across)
    order = [top]
    for distance in range(top - 1, 0, -1):
        order += [distance, -distance]
    order.append(0)
    moment = exact
    height = [units * base for _, units, _ in PHASES]
    moment_at = [sum(height[:phase]) for phase in range(len(PHASES))]
    owners = [
        (xs * 2 + 1, place.own_at(spot * n // 8)) for *_, xs, spot in OWNERS
    ]
    here = place.rep * n + place.own
    is_owner = [here == rep * n + own for rep, own in owners]

    def rows(start, size):
        if isinstance(start, int):
            return pl.ds(start, size)
        return pl.ds(pl.multiple_of(start, size), size)

    def block(start, size):
        return pool.at[rows(start, size)]

    def pieces_of(phase, x):
        array, units, how = PHASES[phase]
        half = unit // 2
        found = []
        for core in range(2):
            for b in range(units):
                if array == GU:
                    own_column = b * unit + x * half
                    column = x * 3 * unit + core * (3 * half) + b * half
                elif how == "wide":
                    own_column = b * half
                    column = core * unit + b * half
                else:
                    own_column = unit + x * half
                    column = (2 + x) * unit + core * half
                found.append((core, b, own_column, column))
        return found

    def columns(start):
        return pl.ds(pl.multiple_of(start, unit // 2), unit // 2)

    def in_block(start, core, b):
        return pool.at[pl.ds(start + b * base, base), pl.ds(core * (unit // 2), unit // 2)]

    def shard_rows(phase, own_index):
        if PHASES[phase][2] != "rows":
            return rows(own_index * base, base)
        return rows(lax.rem(own_index, top) * height[phase], height[phase])

    def landing(phase, own_index, act):
        if PHASES[phase][2] != "rows":
            act()
        else:
            pl.when(own_index // top != summing_core(phase))(act)

    def spread(source, target, size, send, recv, device):
        step = size

        def copy(k, count):
            return remote(block(source + k, count), block(target + k, count), send, recv, device)

        return Several(
            functools.partial(copy, 0, size),
            [functools.partial(copy, k, step) for k in range(0, size, step)],
        )

    def land_copy(phase, i, act):
        array, units, how = PHASES[phase]
        own_index = place.shard(order[i])
        span = shard_rows(phase, own_index)

        def copy(at_columns):
            return remote(
                grads[array].at[span, at_columns], lands[array].at[span, at_columns],
                land_send.at[phase * n + i], land_recv.at[phase * n + i], place.core_partner,
            )

        def do():
            if how == "rows":
                getattr(copy(pl.ds(0, unit)), act)()
            elif act == "start":
                for core, _, column, _ in pieces_of(phase, place.x):
                    if core == 1:
                        copy(columns(column)).start()
            else:
                getattr(copy(pl.ds(0, units * unit // 2)), act)()

        landing(phase, own_index, do)

    def x_index(phase, i):
        return SPLIT.index(phase) * n + i

    def x_copies(phase, i, core, act):
        index = x_index(phase, i)
        array, units, _ = PHASES[phase]
        span = shard_rows(phase, place.shard(order[i]))
        target = at["x_in"][phase][i]

        def copy(source, spot):
            return remote(
                source, spot, x_send.at[index], x_recv.at[core, index], ((1 - place.x) * 2, place.own)
            )

        if act == "start":
            for its_core, b, column, _ in pieces_of(phase, 1 - place.x):
                if its_core == core:
                    copy(grads[array].at[span, columns(column)], in_block(target, core, b)).start()
        else:
            spot = pool.at[pl.ds(target, height[phase]), pl.ds(core * (unit // 2), unit // 2)]
            getattr(copy(spot, spot), act)()

    def ring_copy(phase, way, distance, source, part):
        size = height[phase] // 2
        target = at["ring"][phase][way][distance - 1] + part * size
        index = ((phase * 2 + way) * top + distance - 1) * 2 + part
        return spread(
            source + part * size, target, size,
            ring_send.at[index], ring_recv.at[index], ways[way][1],
        )

    def ring_out(phase, distance, part):
        if distance == 0:
            return []
        if distance == top:
            return [ring_copy(phase, part, top, at["far"][phase], part)]
        way = 0 if distance > 0 else 1
        far = abs(distance)
        return [ring_copy(phase, way, far, at["ring"][phase][way][far], part)]

    def part_copy(phase):
        return spread(
            at["part"][phase], at["other"][phase], height[phase],
            part_send.at[WHOLE.index(phase)], part_recv.at[WHOLE.index(phase)], place.x_partner,
        )

    def gain_copy(src, dst, slot, device):
        return remote(src, dst, gain_send.at[slot], gain_recv.at[slot], device)

    def gain_core_copy():
        return gain_copy(gain_mine, gain_core, 0, place.core_partner)

    def gain_x_copy():
        return gain_copy(gain_core, gain_x, 1, place.x_partner)

    def gain_back_copy():
        return gain_copy(gain_mine, gain_x, 2, place.core_partner)

    def gain_ring(way, hop, distance):
        spot = gain_all.at[place.shard(distance)]
        return gain_copy(spot, spot, 3 + way * top + hop - 1, ways[way][1])

    def grad_place(phase, x):
        array = PHASES[phase][0]
        start = at["grad"][phase]
        if PHASES[phase][2] == "rows":
            return [(outs[array], block(start, height[phase]))]
        return [
            (outs[array].at[:, columns(column)], in_block(start, core, b))
            for core, b, _, column in pieces_of(phase, x)
        ]

    def grad_span(phase, x):
        array, units, how = PHASES[phase]
        if how == "rows":
            return outs[array]
        first = 0 if how == "wide" else x * units * unit
        if how == "split" and array == QKV:
            first = first + 2 * unit
        first = first if isinstance(first, int) else pl.multiple_of(first, unit)
        return outs[array].at[:, pl.ds(first, units * unit)]

    def grad_sent(phase, to, device, x):
        span = grad_span(phase, x)
        return remote(span, span, grad_send.at[phase, to], grad_recv.at[phase, to], device)

    def matrix_rows(matrix, own_index):
        phase, units, tall, _, _ = OWNERS[matrix]
        if tall:
            return [(0, own_index * units * base, units * base)]
        return [(k * base, k * unit + own_index * base, base) for k in range(units)]

    def matrix_span(matrix):
        phase, units, tall, xs, _ = OWNERS[matrix]
        array = PHASES[phase][0]
        if tall:
            return orths[array]
        start = min(column for _, _, _, column in pieces_of(phase, xs))
        return orths[array].at[:, pl.ds(start, units * unit)]

    def answer_parts(matrix, final, own_index):
        phase, units, tall, xs, _ = OWNERS[matrix]
        array = PHASES[phase][0]
        if tall:
            return [(block(final + own_index * units * base, units * base), orths[array])]
        return [
            (
                pool.at[
                    rows(final + b * unit + own_index * base, base),
                    pl.ds(core * (unit // 2), unit // 2),
                ],
                orths[array].at[:, columns(column)],
            )
            for core, b, _, column in pieces_of(phase, xs)
        ]

    def handed(matrix, to, device):
        span = matrix_span(matrix)
        return remote(span, span, pass_send.at[matrix, to], pass_recv.at[matrix, to], device)

    def answered(matrix, target):
        span = matrix_span(matrix)
        return remote(
            span, span, out_send.at[target], out_recv.at[matrix], (place.x * 2, target)
        )

    def summed(pieces, size, store):
        step = 16
        steps = 4 if size % (4 * step) == 0 else 1

        def body(k, carry):
            for j in range(steps):
                shift = (k * steps + j) * step
                total = None
                for start in pieces:
                    value = pool[rows_at(start, shift, step), :].astype(F32)
                    total = value if total is None else total + value
                store(shift, step, total)
            return carry

        lax.fori_loop(0, size // (step * steps), body, 0)

    def rows_at(start, shift, step):
        return pl.ds(pl.multiple_of(start + shift, step), step)

    def keep(start):
        def store(shift, step, total):
            pool[rows_at(start, shift, step), :] = total.astype(BF16)

        return store

    def load_tile(phase, i, slot):
        array, _, how = PHASES[phase]
        own_index = place.shard(order[i])
        span = shard_rows(phase, own_index)
        summing = summing_core(phase)

        def load(source, target):
            pltpu.make_async_copy(source, target, tile_sem.at[slot]).start()

        if how != "rows":
            for core, b, column, _ in pieces_of(phase, place.x):
                load(
                    (grads, lands)[core][array].at[span, columns(column)],
                    in_block(at["own"][summing][slot], core, b),
                )
            return
        for core in range(2):

            @pl.when(own_index // top == core)
            def _():
                load(
                    (lands, grads)[core == summing][array].at[span],
                    block(at["own"][summing][slot], height[phase]),
                )

    def prefetch(rings, index):
        if index < len(rings):
            _, phase, i = rings[index]
            land_copy(phase, i, "wait_recv")
            load_tile(phase, i, index % TILE_SLOTS)

    def moment_copies(phase, act):
        array, units, how = PHASES[phase]
        if how == "rows":
            act(moments[3 if array == OUT else 6], moment.at[pl.ds(moment_at[phase], height[phase])])
            return
        half = unit // 2
        for x in range(2):

            @pl.when(place.x == x)
            def _():
                for core, b, _, column in pieces_of(phase, x):
                    if array == GU:
                        source, first = 4 + x, x * 3 * unit
                    elif how == "wide":
                        source, first = 0, 0
                    else:
                        source, first = 1 + x, (2 + x) * unit
                    act(
                        moments[source].at[:, pl.ds(column - first, half)],
                        moment.at[pl.ds(moment_at[phase] + b * base, base), pl.ds(core * half, half)],
                    )

    def load_moment(phase):
        moment_copies(
            phase, lambda src, dst: pltpu.make_async_copy(src, dst, moment_sem.at[phase]).start()
        )

    def finish(phase, pieces):
        span = moment.at[pl.ds(moment_at[phase], height[phase])]
        pltpu.make_async_copy(span, span, moment_sem.at[phase]).wait()

        def store(shift, step, total):
            pool[rows_at(at["grad"][phase], shift, step), :] = total.astype(BF16)
            ahead = (1.0 + MOMENTUM) * total + MOMENTUM**2 * moment[
                rows_at(moment_at[phase], shift, step), :
            ]
            pool[rows_at(at["ahead"][phase], shift, step), :] = ahead.astype(BF16)

        summed(pieces, height[phase], store)
        for matrix, (its_phase, _, _, xs, _) in enumerate(OWNERS):
            if its_phase != phase:
                continue

            def hand_in(local):
                for source, target, size in matrix_rows(matrix, place.own):
                    source = block(at["ahead"][phase] + source, size)
                    target = block(at["high"][1] + target, size)
                    if local:
                        pltpu.make_async_copy(source, target, in_local).start()
                    else:
                        remote(
                            source, target, in_send.at[matrix], in_recv.at[place.own], owners[matrix]
                        ).start()

            if summing_core(phase) == 0:
                pl.when(place.x == xs)(functools.partial(hand_in, False))
            else:
                pl.when(is_owner[matrix])(functools.partial(hand_in, True))
                pl.when((place.x == xs) & (here != owners[matrix][0] * n + owners[matrix][1]))(
                    functools.partial(hand_in, False)
                )

        for target, source in grad_place(phase, place.x):
            pltpu.make_async_copy(source, target, grad_local.at[phase]).start()
            remote(
                source, target, grad_send.at[phase, 0], grad_recv.at[phase, 0], place.core_partner
            ).start()
            if phase in SPLIT:
                remote(
                    source, target, grad_send.at[phase, 1], grad_recv.at[phase, 1], place.x_partner
                ).start()

    def settle(phase):
        span = block(at["grad"][phase], height[phase])
        pltpu.make_async_copy(span, span, grad_local.at[phase]).wait()
        remote(
            span, span, grad_send.at[phase, 0], grad_recv.at[phase, 0], place.core_partner
        ).wait_send()
        if phase in SPLIT:
            remote(
                span, span, grad_send.at[phase, 1], grad_recv.at[phase, 1], place.x_partner
            ).wait_send()
        for matrix, (its_phase, units, _, xs, _) in enumerate(OWNERS):
            if its_phase != phase:
                continue

            sends = place.x == xs
            if summing_core(phase) == 1:
                sends = sends & (here != owners[matrix][0] * n + owners[matrix][1])

            @pl.when(sends)
            def _():
                span = block(at["high"][1], units * base)
                remote(
                    span, span, in_send.at[matrix], in_recv.at[0], place.core_partner
                ).wait_send()

    def stage_x(phase, i, core, paced):
        before = x_index(phase, i) - X_AHEAD
        if paced and before >= 0:
            x_copies(SPLIT[before // n], before % n, core, "wait_send")
        x_copies(phase, i, core, "start")

    def stage_ring(phase, i, slot):
        distance = order[i]
        start = at["own"][summing_core(phase)][slot]
        span = block(start, height[phase])
        pltpu.make_async_copy(span, span, tile_sem.at[slot]).wait()
        pieces = [start]
        if phase in SPLIT:
            for core in range(2):
                x_copies(phase, i, core, "wait_recv")
            pieces.append(at["x_in"][phase][i])
        size = height[phase]
        mid = size // 2
        if distance == 0:
            for way in range(2):
                held = at["ring"][phase][way][0]
                for part in range(2):
                    ring_copy(phase, way, 1, held, part).wait_recv()
                pieces.append(held)
            if phase in SPLIT:
                finish(phase, pieces)
            else:
                summed(pieces, size, keep(at["part"][phase]))
                part_copy(phase).start()
        else:
            way = 0 if distance > 0 else 1
            far = abs(distance)
            held = at["far"][phase] if far == top else at["ring"][phase][way][far]
            for part in (1 - way, way):
                starts = [start + part * mid for start in pieces]
                if far + 1 < top or (far + 1 == top and part == way):
                    ring_copy(phase, way, far + 1, held, part).wait_recv()
                    starts.append(held + part * mid)
                summed(starts, mid, keep(held + part * mid))
                for copy in ring_out(phase, distance, part):
                    copy.start()
    def ring_sent(phase):
        for distance in order:
            for part in range(2):
                for copy in ring_out(phase, distance, part):
                    copy.wait_send()

    unsent, x_left = [], {}

    def run(core):
        crossed = []
        stages = stage_order(n, core)
        rings = [stage for stage in stages if stage[0] == "ring"]
        landed = [stage for stage in stages if stage[0] == "land"]
        for phase in range(len(PHASES)):
            if summing_core(phase) == core:
                load_moment(phase)
        done, sent, hop = 0, 0, 0
        sums_left = len([stage for stage in stages if stage[0] in ("ring", "final")])
        for index in range(LAND_AHEAD):
            land_copy(*landed[index][1:], "start")
        for index in range(TILE_SLOTS - 1):
            prefetch(rings, index)
        for kind, phase, i in stages:
            paced = core == 0 or sums_left > 0
            sums_left -= kind in ("ring", "final")
            if kind == "x":
                stage_x(phase, i, core, paced)
                crossed.append((phase, i, paced))
            elif kind == "land":
                if paced:
                    land_copy(phase, i, "wait_send")
                else:
                    unsent.append((phase, i))
                if sent + LAND_AHEAD < len(landed):
                    land_copy(*landed[sent + LAND_AHEAD][1:], "start")
                sent += 1
            elif kind == "final":
                part_copy(phase).wait_recv()
                finish(phase, [at["part"][phase], at["other"][phase]])
            else:
                prefetch(rings, done + TILE_SLOTS - 1)
                stage_ring(phase, i, done % TILE_SLOTS)
                done += 1
                if core == 0 and hop <= top + 1:
                    gain_stage(hop)
                    hop += 1
        waited = {x_index(p, i) - X_AHEAD for p, i, paced in crossed if paced}
        x_left[core] = [(p, i) for p, i, _ in crossed if x_index(p, i) not in waited]

    def settle_all(core):
        for phase in range(len(PHASES)):
            if summing_core(phase) == core:
                settle(phase)
                if phase in WHOLE:
                    part_copy(phase).wait_send()
        for phase, i in x_left[core]:
            x_copies(phase, i, core, "wait_send")
        if core == 1:
            for phase, i in unsent:
                land_copy(phase, i, "wait_send")

    def take_sums(core):
        for phase in range(len(PHASES)):
            if summing_core(phase) != core:
                grad_sent(phase, 0, place.core_partner, place.x).wait_recv()
                if phase in SPLIT:
                    grad_sent(phase, 2, place.core_partner, 1 - place.x).wait_recv()

    def gain_stage(hop):
        if hop == 0:
            gain_core_copy().wait_recv()
            gain_core[...] = gain_mine[...] + gain_core[...]
            gain_x_copy().start()
            return
        if hop == 1:
            gain_x_copy().wait_recv()
            gain_all[place.own] = gain_core[...] + gain_x[...]
            for way in range(2):
                gain_ring(way, 1, 0).start()
        for way in range(2):
            if 1 < hop <= hops(n, way, 0) + 1:
                distance = -ways[way][0] * (hop - 1)
                gain_ring(way, hop - 1, distance).wait_recv()
                if hop <= hops(n, way, 0):
                    gain_ring(way, hop, distance).start()

    gain_mine[...] = gains_in[...]

    @pl.when(place.core == 0)
    def _():
        run(0)
        total = gain_all[0]
        for k in range(1, n):
            total = total + gain_all[k]
        gains_out[...] = total
        gain_mine[...] = total
        gain_back_copy().start()

        for phase in SPLIT:
            grad_sent(phase, 1, place.x_partner, 1 - place.x).wait_recv()
            grad_sent(phase, 2, place.core_partner, 1 - place.x).start()

        for matrix in RETURNS:
            xs = OWNERS[matrix][3]

            @pl.when(place.x == xs)
            def _():
                answered(matrix, place.own).wait_recv()
                handed(matrix, 0, place.x_partner).start()
                handed(matrix, 1, place.core_partner).start()

            @pl.when(place.x != xs)
            def _():
                handed(matrix, 0, place.x_partner).wait_recv()
                handed(matrix, 1, place.core_partner).start()

        for matrix, (*_, xs, _) in enumerate(OWNERS):
            handed(matrix, 1, place.core_partner).wait_send()

            @pl.when(place.x == xs)
            def _():
                handed(matrix, 0, place.x_partner).wait_send()

        take_sums(0)
        settle_all(0)
        for phase in range(len(PHASES)):
            if summing_core(phase) == 0:
                ring_sent(phase)
            if phase in SPLIT:
                grad_sent(phase, 2, place.core_partner, 1 - place.x).wait_send()
        gain_x_copy().wait_send()
        gain_back_copy().wait_send()
        for way in range(2):
            for h in range(1, hops(n, way, 0) + 1):
                gain_ring(way, h, -ways[way][0] * (h - 1)).wait_send()

    @pl.when(place.core == 1)
    def _():
        gain_core_copy().start()
        run(1)
        for phase in range(len(PHASES)):
            if summing_core(phase) == 1:
                ring_sent(phase)
        newton_part(n, unit, place, pool, exact, gram, squares, at, is_owner, in_recv, in_local)
        for matrix, (_, units, tall, _, _) in enumerate(OWNERS):

            @pl.when(is_owner[matrix])
            def _():
                final = at["high"][1 - NS_STEPS % 2 if tall else NS_STEPS % 2]

                def send(k, carry):
                    target = lax.rem(place.own + k, n)
                    for source, part in answer_parts(matrix, final, target):
                        remote(
                            source, part, out_send.at[target], out_recv.at[matrix],
                            (place.x * 2, target),
                        ).start()
                    return carry

                lax.fori_loop(0, n, send, 0)

                def sent(k, carry):
                    answered(matrix, lax.rem(place.own + k, n)).wait_send()
                    return carry

                lax.fori_loop(0, n, sent, 0)

        gain_core_copy().wait_send()
        gain_back_copy().wait_recv()
        gains_out[...] = gain_x[...]
        take_sums(1)
        settle_all(1)
        for matrix in RETURNS:
            handed(matrix, 1, place.core_partner).wait_recv()


def newton_part(n, unit, place, pool, exact, gram, squares, at, is_owner, in_recv, in_local):
    base = unit // n
    small = min(256, unit // 2)
    per = unit // small
    wide = unit // 2
    few = 32
    count, tall = 0, 0
    for mine, (_, units, lies_tall, _, _) in zip(is_owner, OWNERS):
        count = count + units * mine.astype(jnp.int32)
        tall = tall + int(lies_tall) * mine.astype(jnp.int32)
    high, poly = at["high"], at["poly"]

    def rows(start, size):
        return pl.ds(pl.multiple_of(start, size), size)

    for matrix, (phase, units, *_) in enumerate(OWNERS):

        @pl.when(is_owner[matrix])
        def _():
            span = pool.at[pl.ds(high[1], units * base)]
            inside = summing_core(phase) == 1
            if inside:
                pltpu.make_async_copy(span, span, in_local).wait()
            for k in range(1 if inside else 0, n):
                own_index = lax.rem(place.own + k, n)
                remote(
                    span, span, in_recv.at[own_index], in_recv.at[own_index], place.core_partner
                ).wait_recv()

    @pl.when(count > 0)
    def _():
        squares[...] = jnp.zeros_like(squares)

        def square(k, carry):
            part = pool[rows(high[1] + k * few, few), :].astype(F32)
            squares[...] += jnp.sum((part * part).reshape(few // 8, 8, unit), 0)
            return carry

        lax.fori_loop(0, count * (unit // few), square, 0)
        total = jnp.sum(jnp.sum(squares[...], 1, keepdims=True), 0, keepdims=True)
        inverse = 1.0 / (jnp.sqrt(total) + 1e-07)

        @pl.when(tall == 0)
        def _():
            def scale(k, carry):
                value = pool[rows(high[1] + k * few, few), :].astype(F32) * inverse
                exact[rows(k * few, few), :] = value
                pool[rows(high[0] + k * few, few), :] = value.astype(BF16)
                return carry

            lax.fori_loop(0, count * (unit // few), scale, 0)

        @pl.when(tall == 1)
        def _():
            def scale(k, carry):
                block, row = k // per, k % per
                for column in range(per):
                    part = pool[
                        rows(high[1] + k * small, small), pl.ds(column * small, small)
                    ].astype(F32)
                    value = (part * inverse).T
                    shift = block * unit + column * small
                    columns = rows(row * small, small)
                    exact[rows(shift, small), columns] = value
                    pool[rows(high[0] + shift, small), columns] = value.astype(BF16)
                return carry

            lax.fori_loop(0, count * per, scale, 0)

        def newton(step, carry):
            even = step % 2
            now = high[0] + even * (high[1] - high[0])
            later = high[1] - even * (high[1] - high[0])

            def keep_symmetric(to, chunk, value):
                pool[pl.ds(to, (chunk + 1) * wide), pl.ds(chunk * wide, wide)] = value.astype(BF16)
                if chunk == 1:
                    pool[pl.ds(to + wide, wide), pl.ds(0, wide)] = value[:wide].T.astype(BF16)

            for chunk in range(2):
                down = (chunk + 1) * wide

                def product(block):
                    left = pool[pl.ds(pl.multiple_of(now + block * unit, unit), down), :]
                    right = pool[rows(now + block * unit + chunk * wide, wide), :]
                    return lax.dot_general(
                        left, right, (((1,), (1,)), ((), ())), preferred_element_type=F32
                    )

                gram[:down, :] = product(0)

                def more(block, carry):
                    gram[:down, :] += product(block)
                    return carry

                lax.fori_loop(1, count, more, 0)
                keep_symmetric(poly[0], chunk, gram[:down, :])

            for chunk in range(2):
                down = (chunk + 1) * wide
                columns = pl.ds(chunk * wide, wide)
                squared = jnp.dot(
                    pool[pl.ds(poly[0], down), :], pool[pl.ds(poly[0], unit), columns],
                    preferred_element_type=F32,
                )
                plain = pool[pl.ds(poly[0], down), columns].astype(F32)
                keep_symmetric(poly[1], chunk, NEWTON_B * plain + NEWTON_C * squared)

            def advance(block, carry):
                for chunk in range(2):
                    columns = pl.ds(chunk * wide, wide)
                    value = NEWTON_A * exact[rows(block * unit, unit), columns] + jnp.dot(
                        pool[pl.ds(poly[1], unit), :],
                        pool[rows(now + block * unit, unit), columns],
                        preferred_element_type=F32,
                    )
                    exact[rows(block * unit, unit), columns] = value
                    pool[rows(later + block * unit, unit), columns] = value.astype(BF16)
                return carry

            lax.fori_loop(0, count, advance, 0)
            return carry

        lax.fori_loop(0, NS_STEPS, newton, 0)

        @pl.when(tall == 1)
        def _():
            free = high[1 - NS_STEPS % 2]
            factor = jnp.sqrt(jnp.full((1, 1), count, jnp.int32).astype(F32))

            def lay(k, carry):
                block, row = k // per, k % per
                for column in range(per):
                    columns = pl.ds(column * small, small)
                    part = exact[rows(k * small, small), columns]
                    pool[
                        rows(free + block * unit + column * small, small), rows(row * small, small)
                    ] = (part * factor).T.astype(BF16)
                return carry

            lax.fori_loop(0, count * per, lay, 0)


def update_all(grads, moments, gains, n, unit):
    top = n // 2
    dma = pltpu.SemaphoreType.DMA
    vmem = pltpu.VMEM
    _, pool_rows = layout(n, unit)
    phases = len(PHASES)
    shapes = [(unit // n, 4 * unit), (2 * unit // n, unit), (unit // n, 6 * unit), (3 * unit // n, unit)]
    own = [jax.ShapeDtypeStruct(shape, BF16) for shape in shapes]
    whole = [jax.ShapeDtypeStruct(grad.shape, BF16) for grad in grads]
    in_vmem = pl.BlockSpec(memory_space=pltpu.VMEM)
    results = pl.pallas_call(
        functools.partial(update_kernel, n, unit),
        out_shape=own + own + whole + [jax.ShapeDtypeStruct(gains.shape, F32)],
        in_specs=[ANY] * 11 + [in_vmem],
        out_specs=[ANY] * 12 + [in_vmem],
        scratch_shapes=[
            vmem((pool_rows, unit), BF16),
            vmem((3 * unit, unit), F32),
            vmem((unit, unit // 2), F32),
            vmem((8, unit), F32),
            vmem(gains.shape, F32),
            vmem(gains.shape, F32),
            vmem(gains.shape, F32),
            vmem((n,) + gains.shape, F32),
            dma((phases * n,)),
            dma((phases * n,)),
            dma((TILE_SLOTS,)),
            dma((2 * n,)),
            dma((2, 2 * n)),
            dma((4 * phases * top,)),
            dma((4 * phases * top,)),
            dma((len(WHOLE),)),
            dma((len(WHOLE),)),
            dma((phases,)),
            dma((phases,)),
            dma((phases, 3)),
            dma((phases, 3)),
            dma((7,)),
            dma((n,)),
            dma,
            dma((n,)),
            dma((7,)),
            dma((7, 2)),
            dma((7, 2)),
            dma((3 + 2 * top,)),
            dma((3 + 2 * top,)),
        ],
        compiler_params=pltpu.CompilerParams(
            collective_id=1, has_side_effects=True, vmem_limit_bytes=56 * 2**20
        ),
    )(*grads, *moments, gains)
    return results[:4], results[4:8], results[12]


def apply_kernel(unit, *refs):
    weights, moments, sums, orths = refs[:7], refs[7:14], refs[14:18], refs[18:22]
    new_weights, new_moments = refs[22:29], refs[29:36]
    weight, moment, grad, orth, weight_out, moment_out, load_sem, store_sem = refs[36:]
    slots, base = weight.shape[0], weight.shape[1]
    arrays = ((QKV, 0), (QKV, 2), (QKV, 3), (OUT, 0), (GU, 0), (GU, 3), (DOWN, 0))
    tiles = []
    for matrix, (array, first) in enumerate(arrays):
        for row in range(weights[matrix].shape[0] // base):
            for column in range(weights[matrix].shape[1] // unit):
                tiles.append((matrix, array, row * base, column * unit, (first + column) * unit))

    def loads(t):
        matrix, array, row, column, array_column = tiles[t]
        here = (pl.ds(row, base), pl.ds(column, unit))
        there = (pl.ds(row, base), pl.ds(array_column, unit))
        slot = t % slots
        return [
            pltpu.make_async_copy(source, target.at[slot], load_sem.at[slot, k])
            for k, (source, target) in enumerate(
                (
                    (weights[matrix].at[here], weight), (moments[matrix].at[here], moment),
                    (sums[array].at[there], grad), (orths[array].at[there], orth),
                )
            )
        ]

    def stores(t):
        matrix, _, row, column, _ = tiles[t]
        here = (pl.ds(row, base), pl.ds(column, unit))
        slot = t % slots
        return [
            pltpu.make_async_copy(weight_out.at[slot], new_weights[matrix].at[here], store_sem.at[slot, 0]),
            pltpu.make_async_copy(moment_out.at[slot], new_moments[matrix].at[here], store_sem.at[slot, 1]),
        ]

    for t in range(slots - 1):
        for copy in loads(t):
            copy.start()
    few = 16
    for t in range(len(tiles)):
        slot = t % slots
        if t + slots - 1 < len(tiles):
            for copy in loads(t + slots - 1):
                copy.start()
        for copy in loads(t):
            copy.wait()
        if t >= slots:
            for copy in stores(t - slots):
                copy.wait()

        def act(k, carry):
            rows = pl.ds(pl.multiple_of(k * few, few), few)
            weight_out[slot, rows, :] = weight[slot, rows, :] * (
                1.0 - LEARN_RATE * WEIGHT_DECAY
            ) - LEARN_RATE * orth[slot, rows, :].astype(F32)
            moment_out[slot, rows, :] = MOMENTUM * moment[slot, rows, :] + grad[
                slot, rows, :
            ].astype(F32)
            return carry

        lax.fori_loop(0, base // few, act, 0)
        for copy in stores(t):
            copy.start()
    for t in range(len(tiles) - slots, len(tiles)):
        for copy in stores(t):
            copy.wait()


def apply_all(weights, moments, sums, orths, n, unit):
    slots, base = 4, unit // n
    dma = pltpu.SemaphoreType.DMA
    vmem = pltpu.VMEM
    results = pl.pallas_call(
        functools.partial(apply_kernel, unit),
        out_shape=[jax.ShapeDtypeStruct(matrix.shape, F32) for matrix in weights] * 2,
        in_specs=[ANY] * 22,
        out_specs=[ANY] * 14,
        scratch_shapes=[
            vmem((slots, base, unit), F32),
            vmem((slots, base, unit), F32),
            vmem((slots, base, unit), BF16),
            vmem((slots, base, unit), BF16),
            vmem((slots, base, unit), F32),
            vmem((slots, base, unit), F32),
            dma((slots, 4)),
            dma((slots, 2)),
        ],
        compiler_params=pltpu.CompilerParams(vmem_limit_bytes=56 * 2**20),
    )(*weights, *moments, *sums, *orths)
    return results[:7], results[7:]


def body(
    layer_input,
    output_grad,
    lengths,
    attention_gain,
    feed_gain,
    query_gain,
    key_gain,
    query_weight,
    key_weight,
    value_weight,
    out_weight,
    gate_weight,
    up_weight,
    down_weight,
    query_moment,
    key_moment,
    value_moment,
    out_moment,
    gate_moment,
    up_moment,
    down_moment,
):
    owned = (
        query_weight, key_weight, value_weight, out_weight, gate_weight, up_weight, down_weight,
    )
    moments = (
        query_moment, key_moment, value_moment, out_moment, gate_moment, up_moment, down_moment,
    )
    n = lax.axis_size("own")
    unit = layer_input.shape[1]
    core = lax.axis_index("rep") % 2

    def halves(*matrices):
        parts = []
        for matrix in matrices:
            width = matrix.shape[1] // 2
            parts.append(lax.dynamic_slice_in_dim(matrix, core * width, width, 1))
        return jnp.concatenate(parts, 1).astype(BF16)

    step = unit // 2
    gate_half, up_half = halves(gate_weight), halves(up_weight)
    shards = (
        halves(query_weight, key_weight, value_weight),
        out_weight.astype(BF16),
        jnp.concatenate(
            [part[:, k * step : (k + 1) * step] for k in range(3) for part in (gate_half, up_half)], 1
        ),
        down_weight.astype(BF16),
    )
    row_count = layer_input.shape[0]
    _, positions = segments(lengths[0], row_count)
    cosine_table, sine_table = rope_tables(positions)
    starts = (jnp.arange(row_count, dtype=jnp.int32) - positions).astype(F32)
    table = jnp.concatenate(
        [
            cosine_table[:, 0], cosine_table[:, 0], -sine_table[:, 0], sine_table[:, 0],
            jnp.broadcast_to(starts[:, None], (row_count, HEAD_DIM)),
        ],
        1,
    )
    gain_rows = [gain[None, :] for gain in (attention_gain, feed_gain, query_gain, key_gain)]
    (block_output, input_grad), gain_grads, grads = layer_pass(
        layer_input, output_grad, table, gain_rows, shards, n
    )
    gains = jnp.concatenate([grad[0] for grad in gain_grads])
    gains = jnp.pad(gains, (0, 24 * 128 - gains.shape[0])).reshape(24, 128)
    reduced, orth, gain_sums = update_all(grads, moments, gains, n, unit)
    new_weights, moments_next = apply_all(owned, moments, reduced, orth, n, unit)
    gain_sums = gain_sums.reshape(-1)
    norm_grads = gain_sums[: 2 * unit].reshape(2, unit)
    head_grads = gain_sums[2 * unit : 2 * unit + 2 * HEAD_DIM].reshape(2, HEAD_DIM)
    return (block_output, input_grad, norm_grads, head_grads, *new_weights, *moments_next)


def solution(mesh):
    tokens, owned = P(("rep", "own"), None), P("own", None)
    return jax.shard_map(
        body,
        mesh=mesh,
        in_specs=(tokens,) * 3 + (P(),) * 4 + (owned,) * 14,
        out_specs=(tokens,) * 2 + (P(),) * 2 + (owned,) * 14,
        check_vma=False,
    )
```

```python
import functools

import jax
import jax.numpy as jnp
from jax import lax
from jax.experimental import pallas as pl
from jax.experimental.pallas import tpu as pltpu
from jax.sharding import PartitionSpec as P

HEADS = 16
KV_HEADS = 8
HEAD_DIM = 128
NS_STEPS = 5

EPSILON = 1e-06
ROPE_BASE = 1000000.0
MOMENTUM = 0.95
LEARN_RATE = 0.8
WEIGHT_DECAY = 0.01
NEWTON_A = 3.4445
NEWTON_B = -4.775
NEWTON_C = 2.0315

BF16 = jnp.bfloat16
F32 = jnp.float32
MESH = pl.DeviceIdType.MESH
ANY = pl.BlockSpec(memory_space=pltpu.HBM)

QKV, OUT, GU, DOWN = range(4)


def segments(lengths, row_count):
    seq_ends = jnp.cumsum(lengths)
    seq_starts = seq_ends - lengths
    row_ids = jnp.arange(row_count, dtype=jnp.int32)
    segment_ids = jnp.sum((row_ids[:, None] >= seq_ends[None, :]).astype(jnp.int32), 1)
    slot_ids = jnp.arange(lengths.shape[0], dtype=jnp.int32)
    row_starts = jnp.sum(
        jnp.where(segment_ids[:, None] == slot_ids[None, :], seq_starts[None, :], 0), 1
    )
    return (segment_ids, row_ids - row_starts)


def rope_tables(positions):
    inverse = ROPE_BASE ** (-jnp.arange(0, HEAD_DIM, 2, dtype=jnp.float32) / HEAD_DIM)
    angles = positions.astype(jnp.float32)[:, None] * inverse[None, :]
    return (jnp.cos(angles)[:, None, :], jnp.sin(angles)[:, None, :])


class Place:
    def __init__(self, n):
        self.n = n
        self.rep = lax.axis_index("rep")
        self.own = lax.axis_index("own")
        self.x = self.rep // 2
        self.core = self.rep % 2
        odd, pair = self.own % 2, self.own // 2
        self.ring = pair * (1 - odd) + odd * (n - 1 - pair)

    def own_at(self, ring):
        odd = ring // (self.n // 2)
        return 2 * (ring * (1 - odd) + odd * (self.n - 1 - ring)) + odd

    def shard(self, distance):
        return self.own_at(lax.rem(self.ring + distance + self.n, self.n))

    def ring_neighbour(self, way):
        return (self.rep, self.shard(way))

    @property
    def core_partner(self):
        return (self.x * 2 + 1 - self.core, self.own)

    @property
    def x_partner(self):
        return ((1 - self.x) * 2 + self.core, self.own)


def greet(devices):
    barrier = pltpu.get_barrier_semaphore()
    for device in devices:
        pl.semaphore_signal(barrier, inc=1, device_id=device, device_id_type=MESH)
    pl.semaphore_wait(barrier, len(devices))


class Several:
    def __init__(self, whole, copies):
        self.whole = whole
        self.copies = copies

    def start(self):
        for copy in self.copies:
            copy().start()

    def wait_send(self):
        self.whole().wait_send()

    def wait_recv(self):
        self.whole().wait_recv()


def remote(src, dst, send, recv, device):
    return pltpu.make_async_remote_copy(
        src_ref=src, dst_ref=dst, send_sem=send, recv_sem=recv, device_id=device, device_id_type=MESH
    )


def hops(n, way, kind):
    return n // 2 if (way == 0) == (kind == 0) else n // 2 - 1


SPREADS = ((QKV, True), (OUT, False), (GU, True), (DOWN, False))


def layer_kernel(n, tokens, unit, *refs):
    (
        x_ref, back_ref, table_ref, attention_gain, feed_gain, query_gain, key_gain,
    ) = refs[:7]
    shards = refs[7:11]
    output, input_grad, grad_attention, grad_feed, grad_query_gain, grad_key_gain = refs[11:17]
    grads = refs[17:21]
    (
        w_qkv, w_out, w_gu, w_down, normed, raw, low, probs, context, hidden, out_low, attended,
        grad_context, activated, gu_back, part, sent, got, middle, tables, stage, turned_left, gain_sums,
        local, ring_send, ring_recv, x_send, x_recv, swap_send, swap_recv, stage_sem,
    ) = refs[21:]
    weights = (w_qkv, w_out, w_gu, w_down)
    place = Place(n)
    top = n // 2
    cw, ccw = place.ring_neighbour(1), place.ring_neighbour(-1)
    ways = ((1, cw), (-1, ccw))
    greet([cw, ccw, place.core_partner, place.x_partner])
    both = 2 * tokens
    mine = pl.multiple_of(place.core * tokens, tokens)
    theirs = pl.multiple_of((1 - place.core) * tokens, tokens)
    my_rows, their_rows = pl.ds(mine, tokens), pl.ds(theirs, tokens)
    chunk = unit // 2
    ff = 3 * unit // 2
    few = 32
    base = unit // n
    heads = unit // HEAD_DIM
    kv_heads = heads // 2
    scale = HEAD_DIM ** (-0.5)

    def holds(which, own_index, act):
        if SPREADS[which][1]:
            act()
        else:
            pl.when(own_index // top == place.core)(act)

    def region(which, own_index, x, across):
        _, split = SPREADS[which]
        height = shards[which].shape[0]
        if split:
            parts = weights[which].shape[1] // unit
            width = unit if across or parts == 2 else 2 * unit
            first = x * (2 * unit) if across and parts == 3 else x * unit
            start = pl.multiple_of(own_index * height, height)
            return weights[which].at[pl.ds(start, height), pl.ds(pl.multiple_of(first, unit), width)]
        start = pl.multiple_of(lax.rem(own_index, top) * height, height)
        return weights[which].at[pl.ds(start, height)]

    def own_copy(which):
        height = shards[which].shape[0]
        index = place.own if SPREADS[which][1] else lax.rem(place.own, top)
        start = pl.multiple_of(index * height, height)
        return pltpu.make_async_copy(
            shards[which], weights[which].at[pl.ds(start, height)], local.at[which]
        )

    def reach(which, way):
        return hops(n, way, 0 if SPREADS[which][1] else 1)

    def ring_copy(which, way, hop, act):
        step, target = ways[way]
        own_index = place.shard(-step * (hop if act == "wait_recv" else hop - 1))
        spot = region(which, own_index, place.x, False)
        index = (which * 2 + way) * top + hop - 1

        def do():
            copy = remote(spot, spot, ring_send.at[index], ring_recv.at[index], target)
            getattr(copy, act)()

        holds(which, own_index, do)

    def send_on(which, way, hop):
        ring_copy(which, way, hop, "start")

    def x_copy(which, way, hop, x):
        spot = region(which, place.shard(-ways[way][0] * hop), x, True)
        index = (which // 2 * 2 + way) * top + hop - 1
        return remote(spot, spot, x_send.at[index], x_recv.at[index], place.x_partner)

    def serve(which, hop):
        for way in range(2):
            if hop > reach(which, way):
                continue
            ring_copy(which, way, hop, "wait_recv")
            if hop < reach(which, way):
                send_on(which, way, hop + 1)
            if SPREADS[which][1]:
                x_copy(which, way, hop, place.x).start()

    def begin(which):
        def act():
            own_copy(which).wait()

        holds(which, place.own, act)
        for way in range(2):
            if reach(which, way) > 0:
                send_on(which, way, 1)

    def take_x(which):
        for way in range(2):
            for hop in range(1, reach(which, way) + 1):
                x_copy(which, way, hop, 1 - place.x).wait_recv()

    def swap(index, src, dst):
        return remote(src, dst, swap_send.at[index], swap_recv.at[index], place.core_partner)

    def rows_swap(index, ref):
        return swap(index, ref.at[my_rows], ref.at[my_rows])

    def part_swap(index, slot):
        return swap(index, sent.at[slot], got.at[slot])

    def loop(size, step, act):
        def body(k, carry):
            act(pl.multiple_of(k * step, step))
            return carry

        lax.fori_loop(0, size // step, body, 0)

    def normalize(source, gain, target):
        def act(k):
            value = source[pl.ds(k, few), :]
            value = value * lax.rsqrt(jnp.mean(value * value, -1, keepdims=True) + EPSILON)
            target[pl.ds(pl.multiple_of(mine + k, few), few), :] = (value * gain[...]).astype(BF16)

        loop(tokens, few, act)

    def normalize_back(k, source, gain, grad):
        value = source[pl.ds(k, few), :]
        inverse = lax.rsqrt(jnp.mean(value * value, -1, keepdims=True) + EPSILON)
        unscaled = value * inverse
        inner = grad * gain[...]
        back = inverse * (inner - unscaled * jnp.mean(inner * unscaled, -1, keepdims=True))
        return back, jnp.sum((grad * unscaled).reshape(few // 8, 8, unit), 0)

    def dot(left, right, across):
        return lax.dot_general(left, right, ((across[0], across[1]), ((), ())), preferred_element_type=F32)

    NN, NT, TN = ((1,), (0,)), ((1,), (1,)), ((0,), (0,))

    def partial_product(index, slot, left, right, across):
        part[...] = dot(left[...], right[...], across)

        def pack(k):
            sent[slot, pl.ds(k, few), :] = part[
                pl.ds(pl.multiple_of(theirs + k, few), few), :
            ].astype(BF16)

        loop(tokens, few, pack)
        part_swap(index, slot).start()

    def whole_rows(k, slot):
        own = part[pl.ds(pl.multiple_of(mine + k, few), few), :]
        return own + got[slot, pl.ds(k, few), :].astype(F32)

    def weight_grad(which, left, right):
        columns = right.shape[1] // unit

        def by_rows(r, carry):
            row = pl.multiple_of(r * chunk, chunk)
            turned_left[...] = left[:, pl.ds(row, chunk)].T

            def by_columns(c, carry):
                column = pl.multiple_of(c * unit, unit)
                index = r * columns + c
                slot = lax.rem(index, 2)

                @pl.when(index >= 2)
                def _():
                    stage_copy(which, slot, row, column, chunk, unit).wait()

                value = dot(turned_left[...], right[:, pl.ds(column, unit)], NN)
                stage[slot] = value.astype(BF16)
                stage_copy(which, slot, row, column, chunk, unit).start()
                return carry

            lax.fori_loop(0, columns, by_columns, 0)
            return carry

        lax.fori_loop(0, left.shape[1] // chunk, by_rows, 0)
        for slot in range(2):
            stage_copy(which, slot, 0, 0, chunk, unit).wait()

    def stage_copy(which, slot, row, column, height, width):
        return pltpu.make_async_copy(
            stage.at[slot], grads[which].at[pl.ds(row, height), pl.ds(column, width)],
            stage_sem.at[slot],
        )

    for which in range(4):
        holds(which, place.own, lambda: own_copy(which).start())
    tables[my_rows, :] = table_ref[...]
    normalize(x_ref, attention_gain, normed)
    rows_swap(0, normed).start()
    rows_swap(1, tables).start()
    begin(0)
    begin(1)

    def round_back(k):
        out_low[pl.ds(pl.multiple_of(mine + k, few), few), :] = back_ref[pl.ds(k, few), :].astype(BF16)

    loop(tokens, few, round_back)
    rows_swap(2, out_low).start()
    gain_sums[...] = jnp.zeros_like(gain_sums)

    late = [(1, top)] if top < 3 else [(1, h) for h in range(3, top + 1)]
    serve(0, 1)
    serve(1, 1)
    begin(2)
    for hop in range(2, top + 1):
        serve(0, hop)
        if (1, hop) not in late:
            serve(1, hop)
        if hop == 2:
            serve(2, 1)
    take_x(0)
    begin(3)
    pending = late + [(2 + w, h - w) for h in range(2, top + 1) for w in range(2)] + [(3, top)]
    for name in (0, 1):
        rows_swap(name, (normed, tables)[name]).wait_recv()

    raw[:, pl.ds(0, unit)] = dot(normed[...], w_qkv[:, pl.ds(0, unit)], NN)
    keys_values = dot(normed[...], w_qkv[:, pl.ds(unit, unit)], NN)
    raw[:, pl.ds(unit, chunk)] = keys_values[:, :chunk]
    low[:, pl.ds(unit + chunk, chunk)] = keys_values[:, chunk:].astype(BF16)
    serve(*pending.pop(0))

    def turned(value, rows):
        return value * tables[rows, pl.ds(0, HEAD_DIM)] + pltpu.roll(
            value, HEAD_DIM // 2, 1
        ) * tables[rows, pl.ds(HEAD_DIM, HEAD_DIM)]

    def turned_back(value, rows):
        return value * tables[rows, pl.ds(0, HEAD_DIM)] - pltpu.roll(
            value, HEAD_DIM // 2, 1
        ) * tables[rows, pl.ds(HEAD_DIM, HEAD_DIM)]

    def head_norm(first, count, gain):
        def act(k):
            for half in range(2):
                rows = pl.ds(half * tokens, tokens)
                columns = pl.ds(pl.multiple_of(first + k, HEAD_DIM), HEAD_DIM)
                value = raw[rows, columns]
                inverse = lax.rsqrt(jnp.mean(value * value, -1, keepdims=True) + EPSILON)
                low[rows, columns] = turned(value * inverse * gain[...], rows).astype(BF16)

        loop(count * HEAD_DIM, HEAD_DIM, act)

    head_norm(0, heads, query_gain)
    if pending:
        serve(*pending.pop(0))
    head_norm(unit, kv_heads, key_gain)

    def spans(k, half):
        queries = [pl.ds(pl.multiple_of((2 * k + g) * HEAD_DIM, HEAD_DIM), HEAD_DIM) for g in range(2)]
        keys = pl.ds(pl.multiple_of(unit + k * HEAD_DIM, HEAD_DIM), HEAD_DIM)
        values = pl.ds(pl.multiple_of(unit + unit // 2 + k * HEAD_DIM, HEAD_DIM), HEAD_DIM)
        return queries, keys, values, pl.ds(half * tokens, tokens)

    def stacked(ref, rows, columns):
        return jnp.concatenate([ref[rows, columns[0]], ref[rows, columns[1]]], 0)

    def attend(k, half):
        queries, keys, values, rows = spans(k, half)
        row_id = lax.broadcasted_iota(jnp.int32, (tokens, tokens), 0)
        column_id = lax.broadcasted_iota(jnp.int32, (tokens, tokens), 1)
        start = tables[rows, pl.ds(2 * HEAD_DIM, HEAD_DIM)][:, :1]
        allowed = (column_id <= row_id) & (column_id.astype(F32) >= start)
        masks = jnp.where(allowed, 0.0, -1e30)
        scores = dot(stacked(low, rows, queries), low[rows, keys], NT) * scale
        scores = scores + jnp.concatenate([masks, masks], 0)
        exponent = jnp.exp(scores - jnp.max(scores, -1, keepdims=True))
        value = exponent / jnp.sum(exponent, -1, keepdims=True)
        probs[k * 2 + half] = value
        result = dot(value.astype(BF16), low[rows, values], NN).astype(BF16)
        for g in range(2):
            context[rows, queries[g]] = result[g * tokens : (g + 1) * tokens]

    slots = 2 * kv_heads
    for k in range(kv_heads):
        for half in range(2):
            attend(k, half)
            slots -= 1
            for _ in range(-(-len(pending) // (slots + 1))):
                serve(*pending.pop(0))

    partial_product(3, 0, context, w_out, NN)
    part_swap(3, 0).wait_recv()

    def add_middle(k):
        middle[pl.ds(k, few), :] = x_ref[pl.ds(k, few), :] + whole_rows(k, 0)

    loop(tokens, few, add_middle)
    normalize(middle, feed_gain, hidden)
    rows_swap(4, hidden).start()
    while pending:
        serve(*pending.pop(0))
    take_x(2)
    rows_swap(4, hidden).wait_recv()
    rows_swap(2, out_low).wait_recv()

    def feed(k):
        span = pl.ds(k, chunk)
        pair = pl.ds(pl.multiple_of(2 * k, unit), unit)
        gate_up = dot(hidden[...], w_gu[:, pair], NN)
        gate, up = gate_up[:, :chunk], gate_up[:, chunk:]
        grad = dot(out_low[...], w_down[span, :], NT)
        sigmoid = 1.0 / (1.0 + jnp.exp(-gate))
        swish = gate * sigmoid
        activated[:, span] = (swish * up).astype(BF16)
        gu_back[:, pl.ds(pl.multiple_of(2 * k, chunk), chunk)] = (
            grad * up * (sigmoid + swish * (1.0 - sigmoid))
        ).astype(BF16)
        gu_back[:, pl.ds(pl.multiple_of(2 * k + chunk, chunk), chunk)] = (grad * swish).astype(BF16)

    loop(ff, chunk, feed)
    part_swap(3, 0).wait_send()
    partial_product(6, 0, gu_back, w_gu, NT)
    weight_grad(3, activated, out_low)
    part_swap(6, 0).wait_recv()

    def middle_back(k):
        back, gain_part = normalize_back(k, middle, feed_gain, whole_rows(k, 0))
        back = back_ref[pl.ds(k, few), :] + back
        input_grad[pl.ds(k, few), :] = back
        attended[pl.ds(pl.multiple_of(mine + k, few), few), :] = back.astype(BF16)
        gain_sums[1] += gain_part

    loop(tokens, few, middle_back)
    rows_swap(7, attended).start()
    partial_product(5, 1, activated, w_down, NN)
    weight_grad(2, hidden, gu_back)
    part_swap(5, 1).wait_recv()

    def add_output(k):
        output[pl.ds(k, few), :] = middle[pl.ds(k, few), :] + whole_rows(k, 1)

    loop(tokens, few, add_output)
    rows_swap(7, attended).wait_recv()

    grad_context[...] = dot(attended[...], w_out[...], NT).astype(BF16)
    weight_grad(1, context, attended)

    def head_back(rows, columns, gain, grad, index):
        value = raw[rows, columns]
        inverse = lax.rsqrt(jnp.mean(value * value, -1, keepdims=True) + EPSILON)
        unscaled = value * inverse
        grad = turned_back(grad, rows)
        gain_sums[index, :, pl.ds(0, HEAD_DIM)] += jnp.sum(
            (grad * unscaled).reshape(tokens // 8, 8, HEAD_DIM), 0
        )
        inner = grad * gain[...]
        back = inverse * (inner - unscaled * jnp.mean(inner * unscaled, -1, keepdims=True))
        low[rows, columns] = back.astype(BF16)

    def attend_back(k, half):
        queries, keys, values, rows = spans(k, half)
        prob = probs[k * 2 + half]
        above = stacked(grad_context, rows, queries)
        query_pair = stacked(low, rows, queries)
        grad_values = dot(prob.astype(BF16), above, TN)
        grad_probs = dot(above, low[rows, values], NT)
        grad_scores = prob * (grad_probs - jnp.sum(prob * grad_probs, -1, keepdims=True))
        grad_scores = grad_scores.astype(BF16)
        grad_queries = dot(grad_scores, low[rows, keys], NN) * scale
        grad_keys = dot(grad_scores, query_pair, TN) * scale
        for g in range(2):
            head_back(rows, queries[g], query_gain, grad_queries[g * tokens : (g + 1) * tokens], 2)
        head_back(rows, keys, key_gain, grad_keys, 3)
        low[rows, values] = grad_values.astype(BF16)

    def back_body(k, carry):
        for half in range(2):
            attend_back(k, half)
        return carry

    lax.fori_loop(0, kv_heads, back_body, 0)

    part_swap(6, 0).wait_send()
    partial_product(8, 0, low, w_qkv, NT)
    weight_grad(0, normed, low)
    part_swap(8, 0).wait_recv()

    def input_back(k):
        back, gain_part = normalize_back(k, x_ref, attention_gain, whole_rows(k, 0))
        input_grad[pl.ds(k, few), :] += back
        gain_sums[0] += gain_part

    loop(tokens, few, input_back)
    grad_attention[...] = jnp.sum(gain_sums[0], 0, keepdims=True)
    grad_feed[...] = jnp.sum(gain_sums[1], 0, keepdims=True)
    grad_query_gain[...] = jnp.sum(gain_sums[2, :, pl.ds(0, HEAD_DIM)], 0, keepdims=True)
    grad_key_gain[...] = jnp.sum(gain_sums[3, :, pl.ds(0, HEAD_DIM)], 0, keepdims=True)

    for index, ref in ((0, normed), (1, tables), (2, out_low), (4, hidden), (7, attended)):
        rows_swap(index, ref).wait_send()
    part_swap(5, 1).wait_send()
    part_swap(8, 0).wait_send()
    for which in range(4):
        for way in range(2):
            for hop in range(1, reach(which, way) + 1):
                ring_copy(which, way, hop, "wait_send")
                if SPREADS[which][1]:
                    x_copy(which, way, hop, place.x).wait_send()


def layer_pass(values, back, table, gains, shards, n):
    tokens, unit = values.shape
    top = n // 2
    dma = pltpu.SemaphoreType.DMA
    vmem = pltpu.VMEM
    both = 2 * tokens
    heads = unit // HEAD_DIM
    in_vmem = pl.BlockSpec(memory_space=pltpu.VMEM)
    row = lambda width: jax.ShapeDtypeStruct((1, width), F32)
    shapes = [(unit, 2 * unit), (unit, unit), (unit, 3 * unit), (3 * unit // 2, unit)]
    results = pl.pallas_call(
        functools.partial(layer_kernel, n, tokens, unit),
        out_shape=[jax.ShapeDtypeStruct((tokens, unit), F32)] * 2
        + [row(unit), row(unit), row(HEAD_DIM), row(HEAD_DIM)]
        + [jax.ShapeDtypeStruct(shape, BF16) for shape in shapes],
        in_specs=[in_vmem] * 7 + [ANY] * 4,
        out_specs=[in_vmem] * 6 + [ANY] * 4,
        scratch_shapes=[vmem(shape, BF16) for shape in shapes]
        + [
            vmem((both, unit), BF16),
            vmem((both, 3 * unit // 2), F32),
            vmem((both, 2 * unit), BF16),
            vmem((heads, both, tokens), F32),
            vmem((both, unit), BF16),
            vmem((both, unit), BF16),
            vmem((both, unit), BF16),
            vmem((both, unit), BF16),
            vmem((both, unit), BF16),
            vmem((both, 3 * unit // 2), BF16),
            vmem((both, 3 * unit), BF16),
            vmem((both, unit), F32),
            vmem((2, tokens, unit), BF16),
            vmem((2, tokens, unit), BF16),
            vmem((tokens, unit), F32),
            vmem((both, 3 * HEAD_DIM), F32),
            vmem((2, unit // 2, unit), BF16),
            vmem((unit // 2, both), BF16),
            vmem((4, 8, unit), F32),
            dma((4,)),
            dma((8 * top,)),
            dma((8 * top,)),
            dma((4 * top,)),
            dma((4 * top,)),
            dma((9,)),
            dma((9,)),
            dma((2,)),
        ],
        compiler_params=pltpu.CompilerParams(
            collective_id=0, has_side_effects=True, vmem_limit_bytes=56 * 2**20
        ),
    )(values, back, table, *gains, *shards)
    return results[:2], results[2:6], results[6:]


PHASES = (
    (DOWN, 3, "rows"), (GU, 2, "split"), (GU, 2, "wide"), (OUT, 2, "rows"), (QKV, 2, "wide"),
    (QKV, 1, "split"),
)
SPLIT = tuple(p for p, (_, _, how) in enumerate(PHASES) if how == "split")
WHOLE = tuple(p for p, (_, _, how) in enumerate(PHASES) if how != "split")

OWNERS = (
    (1, False, 0, 3, ((5, 0, 0, 1),)),
    (1, False, 1, 3, ((5, 0, 0, 1),)),
    (2, False, 1, 6, ((4, 0, 0, 2),)),
    (2, True, 1, 5, ((3, 0, 0, 2),)),
    (3, False, 0, 5, ((1, 0, 0, 2), (2, 0, 2, 1))),
    (3, False, 1, 1, ((1, 0, 0, 2), (2, 1, 2, 1))),
    (3, True, 0, 1, ((0, 0, 0, 3),)),
)
KEY, VALUE, QUERY, OUTM, GATE, UP, DOWNM = range(7)
RETURNS = (OUTM, KEY, VALUE, QUERY, DOWNM, GATE, UP)
TILE_SLOTS = 3
X_AHEAD = 3
LAND_AHEAD = 6


def summing_core(phase):
    return 1 if PHASES[phase][2] == "rows" else 0


def stage_order(n, core):
    rings = ((3.0, 4.5), (12.0, 7.5), (4.0, 4.5), (38.0, 3.5), (36.0, 6.0), (72.0, 4.0))
    crossings = {1: (-10.0, 7.0), 5: (52.0, 3.7)}
    finals = {0: 48.0, 2: 52.0, 3: 76.0, 4: 92.0}
    keys, needs = {}, {}
    for phase in range(len(PHASES)):
        first, step = rings[phase]
        for i in range(n):
            key = first + step * i * 8 / n
            if summing_core(phase) == core:
                keys["ring", phase, i] = key
                needs["ring", phase, i] = [("ring", phase, i - 1)] if i else []
                if phase in crossings:
                    needs["ring", phase, i].append(("x", phase, i))
            else:
                keys["land", phase, i] = key - 16.0
                needs["land", phase, i] = [("land", phase, i - 1)] if i else []
        if phase in crossings:
            first, step = crossings[phase]
            for i in range(n):
                keys["x", phase, i] = first + step * i * 8 / n
                needs["x", phase, i] = [("x", phase, i - 1)] if i else [("x", 1, n - 1)] * (phase == 5)
        elif summing_core(phase) == core:
            keys["final", phase, 0] = finals[phase]
            needs["final", phase, 0] = [("ring", phase, n - 1)]
    left, found = sorted(keys, key=lambda stage: (keys[stage], stage)), []
    while left:
        stage = next(stage for stage in left if all(need in found for need in needs[stage]))
        left.remove(stage)
        found.append(stage)
    return found


class Rows:
    def __init__(self):
        self.next = 0

    def take(self, rows):
        start = self.next
        self.next += rows
        return start


def layout(n, unit):
    base = unit // n
    top = n // 2
    place = {}
    rows = (Rows(), Rows())
    place["high"] = [None, rows[1].take(3 * unit)]
    for name in ("grad", "ahead"):
        place[name] = [rows[summing_core(p)].take(PHASES[p][1] * base) for p in range(len(PHASES))]
    for name in ("part", "other"):
        place[name] = {p: rows[summing_core(p)].take(PHASES[p][1] * base) for p in WHOLE}
    newton = Rows()
    newton.next = -(-rows[1].next // unit) * unit
    place["high"][0] = newton.take(3 * unit)
    place["poly"] = [newton.take(unit) for _ in range(2)]
    place["x_in"] = {p: [rows[0].take(PHASES[p][1] * base) for _ in range(n)] for p in SPLIT}
    most = [max(u for p, (_, u, _) in enumerate(PHASES) if summing_core(p) == c) for c in range(2)]
    place["own"] = [[rows[c].take(most[c] * base) for _ in range(TILE_SLOTS)] for c in range(2)]
    place["ring"], place["far"] = [], []
    for phase, (_, units, _) in enumerate(PHASES):
        take = rows[summing_core(phase)].take
        place["ring"].append([[take(units * base) for _ in range(top)] for _ in range(2)])
        place["far"].append(take(units * base))
    return place, max(rows[0].next, rows[1].next, newton.next)


def update_kernel(n, unit, *refs):
    grads, moments, gains_in = refs[:4], refs[4:11], refs[11]
    outs, orths, lands, gains_out = refs[12:16], refs[16:20], refs[20:24], refs[24]
    (
        pool, exact, gram, squares, gain_mine, gain_core, gain_x, gain_all,
        land_send, land_recv, tile_sem, x_send, x_recv, ring_send, ring_recv, part_send, part_recv,
        moment_sem, grad_local, grad_send, grad_recv, in_send, in_recv, in_local,
        out_send, out_recv, pass_send, pass_recv, gain_send, gain_recv,
    ) = refs[25:]
    place = Place(n)
    base = unit // n
    top = n // 2
    at, _ = layout(n, unit)
    cw, ccw = place.ring_neighbour(1), place.ring_neighbour(-1)
    ways = ((1, cw), (-1, ccw))
    side = [(place.x * 2 + core, lax.rem(place.own + k, n)) for k in range(1, n) for core in range(2)]
    across = [((1 - place.x) * 2 + core, place.own) for core in range(2)]
    greet(side + [place.core_partner] + across)
    order = [top]
    for distance in range(top - 1, 0, -1):
        order += [distance, -distance]
    order.append(0)
    moment = exact
    height = [units * base for _, units, _ in PHASES]
    moment_at = [sum(height[:phase]) for phase in range(len(PHASES))]
    owners = [
        (xs * 2 + 1, place.own_at(spot * n // 8)) for _, _, xs, spot, _ in OWNERS
    ]
    here = place.rep * n + place.own
    is_owner = [here == rep * n + own for rep, own in owners]

    def rows(start, size):
        if isinstance(start, int):
            return pl.ds(start, size)
        return pl.ds(pl.multiple_of(start, size), size)

    def block(start, size):
        return pool.at[rows(start, size)]

    def pieces_of(phase, x):
        array, units, how = PHASES[phase]
        half = unit // 2
        found = []
        for core in range(2):
            for b in range(units):
                if array == GU and how == "wide":
                    own_column = 2 * unit + b * half
                    column = b * 3 * unit + core * (3 * half) + 2 * half
                elif array == GU:
                    own_column = b * unit + x * half
                    column = x * 3 * unit + core * (3 * half) + b * half
                elif how == "wide":
                    own_column = b * half
                    column = core * unit + b * half
                else:
                    own_column = unit + x * half
                    column = (2 + x) * unit + core * half
                found.append((core, b, own_column, column))
        return found

    def columns(start):
        return pl.ds(pl.multiple_of(start, unit // 2), unit // 2)

    def in_block(start, core, b):
        return pool.at[pl.ds(start + b * base, base), pl.ds(core * (unit // 2), unit // 2)]

    def shard_rows(phase, own_index):
        if PHASES[phase][2] != "rows":
            return rows(own_index * base, base)
        return rows(lax.rem(own_index, top) * height[phase], height[phase])

    def landing(phase, own_index, act):
        if PHASES[phase][2] != "rows":
            act()
        else:
            pl.when(own_index // top != summing_core(phase))(act)

    def spread(source, target, size, send, recv, device):
        step = size

        def copy(k, count):
            return remote(block(source + k, count), block(target + k, count), send, recv, device)

        return Several(
            functools.partial(copy, 0, size),
            [functools.partial(copy, k, step) for k in range(0, size, step)],
        )

    def land_copy(phase, i, act):
        array, units, how = PHASES[phase]
        own_index = place.shard(order[i])
        span = shard_rows(phase, own_index)

        def copy(at_columns):
            return remote(
                grads[array].at[span, at_columns], lands[array].at[span, at_columns],
                land_send.at[phase * n + i], land_recv.at[phase * n + i], place.core_partner,
            )

        def do():
            if how == "rows":
                getattr(copy(pl.ds(0, unit)), act)()
            elif act == "start":
                for core, _, column, _ in pieces_of(phase, place.x):
                    if core == 1:
                        copy(columns(column)).start()
            else:
                getattr(copy(pl.ds(0, units * unit // 2)), act)()

        landing(phase, own_index, do)

    def x_index(phase, i):
        return SPLIT.index(phase) * n + i

    def x_copies(phase, i, core, act):
        index = x_index(phase, i)
        array, units, _ = PHASES[phase]
        span = shard_rows(phase, place.shard(order[i]))
        target = at["x_in"][phase][i]

        def copy(source, spot):
            return remote(
                source, spot, x_send.at[index], x_recv.at[core, index], ((1 - place.x) * 2, place.own)
            )

        if act == "start":
            for its_core, b, column, _ in pieces_of(phase, 1 - place.x):
                if its_core == core:
                    copy(grads[array].at[span, columns(column)], in_block(target, core, b)).start()
        else:
            spot = pool.at[pl.ds(target, height[phase]), pl.ds(core * (unit // 2), unit // 2)]
            getattr(copy(spot, spot), act)()

    def ring_copy(phase, way, distance, source, part):
        size = height[phase] // 2
        target = at["ring"][phase][way][distance - 1] + part * size
        index = ((phase * 2 + way) * top + distance - 1) * 2 + part
        return spread(
            source + part * size, target, size,
            ring_send.at[index], ring_recv.at[index], ways[way][1],
        )

    def ring_out(phase, distance, part):
        if distance == 0:
            return []
        if distance == top:
            return [ring_copy(phase, part, top, at["far"][phase], part)]
        way = 0 if distance > 0 else 1
        far = abs(distance)
        return [ring_copy(phase, way, far, at["ring"][phase][way][far], part)]

    def part_copy(phase):
        return spread(
            at["part"][phase], at["other"][phase], height[phase],
            part_send.at[WHOLE.index(phase)], part_recv.at[WHOLE.index(phase)], place.x_partner,
        )

    def gain_copy(src, dst, slot, device):
        return remote(src, dst, gain_send.at[slot], gain_recv.at[slot], device)

    def gain_core_copy():
        return gain_copy(gain_mine, gain_core, 0, place.core_partner)

    def gain_x_copy():
        return gain_copy(gain_core, gain_x, 1, place.x_partner)

    def gain_back_copy():
        return gain_copy(gain_mine, gain_x, 2, place.core_partner)

    def gain_ring(way, hop, distance):
        spot = gain_all.at[place.shard(distance)]
        return gain_copy(spot, spot, 3 + way * top + hop - 1, ways[way][1])

    def grad_place(phase, x):
        array = PHASES[phase][0]
        start = at["grad"][phase]
        if PHASES[phase][2] == "rows":
            return [(outs[array], block(start, height[phase]))]
        return [
            (outs[array].at[:, columns(column)], in_block(start, core, b))
            for core, b, _, column in pieces_of(phase, x)
        ]

    def grad_sent(phase, to, device, x, act):
        array, units, how = PHASES[phase]
        if act == "start":
            if array == GU:
                ranges = [(x * 3 * unit + core * 3 * unit // 2, units * unit // 2) for core in range(2)]
            else:
                ranges = [((2 + x) * unit, unit)]
        else:
            ranges = [(0, units * unit)]
        for first, width in ranges:
            if not isinstance(first, int):
                first = pl.multiple_of(first, unit // 2)
            span = outs[array].at[:, pl.ds(first, width)] if how != "rows" else outs[array]
            copy = remote(span, span, grad_send.at[phase, to], grad_recv.at[phase, to], device)
            getattr(copy, act)()

    def matrix_rows(matrix, part, own_index):
        units, tall, _, _, parts = OWNERS[matrix]
        _, first, to, count = parts[part]
        if tall:
            return [(0, own_index * units * base, units * base)]
        return [((first + k) * base, (to + k) * unit + own_index * base, base) for k in range(count)]

    def matrix_columns(matrix):
        _, _, xs, _, parts = OWNERS[matrix]
        return [
            (core, to + b - first, column)
            for phase, first, to, count in parts
            for core, b, _, column in pieces_of(phase, xs)
            if first <= b < first + count
        ]

    def matrix_span(matrix):
        units, tall, _, _, parts = OWNERS[matrix]
        array = PHASES[parts[0][0]][0]
        if tall:
            return orths[array]
        start = min(column for _, _, column in matrix_columns(matrix))
        return orths[array].at[:, pl.ds(start, units * unit)]

    def answer_parts(matrix, final, own_index):
        units, tall, _, _, parts = OWNERS[matrix]
        array = PHASES[parts[0][0]][0]
        if tall:
            return [(block(final + own_index * units * base, units * base), orths[array])]
        return [
            (
                pool.at[
                    rows(final + b * unit + own_index * base, base),
                    pl.ds(core * (unit // 2), unit // 2),
                ],
                orths[array].at[:, columns(column)],
            )
            for core, b, column in matrix_columns(matrix)
        ]

    def handed(matrix, to, device):
        span = matrix_span(matrix)
        return remote(span, span, pass_send.at[matrix, to], pass_recv.at[matrix, to], device)

    def answered(matrix, target):
        span = matrix_span(matrix)
        return remote(
            span, span, out_send.at[target], out_recv.at[matrix], (place.x * 2, target)
        )

    def summed(pieces, size, store):
        step = 16
        steps = 4 if size % (4 * step) == 0 else 1

        def body(k, carry):
            for j in range(steps):
                shift = (k * steps + j) * step
                total = None
                for start in pieces:
                    value = pool[rows_at(start, shift, step), :].astype(F32)
                    total = value if total is None else total + value
                store(shift, step, total)
            return carry

        lax.fori_loop(0, size // (step * steps), body, 0)

    def rows_at(start, shift, step):
        return pl.ds(pl.multiple_of(start + shift, step), step)

    def keep(start):
        def store(shift, step, total):
            pool[rows_at(start, shift, step), :] = total.astype(BF16)

        return store

    def load_tile(phase, i, slot):
        array, _, how = PHASES[phase]
        own_index = place.shard(order[i])
        span = shard_rows(phase, own_index)
        summing = summing_core(phase)

        def load(source, target):
            pltpu.make_async_copy(source, target, tile_sem.at[slot]).start()

        if how != "rows":
            for core, b, column, _ in pieces_of(phase, place.x):
                load(
                    (grads, lands)[core][array].at[span, columns(column)],
                    in_block(at["own"][summing][slot], core, b),
                )
            return
        for core in range(2):

            @pl.when(own_index // top == core)
            def _():
                load(
                    (lands, grads)[core == summing][array].at[span],
                    block(at["own"][summing][slot], height[phase]),
                )

    def prefetch(rings, index):
        if index < len(rings):
            _, phase, i = rings[index]
            land_copy(phase, i, "wait_recv")
            load_tile(phase, i, index % TILE_SLOTS)

    def moment_copies(phase, act):
        array, units, how = PHASES[phase]
        if how == "rows":
            act(moments[3 if array == OUT else 6], moment.at[pl.ds(moment_at[phase], height[phase])])
            return
        half = unit // 2
        for x in range(2):

            @pl.when(place.x == x)
            def _():
                for core, b, _, column in pieces_of(phase, x):
                    if array == GU:
                        side = b if how == "wide" else x
                        source, first = 4 + side, side * 3 * unit
                    elif how == "wide":
                        source, first = 0, 0
                    else:
                        source, first = 1 + x, (2 + x) * unit
                    act(
                        moments[source].at[:, pl.ds(column - first, half)],
                        moment.at[pl.ds(moment_at[phase] + b * base, base), pl.ds(core * half, half)],
                    )

    def load_moment(phase):
        moment_copies(
            phase, lambda src, dst: pltpu.make_async_copy(src, dst, moment_sem.at[phase]).start()
        )

    def parts_in(phase):
        return [
            (matrix, part, owner[2])
            for matrix, owner in enumerate(OWNERS)
            for part, (its_phase, *_) in enumerate(owner[4])
            if its_phase == phase
        ]

    def finish(phase, pieces):
        span = moment.at[pl.ds(moment_at[phase], height[phase])]
        pltpu.make_async_copy(span, span, moment_sem.at[phase]).wait()

        def store(shift, step, total):
            pool[rows_at(at["grad"][phase], shift, step), :] = total.astype(BF16)
            ahead = (1.0 + MOMENTUM) * total + MOMENTUM**2 * moment[
                rows_at(moment_at[phase], shift, step), :
            ]
            pool[rows_at(at["ahead"][phase], shift, step), :] = ahead.astype(BF16)

        summed(pieces, height[phase], store)
        for matrix, part, xs in parts_in(phase):

            def hand_in(local):
                for source, target, size in matrix_rows(matrix, part, place.own):
                    source = block(at["ahead"][phase] + source, size)
                    target = block(at["high"][1] + target, size)
                    if local:
                        pltpu.make_async_copy(source, target, in_local).start()
                    else:
                        remote(
                            source, target, in_send.at[matrix, part], in_recv.at[place.own],
                            owners[matrix],
                        ).start()

            if summing_core(phase) == 0:
                pl.when(place.x == xs)(functools.partial(hand_in, False))
            else:
                pl.when(is_owner[matrix])(functools.partial(hand_in, True))
                pl.when((place.x == xs) & (here != owners[matrix][0] * n + owners[matrix][1]))(
                    functools.partial(hand_in, False)
                )

        for target, source in grad_place(phase, place.x):
            pltpu.make_async_copy(source, target, grad_local.at[phase]).start()
            remote(
                source, target, grad_send.at[phase, 0], grad_recv.at[phase, 0], place.core_partner
            ).start()
            if phase in SPLIT:
                remote(
                    source, target, grad_send.at[phase, 1], grad_recv.at[phase, 1], place.x_partner
                ).start()

    def settle(phase):
        span = block(at["grad"][phase], height[phase])
        pltpu.make_async_copy(span, span, grad_local.at[phase]).wait()
        remote(
            span, span, grad_send.at[phase, 0], grad_recv.at[phase, 0], place.core_partner
        ).wait_send()
        if phase in SPLIT:
            remote(
                span, span, grad_send.at[phase, 1], grad_recv.at[phase, 1], place.x_partner
            ).wait_send()
        for matrix, part, xs in parts_in(phase):
            sends = place.x == xs
            if summing_core(phase) == 1:
                sends = sends & (here != owners[matrix][0] * n + owners[matrix][1])

            @pl.when(sends)
            def _():
                span = block(at["high"][1], sum(size for *_, size in matrix_rows(matrix, part, 0)))
                remote(
                    span, span, in_send.at[matrix, part], in_recv.at[0], place.core_partner
                ).wait_send()

    def stage_x(phase, i, core, paced):
        before = x_index(phase, i) - X_AHEAD
        if paced and before >= 0:
            x_copies(SPLIT[before // n], before % n, core, "wait_send")
        x_copies(phase, i, core, "start")

    def stage_ring(phase, i, slot):
        distance = order[i]
        start = at["own"][summing_core(phase)][slot]
        span = block(start, height[phase])
        pltpu.make_async_copy(span, span, tile_sem.at[slot]).wait()
        pieces = [start]
        if phase in SPLIT:
            for core in range(2):
                x_copies(phase, i, core, "wait_recv")
            pieces.append(at["x_in"][phase][i])
        size = height[phase]
        mid = size // 2
        if distance == 0:
            for way in range(2):
                held = at["ring"][phase][way][0]
                for part in range(2):
                    ring_copy(phase, way, 1, held, part).wait_recv()
                pieces.append(held)
            if phase in SPLIT:
                finish(phase, pieces)
            else:
                summed(pieces, size, keep(at["part"][phase]))
                part_copy(phase).start()
        else:
            way = 0 if distance > 0 else 1
            far = abs(distance)
            held = at["far"][phase] if far == top else at["ring"][phase][way][far]
            for part in (1 - way, way):
                starts = [start + part * mid for start in pieces]
                if far + 1 < top or (far + 1 == top and part == way):
                    ring_copy(phase, way, far + 1, held, part).wait_recv()
                    starts.append(held + part * mid)
                summed(starts, mid, keep(held + part * mid))
                for copy in ring_out(phase, distance, part):
                    copy.start()
    def ring_sent(phase):
        for distance in order:
            for part in range(2):
                for copy in ring_out(phase, distance, part):
                    copy.wait_send()

    unsent, x_left = [], {}

    def run(core):
        crossed = []
        stages = stage_order(n, core)
        rings = [stage for stage in stages if stage[0] == "ring"]
        landed = [stage for stage in stages if stage[0] == "land"]
        for phase in range(len(PHASES)):
            if summing_core(phase) == core:
                load_moment(phase)
        done, sent, hop = 0, 0, 0
        sums_left = len([stage for stage in stages if stage[0] in ("ring", "final")])
        for index in range(LAND_AHEAD):
            land_copy(*landed[index][1:], "start")
        for index in range(TILE_SLOTS - 1):
            prefetch(rings, index)
        for kind, phase, i in stages:
            paced = core == 0 or sums_left > 0
            sums_left -= kind in ("ring", "final")
            if kind == "x":
                stage_x(phase, i, core, paced)
                crossed.append((phase, i, paced))
            elif kind == "land":
                if paced:
                    land_copy(phase, i, "wait_send")
                else:
                    unsent.append((phase, i))
                if sent + LAND_AHEAD < len(landed):
                    land_copy(*landed[sent + LAND_AHEAD][1:], "start")
                sent += 1
            elif kind == "final":
                part_copy(phase).wait_recv()
                finish(phase, [at["part"][phase], at["other"][phase]])
            else:
                prefetch(rings, done + TILE_SLOTS - 1)
                stage_ring(phase, i, done % TILE_SLOTS)
                done += 1
                if core == 0 and hop <= top + 1:
                    gain_stage(hop)
                    hop += 1
        waited = {x_index(p, i) - X_AHEAD for p, i, paced in crossed if paced}
        x_left[core] = [(p, i) for p, i, _ in crossed if x_index(p, i) not in waited]

    def settle_all(core):
        for phase in range(len(PHASES)):
            if summing_core(phase) == core:
                settle(phase)
                if phase in WHOLE:
                    part_copy(phase).wait_send()
        for phase, i in x_left[core]:
            x_copies(phase, i, core, "wait_send")
        if core == 1:
            for phase, i in unsent:
                land_copy(phase, i, "wait_send")

    def take_sums(core):
        for phase in range(len(PHASES)):
            if summing_core(phase) != core:
                grad_sent(phase, 0, place.core_partner, place.x, "wait_recv")
                if phase in SPLIT:
                    grad_sent(phase, 2, place.core_partner, 1 - place.x, "wait_recv")

    def gain_stage(hop):
        if hop == 0:
            gain_core_copy().wait_recv()
            gain_core[...] = gain_mine[...] + gain_core[...]
            gain_x_copy().start()
            return
        if hop == 1:
            gain_x_copy().wait_recv()
            gain_all[place.own] = gain_core[...] + gain_x[...]
            for way in range(2):
                gain_ring(way, 1, 0).start()
        for way in range(2):
            if 1 < hop <= hops(n, way, 0) + 1:
                distance = -ways[way][0] * (hop - 1)
                gain_ring(way, hop - 1, distance).wait_recv()
                if hop <= hops(n, way, 0):
                    gain_ring(way, hop, distance).start()

    gain_mine[...] = gains_in[...]

    @pl.when(place.core == 0)
    def _():
        run(0)
        total = gain_all[0]
        for k in range(1, n):
            total = total + gain_all[k]
        gains_out[...] = total
        gain_mine[...] = total
        gain_back_copy().start()

        for phase in SPLIT:
            grad_sent(phase, 1, place.x_partner, 1 - place.x, "wait_recv")
            grad_sent(phase, 2, place.core_partner, 1 - place.x, "start")

        for matrix in RETURNS:
            xs = OWNERS[matrix][2]

            @pl.when(place.x == xs)
            def _():
                answered(matrix, place.own).wait_recv()
                handed(matrix, 0, place.x_partner).start()
                handed(matrix, 1, place.core_partner).start()

            @pl.when(place.x != xs)
            def _():
                handed(matrix, 0, place.x_partner).wait_recv()
                handed(matrix, 1, place.core_partner).start()

        for matrix, (_, _, xs, _, _) in enumerate(OWNERS):
            handed(matrix, 1, place.core_partner).wait_send()

            @pl.when(place.x == xs)
            def _():
                handed(matrix, 0, place.x_partner).wait_send()

        take_sums(0)
        settle_all(0)
        for phase in range(len(PHASES)):
            if summing_core(phase) == 0:
                ring_sent(phase)
            if phase in SPLIT:
                grad_sent(phase, 2, place.core_partner, 1 - place.x, "wait_send")
        gain_x_copy().wait_send()
        gain_back_copy().wait_send()
        for way in range(2):
            for h in range(1, hops(n, way, 0) + 1):
                gain_ring(way, h, -ways[way][0] * (h - 1)).wait_send()

    @pl.when(place.core == 1)
    def _():
        gain_core_copy().start()
        run(1)
        for phase in range(len(PHASES)):
            if summing_core(phase) == 1:
                ring_sent(phase)
        newton_part(n, unit, place, pool, exact, gram, squares, at, is_owner, in_recv, in_local)
        for matrix, (units, tall, *_) in enumerate(OWNERS):

            @pl.when(is_owner[matrix])
            def _():
                final = at["high"][1 - NS_STEPS % 2 if tall else NS_STEPS % 2]

                def send(k, carry):
                    target = lax.rem(place.own + k, n)
                    for source, part in answer_parts(matrix, final, target):
                        remote(
                            source, part, out_send.at[target], out_recv.at[matrix],
                            (place.x * 2, target),
                        ).start()
                    return carry

                lax.fori_loop(0, n, send, 0)

                def sent(k, carry):
                    answered(matrix, lax.rem(place.own + k, n)).wait_send()
                    return carry

                lax.fori_loop(0, n, sent, 0)

        gain_core_copy().wait_send()
        gain_back_copy().wait_recv()
        gains_out[...] = gain_x[...]
        take_sums(1)
        settle_all(1)
        for matrix in RETURNS:
            handed(matrix, 1, place.core_partner).wait_recv()


def newton_part(n, unit, place, pool, exact, gram, squares, at, is_owner, in_recv, in_local):
    base = unit // n
    small = min(256, unit // 2)
    per = unit // small
    wide = unit // 2
    few = 32
    count, tall = 0, 0
    for mine, (units, lies_tall, *_) in zip(is_owner, OWNERS):
        count = count + units * mine.astype(jnp.int32)
        tall = tall + int(lies_tall) * mine.astype(jnp.int32)
    high, poly = at["high"], at["poly"]

    def rows(start, size):
        return pl.ds(pl.multiple_of(start, size), size)

    for matrix, (units, _, _, _, parts) in enumerate(OWNERS):

        @pl.when(is_owner[matrix])
        def _():
            span = pool.at[pl.ds(high[1], units * base)]
            inside = summing_core(parts[0][0]) == 1
            if inside:
                pltpu.make_async_copy(span, span, in_local).wait()
            for k in range(1 if inside else 0, n):
                own_index = lax.rem(place.own + k, n)
                remote(
                    span, span, in_recv.at[own_index], in_recv.at[own_index], place.core_partner
                ).wait_recv()

    @pl.when(count > 0)
    def _():
        squares[...] = jnp.zeros_like(squares)

        def square(k, carry):
            part = pool[rows(high[1] + k * few, few), :].astype(F32)
            squares[...] += jnp.sum((part * part).reshape(few // 8, 8, unit), 0)
            return carry

        lax.fori_loop(0, count * (unit // few), square, 0)
        total = jnp.sum(jnp.sum(squares[...], 1, keepdims=True), 0, keepdims=True)
        inverse = 1.0 / (jnp.sqrt(total) + 1e-07)

        @pl.when(tall == 0)
        def _():
            def scale(k, carry):
                value = pool[rows(high[1] + k * few, few), :].astype(F32) * inverse
                exact[rows(k * few, few), :] = value
                pool[rows(high[0] + k * few, few), :] = value.astype(BF16)
                return carry

            lax.fori_loop(0, count * (unit // few), scale, 0)

        @pl.when(tall == 1)
        def _():
            def scale(k, carry):
                block, row = k // per, k % per
                for column in range(per):
                    part = pool[
                        rows(high[1] + k * small, small), pl.ds(column * small, small)
                    ].astype(F32)
                    value = (part * inverse).T
                    shift = block * unit + column * small
                    columns = rows(row * small, small)
                    exact[rows(shift, small), columns] = value
                    pool[rows(high[0] + shift, small), columns] = value.astype(BF16)
                return carry

            lax.fori_loop(0, count * per, scale, 0)

        def newton(step, carry):
            even = step % 2
            now = high[0] + even * (high[1] - high[0])
            later = high[1] - even * (high[1] - high[0])

            def keep_symmetric(to, chunk, value):
                pool[pl.ds(to, (chunk + 1) * wide), pl.ds(chunk * wide, wide)] = value.astype(BF16)
                if chunk == 1:
                    pool[pl.ds(to + wide, wide), pl.ds(0, wide)] = value[:wide].T.astype(BF16)

            for chunk in range(2):
                down = (chunk + 1) * wide

                def product(block):
                    left = pool[pl.ds(pl.multiple_of(now + block * unit, unit), down), :]
                    right = pool[rows(now + block * unit + chunk * wide, wide), :]
                    return lax.dot_general(
                        left, right, (((1,), (1,)), ((), ())), preferred_element_type=F32
                    )

                gram[:down, :] = product(0)

                def more(block, carry):
                    gram[:down, :] += product(block)
                    return carry

                lax.fori_loop(1, count, more, 0)
                keep_symmetric(poly[0], chunk, gram[:down, :])

            for chunk in range(2):
                down = (chunk + 1) * wide
                columns = pl.ds(chunk * wide, wide)
                squared = jnp.dot(
                    pool[pl.ds(poly[0], down), :], pool[pl.ds(poly[0], unit), columns],
                    preferred_element_type=F32,
                )
                plain = pool[pl.ds(poly[0], down), columns].astype(F32)
                keep_symmetric(poly[1], chunk, NEWTON_B * plain + NEWTON_C * squared)

            def advance(block, carry):
                for chunk in range(2):
                    columns = pl.ds(chunk * wide, wide)
                    value = NEWTON_A * exact[rows(block * unit, unit), columns] + jnp.dot(
                        pool[pl.ds(poly[1], unit), :],
                        pool[rows(now + block * unit, unit), columns],
                        preferred_element_type=F32,
                    )
                    exact[rows(block * unit, unit), columns] = value
                    pool[rows(later + block * unit, unit), columns] = value.astype(BF16)
                return carry

            lax.fori_loop(0, count, advance, 0)
            return carry

        lax.fori_loop(0, NS_STEPS, newton, 0)

        @pl.when(tall == 1)
        def _():
            free = high[1 - NS_STEPS % 2]
            factor = jnp.sqrt(jnp.full((1, 1), count, jnp.int32).astype(F32))

            def lay(k, carry):
                block, row = k // per, k % per
                for column in range(per):
                    columns = pl.ds(column * small, small)
                    part = exact[rows(k * small, small), columns]
                    pool[
                        rows(free + block * unit + column * small, small), rows(row * small, small)
                    ] = (part * factor).T.astype(BF16)
                return carry

            lax.fori_loop(0, count * per, lay, 0)


def update_all(grads, moments, gains, n, unit):
    top = n // 2
    dma = pltpu.SemaphoreType.DMA
    vmem = pltpu.VMEM
    _, pool_rows = layout(n, unit)
    phases = len(PHASES)
    shapes = [(unit // n, 4 * unit), (2 * unit // n, unit), (unit // n, 6 * unit), (3 * unit // n, unit)]
    own = [jax.ShapeDtypeStruct(shape, BF16) for shape in shapes]
    whole = [jax.ShapeDtypeStruct(grad.shape, BF16) for grad in grads]
    in_vmem = pl.BlockSpec(memory_space=pltpu.VMEM)
    results = pl.pallas_call(
        functools.partial(update_kernel, n, unit),
        out_shape=own + own + whole + [jax.ShapeDtypeStruct(gains.shape, F32)],
        in_specs=[ANY] * 11 + [in_vmem],
        out_specs=[ANY] * 12 + [in_vmem],
        scratch_shapes=[
            vmem((pool_rows, unit), BF16),
            vmem((3 * unit, unit), F32),
            vmem((unit, unit // 2), F32),
            vmem((8, unit), F32),
            vmem(gains.shape, F32),
            vmem(gains.shape, F32),
            vmem(gains.shape, F32),
            vmem((n,) + gains.shape, F32),
            dma((phases * n,)),
            dma((phases * n,)),
            dma((TILE_SLOTS,)),
            dma((2 * n,)),
            dma((2, 2 * n)),
            dma((4 * phases * top,)),
            dma((4 * phases * top,)),
            dma((len(WHOLE),)),
            dma((len(WHOLE),)),
            dma((phases,)),
            dma((phases,)),
            dma((phases, 3)),
            dma((phases, 3)),
            dma((7, 2)),
            dma((n,)),
            dma,
            dma((n,)),
            dma((7,)),
            dma((7, 2)),
            dma((7, 2)),
            dma((3 + 2 * top,)),
            dma((3 + 2 * top,)),
        ],
        compiler_params=pltpu.CompilerParams(
            collective_id=1, has_side_effects=True, vmem_limit_bytes=56 * 2**20
        ),
    )(*grads, *moments, gains)
    return results[:4], results[4:8], results[12]


def apply_kernel(unit, *refs):
    weights, moments, sums, orths = refs[:7], refs[7:14], refs[14:18], refs[18:22]
    new_weights, new_moments = refs[22:29], refs[29:36]
    weight, moment, grad, orth, weight_out, moment_out, load_sem, store_sem = refs[36:]
    slots, base = weight.shape[0], weight.shape[1]
    arrays = ((QKV, 0), (QKV, 2), (QKV, 3), (OUT, 0), (GU, 0), (GU, 3), (DOWN, 0))
    tiles = []
    for matrix, (array, first) in enumerate(arrays):
        for row in range(weights[matrix].shape[0] // base):
            for column in range(weights[matrix].shape[1] // unit):
                tiles.append((matrix, array, row * base, column * unit, (first + column) * unit))

    def loads(t):
        matrix, array, row, column, array_column = tiles[t]
        here = (pl.ds(row, base), pl.ds(column, unit))
        there = (pl.ds(row, base), pl.ds(array_column, unit))
        slot = t % slots
        return [
            pltpu.make_async_copy(source, target.at[slot], load_sem.at[slot, k])
            for k, (source, target) in enumerate(
                (
                    (weights[matrix].at[here], weight), (moments[matrix].at[here], moment),
                    (sums[array].at[there], grad), (orths[array].at[there], orth),
                )
            )
        ]

    def stores(t):
        matrix, _, row, column, _ = tiles[t]
        here = (pl.ds(row, base), pl.ds(column, unit))
        slot = t % slots
        return [
            pltpu.make_async_copy(weight_out.at[slot], new_weights[matrix].at[here], store_sem.at[slot, 0]),
            pltpu.make_async_copy(moment_out.at[slot], new_moments[matrix].at[here], store_sem.at[slot, 1]),
        ]

    for t in range(slots - 1):
        for copy in loads(t):
            copy.start()
    few = 16
    for t in range(len(tiles)):
        slot = t % slots
        if t + slots - 1 < len(tiles):
            for copy in loads(t + slots - 1):
                copy.start()
        for copy in loads(t):
            copy.wait()
        if t >= slots:
            for copy in stores(t - slots):
                copy.wait()

        def act(k, carry):
            rows = pl.ds(pl.multiple_of(k * few, few), few)
            weight_out[slot, rows, :] = weight[slot, rows, :] * (
                1.0 - LEARN_RATE * WEIGHT_DECAY
            ) - LEARN_RATE * orth[slot, rows, :].astype(F32)
            moment_out[slot, rows, :] = MOMENTUM * moment[slot, rows, :] + grad[
                slot, rows, :
            ].astype(F32)
            return carry

        lax.fori_loop(0, base // few, act, 0)
        for copy in stores(t):
            copy.start()
    for t in range(len(tiles) - slots, len(tiles)):
        for copy in stores(t):
            copy.wait()


def apply_all(weights, moments, sums, orths, n, unit):
    slots, base = 4, unit // n
    dma = pltpu.SemaphoreType.DMA
    vmem = pltpu.VMEM
    results = pl.pallas_call(
        functools.partial(apply_kernel, unit),
        out_shape=[jax.ShapeDtypeStruct(matrix.shape, F32) for matrix in weights] * 2,
        in_specs=[ANY] * 22,
        out_specs=[ANY] * 14,
        scratch_shapes=[
            vmem((slots, base, unit), F32),
            vmem((slots, base, unit), F32),
            vmem((slots, base, unit), BF16),
            vmem((slots, base, unit), BF16),
            vmem((slots, base, unit), F32),
            vmem((slots, base, unit), F32),
            dma((slots, 4)),
            dma((slots, 2)),
        ],
        compiler_params=pltpu.CompilerParams(vmem_limit_bytes=56 * 2**20),
    )(*weights, *moments, *sums, *orths)
    return results[:7], results[7:]


def body(
    layer_input,
    output_grad,
    lengths,
    attention_gain,
    feed_gain,
    query_gain,
    key_gain,
    query_weight,
    key_weight,
    value_weight,
    out_weight,
    gate_weight,
    up_weight,
    down_weight,
    query_moment,
    key_moment,
    value_moment,
    out_moment,
    gate_moment,
    up_moment,
    down_moment,
):
    owned = (
        query_weight, key_weight, value_weight, out_weight, gate_weight, up_weight, down_weight,
    )
    moments = (
        query_moment, key_moment, value_moment, out_moment, gate_moment, up_moment, down_moment,
    )
    n = lax.axis_size("own")
    unit = layer_input.shape[1]
    core = lax.axis_index("rep") % 2

    def halves(*matrices):
        parts = []
        for matrix in matrices:
            width = matrix.shape[1] // 2
            parts.append(lax.dynamic_slice_in_dim(matrix, core * width, width, 1))
        return jnp.concatenate(parts, 1).astype(BF16)

    step = unit // 2
    gate_half, up_half = halves(gate_weight), halves(up_weight)
    shards = (
        halves(query_weight, key_weight, value_weight),
        out_weight.astype(BF16),
        jnp.concatenate(
            [part[:, k * step : (k + 1) * step] for k in range(3) for part in (gate_half, up_half)], 1
        ),
        down_weight.astype(BF16),
    )
    row_count = layer_input.shape[0]
    _, positions = segments(lengths[0], row_count)
    cosine_table, sine_table = rope_tables(positions)
    starts = (jnp.arange(row_count, dtype=jnp.int32) - positions).astype(F32)
    table = jnp.concatenate(
        [
            cosine_table[:, 0], cosine_table[:, 0], -sine_table[:, 0], sine_table[:, 0],
            jnp.broadcast_to(starts[:, None], (row_count, HEAD_DIM)),
        ],
        1,
    )
    gain_rows = [gain[None, :] for gain in (attention_gain, feed_gain, query_gain, key_gain)]
    (block_output, input_grad), gain_grads, grads = layer_pass(
        layer_input, output_grad, table, gain_rows, shards, n
    )
    gains = jnp.concatenate([grad[0] for grad in gain_grads])
    gains = jnp.pad(gains, (0, 24 * 128 - gains.shape[0])).reshape(24, 128)
    reduced, orth, gain_sums = update_all(grads, moments, gains, n, unit)
    new_weights, moments_next = apply_all(owned, moments, reduced, orth, n, unit)
    gain_sums = gain_sums.reshape(-1)
    norm_grads = gain_sums[: 2 * unit].reshape(2, unit)
    head_grads = gain_sums[2 * unit : 2 * unit + 2 * HEAD_DIM].reshape(2, HEAD_DIM)
    return (block_output, input_grad, norm_grads, head_grads, *new_weights, *moments_next)


def solution(mesh):
    tokens, owned = P(("rep", "own"), None), P("own", None)
    return jax.shard_map(
        body,
        mesh=mesh,
        in_specs=(tokens,) * 3 + (P(),) * 4 + (owned,) * 14,
        out_specs=(tokens,) * 2 + (P(),) * 2 + (owned,) * 14,
        check_vma=False,
    )
```

```python
import functools

import jax
import jax.numpy as jnp
from jax import lax
from jax.experimental import pallas as pl
from jax.experimental.pallas import tpu as pltpu
from jax.sharding import PartitionSpec as P

HEADS = 16
KV_HEADS = 8
HEAD_DIM = 128
NS_STEPS = 5

EPSILON = 1e-06
ROPE_BASE = 1000000.0
MOMENTUM = 0.95
LEARN_RATE = 0.8
WEIGHT_DECAY = 0.01
NEWTON_A = 3.4445
NEWTON_B = -4.775
NEWTON_C = 2.0315

BF16 = jnp.bfloat16
F32 = jnp.float32
MESH = pl.DeviceIdType.MESH
ANY = pl.BlockSpec(memory_space=pltpu.HBM)

QKV, OUT, GU, DOWN = range(4)


def segments(lengths, row_count):
    seq_ends = jnp.cumsum(lengths)
    seq_starts = seq_ends - lengths
    row_ids = jnp.arange(row_count, dtype=jnp.int32)
    segment_ids = jnp.sum((row_ids[:, None] >= seq_ends[None, :]).astype(jnp.int32), 1)
    slot_ids = jnp.arange(lengths.shape[0], dtype=jnp.int32)
    row_starts = jnp.sum(
        jnp.where(segment_ids[:, None] == slot_ids[None, :], seq_starts[None, :], 0), 1
    )
    return (segment_ids, row_ids - row_starts)


def rope_tables(positions):
    inverse = ROPE_BASE ** (-jnp.arange(0, HEAD_DIM, 2, dtype=jnp.float32) / HEAD_DIM)
    angles = positions.astype(jnp.float32)[:, None] * inverse[None, :]
    return (jnp.cos(angles)[:, None, :], jnp.sin(angles)[:, None, :])


class Place:
    def __init__(self, n):
        self.n = n
        self.rep = lax.axis_index("rep")
        self.own = lax.axis_index("own")
        self.x = self.rep // 2
        self.core = self.rep % 2
        odd, pair = self.own % 2, self.own // 2
        self.ring = pair * (1 - odd) + odd * (n - 1 - pair)

    def own_at(self, ring):
        odd = ring // (self.n // 2)
        return 2 * (ring * (1 - odd) + odd * (self.n - 1 - ring)) + odd

    def shard(self, distance):
        return self.own_at(lax.rem(self.ring + distance + self.n, self.n))

    def ring_neighbour(self, way):
        return (self.rep, self.shard(way))

    @property
    def core_partner(self):
        return (self.x * 2 + 1 - self.core, self.own)

    @property
    def x_partner(self):
        return ((1 - self.x) * 2 + self.core, self.own)


def greet(devices):
    barrier = pltpu.get_barrier_semaphore()
    for device in devices:
        pl.semaphore_signal(barrier, inc=1, device_id=device, device_id_type=MESH)
    pl.semaphore_wait(barrier, len(devices))


class Several:
    def __init__(self, whole, copies):
        self.whole = whole
        self.copies = copies

    def start(self):
        for copy in self.copies:
            copy().start()

    def wait_send(self):
        self.whole().wait_send()

    def wait_recv(self):
        self.whole().wait_recv()


def remote(src, dst, send, recv, device):
    return pltpu.make_async_remote_copy(
        src_ref=src, dst_ref=dst, send_sem=send, recv_sem=recv, device_id=device, device_id_type=MESH
    )


def hops(n, way, kind):
    return n // 2 if (way == 0) == (kind == 0) else n // 2 - 1


SPREADS = ((QKV, True), (OUT, False), (GU, True), (DOWN, False))


def layer_kernel(n, tokens, unit, *refs):
    (
        x_ref, back_ref, table_ref, attention_gain, feed_gain, query_gain, key_gain,
    ) = refs[:7]
    shards = refs[7:11]
    output, input_grad, grad_attention, grad_feed, grad_query_gain, grad_key_gain = refs[11:17]
    grads = refs[17:21]
    (
        w_qkv, w_out, w_gu, w_down, normed, raw, low, probs, context, hidden, out_low, attended,
        grad_context, activated, gu_back, part, sent, got, middle, tables, stage, turned_left, gain_sums,
        local, ring_send, ring_recv, x_send, x_recv, swap_send, swap_recv, stage_sem,
    ) = refs[21:]
    weights = (w_qkv, w_out, w_gu, w_down)
    place = Place(n)
    top = n // 2
    cw, ccw = place.ring_neighbour(1), place.ring_neighbour(-1)
    ways = ((1, cw), (-1, ccw))
    greet([cw, ccw, place.core_partner, place.x_partner])
    both = 2 * tokens
    mine = pl.multiple_of(place.core * tokens, tokens)
    theirs = pl.multiple_of((1 - place.core) * tokens, tokens)
    my_rows, their_rows = pl.ds(mine, tokens), pl.ds(theirs, tokens)
    chunk = unit // 2
    ff = 3 * unit // 2
    few = 32
    base = unit // n
    heads = unit // HEAD_DIM
    kv_heads = heads // 2
    scale = HEAD_DIM ** (-0.5)

    def holds(which, own_index, act):
        if SPREADS[which][1]:
            act()
        else:
            pl.when(own_index // top == place.core)(act)

    def region(which, own_index, x):
        array, split = SPREADS[which]
        height = shards[which].shape[0]
        if split:
            width = weights[which].shape[1] // 2
            start = pl.multiple_of(own_index * height, height)
            return weights[which].at[pl.ds(start, height), pl.ds(pl.multiple_of(x * width, width), width)]
        start = pl.multiple_of(lax.rem(own_index, top) * height, height)
        return weights[which].at[pl.ds(start, height)]

    def own_copy(which):
        height = shards[which].shape[0]
        index = place.own if SPREADS[which][1] else lax.rem(place.own, top)
        start = pl.multiple_of(index * height, height)
        return pltpu.make_async_copy(
            shards[which], weights[which].at[pl.ds(start, height)], local.at[which]
        )

    def reach(which, way):
        return hops(n, way, 0 if SPREADS[which][1] else 1)

    def ring_copy(which, way, hop, act):
        step, target = ways[way]
        own_index = place.shard(-step * (hop if act == "wait_recv" else hop - 1))
        spot = region(which, own_index, place.x)
        index = (which * 2 + way) * top + hop - 1

        def do():
            copy = remote(spot, spot, ring_send.at[index], ring_recv.at[index], target)
            getattr(copy, act)()

        holds(which, own_index, do)

    def send_on(which, way, hop):
        ring_copy(which, way, hop, "start")

    def x_copy(which, way, hop, x):
        spot = region(which, place.shard(-ways[way][0] * hop), x)
        index = (which // 2 * 2 + way) * top + hop - 1
        return remote(spot, spot, x_send.at[index], x_recv.at[index], place.x_partner)

    def serve(which, hop):
        for way in range(2):
            if hop > reach(which, way):
                continue
            ring_copy(which, way, hop, "wait_recv")
            if hop < reach(which, way):
                send_on(which, way, hop + 1)
            if SPREADS[which][1]:
                x_copy(which, way, hop, place.x).start()

    def begin(which):
        def act():
            own_copy(which).wait()

        holds(which, place.own, act)
        for way in range(2):
            if reach(which, way) > 0:
                send_on(which, way, 1)

    def take_x(which):
        for way in range(2):
            for hop in range(1, reach(which, way) + 1):
                x_copy(which, way, hop, 1 - place.x).wait_recv()

    def swap(index, src, dst):
        return remote(src, dst, swap_send.at[index], swap_recv.at[index], place.core_partner)

    def rows_swap(index, ref):
        return swap(index, ref.at[my_rows], ref.at[my_rows])

    def part_swap(index, slot):
        return swap(index, sent.at[slot], got.at[slot])

    def loop(size, step, act):
        def body(k, carry):
            act(pl.multiple_of(k * step, step))
            return carry

        lax.fori_loop(0, size // step, body, 0)

    def normalize(source, gain, target):
        def act(k):
            value = source[pl.ds(k, few), :]
            value = value * lax.rsqrt(jnp.mean(value * value, -1, keepdims=True) + EPSILON)
            target[pl.ds(pl.multiple_of(mine + k, few), few), :] = (value * gain[...]).astype(BF16)

        loop(tokens, few, act)

    def normalize_back(k, source, gain, grad):
        value = source[pl.ds(k, few), :]
        inverse = lax.rsqrt(jnp.mean(value * value, -1, keepdims=True) + EPSILON)
        unscaled = value * inverse
        inner = grad * gain[...]
        back = inverse * (inner - unscaled * jnp.mean(inner * unscaled, -1, keepdims=True))
        return back, jnp.sum((grad * unscaled).reshape(few // 8, 8, unit), 0)

    def dot(left, right, across):
        return lax.dot_general(left, right, ((across[0], across[1]), ((), ())), preferred_element_type=F32)

    NN, NT, TN = ((1,), (0,)), ((1,), (1,)), ((0,), (0,))

    def partial_product(index, slot, left, right, across):
        part[...] = dot(left[...], right[...], across)

        def pack(k):
            sent[slot, pl.ds(k, few), :] = part[
                pl.ds(pl.multiple_of(theirs + k, few), few), :
            ].astype(BF16)

        loop(tokens, few, pack)
        part_swap(index, slot).start()

    def whole_rows(k, slot):
        own = part[pl.ds(pl.multiple_of(mine + k, few), few), :]
        return own + got[slot, pl.ds(k, few), :].astype(F32)

    def weight_grad(which, left, right):
        columns = right.shape[1] // unit

        def by_rows(r, carry):
            row = pl.multiple_of(r * chunk, chunk)
            turned_left[...] = left[:, pl.ds(row, chunk)].T

            def by_columns(c, carry):
                column = pl.multiple_of(c * unit, unit)
                index = r * columns + c
                slot = lax.rem(index, 2)

                @pl.when(index >= 2)
                def _():
                    stage_copy(which, slot, row, column, chunk, unit).wait()

                value = dot(turned_left[...], right[:, pl.ds(column, unit)], NN)
                stage[slot] = value.astype(BF16)
                stage_copy(which, slot, row, column, chunk, unit).start()
                return carry

            lax.fori_loop(0, columns, by_columns, 0)
            return carry

        lax.fori_loop(0, left.shape[1] // chunk, by_rows, 0)
        for slot in range(2):
            stage_copy(which, slot, 0, 0, chunk, unit).wait()

    def stage_copy(which, slot, row, column, height, width):
        return pltpu.make_async_copy(
            stage.at[slot], grads[which].at[pl.ds(row, height), pl.ds(column, width)],
            stage_sem.at[slot],
        )

    for which in range(4):
        holds(which, place.own, lambda: own_copy(which).start())
    tables[my_rows, :] = table_ref[...]
    normalize(x_ref, attention_gain, normed)
    rows_swap(0, normed).start()
    rows_swap(1, tables).start()
    begin(0)
    begin(1)

    def round_back(k):
        out_low[pl.ds(pl.multiple_of(mine + k, few), few), :] = back_ref[pl.ds(k, few), :].astype(BF16)

    loop(tokens, few, round_back)
    rows_swap(2, out_low).start()
    gain_sums[...] = jnp.zeros_like(gain_sums)

    late = [(1, top)] if top < 3 else [(1, h) for h in range(3, top + 1)]
    serve(0, 1)
    serve(1, 1)
    begin(2)
    for hop in range(2, top + 1):
        serve(0, hop)
        if (1, hop) not in late:
            serve(1, hop)
        if hop == 2:
            serve(2, 1)
    take_x(0)
    begin(3)
    pending = late + [(2, h) for h in range(2, top)] + [(3, 1), (2, top)]
    pending += [(3, h) for h in range(2, top + 1)]
    for name in (0, 1):
        rows_swap(name, (normed, tables)[name]).wait_recv()

    raw[:, pl.ds(0, unit)] = dot(normed[...], w_qkv[:, pl.ds(0, unit)], NN)
    keys_values = dot(normed[...], w_qkv[:, pl.ds(unit, unit)], NN)
    raw[:, pl.ds(unit, chunk)] = keys_values[:, :chunk]
    low[:, pl.ds(unit + chunk, chunk)] = keys_values[:, chunk:].astype(BF16)
    serve(*pending.pop(0))

    def turned(value, rows):
        return value * tables[rows, pl.ds(0, HEAD_DIM)] + pltpu.roll(
            value, HEAD_DIM // 2, 1
        ) * tables[rows, pl.ds(HEAD_DIM, HEAD_DIM)]

    def turned_back(value, rows):
        return value * tables[rows, pl.ds(0, HEAD_DIM)] - pltpu.roll(
            value, HEAD_DIM // 2, 1
        ) * tables[rows, pl.ds(HEAD_DIM, HEAD_DIM)]

    def head_norm(first, count, gain):
        def act(k):
            for half in range(2):
                rows = pl.ds(half * tokens, tokens)
                columns = pl.ds(pl.multiple_of(first + k, HEAD_DIM), HEAD_DIM)
                value = raw[rows, columns]
                inverse = lax.rsqrt(jnp.mean(value * value, -1, keepdims=True) + EPSILON)
                low[rows, columns] = turned(value * inverse * gain[...], rows).astype(BF16)

        loop(count * HEAD_DIM, HEAD_DIM, act)

    head_norm(0, heads, query_gain)
    if pending:
        serve(*pending.pop(0))
    head_norm(unit, kv_heads, key_gain)

    def spans(k, half):
        queries = [pl.ds(pl.multiple_of((2 * k + g) * HEAD_DIM, HEAD_DIM), HEAD_DIM) for g in range(2)]
        keys = pl.ds(pl.multiple_of(unit + k * HEAD_DIM, HEAD_DIM), HEAD_DIM)
        values = pl.ds(pl.multiple_of(unit + unit // 2 + k * HEAD_DIM, HEAD_DIM), HEAD_DIM)
        return queries, keys, values, pl.ds(half * tokens, tokens)

    def stacked(ref, rows, columns):
        return jnp.concatenate([ref[rows, columns[0]], ref[rows, columns[1]]], 0)

    def attend(k, half):
        queries, keys, values, rows = spans(k, half)
        row_id = lax.broadcasted_iota(jnp.int32, (tokens, tokens), 0)
        column_id = lax.broadcasted_iota(jnp.int32, (tokens, tokens), 1)
        start = tables[rows, pl.ds(2 * HEAD_DIM, HEAD_DIM)][:, :1]
        allowed = (column_id <= row_id) & (column_id.astype(F32) >= start)
        masks = jnp.where(allowed, 0.0, -1e30)
        scores = dot(stacked(low, rows, queries), low[rows, keys], NT) * scale
        scores = scores + jnp.concatenate([masks, masks], 0)
        exponent = jnp.exp(scores - jnp.max(scores, -1, keepdims=True))
        value = exponent / jnp.sum(exponent, -1, keepdims=True)
        probs[k * 2 + half] = value
        result = dot(value.astype(BF16), low[rows, values], NN).astype(BF16)
        for g in range(2):
            context[rows, queries[g]] = result[g * tokens : (g + 1) * tokens]

    for k in range(kv_heads):
        for half in range(2):
            attend(k, half)
        if pending and k % 2 == 0:
            serve(*pending.pop(0))

    while pending and pending[0][0] == 1:
        serve(*pending.pop(0))
    partial_product(3, 0, context, w_out, NN)
    if pending and pending[0][0] == 2:
        serve(*pending.pop(0))
    part_swap(3, 0).wait_recv()

    def add_middle(k):
        middle[pl.ds(k, few), :] = x_ref[pl.ds(k, few), :] + whole_rows(k, 0)

    loop(tokens, few, add_middle)
    normalize(middle, feed_gain, hidden)
    rows_swap(4, hidden).start()
    while pending:
        serve(*pending.pop(0))
    take_x(2)
    rows_swap(4, hidden).wait_recv()
    rows_swap(2, out_low).wait_recv()

    def feed(k):
        span = pl.ds(k, chunk)
        pair = pl.ds(pl.multiple_of(2 * k, unit), unit)
        gate_up = dot(hidden[...], w_gu[:, pair], NN)
        gate, up = gate_up[:, :chunk], gate_up[:, chunk:]
        grad = dot(out_low[...], w_down[span, :], NT)
        sigmoid = 1.0 / (1.0 + jnp.exp(-gate))
        swish = gate * sigmoid
        activated[:, span] = (swish * up).astype(BF16)
        gu_back[:, pl.ds(pl.multiple_of(2 * k, chunk), chunk)] = (
            grad * up * (sigmoid + swish * (1.0 - sigmoid))
        ).astype(BF16)
        gu_back[:, pl.ds(pl.multiple_of(2 * k + chunk, chunk), chunk)] = (grad * swish).astype(BF16)

    loop(ff, chunk, feed)
    part_swap(3, 0).wait_send()
    partial_product(6, 0, gu_back, w_gu, NT)
    weight_grad(3, activated, out_low)
    part_swap(6, 0).wait_recv()

    def middle_back(k):
        back, gain_part = normalize_back(k, middle, feed_gain, whole_rows(k, 0))
        back = back_ref[pl.ds(k, few), :] + back
        input_grad[pl.ds(k, few), :] = back
        attended[pl.ds(pl.multiple_of(mine + k, few), few), :] = back.astype(BF16)
        gain_sums[1] += gain_part

    loop(tokens, few, middle_back)
    rows_swap(7, attended).start()
    partial_product(5, 1, activated, w_down, NN)
    weight_grad(2, hidden, gu_back)
    part_swap(5, 1).wait_recv()

    def add_output(k):
        output[pl.ds(k, few), :] = middle[pl.ds(k, few), :] + whole_rows(k, 1)

    loop(tokens, few, add_output)
    rows_swap(7, attended).wait_recv()

    grad_context[...] = dot(attended[...], w_out[...], NT).astype(BF16)
    weight_grad(1, context, attended)

    def head_back(rows, columns, gain, grad, index):
        value = raw[rows, columns]
        inverse = lax.rsqrt(jnp.mean(value * value, -1, keepdims=True) + EPSILON)
        unscaled = value * inverse
        grad = turned_back(grad, rows)
        gain_sums[index, :, pl.ds(0, HEAD_DIM)] += jnp.sum(
            (grad * unscaled).reshape(tokens // 8, 8, HEAD_DIM), 0
        )
        inner = grad * gain[...]
        back = inverse * (inner - unscaled * jnp.mean(inner * unscaled, -1, keepdims=True))
        low[rows, columns] = back.astype(BF16)

    def attend_back(k, half):
        queries, keys, values, rows = spans(k, half)
        prob = probs[k * 2 + half]
        above = stacked(grad_context, rows, queries)
        query_pair = stacked(low, rows, queries)
        grad_values = dot(prob.astype(BF16), above, TN)
        grad_probs = dot(above, low[rows, values], NT)
        grad_scores = prob * (grad_probs - jnp.sum(prob * grad_probs, -1, keepdims=True))
        grad_scores = grad_scores.astype(BF16)
        grad_queries = dot(grad_scores, low[rows, keys], NN) * scale
        grad_keys = dot(grad_scores, query_pair, TN) * scale
        for g in range(2):
            head_back(rows, queries[g], query_gain, grad_queries[g * tokens : (g + 1) * tokens], 2)
        head_back(rows, keys, key_gain, grad_keys, 3)
        low[rows, values] = grad_values.astype(BF16)

    def back_body(k, carry):
        for half in range(2):
            attend_back(k, half)
        return carry

    lax.fori_loop(0, kv_heads, back_body, 0)

    part_swap(6, 0).wait_send()
    partial_product(8, 0, low, w_qkv, NT)
    weight_grad(0, normed, low)
    part_swap(8, 0).wait_recv()

    def input_back(k):
        back, gain_part = normalize_back(k, x_ref, attention_gain, whole_rows(k, 0))
        input_grad[pl.ds(k, few), :] += back
        gain_sums[0] += gain_part

    loop(tokens, few, input_back)
    grad_attention[...] = jnp.sum(gain_sums[0], 0, keepdims=True)
    grad_feed[...] = jnp.sum(gain_sums[1], 0, keepdims=True)
    grad_query_gain[...] = jnp.sum(gain_sums[2, :, pl.ds(0, HEAD_DIM)], 0, keepdims=True)
    grad_key_gain[...] = jnp.sum(gain_sums[3, :, pl.ds(0, HEAD_DIM)], 0, keepdims=True)

    for index, ref in ((0, normed), (1, tables), (2, out_low), (4, hidden), (7, attended)):
        rows_swap(index, ref).wait_send()
    part_swap(5, 1).wait_send()
    part_swap(8, 0).wait_send()
    for which in range(4):
        for way in range(2):
            for hop in range(1, reach(which, way) + 1):
                ring_copy(which, way, hop, "wait_send")
                if SPREADS[which][1]:
                    x_copy(which, way, hop, place.x).wait_send()


def layer_pass(values, back, table, gains, shards, n):
    tokens, unit = values.shape
    top = n // 2
    dma = pltpu.SemaphoreType.DMA
    vmem = pltpu.VMEM
    both = 2 * tokens
    heads = unit // HEAD_DIM
    in_vmem = pl.BlockSpec(memory_space=pltpu.VMEM)
    row = lambda width: jax.ShapeDtypeStruct((1, width), F32)
    shapes = [(unit, 2 * unit), (unit, unit), (unit, 3 * unit), (3 * unit // 2, unit)]
    results = pl.pallas_call(
        functools.partial(layer_kernel, n, tokens, unit),
        out_shape=[jax.ShapeDtypeStruct((tokens, unit), F32)] * 2
        + [row(unit), row(unit), row(HEAD_DIM), row(HEAD_DIM)]
        + [jax.ShapeDtypeStruct(shape, BF16) for shape in shapes],
        in_specs=[in_vmem] * 7 + [ANY] * 4,
        out_specs=[in_vmem] * 6 + [ANY] * 4,
        scratch_shapes=[vmem(shape, BF16) for shape in shapes]
        + [
            vmem((both, unit), BF16),
            vmem((both, 3 * unit // 2), F32),
            vmem((both, 2 * unit), BF16),
            vmem((heads, both, tokens), F32),
            vmem((both, unit), BF16),
            vmem((both, unit), BF16),
            vmem((both, unit), BF16),
            vmem((both, unit), BF16),
            vmem((both, unit), BF16),
            vmem((both, 3 * unit // 2), BF16),
            vmem((both, 3 * unit), BF16),
            vmem((both, unit), F32),
            vmem((2, tokens, unit), BF16),
            vmem((2, tokens, unit), BF16),
            vmem((tokens, unit), F32),
            vmem((both, 3 * HEAD_DIM), F32),
            vmem((2, unit // 2, unit), BF16),
            vmem((unit // 2, both), BF16),
            vmem((4, 8, unit), F32),
            dma((4,)),
            dma((8 * top,)),
            dma((8 * top,)),
            dma((4 * top,)),
            dma((4 * top,)),
            dma((9,)),
            dma((9,)),
            dma((2,)),
        ],
        compiler_params=pltpu.CompilerParams(
            collective_id=0, has_side_effects=True, vmem_limit_bytes=56 * 2**20
        ),
    )(values, back, table, *gains, *shards)
    return results[:2], results[2:6], results[6:]


PHASES = ((DOWN, 3, False), (GU, 3, True), (OUT, 2, False), (QKV, 2, True))

OWNERS = (
    (3, 0, 1, False, 1, 2),
    (3, 1, 1, False, 1, 6),
    (3, 0, 2, False, 0, 2),
    (2, 0, 2, True, 1, 5),
    (1, 0, 3, False, 0, 5),
    (1, 0, 3, False, 1, 1),
    (0, 0, 3, True, 0, 1),
)
KEY, VALUE, QUERY, OUTM, GATE, UP, DOWNM = range(7)
RETURNS = (OUTM, KEY, VALUE, DOWNM, GATE, UP, QUERY)
TILE_SLOTS = 4
X_AHEAD = 4
LAND_AHEAD = 6


def summing_core(phase):
    return 0 if PHASES[phase][2] else 1


def stage_order(n, core):
    rings = ((1.0, 1.5), (4.0, 2.7), (13.0, 1.1), (26.6, 1.7))
    crossings = {1: (-6.0, 2.5), 3: (16.0, 1.5)}
    keys, needs = {}, {}
    for phase in range(4):
        first, step = rings[phase]
        for i in range(n):
            key = first + step * i * 8 / n
            if summing_core(phase) == core:
                keys["ring", phase, i] = key
                needs["ring", phase, i] = [("ring", phase, i - 1)] if i else []
                if phase in crossings:
                    needs["ring", phase, i].append(("x", phase, i))
            else:
                keys["land", phase, i] = key - 6.0
                needs["land", phase, i] = [("land", phase, i - 1)] if i else []
        if phase in crossings:
            first, step = crossings[phase]
            for i in range(n):
                keys["x", phase, i] = first + step * i * 8 / n
                needs["x", phase, i] = [("x", phase, i - 1)] if i else [("x", 1, n - 1)] * (phase == 3)
                if core == 0 and phase == 3:
                    needs["x", phase, i].append(("ring", 1, i))
        elif core == 1:
            keys["final", phase, 0] = {0: 16.0, 2: 27.0}[phase]
            needs["final", phase, 0] = [("ring", phase, n - 1)]
    left, found = sorted(keys, key=lambda stage: (keys[stage], stage)), []
    while left:
        stage = next(stage for stage in left if all(need in found for need in needs[stage]))
        left.remove(stage)
        found.append(stage)
    return found


class Rows:
    def __init__(self):
        self.next = 0

    def take(self, rows):
        start = self.next
        self.next += rows
        return start


def layout(n, unit):
    base = unit // n
    top = n // 2
    place = {}
    rows = (Rows(), Rows())
    place["high"] = [None, rows[1].take(3 * unit)]
    for name in ("grad", "ahead"):
        place[name] = [rows[summing_core(p)].take(PHASES[p][1] * base) for p in range(4)]
    for name in ("part", "other"):
        place[name] = [0 if split else rows[1].take(units * base) for _, units, split in PHASES]
    newton = Rows()
    newton.next = -(-rows[1].next // unit) * unit
    place["high"][0] = newton.take(3 * unit)
    place["poly"] = [newton.take(unit) for _ in range(2)]
    place["x_in"] = [rows[0].take(3 * base) for _ in range(n)]
    place["own"] = [[rows[core].take(3 * base) for _ in range(TILE_SLOTS)] for core in range(2)]
    place["ring"], place["far"] = [], []
    for phase, (_, units, _) in enumerate(PHASES):
        take = rows[summing_core(phase)].take
        place["ring"].append([[take(units * base) for _ in range(top)] for _ in range(2)])
        place["far"].append(take(units * base))
    return place, max(rows[0].next, rows[1].next, newton.next)


def update_kernel(n, unit, *refs):
    grads, moments, gains_in = refs[:4], refs[4:11], refs[11]
    outs, orths, lands, gains_out = refs[12:16], refs[16:20], refs[20:24], refs[24]
    (
        pool, exact, gram, squares, gain_mine, gain_core, gain_x, gain_all,
        land_send, land_recv, tile_sem, x_send, x_recv, x_free, ring_send, ring_recv, part_send, part_recv,
        moment_sem, grad_local, grad_send, grad_recv, in_send, in_recv, in_local,
        out_send, out_recv, pass_send, pass_recv, gain_send, gain_recv,
    ) = refs[25:]
    place = Place(n)
    base = unit // n
    top = n // 2
    at, _ = layout(n, unit)
    cw, ccw = place.ring_neighbour(1), place.ring_neighbour(-1)
    ways = ((1, cw), (-1, ccw))
    side = [(place.x * 2 + core, lax.rem(place.own + k, n)) for k in range(1, n) for core in range(2)]
    across = [((1 - place.x) * 2 + core, place.own) for core in range(2)]
    greet(side + [place.core_partner] + across)
    order = [top]
    for distance in range(top - 1, 0, -1):
        order += [distance, -distance]
    order.append(0)
    moment = exact
    height = [units * base for _, units, _ in PHASES]
    moment_at = [sum(height[:phase]) for phase in range(4)]
    owners = [
        (xs * 2 + 1, place.own_at(spot * n // 8)) for _, _, _, _, xs, spot in OWNERS
    ]
    here = place.rep * n + place.own
    is_owner = [here == rep * n + own for rep, own in owners]

    def rows(start, size):
        if isinstance(start, int):
            return pl.ds(start, size)
        return pl.ds(pl.multiple_of(start, size), size)

    def block(start, size):
        return pool.at[rows(start, size)]

    def pieces_of(phase, x):
        array, units, _ = PHASES[phase]
        half = unit // 2
        found = []
        for core in range(2):
            for b in range(units):
                if array == GU:
                    own_column = b * unit + x * half
                    column = x * 3 * unit + core * (3 * half) + b * half
                else:
                    own_column = x * units * half + b * half
                    column = x * 2 * unit + core * (unit - x * half) + b * (half + x * half)
                found.append((core, b, own_column, column))
        return found

    def columns(start):
        return pl.ds(pl.multiple_of(start, unit // 2), unit // 2)

    def in_block(start, core, b):
        return pool.at[pl.ds(start + b * base, base), pl.ds(core * (unit // 2), unit // 2)]

    def shard_rows(phase, own_index):
        if PHASES[phase][2]:
            return rows(own_index * base, base)
        return rows(lax.rem(own_index, top) * height[phase], height[phase])

    def landing(phase, own_index, act):
        if PHASES[phase][2]:
            act()
        else:
            pl.when(own_index // top != summing_core(phase))(act)

    def spread(source, target, size, send, recv, device):
        step = size

        def copy(k, count):
            return remote(block(source + k, count), block(target + k, count), send, recv, device)

        return Several(
            functools.partial(copy, 0, size),
            [functools.partial(copy, k, step) for k in range(0, size, step)],
        )

    def land_copy(phase, i, act):
        array, units, split = PHASES[phase]
        own_index = place.shard(order[i])
        span = shard_rows(phase, own_index)

        def copy(at_columns):
            return remote(
                grads[array].at[span, at_columns], lands[array].at[span, at_columns],
                land_send.at[phase * n + i], land_recv.at[phase * n + i], place.core_partner,
            )

        def do():
            if not split:
                getattr(copy(pl.ds(0, unit)), act)()
            elif act == "start":
                for core, _, column, _ in pieces_of(phase, place.x):
                    if core == 1:
                        copy(columns(column)).start()
            else:
                getattr(copy(pl.ds(0, units * unit // 2)), act)()

        landing(phase, own_index, do)

    def x_index(phase, i):
        return (phase // 2) * n + i

    def x_copies(phase, i, core, act):
        index = x_index(phase, i)
        array, units, _ = PHASES[phase]
        span = shard_rows(phase, place.shard(order[i]))
        target = at["x_in"][i]

        def copy(source, spot):
            return remote(
                source, spot, x_send.at[index], x_recv.at[core, index], ((1 - place.x) * 2, place.own)
            )

        if act == "start":
            for its_core, b, column, _ in pieces_of(phase, 1 - place.x):
                if its_core == core:
                    copy(grads[array].at[span, columns(column)], in_block(target, core, b)).start()
        else:
            spot = pool.at[pl.ds(target, height[phase]), pl.ds(core * (unit // 2), unit // 2)]
            getattr(copy(spot, spot), act)()

    def ring_copy(phase, way, distance, source, part):
        size = height[phase] // 2
        target = at["ring"][phase][way][distance - 1] + part * size
        index = ((phase * 2 + way) * top + distance - 1) * 2 + part
        return spread(
            source + part * size, target, size,
            ring_send.at[index], ring_recv.at[index], ways[way][1],
        )

    def ring_out(phase, distance, part):
        if distance == 0:
            return []
        if distance == top:
            return [ring_copy(phase, part, top, at["far"][phase], part)]
        way = 0 if distance > 0 else 1
        far = abs(distance)
        return [ring_copy(phase, way, far, at["ring"][phase][way][far], part)]

    def part_copy(phase):
        return spread(
            at["part"][phase], at["other"][phase], height[phase],
            part_send.at[phase // 2], part_recv.at[phase // 2], place.x_partner,
        )

    def gain_copy(src, dst, slot, device):
        return remote(src, dst, gain_send.at[slot], gain_recv.at[slot], device)

    def gain_core_copy():
        return gain_copy(gain_mine, gain_core, 0, place.core_partner)

    def gain_x_copy():
        return gain_copy(gain_core, gain_x, 1, place.x_partner)

    def gain_back_copy():
        return gain_copy(gain_mine, gain_x, 2, place.core_partner)

    def gain_ring(way, hop, distance):
        spot = gain_all.at[place.shard(distance)]
        return gain_copy(spot, spot, 3 + way * top + hop - 1, ways[way][1])

    def grad_place(phase, x):
        array = PHASES[phase][0]
        start = at["grad"][phase]
        if not PHASES[phase][2]:
            return [(outs[array], block(start, height[phase]))]
        return [
            (outs[array].at[:, columns(column)], in_block(start, core, b))
            for core, b, _, column in pieces_of(phase, x)
        ]

    def grad_span(phase, x):
        array, units, split = PHASES[phase]
        if not split:
            return outs[array]
        first = pl.multiple_of(x * units * unit, unit)
        return outs[array].at[:, pl.ds(first, units * unit)]

    def grad_sent(phase, to, device, x):
        span = grad_span(phase, x)
        return remote(span, span, grad_send.at[phase, to], grad_recv.at[phase, to], device)

    def matrix_rows(matrix, own_index):
        phase, first, units, tall, _, _ = OWNERS[matrix]
        if tall:
            return [(0, own_index * units * base, units * base)]
        return [
            ((first + k) * base, k * unit + own_index * base, base) for k in range(units)
        ]

    def matrix_span(matrix):
        phase, first, units, tall, xs, _ = OWNERS[matrix]
        array = PHASES[phase][0]
        if tall:
            return orths[array]
        start = (xs * PHASES[phase][1] + first) * unit
        return orths[array].at[:, pl.ds(start, units * unit)]

    def answer_parts(matrix, final, own_index):
        phase, first, units, tall, xs, _ = OWNERS[matrix]
        array = PHASES[phase][0]
        if tall:
            return [(block(final + own_index * units * base, units * base), orths[array])]
        return [
            (
                pool.at[
                    rows(final + (b - first) * unit + own_index * base, base),
                    pl.ds(core * (unit // 2), unit // 2),
                ],
                orths[array].at[:, columns(column)],
            )
            for core, b, _, column in pieces_of(phase, xs)
            if first <= b < first + units
        ]

    def handed(matrix, to, device):
        span = matrix_span(matrix)
        return remote(span, span, pass_send.at[matrix, to], pass_recv.at[matrix, to], device)

    def answered(matrix, target):
        span = matrix_span(matrix)
        return remote(
            span, span, out_send.at[target], out_recv.at[matrix], (place.x * 2, target)
        )

    def summed(pieces, size, store):
        step = 16
        steps = 4 if size % (4 * step) == 0 else 1

        def body(k, carry):
            for j in range(steps):
                shift = (k * steps + j) * step
                total = None
                for start in pieces:
                    value = pool[rows_at(start, shift, step), :].astype(F32)
                    total = value if total is None else total + value
                store(shift, step, total)
            return carry

        lax.fori_loop(0, size // (step * steps), body, 0)

    def rows_at(start, shift, step):
        return pl.ds(pl.multiple_of(start + shift, step), step)

    def keep(start):
        def store(shift, step, total):
            pool[rows_at(start, shift, step), :] = total.astype(BF16)

        return store

    def load_tile(phase, i, slot):
        array, _, split = PHASES[phase]
        own_index = place.shard(order[i])
        span = shard_rows(phase, own_index)
        summing = summing_core(phase)

        def load(source, target):
            pltpu.make_async_copy(source, target, tile_sem.at[slot]).start()

        if split:
            for core, b, column, _ in pieces_of(phase, place.x):
                load(
                    (grads, lands)[core][array].at[span, columns(column)],
                    in_block(at["own"][summing][slot], core, b),
                )
            return
        for core in range(2):

            @pl.when(own_index // top == core)
            def _():
                load(
                    (lands, grads)[core == summing][array].at[span],
                    block(at["own"][summing][slot], height[phase]),
                )

    def prefetch(rings, index):
        if index < len(rings):
            _, phase, i = rings[index]
            land_copy(phase, i, "wait_recv")
            load_tile(phase, i, index % TILE_SLOTS)

    def moment_copies(phase, act):
        array, units, split = PHASES[phase]
        if not split:
            act(moments[3 if array == OUT else 6], moment.at[pl.ds(moment_at[phase], height[phase])])
            return
        half = unit // 2
        for x in range(2):

            @pl.when(place.x == x)
            def _():
                for core, b, _, column in pieces_of(phase, x):
                    if array == GU:
                        source, first = 4 + x, x * 3 * unit
                    elif x == 0:
                        source, first = 0, 0
                    else:
                        source, first = 1 + b, (2 + b) * unit
                    act(
                        moments[source].at[:, pl.ds(column - first, half)],
                        moment.at[pl.ds(moment_at[phase] + b * base, base), pl.ds(core * half, half)],
                    )

    def load_moment(phase):
        moment_copies(
            phase, lambda src, dst: pltpu.make_async_copy(src, dst, moment_sem.at[phase]).start()
        )

    def finish(phase, pieces):
        span = moment.at[pl.ds(moment_at[phase], height[phase])]
        pltpu.make_async_copy(span, span, moment_sem.at[phase]).wait()

        def store(shift, step, total):
            pool[rows_at(at["grad"][phase], shift, step), :] = total.astype(BF16)
            ahead = (1.0 + MOMENTUM) * total + MOMENTUM**2 * moment[
                rows_at(moment_at[phase], shift, step), :
            ]
            pool[rows_at(at["ahead"][phase], shift, step), :] = ahead.astype(BF16)

        summed(pieces, height[phase], store)
        for matrix, (its_phase, _, _, _, xs, _) in enumerate(OWNERS):
            if its_phase != phase:
                continue

            def hand_in(local):
                for source, target, size in matrix_rows(matrix, place.own):
                    source = block(at["ahead"][phase] + source, size)
                    target = block(at["high"][1] + target, size)
                    if local:
                        pltpu.make_async_copy(source, target, in_local).start()
                    else:
                        remote(
                            source, target, in_send.at[matrix], in_recv.at[place.own], owners[matrix]
                        ).start()

            if summing_core(phase) == 0:
                pl.when(place.x == xs)(functools.partial(hand_in, False))
            else:
                pl.when(is_owner[matrix])(functools.partial(hand_in, True))
                pl.when((place.x == xs) & (here != owners[matrix][0] * n + owners[matrix][1]))(
                    functools.partial(hand_in, False)
                )

        for target, source in grad_place(phase, place.x):
            pltpu.make_async_copy(source, target, grad_local.at[phase]).start()
            remote(
                source, target, grad_send.at[phase, 0], grad_recv.at[phase, 0], place.core_partner
            ).start()
            if PHASES[phase][2]:
                remote(
                    source, target, grad_send.at[phase, 1], grad_recv.at[phase, 1], place.x_partner
                ).start()

    def settle(phase):
        span = block(at["grad"][phase], height[phase])
        pltpu.make_async_copy(span, span, grad_local.at[phase]).wait()
        remote(
            span, span, grad_send.at[phase, 0], grad_recv.at[phase, 0], place.core_partner
        ).wait_send()
        if PHASES[phase][2]:
            remote(
                span, span, grad_send.at[phase, 1], grad_recv.at[phase, 1], place.x_partner
            ).wait_send()
        for matrix, (its_phase, _, units, _, xs, _) in enumerate(OWNERS):
            if its_phase != phase:
                continue

            sends = place.x == xs
            if summing_core(phase) == 1:
                sends = sends & (here != owners[matrix][0] * n + owners[matrix][1])

            @pl.when(sends)
            def _():
                span = block(at["high"][1], units * base)
                remote(
                    span, span, in_send.at[matrix], in_recv.at[0], place.core_partner
                ).wait_send()

    def stage_x(phase, i, core):
        index = x_index(phase, i)
        if index >= X_AHEAD:
            before = index - X_AHEAD
            x_copies(1 if before < n else 3, before % n, core, "wait_send")
        if phase == 3:
            pl.semaphore_wait(x_free, 1)
        x_copies(phase, i, core, "start")

    def stage_ring(phase, i, slot):
        distance = order[i]
        start = at["own"][summing_core(phase)][slot]
        span = block(start, height[phase])
        pltpu.make_async_copy(span, span, tile_sem.at[slot]).wait()
        pieces = [start]
        if PHASES[phase][2]:
            for core in range(2):
                x_copies(phase, i, core, "wait_recv")
            pieces.append(at["x_in"][i])
        size = height[phase]
        mid = size // 2
        if distance == 0:
            for way in range(2):
                held = at["ring"][phase][way][0]
                for part in range(2):
                    ring_copy(phase, way, 1, held, part).wait_recv()
                pieces.append(held)
            if PHASES[phase][2]:
                finish(phase, pieces)
            else:
                summed(pieces, size, keep(at["part"][phase]))
                part_copy(phase).start()
        else:
            way = 0 if distance > 0 else 1
            far = abs(distance)
            held = at["far"][phase] if far == top else at["ring"][phase][way][far]
            for part in (1 - way, way):
                starts = [start + part * mid for start in pieces]
                if far + 1 < top or (far + 1 == top and part == way):
                    ring_copy(phase, way, far + 1, held, part).wait_recv()
                    starts.append(held + part * mid)
                summed(starts, mid, keep(held + part * mid))
                for copy in ring_out(phase, distance, part):
                    copy.start()
        if phase == 1:
            for device in across:
                pl.semaphore_signal(x_free, inc=1, device_id=device, device_id_type=MESH)

    def ring_sent(phase):
        for distance in order:
            for part in range(2):
                for copy in ring_out(phase, distance, part):
                    copy.wait_send()

    def run(core):
        stages = stage_order(n, core)
        rings = [stage for stage in stages if stage[0] == "ring"]
        landed = [stage for stage in stages if stage[0] == "land"]
        for phase in range(4):
            if summing_core(phase) == core:
                load_moment(phase)
        done, sent, hop = 0, 0, 0
        for index in range(LAND_AHEAD):
            land_copy(*landed[index][1:], "start")
        for index in range(TILE_SLOTS - 1):
            prefetch(rings, index)
        for kind, phase, i in stages:
            if kind == "x":
                stage_x(phase, i, core)
            elif kind == "land":
                land_copy(phase, i, "wait_send")
                if sent + LAND_AHEAD < len(landed):
                    land_copy(*landed[sent + LAND_AHEAD][1:], "start")
                sent += 1
            elif kind == "final":
                part_copy(phase).wait_recv()
                finish(phase, [at["part"][phase], at["other"][phase]])
            else:
                prefetch(rings, done + TILE_SLOTS - 1)
                stage_ring(phase, i, done % TILE_SLOTS)
                done += 1
                if core == 0 and hop <= top + 1:
                    gain_stage(hop)
                    hop += 1

    def settle_all(core):
        for phase, (_, _, split) in enumerate(PHASES):
            if summing_core(phase) == core:
                settle(phase)
                if not split:
                    part_copy(phase).wait_send()
        for index in range(2 * n - X_AHEAD, 2 * n):
            x_copies(1 if index < n else 3, index % n, core, "wait_send")

    def take_sums(core):
        for phase, (_, _, split) in enumerate(PHASES):
            if summing_core(phase) != core:
                grad_sent(phase, 0, place.core_partner, place.x).wait_recv()
                if split:
                    grad_sent(phase, 2, place.core_partner, 1 - place.x).wait_recv()

    def gain_stage(hop):
        if hop == 0:
            gain_core_copy().wait_recv()
            gain_core[...] = gain_mine[...] + gain_core[...]
            gain_x_copy().start()
            return
        if hop == 1:
            gain_x_copy().wait_recv()
            gain_all[place.own] = gain_core[...] + gain_x[...]
            for way in range(2):
                gain_ring(way, 1, 0).start()
        for way in range(2):
            if 1 < hop <= hops(n, way, 0) + 1:
                distance = -ways[way][0] * (hop - 1)
                gain_ring(way, hop - 1, distance).wait_recv()
                if hop <= hops(n, way, 0):
                    gain_ring(way, hop, distance).start()

    gain_mine[...] = gains_in[...]

    @pl.when(place.core == 0)
    def _():
        run(0)
        total = gain_all[0]
        for k in range(1, n):
            total = total + gain_all[k]
        gains_out[...] = total
        gain_mine[...] = total
        gain_back_copy().start()

        for phase in (1, 3):
            grad_sent(phase, 1, place.x_partner, 1 - place.x).wait_recv()
            grad_sent(phase, 2, place.core_partner, 1 - place.x).start()

        for matrix in RETURNS:
            xs = OWNERS[matrix][4]

            @pl.when(place.x == xs)
            def _():
                answered(matrix, place.own).wait_recv()
                handed(matrix, 0, place.x_partner).start()
                handed(matrix, 1, place.core_partner).start()

            @pl.when(place.x != xs)
            def _():
                handed(matrix, 0, place.x_partner).wait_recv()
                handed(matrix, 1, place.core_partner).start()

        for matrix, (phase, _, units, _, xs, _) in enumerate(OWNERS):
            handed(matrix, 1, place.core_partner).wait_send()

            @pl.when(place.x == xs)
            def _():
                handed(matrix, 0, place.x_partner).wait_send()

        take_sums(0)
        settle_all(0)
        for phase in (1, 3):
            ring_sent(phase)
            grad_sent(phase, 2, place.core_partner, 1 - place.x).wait_send()
        gain_x_copy().wait_send()
        gain_back_copy().wait_send()
        for way in range(2):
            for h in range(1, hops(n, way, 0) + 1):
                gain_ring(way, h, -ways[way][0] * (h - 1)).wait_send()

    @pl.when(place.core == 1)
    def _():
        gain_core_copy().start()
        run(1)
        for phase in (0, 2):
            ring_sent(phase)
        newton_part(n, unit, place, pool, exact, gram, squares, at, is_owner, in_recv, in_local)
        for matrix, (_, _, units, tall, _, _) in enumerate(OWNERS):

            @pl.when(is_owner[matrix])
            def _():
                final = at["high"][1 - NS_STEPS % 2 if tall else NS_STEPS % 2]

                def send(k, carry):
                    target = lax.rem(place.own + k, n)
                    for source, part in answer_parts(matrix, final, target):
                        remote(
                            source, part, out_send.at[target], out_recv.at[matrix],
                            (place.x * 2, target),
                        ).start()
                    return carry

                lax.fori_loop(0, n, send, 0)

                def sent(k, carry):
                    answered(matrix, lax.rem(place.own + k, n)).wait_send()
                    return carry

                lax.fori_loop(0, n, sent, 0)

        gain_core_copy().wait_send()
        gain_back_copy().wait_recv()
        gains_out[...] = gain_x[...]
        take_sums(1)
        settle_all(1)
        for matrix in RETURNS:
            handed(matrix, 1, place.core_partner).wait_recv()


def newton_part(n, unit, place, pool, exact, gram, squares, at, is_owner, in_recv, in_local):
    base = unit // n
    small = min(256, unit // 2)
    per = unit // small
    wide = unit // 2
    few = 32
    count, tall = 0, 0
    for mine, (_, _, units, lies_tall, _, _) in zip(is_owner, OWNERS):
        count = count + units * mine.astype(jnp.int32)
        tall = tall + int(lies_tall) * mine.astype(jnp.int32)
    high, poly = at["high"], at["poly"]

    def rows(start, size):
        return pl.ds(pl.multiple_of(start, size), size)

    for matrix, (phase, _, units, *_) in enumerate(OWNERS):

        @pl.when(is_owner[matrix])
        def _():
            span = pool.at[pl.ds(high[1], units * base)]
            inside = summing_core(phase) == 1
            if inside:
                pltpu.make_async_copy(span, span, in_local).wait()
            for k in range(1 if inside else 0, n):
                own_index = lax.rem(place.own + k, n)
                remote(
                    span, span, in_recv.at[own_index], in_recv.at[own_index], place.core_partner
                ).wait_recv()

    @pl.when(count > 0)
    def _():
        squares[...] = jnp.zeros_like(squares)

        def square(k, carry):
            part = pool[rows(high[1] + k * few, few), :].astype(F32)
            squares[...] += jnp.sum((part * part).reshape(few // 8, 8, unit), 0)
            return carry

        lax.fori_loop(0, count * (unit // few), square, 0)
        total = jnp.sum(jnp.sum(squares[...], 1, keepdims=True), 0, keepdims=True)
        inverse = 1.0 / (jnp.sqrt(total) + 1e-07)

        @pl.when(tall == 0)
        def _():
            def scale(k, carry):
                value = pool[rows(high[1] + k * few, few), :].astype(F32) * inverse
                exact[rows(k * few, few), :] = value
                pool[rows(high[0] + k * few, few), :] = value.astype(BF16)
                return carry

            lax.fori_loop(0, count * (unit // few), scale, 0)

        @pl.when(tall == 1)
        def _():
            def scale(k, carry):
                block, row = k // per, k % per
                for column in range(per):
                    part = pool[
                        rows(high[1] + k * small, small), pl.ds(column * small, small)
                    ].astype(F32)
                    value = (part * inverse).T
                    shift = block * unit + column * small
                    columns = rows(row * small, small)
                    exact[rows(shift, small), columns] = value
                    pool[rows(high[0] + shift, small), columns] = value.astype(BF16)
                return carry

            lax.fori_loop(0, count * per, scale, 0)

        def newton(step, carry):
            even = step % 2
            now = high[0] + even * (high[1] - high[0])
            later = high[1] - even * (high[1] - high[0])

            def keep_symmetric(to, chunk, value):
                pool[pl.ds(to, (chunk + 1) * wide), pl.ds(chunk * wide, wide)] = value.astype(BF16)
                if chunk == 1:
                    pool[pl.ds(to + wide, wide), pl.ds(0, wide)] = value[:wide].T.astype(BF16)

            for chunk in range(2):
                down = (chunk + 1) * wide

                def product(block):
                    left = pool[pl.ds(pl.multiple_of(now + block * unit, unit), down), :]
                    right = pool[rows(now + block * unit + chunk * wide, wide), :]
                    return lax.dot_general(
                        left, right, (((1,), (1,)), ((), ())), preferred_element_type=F32
                    )

                gram[:down, :] = product(0)

                def more(block, carry):
                    gram[:down, :] += product(block)
                    return carry

                lax.fori_loop(1, count, more, 0)
                keep_symmetric(poly[0], chunk, gram[:down, :])

            for chunk in range(2):
                down = (chunk + 1) * wide
                columns = pl.ds(chunk * wide, wide)
                squared = jnp.dot(
                    pool[pl.ds(poly[0], down), :], pool[pl.ds(poly[0], unit), columns],
                    preferred_element_type=F32,
                )
                plain = pool[pl.ds(poly[0], down), columns].astype(F32)
                keep_symmetric(poly[1], chunk, NEWTON_B * plain + NEWTON_C * squared)

            def advance(block, carry):
                for chunk in range(2):
                    columns = pl.ds(chunk * wide, wide)
                    value = NEWTON_A * exact[rows(block * unit, unit), columns] + jnp.dot(
                        pool[pl.ds(poly[1], unit), :],
                        pool[rows(now + block * unit, unit), columns],
                        preferred_element_type=F32,
                    )
                    exact[rows(block * unit, unit), columns] = value
                    pool[rows(later + block * unit, unit), columns] = value.astype(BF16)
                return carry

            lax.fori_loop(0, count, advance, 0)
            return carry

        lax.fori_loop(0, NS_STEPS, newton, 0)

        @pl.when(tall == 1)
        def _():
            free = high[1 - NS_STEPS % 2]
            factor = jnp.sqrt(jnp.full((1, 1), count, jnp.int32).astype(F32))

            def lay(k, carry):
                block, row = k // per, k % per
                for column in range(per):
                    columns = pl.ds(column * small, small)
                    part = exact[rows(k * small, small), columns]
                    pool[
                        rows(free + block * unit + column * small, small), rows(row * small, small)
                    ] = (part * factor).T.astype(BF16)
                return carry

            lax.fori_loop(0, count * per, lay, 0)


def update_all(grads, moments, gains, n, unit):
    top = n // 2
    dma = pltpu.SemaphoreType.DMA
    vmem = pltpu.VMEM
    _, pool_rows = layout(n, unit)
    shapes = [(unit // n, 4 * unit), (2 * unit // n, unit), (unit // n, 6 * unit), (3 * unit // n, unit)]
    own = [jax.ShapeDtypeStruct(shape, BF16) for shape in shapes]
    whole = [jax.ShapeDtypeStruct(grad.shape, BF16) for grad in grads]
    in_vmem = pl.BlockSpec(memory_space=pltpu.VMEM)
    results = pl.pallas_call(
        functools.partial(update_kernel, n, unit),
        out_shape=own + own + whole + [jax.ShapeDtypeStruct(gains.shape, F32)],
        in_specs=[ANY] * 11 + [in_vmem],
        out_specs=[ANY] * 12 + [in_vmem],
        scratch_shapes=[
            vmem((pool_rows, unit), BF16),
            vmem((3 * unit, unit), F32),
            vmem((unit, unit // 2), F32),
            vmem((8, unit), F32),
            vmem(gains.shape, F32),
            vmem(gains.shape, F32),
            vmem(gains.shape, F32),
            vmem((n,) + gains.shape, F32),
            dma((4 * n,)),
            dma((4 * n,)),
            dma((TILE_SLOTS,)),
            dma((2 * n,)),
            dma((2, 2 * n)),
            pltpu.SemaphoreType.REGULAR,
            dma((16 * top,)),
            dma((16 * top,)),
            dma((2,)),
            dma((2,)),
            dma((4,)),
            dma((4,)),
            dma((4, 3)),
            dma((4, 3)),
            dma((7,)),
            dma((n,)),
            dma,
            dma((n,)),
            dma((7,)),
            dma((7, 2)),
            dma((7, 2)),
            dma((3 + 2 * top,)),
            dma((3 + 2 * top,)),
        ],
        compiler_params=pltpu.CompilerParams(
            collective_id=1, has_side_effects=True, vmem_limit_bytes=56 * 2**20
        ),
    )(*grads, *moments, gains)
    return results[:4], results[4:8], results[12]


def apply_kernel(unit, *refs):
    weights, moments, sums, orths = refs[:7], refs[7:14], refs[14:18], refs[18:22]
    new_weights, new_moments = refs[22:29], refs[29:36]
    weight, moment, grad, orth, weight_out, moment_out, load_sem, store_sem = refs[36:]
    slots, base = weight.shape[0], weight.shape[1]
    arrays = ((QKV, 0), (QKV, 2), (QKV, 3), (OUT, 0), (GU, 0), (GU, 3), (DOWN, 0))
    tiles = []
    for matrix, (array, first) in enumerate(arrays):
        for row in range(weights[matrix].shape[0] // base):
            for column in range(weights[matrix].shape[1] // unit):
                tiles.append((matrix, array, row * base, column * unit, (first + column) * unit))

    def loads(t):
        matrix, array, row, column, array_column = tiles[t]
        here = (pl.ds(row, base), pl.ds(column, unit))
        there = (pl.ds(row, base), pl.ds(array_column, unit))
        slot = t % slots
        return [
            pltpu.make_async_copy(source, target.at[slot], load_sem.at[slot, k])
            for k, (source, target) in enumerate(
                (
                    (weights[matrix].at[here], weight), (moments[matrix].at[here], moment),
                    (sums[array].at[there], grad), (orths[array].at[there], orth),
                )
            )
        ]

    def stores(t):
        matrix, _, row, column, _ = tiles[t]
        here = (pl.ds(row, base), pl.ds(column, unit))
        slot = t % slots
        return [
            pltpu.make_async_copy(weight_out.at[slot], new_weights[matrix].at[here], store_sem.at[slot, 0]),
            pltpu.make_async_copy(moment_out.at[slot], new_moments[matrix].at[here], store_sem.at[slot, 1]),
        ]

    for t in range(slots - 1):
        for copy in loads(t):
            copy.start()
    few = 16
    for t in range(len(tiles)):
        slot = t % slots
        if t + slots - 1 < len(tiles):
            for copy in loads(t + slots - 1):
                copy.start()
        for copy in loads(t):
            copy.wait()
        if t >= slots:
            for copy in stores(t - slots):
                copy.wait()

        def act(k, carry):
            rows = pl.ds(pl.multiple_of(k * few, few), few)
            weight_out[slot, rows, :] = weight[slot, rows, :] * (
                1.0 - LEARN_RATE * WEIGHT_DECAY
            ) - LEARN_RATE * orth[slot, rows, :].astype(F32)
            moment_out[slot, rows, :] = MOMENTUM * moment[slot, rows, :] + grad[
                slot, rows, :
            ].astype(F32)
            return carry

        lax.fori_loop(0, base // few, act, 0)
        for copy in stores(t):
            copy.start()
    for t in range(len(tiles) - slots, len(tiles)):
        for copy in stores(t):
            copy.wait()


def apply_all(weights, moments, sums, orths, n, unit):
    slots, base = 4, unit // n
    dma = pltpu.SemaphoreType.DMA
    vmem = pltpu.VMEM
    results = pl.pallas_call(
        functools.partial(apply_kernel, unit),
        out_shape=[jax.ShapeDtypeStruct(matrix.shape, F32) for matrix in weights] * 2,
        in_specs=[ANY] * 22,
        out_specs=[ANY] * 14,
        scratch_shapes=[
            vmem((slots, base, unit), F32),
            vmem((slots, base, unit), F32),
            vmem((slots, base, unit), BF16),
            vmem((slots, base, unit), BF16),
            vmem((slots, base, unit), F32),
            vmem((slots, base, unit), F32),
            dma((slots, 4)),
            dma((slots, 2)),
        ],
        compiler_params=pltpu.CompilerParams(vmem_limit_bytes=56 * 2**20),
    )(*weights, *moments, *sums, *orths)
    return results[:7], results[7:]


def body(
    layer_input,
    output_grad,
    lengths,
    attention_gain,
    feed_gain,
    query_gain,
    key_gain,
    query_weight,
    key_weight,
    value_weight,
    out_weight,
    gate_weight,
    up_weight,
    down_weight,
    query_moment,
    key_moment,
    value_moment,
    out_moment,
    gate_moment,
    up_moment,
    down_moment,
):
    owned = (
        query_weight, key_weight, value_weight, out_weight, gate_weight, up_weight, down_weight,
    )
    moments = (
        query_moment, key_moment, value_moment, out_moment, gate_moment, up_moment, down_moment,
    )
    n = lax.axis_size("own")
    unit = layer_input.shape[1]
    core = lax.axis_index("rep") % 2

    def halves(*matrices):
        parts = []
        for matrix in matrices:
            width = matrix.shape[1] // 2
            parts.append(lax.dynamic_slice_in_dim(matrix, core * width, width, 1))
        return jnp.concatenate(parts, 1).astype(BF16)

    step = unit // 2
    gate_half, up_half = halves(gate_weight), halves(up_weight)
    shards = (
        halves(query_weight, key_weight, value_weight),
        out_weight.astype(BF16),
        jnp.concatenate(
            [part[:, k * step : (k + 1) * step] for k in range(3) for part in (gate_half, up_half)], 1
        ),
        down_weight.astype(BF16),
    )
    row_count = layer_input.shape[0]
    _, positions = segments(lengths[0], row_count)
    cosine_table, sine_table = rope_tables(positions)
    starts = (jnp.arange(row_count, dtype=jnp.int32) - positions).astype(F32)
    table = jnp.concatenate(
        [
            cosine_table[:, 0], cosine_table[:, 0], -sine_table[:, 0], sine_table[:, 0],
            jnp.broadcast_to(starts[:, None], (row_count, HEAD_DIM)),
        ],
        1,
    )
    gain_rows = [gain[None, :] for gain in (attention_gain, feed_gain, query_gain, key_gain)]
    (block_output, input_grad), gain_grads, grads = layer_pass(
        layer_input, output_grad, table, gain_rows, shards, n
    )
    gains = jnp.concatenate([grad[0] for grad in gain_grads])
    gains = jnp.pad(gains, (0, 24 * 128 - gains.shape[0])).reshape(24, 128)
    reduced, orth, gain_sums = update_all(grads, moments, gains, n, unit)
    new_weights, moments_next = apply_all(owned, moments, reduced, orth, n, unit)
    gain_sums = gain_sums.reshape(-1)
    norm_grads = gain_sums[: 2 * unit].reshape(2, unit)
    head_grads = gain_sums[2 * unit : 2 * unit + 2 * HEAD_DIM].reshape(2, HEAD_DIM)
    return (block_output, input_grad, norm_grads, head_grads, *new_weights, *moments_next)


def solution(mesh):
    tokens, owned = P(("rep", "own"), None), P("own", None)
    return jax.shard_map(
        body,
        mesh=mesh,
        in_specs=(tokens,) * 3 + (P(),) * 4 + (owned,) * 14,
        out_specs=(tokens,) * 2 + (P(),) * 2 + (owned,) * 14,
        check_vma=False,
    )
```

```python
import functools

import jax
import jax.numpy as jnp
from jax import lax
from jax.experimental import pallas as pl
from jax.experimental.pallas import tpu as pltpu
from jax.sharding import PartitionSpec as P

HEADS = 16
KV_HEADS = 8
HEAD_DIM = 128
NS_STEPS = 5

EPSILON = 1e-06
ROPE_BASE = 1000000.0
MOMENTUM = 0.95
LEARN_RATE = 0.8
WEIGHT_DECAY = 0.01
NEWTON_A = 3.4445
NEWTON_B = -4.775
NEWTON_C = 2.0315

BF16 = jnp.bfloat16
F32 = jnp.float32
MESH = pl.DeviceIdType.MESH
ANY = pl.BlockSpec(memory_space=pltpu.HBM)

QKV, OUT, GU, DOWN = range(4)


def segments(lengths, row_count):
    seq_ends = jnp.cumsum(lengths)
    seq_starts = seq_ends - lengths
    row_ids = jnp.arange(row_count, dtype=jnp.int32)
    segment_ids = jnp.sum((row_ids[:, None] >= seq_ends[None, :]).astype(jnp.int32), 1)
    slot_ids = jnp.arange(lengths.shape[0], dtype=jnp.int32)
    row_starts = jnp.sum(
        jnp.where(segment_ids[:, None] == slot_ids[None, :], seq_starts[None, :], 0), 1
    )
    return (segment_ids, row_ids - row_starts)


def rope_tables(positions):
    inverse = ROPE_BASE ** (-jnp.arange(0, HEAD_DIM, 2, dtype=jnp.float32) / HEAD_DIM)
    angles = positions.astype(jnp.float32)[:, None] * inverse[None, :]
    return (jnp.cos(angles)[:, None, :], jnp.sin(angles)[:, None, :])


class Place:
    def __init__(self, n):
        self.n = n
        self.rep = lax.axis_index("rep")
        self.own = lax.axis_index("own")
        self.x = self.rep // 2
        self.core = self.rep % 2
        odd, pair = self.own % 2, self.own // 2
        self.ring = pair * (1 - odd) + odd * (n - 1 - pair)

    def own_at(self, ring):
        odd = ring // (self.n // 2)
        return 2 * (ring * (1 - odd) + odd * (self.n - 1 - ring)) + odd

    def shard(self, distance):
        return self.own_at(lax.rem(self.ring + distance + self.n, self.n))

    def ring_neighbour(self, way):
        return (self.rep, self.shard(way))

    @property
    def core_partner(self):
        return (self.x * 2 + 1 - self.core, self.own)

    @property
    def x_partner(self):
        return ((1 - self.x) * 2 + self.core, self.own)


def greet(devices):
    barrier = pltpu.get_barrier_semaphore()
    for device in devices:
        pl.semaphore_signal(barrier, inc=1, device_id=device, device_id_type=MESH)
    pl.semaphore_wait(barrier, len(devices))


class Several:
    def __init__(self, whole, copies):
        self.whole = whole
        self.copies = copies

    def start(self):
        for copy in self.copies:
            copy().start()

    def wait_send(self):
        self.whole().wait_send()

    def wait_recv(self):
        self.whole().wait_recv()


def remote(src, dst, send, recv, device):
    return pltpu.make_async_remote_copy(
        src_ref=src, dst_ref=dst, send_sem=send, recv_sem=recv, device_id=device, device_id_type=MESH
    )


def hops(n, way, kind):
    return n // 2 if (way == 0) == (kind == 0) else n // 2 - 1


SPREADS = ((QKV, True), (OUT, False), (GU, True), (DOWN, False))


def layer_kernel(n, tokens, unit, *refs):
    (
        x_ref, back_ref, table_ref, attention_gain, feed_gain, query_gain, key_gain,
    ) = refs[:7]
    shards = refs[7:11]
    output, input_grad, grad_attention, grad_feed, grad_query_gain, grad_key_gain = refs[11:17]
    grads = refs[17:21]
    (
        w_qkv, w_out, w_gu, w_down, normed, raw, low, probs, context, hidden, out_low, activated, gu_back, part, sent, got, middle, tables, stage, turned_left, normed_turned, context_turned, hidden_turned,
        gain_sums,
        local, ring_send, ring_recv, x_send, x_recv, swap_send, swap_recv, stage_sem,
    ) = refs[21:]
    weights = (w_qkv, w_out, w_gu, w_down)
    grad_context, attended = normed, context
    place = Place(n)
    top = n // 2
    cw, ccw = place.ring_neighbour(1), place.ring_neighbour(-1)
    ways = ((1, cw), (-1, ccw))
    greet([cw, ccw, place.core_partner, place.x_partner])
    both = 2 * tokens
    mine = pl.multiple_of(place.core * tokens, tokens)
    theirs = pl.multiple_of((1 - place.core) * tokens, tokens)
    my_rows, their_rows = pl.ds(mine, tokens), pl.ds(theirs, tokens)
    chunk = unit // 2
    ff = 3 * unit // 2
    few = 32
    base = unit // n
    heads = unit // HEAD_DIM
    kv_heads = heads // 2
    scale = HEAD_DIM ** (-0.5)

    def holds(which, own_index, act):
        if SPREADS[which][1]:
            act()
        else:
            pl.when(own_index // top == place.core)(act)

    def region(which, own_index, x):
        array, split = SPREADS[which]
        height = shards[which].shape[0]
        if split:
            width = weights[which].shape[1] // 2
            start = pl.multiple_of(own_index * height, height)
            return weights[which].at[pl.ds(start, height), pl.ds(pl.multiple_of(x * width, width), width)]
        start = pl.multiple_of(lax.rem(own_index, top) * height, height)
        return weights[which].at[pl.ds(start, height)]

    def own_copy(which):
        height = shards[which].shape[0]
        index = place.own if SPREADS[which][1] else lax.rem(place.own, top)
        start = pl.multiple_of(index * height, height)
        return pltpu.make_async_copy(
            shards[which], weights[which].at[pl.ds(start, height)], local.at[which]
        )

    def reach(which, way):
        return hops(n, way, 0 if SPREADS[which][1] else 1)

    def ring_copy(which, way, hop, act):
        step, target = ways[way]
        own_index = place.shard(-step * (hop if act == "wait_recv" else hop - 1))
        spot = region(which, own_index, place.x)
        index = (which * 2 + way) * top + hop - 1

        def do():
            copy = remote(spot, spot, ring_send.at[index], ring_recv.at[index], target)
            getattr(copy, act)()

        holds(which, own_index, do)

    def send_on(which, way, hop):
        ring_copy(which, way, hop, "start")

    def x_copy(which, way, hop, x):
        spot = region(which, place.shard(-ways[way][0] * hop), x)
        index = (which // 2 * 2 + way) * top + hop - 1
        return remote(spot, spot, x_send.at[index], x_recv.at[index], place.x_partner)

    def serve(which, hop):
        for way in range(2):
            if hop > reach(which, way):
                continue
            ring_copy(which, way, hop, "wait_recv")
            if hop < reach(which, way):
                send_on(which, way, hop + 1)
            if SPREADS[which][1]:
                x_copy(which, way, hop, place.x).start()

    def begin(which):
        def act():
            own_copy(which).wait()

        holds(which, place.own, act)
        for way in range(2):
            if reach(which, way) > 0:
                send_on(which, way, 1)

    def take_x(which):
        for way in range(2):
            for hop in range(1, reach(which, way) + 1):
                x_copy(which, way, hop, 1 - place.x).wait_recv()

    def swap(index, src, dst):
        return remote(src, dst, swap_send.at[index], swap_recv.at[index], place.core_partner)

    def rows_swap(index, ref):
        return swap(index, ref.at[my_rows], ref.at[my_rows])

    def part_swap(index, slot):
        return swap(index, sent.at[slot], got.at[slot])

    def loop(size, step, act):
        def body(k, carry):
            act(pl.multiple_of(k * step, step))
            return carry

        lax.fori_loop(0, size // step, body, 0)

    def normalize(source, gain, target):
        def act(k):
            value = source[pl.ds(k, few), :]
            value = value * lax.rsqrt(jnp.mean(value * value, -1, keepdims=True) + EPSILON)
            target[pl.ds(pl.multiple_of(mine + k, few), few), :] = (value * gain[...]).astype(BF16)

        loop(tokens, few, act)

    def normalize_back(k, source, gain, grad):
        value = source[pl.ds(k, few), :]
        inverse = lax.rsqrt(jnp.mean(value * value, -1, keepdims=True) + EPSILON)
        unscaled = value * inverse
        inner = grad * gain[...]
        back = inverse * (inner - unscaled * jnp.mean(inner * unscaled, -1, keepdims=True))
        return back, jnp.sum((grad * unscaled).reshape(few // 8, 8, unit), 0)

    def dot(left, right, across):
        return lax.dot_general(left, right, ((across[0], across[1]), ((), ())), preferred_element_type=F32)

    NN, NT, TN = ((1,), (0,)), ((1,), (1,)), ((0,), (0,))

    def partial_product(index, slot, left, right, across):
        part[...] = dot(left[...], right[...], across)

        def pack(k):
            sent[slot, pl.ds(k, few), :] = part[
                pl.ds(pl.multiple_of(theirs + k, few), few), :
            ].astype(BF16)

        loop(tokens, few, pack)
        part_swap(index, slot).start()

    def whole_rows(k, slot):
        own = part[pl.ds(pl.multiple_of(mine + k, few), few), :]
        return own + got[slot, pl.ds(k, few), :].astype(F32)

    def turn(left, target):
        def act(k):
            target[pl.ds(k, chunk), :] = left[:, pl.ds(k, chunk)].T

        loop(left.shape[1], chunk, act)

    def weight_grad(which, left, right, turned):
        columns = right.shape[1] // unit

        def by_rows(r, carry):
            row = pl.multiple_of(r * chunk, chunk)
            if turned is None:
                turned_left[...] = left[:, pl.ds(row, chunk)].T

            def by_columns(c, carry):
                column = pl.multiple_of(c * unit, unit)
                index = r * columns + c
                slot = lax.rem(index, 2)

                @pl.when(index >= 2)
                def _():
                    stage_copy(which, slot, row, column, chunk, unit).wait()

                block = turned_left[...] if turned is None else turned[pl.ds(row, chunk), :]
                value = dot(block, right[:, pl.ds(column, unit)], NN)
                stage[slot] = value.astype(BF16)
                stage_copy(which, slot, row, column, chunk, unit).start()
                return carry

            lax.fori_loop(0, columns, by_columns, 0)
            return carry

        lax.fori_loop(0, left.shape[1] // chunk, by_rows, 0)
        for slot in range(2):
            stage_copy(which, slot, 0, 0, chunk, unit).wait()

    def stage_copy(which, slot, row, column, height, width):
        return pltpu.make_async_copy(
            stage.at[slot], grads[which].at[pl.ds(row, height), pl.ds(column, width)],
            stage_sem.at[slot],
        )

    for which in range(4):
        holds(which, place.own, lambda: own_copy(which).start())
    tables[my_rows, :] = table_ref[...]
    normalize(x_ref, attention_gain, normed)
    rows_swap(0, normed).start()
    rows_swap(1, tables).start()
    begin(0)
    begin(1)

    def round_back(k):
        out_low[pl.ds(pl.multiple_of(mine + k, few), few), :] = back_ref[pl.ds(k, few), :].astype(BF16)

    loop(tokens, few, round_back)
    rows_swap(2, out_low).start()
    gain_sums[...] = jnp.zeros_like(gain_sums)

    late = [(1, top)] if top < 3 else [(1, h) for h in range(3, top + 1)]
    serve(0, 1)
    serve(1, 1)
    begin(2)
    for hop in range(2, top + 1):
        serve(0, hop)
        if (1, hop) not in late:
            serve(1, hop)
        if hop == 2:
            serve(2, 1)
    take_x(0)
    begin(3)
    pending = late + [(2, h) for h in range(2, top)] + [(3, 1), (2, top)]
    pending += [(3, h) for h in range(2, top + 1)]
    for name in (0, 1):
        rows_swap(name, (normed, tables)[name]).wait_recv()

    raw[:, pl.ds(0, unit)] = dot(normed[...], w_qkv[:, pl.ds(0, unit)], NN)
    keys_values = dot(normed[...], w_qkv[:, pl.ds(unit, unit)], NN)
    raw[:, pl.ds(unit, chunk)] = keys_values[:, :chunk]
    low[:, pl.ds(unit + chunk, chunk)] = keys_values[:, chunk:].astype(BF16)
    serve(*pending.pop(0))
    turn(normed, normed_turned)

    def turned(value, rows):
        return value * tables[rows, pl.ds(0, HEAD_DIM)] + pltpu.roll(
            value, HEAD_DIM // 2, 1
        ) * tables[rows, pl.ds(HEAD_DIM, HEAD_DIM)]

    def turned_back(value, rows):
        return value * tables[rows, pl.ds(0, HEAD_DIM)] - pltpu.roll(
            value, HEAD_DIM // 2, 1
        ) * tables[rows, pl.ds(HEAD_DIM, HEAD_DIM)]

    def head_norm(first, count, gain):
        def act(k):
            for half in range(2):
                rows = pl.ds(half * tokens, tokens)
                columns = pl.ds(pl.multiple_of(first + k, HEAD_DIM), HEAD_DIM)
                value = raw[rows, columns]
                inverse = lax.rsqrt(jnp.mean(value * value, -1, keepdims=True) + EPSILON)
                low[rows, columns] = turned(value * inverse * gain[...], rows).astype(BF16)

        loop(count * HEAD_DIM, HEAD_DIM, act)

    head_norm(0, heads, query_gain)
    if pending:
        serve(*pending.pop(0))
    head_norm(unit, kv_heads, key_gain)

    def spans(k, half):
        queries = [pl.ds(pl.multiple_of((2 * k + g) * HEAD_DIM, HEAD_DIM), HEAD_DIM) for g in range(2)]
        keys = pl.ds(pl.multiple_of(unit + k * HEAD_DIM, HEAD_DIM), HEAD_DIM)
        values = pl.ds(pl.multiple_of(unit + unit // 2 + k * HEAD_DIM, HEAD_DIM), HEAD_DIM)
        return queries, keys, values, pl.ds(half * tokens, tokens)

    def stacked(ref, rows, columns):
        return jnp.concatenate([ref[rows, columns[0]], ref[rows, columns[1]]], 0)

    def attend(k, half):
        queries, keys, values, rows = spans(k, half)
        row_id = lax.broadcasted_iota(jnp.int32, (tokens, tokens), 0)
        column_id = lax.broadcasted_iota(jnp.int32, (tokens, tokens), 1)
        start = tables[rows, pl.ds(2 * HEAD_DIM, HEAD_DIM)][:, :1]
        allowed = (column_id <= row_id) & (column_id.astype(F32) >= start)
        masks = jnp.where(allowed, 0.0, -1e30)
        scores = dot(stacked(low, rows, queries), low[rows, keys], NT) * scale
        scores = scores + jnp.concatenate([masks, masks], 0)
        exponent = jnp.exp(scores - jnp.max(scores, -1, keepdims=True))
        value = exponent / jnp.sum(exponent, -1, keepdims=True)
        probs[k * 2 + half] = value
        result = dot(value.astype(BF16), low[rows, values], NN).astype(BF16)
        for g in range(2):
            context[rows, queries[g]] = result[g * tokens : (g + 1) * tokens]

    for k in range(kv_heads):
        for half in range(2):
            attend(k, half)
        if pending and k % 2 == 0:
            serve(*pending.pop(0))

    while pending and pending[0][0] == 1:
        serve(*pending.pop(0))
    partial_product(3, 0, context, w_out, NN)
    turn(context, context_turned)
    if pending and pending[0][0] == 2:
        serve(*pending.pop(0))
    part_swap(3, 0).wait_recv()

    def add_middle(k):
        middle[pl.ds(k, few), :] = x_ref[pl.ds(k, few), :] + whole_rows(k, 0)

    loop(tokens, few, add_middle)
    normalize(middle, feed_gain, hidden)
    rows_swap(4, hidden).start()
    if pending:
        serve(*pending.pop(0))
    rows_swap(4, hidden).wait_recv()
    turn(hidden, hidden_turned)
    while pending:
        serve(*pending.pop(0))
    take_x(2)
    rows_swap(2, out_low).wait_recv()

    def feed(k):
        span = pl.ds(k, chunk)
        pair = pl.ds(pl.multiple_of(2 * k, unit), unit)
        gate_up = dot(hidden[...], w_gu[:, pair], NN)
        gate, up = gate_up[:, :chunk], gate_up[:, chunk:]
        grad = dot(out_low[...], w_down[span, :], NT)
        sigmoid = 1.0 / (1.0 + jnp.exp(-gate))
        swish = gate * sigmoid
        activated[:, span] = (swish * up).astype(BF16)
        gu_back[:, pl.ds(pl.multiple_of(2 * k, chunk), chunk)] = (
            grad * up * (sigmoid + swish * (1.0 - sigmoid))
        ).astype(BF16)
        gu_back[:, pl.ds(pl.multiple_of(2 * k + chunk, chunk), chunk)] = (grad * swish).astype(BF16)

    loop(ff, chunk, feed)
    part_swap(3, 0).wait_send()
    partial_product(6, 0, gu_back, w_gu, NT)
    weight_grad(3, activated, out_low, None)
    part_swap(6, 0).wait_recv()

    def middle_back(k):
        back, gain_part = normalize_back(k, middle, feed_gain, whole_rows(k, 0))
        back = back_ref[pl.ds(k, few), :] + back
        input_grad[pl.ds(k, few), :] = back
        attended[pl.ds(pl.multiple_of(mine + k, few), few), :] = back.astype(BF16)
        gain_sums[1] += gain_part

    loop(tokens, few, middle_back)
    rows_swap(7, attended).start()
    partial_product(5, 1, activated, w_down, NN)
    weight_grad(2, hidden, gu_back, hidden_turned)
    part_swap(5, 1).wait_recv()

    def add_output(k):
        output[pl.ds(k, few), :] = middle[pl.ds(k, few), :] + whole_rows(k, 1)

    loop(tokens, few, add_output)
    rows_swap(7, attended).wait_recv()

    rows_swap(0, normed).wait_send()
    grad_context[...] = dot(attended[...], w_out[...], NT).astype(BF16)
    weight_grad(1, context, attended, context_turned)

    def head_back(rows, columns, gain, grad, index):
        value = raw[rows, columns]
        inverse = lax.rsqrt(jnp.mean(value * value, -1, keepdims=True) + EPSILON)
        unscaled = value * inverse
        grad = turned_back(grad, rows)
        gain_sums[index, :, pl.ds(0, HEAD_DIM)] += jnp.sum(
            (grad * unscaled).reshape(tokens // 8, 8, HEAD_DIM), 0
        )
        inner = grad * gain[...]
        back = inverse * (inner - unscaled * jnp.mean(inner * unscaled, -1, keepdims=True))
        low[rows, columns] = back.astype(BF16)

    def attend_back(k, half):
        queries, keys, values, rows = spans(k, half)
        prob = probs[k * 2 + half]
        above = stacked(grad_context, rows, queries)
        query_pair = stacked(low, rows, queries)
        grad_values = dot(prob.astype(BF16), above, TN)
        grad_probs = dot(above, low[rows, values], NT)
        grad_scores = prob * (grad_probs - jnp.sum(prob * grad_probs, -1, keepdims=True))
        grad_scores = grad_scores.astype(BF16)
        grad_queries = dot(grad_scores, low[rows, keys], NN) * scale
        grad_keys = dot(grad_scores, query_pair, TN) * scale
        for g in range(2):
            head_back(rows, queries[g], query_gain, grad_queries[g * tokens : (g + 1) * tokens], 2)
        head_back(rows, keys, key_gain, grad_keys, 3)
        low[rows, values] = grad_values.astype(BF16)

    def back_body(k, carry):
        for half in range(2):
            attend_back(k, half)
        return carry

    lax.fori_loop(0, kv_heads, back_body, 0)

    part_swap(6, 0).wait_send()
    partial_product(8, 0, low, w_qkv, NT)
    weight_grad(0, normed, low, normed_turned)
    part_swap(8, 0).wait_recv()

    def input_back(k):
        back, gain_part = normalize_back(k, x_ref, attention_gain, whole_rows(k, 0))
        input_grad[pl.ds(k, few), :] += back
        gain_sums[0] += gain_part

    loop(tokens, few, input_back)
    grad_attention[...] = jnp.sum(gain_sums[0], 0, keepdims=True)
    grad_feed[...] = jnp.sum(gain_sums[1], 0, keepdims=True)
    grad_query_gain[...] = jnp.sum(gain_sums[2, :, pl.ds(0, HEAD_DIM)], 0, keepdims=True)
    grad_key_gain[...] = jnp.sum(gain_sums[3, :, pl.ds(0, HEAD_DIM)], 0, keepdims=True)

    for index, ref in ((1, tables), (2, out_low), (4, hidden), (7, attended)):
        rows_swap(index, ref).wait_send()
    part_swap(5, 1).wait_send()
    part_swap(8, 0).wait_send()
    for which in range(4):
        for way in range(2):
            for hop in range(1, reach(which, way) + 1):
                ring_copy(which, way, hop, "wait_send")
                if SPREADS[which][1]:
                    x_copy(which, way, hop, place.x).wait_send()


def layer_pass(values, back, table, gains, shards, n):
    tokens, unit = values.shape
    top = n // 2
    dma = pltpu.SemaphoreType.DMA
    vmem = pltpu.VMEM
    both = 2 * tokens
    heads = unit // HEAD_DIM
    in_vmem = pl.BlockSpec(memory_space=pltpu.VMEM)
    row = lambda width: jax.ShapeDtypeStruct((1, width), F32)
    shapes = [(unit, 2 * unit), (unit, unit), (unit, 3 * unit), (3 * unit // 2, unit)]
    results = pl.pallas_call(
        functools.partial(layer_kernel, n, tokens, unit),
        out_shape=[jax.ShapeDtypeStruct((tokens, unit), F32)] * 2
        + [row(unit), row(unit), row(HEAD_DIM), row(HEAD_DIM)]
        + [jax.ShapeDtypeStruct(shape, BF16) for shape in shapes],
        in_specs=[in_vmem] * 7 + [ANY] * 4,
        out_specs=[in_vmem] * 6 + [ANY] * 4,
        scratch_shapes=[vmem(shape, BF16) for shape in shapes]
        + [
            vmem((both, unit), BF16),
            vmem((both, 3 * unit // 2), F32),
            vmem((both, 2 * unit), BF16),
            vmem((heads, both, tokens), F32),
            vmem((both, unit), BF16),
            vmem((both, unit), BF16),
            vmem((both, unit), BF16),
            vmem((both, 3 * unit // 2), BF16),
            vmem((both, 3 * unit), BF16),
            vmem((both, unit), F32),
            vmem((2, tokens, unit), BF16),
            vmem((2, tokens, unit), BF16),
            vmem((tokens, unit), F32),
            vmem((both, 3 * HEAD_DIM), F32),
            vmem((2, unit // 2, unit), BF16),
            vmem((unit // 2, both), BF16),
            vmem((unit, both), BF16),
            vmem((unit, both), BF16),
            vmem((unit, both), BF16),
            vmem((4, 8, unit), F32),
            dma((4,)),
            dma((8 * top,)),
            dma((8 * top,)),
            dma((4 * top,)),
            dma((4 * top,)),
            dma((9,)),
            dma((9,)),
            dma((2,)),
        ],
        compiler_params=pltpu.CompilerParams(
            collective_id=0, has_side_effects=True, vmem_limit_bytes=56 * 2**20
        ),
    )(values, back, table, *gains, *shards)
    return results[:2], results[2:6], results[6:]


PHASES = ((DOWN, 3, False), (GU, 3, True), (OUT, 2, False), (QKV, 2, True))

OWNERS = (
    (3, 0, 1, False, 1, 2),
    (3, 1, 1, False, 1, 6),
    (3, 0, 2, False, 0, 2),
    (2, 0, 2, True, 1, 5),
    (1, 0, 3, False, 0, 5),
    (1, 0, 3, False, 1, 1),
    (0, 0, 3, True, 0, 1),
)
KEY, VALUE, QUERY, OUTM, GATE, UP, DOWNM = range(7)
RETURNS = (OUTM, KEY, VALUE, DOWNM, GATE, UP, QUERY)
TILE_SLOTS = 4
X_AHEAD = 8
LAND_AHEAD = 16


def summing_core(phase):
    return 0 if PHASES[phase][2] else 1


def stage_order(n, core):
    rings = ((1.0, 1.5), (4.0, 2.7), (13.0, 1.1), (26.6, 1.7))
    crossings = {1: (-6.0, 2.5), 3: (16.0, 1.5)}
    keys, needs = {}, {}
    for phase in range(4):
        first, step = rings[phase]
        for i in range(n):
            key = first + step * i * 8 / n
            if summing_core(phase) == core:
                keys["ring", phase, i] = key
                needs["ring", phase, i] = [("ring", phase, i - 1)] if i else []
                if phase in crossings:
                    needs["ring", phase, i].append(("x", phase, i))
            else:
                keys["land", phase, i] = key - 6.0
                needs["land", phase, i] = [("land", phase, i - 1)] if i else []
        if phase in crossings:
            first, step = crossings[phase]
            for i in range(n):
                keys["x", phase, i] = first + step * i * 8 / n
                needs["x", phase, i] = [("x", phase, i - 1)] if i else [("x", 1, n - 1)] * (phase == 3)
                if core == 0 and phase == 3:
                    needs["x", phase, i].append(("ring", 1, i))
        elif core == 1:
            keys["final", phase, 0] = {0: 16.0, 2: 27.0}[phase]
            needs["final", phase, 0] = [("ring", phase, n - 1)]
    left, found = sorted(keys, key=lambda stage: (keys[stage], stage)), []
    while left:
        stage = next(stage for stage in left if all(need in found for need in needs[stage]))
        left.remove(stage)
        found.append(stage)
    return found


class Rows:
    def __init__(self):
        self.next = 0

    def take(self, rows):
        start = self.next
        self.next += rows
        return start


def layout(n, unit):
    base = unit // n
    top = n // 2
    place = {}
    rows = (Rows(), Rows())
    place["high"] = [None, rows[1].take(3 * unit)]
    for name in ("grad", "ahead"):
        place[name] = [rows[summing_core(p)].take(PHASES[p][1] * base) for p in range(4)]
    for name in ("part", "other"):
        place[name] = [0 if split else rows[1].take(units * base) for _, units, split in PHASES]
    newton = Rows()
    newton.next = -(-rows[1].next // unit) * unit
    place["high"][0] = newton.take(3 * unit)
    place["poly"] = [newton.take(unit) for _ in range(2)]
    place["x_in"] = [rows[0].take(3 * base) for _ in range(n)]
    place["own"] = [[rows[core].take(3 * base) for _ in range(TILE_SLOTS)] for core in range(2)]
    place["ring"], place["far"] = [], []
    for phase, (_, units, _) in enumerate(PHASES):
        take = rows[summing_core(phase)].take
        place["ring"].append([[take(units * base) for _ in range(top)] for _ in range(2)])
        place["far"].append(take(units * base))
    return place, max(rows[0].next, rows[1].next, newton.next)


def update_kernel(n, unit, *refs):
    grads, moments, gains_in = refs[:4], refs[4:11], refs[11]
    outs, orths, lands, gains_out = refs[12:16], refs[16:20], refs[20:24], refs[24]
    (
        pool, exact, gram, squares, gain_mine, gain_core, gain_x, gain_all,
        land_send, land_recv, tile_sem, x_send, x_recv, x_free, ring_send, ring_recv, part_send, part_recv,
        moment_sem, grad_local, grad_send, grad_recv, in_send, in_recv, in_local,
        out_send, out_recv, pass_send, pass_recv, gain_send, gain_recv,
    ) = refs[25:]
    place = Place(n)
    base = unit // n
    top = n // 2
    at, _ = layout(n, unit)
    cw, ccw = place.ring_neighbour(1), place.ring_neighbour(-1)
    ways = ((1, cw), (-1, ccw))
    side = [(place.x * 2 + core, lax.rem(place.own + k, n)) for k in range(1, n) for core in range(2)]
    across = [((1 - place.x) * 2 + core, place.own) for core in range(2)]
    greet(side + [place.core_partner] + across)
    order = [top]
    for distance in range(top - 1, 0, -1):
        order += [distance, -distance]
    order.append(0)
    moment = exact
    height = [units * base for _, units, _ in PHASES]
    moment_at = [sum(height[:phase]) for phase in range(4)]
    owners = [
        (xs * 2 + 1, place.own_at(spot * n // 8)) for _, _, _, _, xs, spot in OWNERS
    ]
    here = place.rep * n + place.own
    is_owner = [here == rep * n + own for rep, own in owners]

    def rows(start, size):
        if isinstance(start, int):
            return pl.ds(start, size)
        return pl.ds(pl.multiple_of(start, size), size)

    def block(start, size):
        return pool.at[rows(start, size)]

    def pieces_of(phase, x):
        array, units, _ = PHASES[phase]
        half = unit // 2
        found = []
        for core in range(2):
            for b in range(units):
                if array == GU:
                    own_column = b * unit + x * half
                    column = x * 3 * unit + core * (3 * half) + b * half
                else:
                    own_column = x * units * half + b * half
                    column = x * 2 * unit + core * (unit - x * half) + b * (half + x * half)
                found.append((core, b, own_column, column))
        return found

    def columns(start):
        return pl.ds(pl.multiple_of(start, unit // 2), unit // 2)

    def in_block(start, core, b):
        return pool.at[pl.ds(start + b * base, base), pl.ds(core * (unit // 2), unit // 2)]

    def shard_rows(phase, own_index):
        if PHASES[phase][2]:
            return rows(own_index * base, base)
        return rows(lax.rem(own_index, top) * height[phase], height[phase])

    def landing(phase, own_index, act):
        if PHASES[phase][2]:
            act()
        else:
            pl.when(own_index // top != summing_core(phase))(act)

    def spread(source, target, size, send, recv, device):
        step = size

        def copy(k, count):
            return remote(block(source + k, count), block(target + k, count), send, recv, device)

        return Several(
            functools.partial(copy, 0, size),
            [functools.partial(copy, k, step) for k in range(0, size, step)],
        )

    def land_copy(phase, i, act):
        array, units, split = PHASES[phase]
        own_index = place.shard(order[i])
        span = shard_rows(phase, own_index)

        def copy(at_columns):
            return remote(
                grads[array].at[span, at_columns], lands[array].at[span, at_columns],
                land_send.at[phase * n + i], land_recv.at[phase * n + i], place.core_partner,
            )

        def do():
            if not split:
                getattr(copy(pl.ds(0, unit)), act)()
            elif act == "start":
                for core, _, column, _ in pieces_of(phase, place.x):
                    if core == 1:
                        copy(columns(column)).start()
            else:
                getattr(copy(pl.ds(0, units * unit // 2)), act)()

        landing(phase, own_index, do)

    def x_index(phase, i):
        return (phase // 2) * n + i

    def x_copies(phase, i, core, act):
        index = x_index(phase, i)
        array, units, _ = PHASES[phase]
        span = shard_rows(phase, place.shard(order[i]))
        target = at["x_in"][i]

        def copy(source, spot):
            return remote(
                source, spot, x_send.at[index], x_recv.at[core, index], ((1 - place.x) * 2, place.own)
            )

        if act == "start":
            for its_core, b, column, _ in pieces_of(phase, 1 - place.x):
                if its_core == core:
                    copy(grads[array].at[span, columns(column)], in_block(target, core, b)).start()
        else:
            spot = pool.at[pl.ds(target, height[phase]), pl.ds(core * (unit // 2), unit // 2)]
            getattr(copy(spot, spot), act)()

    def ring_copy(phase, way, distance, source, part):
        size = height[phase] // 2
        target = at["ring"][phase][way][distance - 1] + part * size
        index = ((phase * 2 + way) * top + distance - 1) * 2 + part
        return spread(
            source + part * size, target, size,
            ring_send.at[index], ring_recv.at[index], ways[way][1],
        )

    def ring_out(phase, distance, part):
        if distance == 0:
            return []
        if distance == top:
            return [ring_copy(phase, part, top, at["far"][phase], part)]
        way = 0 if distance > 0 else 1
        far = abs(distance)
        return [ring_copy(phase, way, far, at["ring"][phase][way][far], part)]

    def part_copy(phase):
        return spread(
            at["part"][phase], at["other"][phase], height[phase],
            part_send.at[phase // 2], part_recv.at[phase // 2], place.x_partner,
        )

    def gain_copy(src, dst, slot, device):
        return remote(src, dst, gain_send.at[slot], gain_recv.at[slot], device)

    def gain_core_copy():
        return gain_copy(gain_mine, gain_core, 0, place.core_partner)

    def gain_x_copy():
        return gain_copy(gain_core, gain_x, 1, place.x_partner)

    def gain_back_copy():
        return gain_copy(gain_mine, gain_x, 2, place.core_partner)

    def gain_ring(way, hop, distance):
        spot = gain_all.at[place.shard(distance)]
        return gain_copy(spot, spot, 3 + way * top + hop - 1, ways[way][1])

    def grad_place(phase, x):
        array = PHASES[phase][0]
        start = at["grad"][phase]
        if not PHASES[phase][2]:
            return [(outs[array], block(start, height[phase]))]
        return [
            (outs[array].at[:, columns(column)], in_block(start, core, b))
            for core, b, _, column in pieces_of(phase, x)
        ]

    def grad_span(phase, x):
        array, units, split = PHASES[phase]
        if not split:
            return outs[array]
        first = pl.multiple_of(x * units * unit, unit)
        return outs[array].at[:, pl.ds(first, units * unit)]

    def grad_sent(phase, to, device, x):
        span = grad_span(phase, x)
        return remote(span, span, grad_send.at[phase, to], grad_recv.at[phase, to], device)

    def matrix_rows(matrix, own_index):
        phase, first, units, tall, _, _ = OWNERS[matrix]
        if tall:
            return [(0, own_index * units * base, units * base)]
        return [
            ((first + k) * base, k * unit + own_index * base, base) for k in range(units)
        ]

    def matrix_span(matrix):
        phase, first, units, tall, xs, _ = OWNERS[matrix]
        array = PHASES[phase][0]
        if tall:
            return orths[array]
        start = (xs * PHASES[phase][1] + first) * unit
        return orths[array].at[:, pl.ds(start, units * unit)]

    def answer_parts(matrix, final, own_index):
        phase, first, units, tall, xs, _ = OWNERS[matrix]
        array = PHASES[phase][0]
        if tall:
            return [(block(final + own_index * units * base, units * base), orths[array])]
        return [
            (
                pool.at[
                    rows(final + (b - first) * unit + own_index * base, base),
                    pl.ds(core * (unit // 2), unit // 2),
                ],
                orths[array].at[:, columns(column)],
            )
            for core, b, _, column in pieces_of(phase, xs)
            if first <= b < first + units
        ]

    def handed(matrix, to, device):
        span = matrix_span(matrix)
        return remote(span, span, pass_send.at[matrix, to], pass_recv.at[matrix, to], device)

    def answered(matrix, target):
        span = matrix_span(matrix)
        return remote(
            span, span, out_send.at[target], out_recv.at[matrix], (place.x * 2, target)
        )

    def summed(pieces, size, store):
        step = 16
        steps = 4 if size % (4 * step) == 0 else 1

        def body(k, carry):
            for j in range(steps):
                shift = (k * steps + j) * step
                total = None
                for start in pieces:
                    value = pool[rows_at(start, shift, step), :].astype(F32)
                    total = value if total is None else total + value
                store(shift, step, total)
            return carry

        lax.fori_loop(0, size // (step * steps), body, 0)

    def rows_at(start, shift, step):
        return pl.ds(pl.multiple_of(start + shift, step), step)

    def keep(start):
        def store(shift, step, total):
            pool[rows_at(start, shift, step), :] = total.astype(BF16)

        return store

    def load_tile(phase, i, slot):
        array, _, split = PHASES[phase]
        own_index = place.shard(order[i])
        span = shard_rows(phase, own_index)
        summing = summing_core(phase)

        def load(source, target):
            pltpu.make_async_copy(source, target, tile_sem.at[slot]).start()

        if split:
            for core, b, column, _ in pieces_of(phase, place.x):
                load(
                    (grads, lands)[core][array].at[span, columns(column)],
                    in_block(at["own"][summing][slot], core, b),
                )
            return
        for core in range(2):

            @pl.when(own_index // top == core)
            def _():
                load(
                    (lands, grads)[core == summing][array].at[span],
                    block(at["own"][summing][slot], height[phase]),
                )

    def prefetch(rings, index):
        if index < len(rings):
            _, phase, i = rings[index]
            land_copy(phase, i, "wait_recv")
            load_tile(phase, i, index % TILE_SLOTS)

    def moment_copies(phase, act):
        array, units, split = PHASES[phase]
        if not split:
            act(moments[3 if array == OUT else 6], moment.at[pl.ds(moment_at[phase], height[phase])])
            return
        half = unit // 2
        for x in range(2):

            @pl.when(place.x == x)
            def _():
                for core, b, _, column in pieces_of(phase, x):
                    if array == GU:
                        source, first = 4 + x, x * 3 * unit
                    elif x == 0:
                        source, first = 0, 0
                    else:
                        source, first = 1 + b, (2 + b) * unit
                    act(
                        moments[source].at[:, pl.ds(column - first, half)],
                        moment.at[pl.ds(moment_at[phase] + b * base, base), pl.ds(core * half, half)],
                    )

    def load_moment(phase):
        moment_copies(
            phase, lambda src, dst: pltpu.make_async_copy(src, dst, moment_sem.at[phase]).start()
        )

    def finish(phase, pieces):
        span = moment.at[pl.ds(moment_at[phase], height[phase])]
        pltpu.make_async_copy(span, span, moment_sem.at[phase]).wait()

        def store(shift, step, total):
            pool[rows_at(at["grad"][phase], shift, step), :] = total.astype(BF16)
            ahead = (1.0 + MOMENTUM) * total + MOMENTUM**2 * moment[
                rows_at(moment_at[phase], shift, step), :
            ]
            pool[rows_at(at["ahead"][phase], shift, step), :] = ahead.astype(BF16)

        summed(pieces, height[phase], store)
        for matrix, (its_phase, _, _, _, xs, _) in enumerate(OWNERS):
            if its_phase != phase:
                continue

            def hand_in(local):
                for source, target, size in matrix_rows(matrix, place.own):
                    source = block(at["ahead"][phase] + source, size)
                    target = block(at["high"][1] + target, size)
                    if local:
                        pltpu.make_async_copy(source, target, in_local).start()
                    else:
                        remote(
                            source, target, in_send.at[matrix], in_recv.at[place.own], owners[matrix]
                        ).start()

            if summing_core(phase) == 0:
                pl.when(place.x == xs)(functools.partial(hand_in, False))
            else:
                pl.when(is_owner[matrix])(functools.partial(hand_in, True))
                pl.when((place.x == xs) & (here != owners[matrix][0] * n + owners[matrix][1]))(
                    functools.partial(hand_in, False)
                )

        for target, source in grad_place(phase, place.x):
            pltpu.make_async_copy(source, target, grad_local.at[phase]).start()
            remote(
                source, target, grad_send.at[phase, 0], grad_recv.at[phase, 0], place.core_partner
            ).start()
            if PHASES[phase][2]:
                remote(
                    source, target, grad_send.at[phase, 1], grad_recv.at[phase, 1], place.x_partner
                ).start()

    def settle(phase):
        span = block(at["grad"][phase], height[phase])
        pltpu.make_async_copy(span, span, grad_local.at[phase]).wait()
        remote(
            span, span, grad_send.at[phase, 0], grad_recv.at[phase, 0], place.core_partner
        ).wait_send()
        if PHASES[phase][2]:
            remote(
                span, span, grad_send.at[phase, 1], grad_recv.at[phase, 1], place.x_partner
            ).wait_send()
        for matrix, (its_phase, _, units, _, xs, _) in enumerate(OWNERS):
            if its_phase != phase:
                continue

            sends = place.x == xs
            if summing_core(phase) == 1:
                sends = sends & (here != owners[matrix][0] * n + owners[matrix][1])

            @pl.when(sends)
            def _():
                span = block(at["high"][1], units * base)
                remote(
                    span, span, in_send.at[matrix], in_recv.at[0], place.core_partner
                ).wait_send()

    def stage_x(phase, i, core):
        index = x_index(phase, i)
        if index >= X_AHEAD:
            before = index - X_AHEAD
            x_copies(1 if before < n else 3, before % n, core, "wait_send")
        if phase == 3:
            pl.semaphore_wait(x_free, 1)
        x_copies(phase, i, core, "start")

    def stage_ring(phase, i, slot):
        distance = order[i]
        start = at["own"][summing_core(phase)][slot]
        span = block(start, height[phase])
        pltpu.make_async_copy(span, span, tile_sem.at[slot]).wait()
        pieces = [start]
        if PHASES[phase][2]:
            for core in range(2):
                x_copies(phase, i, core, "wait_recv")
            pieces.append(at["x_in"][i])
        size = height[phase]
        mid = size // 2
        if distance == 0:
            for way in range(2):
                held = at["ring"][phase][way][0]
                for part in range(2):
                    ring_copy(phase, way, 1, held, part).wait_recv()
                pieces.append(held)
            if PHASES[phase][2]:
                finish(phase, pieces)
            else:
                summed(pieces, size, keep(at["part"][phase]))
                part_copy(phase).start()
        else:
            way = 0 if distance > 0 else 1
            far = abs(distance)
            held = at["far"][phase] if far == top else at["ring"][phase][way][far]
            for part in (1 - way, way):
                starts = [start + part * mid for start in pieces]
                if far + 1 < top or (far + 1 == top and part == way):
                    ring_copy(phase, way, far + 1, held, part).wait_recv()
                    starts.append(held + part * mid)
                summed(starts, mid, keep(held + part * mid))
                for copy in ring_out(phase, distance, part):
                    copy.start()
        if phase == 1:
            for device in across:
                pl.semaphore_signal(x_free, inc=1, device_id=device, device_id_type=MESH)

    def ring_sent(phase):
        for distance in order:
            for part in range(2):
                for copy in ring_out(phase, distance, part):
                    copy.wait_send()

    def run(core):
        stages = stage_order(n, core)
        rings = [stage for stage in stages if stage[0] == "ring"]
        landed = [stage for stage in stages if stage[0] == "land"]
        for phase in range(4):
            if summing_core(phase) == core:
                load_moment(phase)
        done, sent, hop = 0, 0, 0
        for index in range(min(LAND_AHEAD, len(landed))):
            land_copy(*landed[index][1:], "start")
        for index in range(TILE_SLOTS - 1):
            prefetch(rings, index)
        for kind, phase, i in stages:
            if kind == "x":
                stage_x(phase, i, core)
            elif kind == "land":
                land_copy(phase, i, "wait_send")
                if sent + LAND_AHEAD < len(landed):
                    land_copy(*landed[sent + LAND_AHEAD][1:], "start")
                sent += 1
            elif kind == "final":
                part_copy(phase).wait_recv()
                finish(phase, [at["part"][phase], at["other"][phase]])
            else:
                prefetch(rings, done + TILE_SLOTS - 1)
                stage_ring(phase, i, done % TILE_SLOTS)
                done += 1
                if core == 0 and hop <= top + 1:
                    gain_stage(hop)
                    hop += 1

    def settle_all(core):
        for phase, (_, _, split) in enumerate(PHASES):
            if summing_core(phase) == core:
                settle(phase)
                if not split:
                    part_copy(phase).wait_send()
        for index in range(2 * n - X_AHEAD, 2 * n):
            x_copies(1 if index < n else 3, index % n, core, "wait_send")

    def take_sums(core):
        for phase, (_, _, split) in enumerate(PHASES):
            if summing_core(phase) != core:
                grad_sent(phase, 0, place.core_partner, place.x).wait_recv()
                if split:
                    grad_sent(phase, 2, place.core_partner, 1 - place.x).wait_recv()

    def gain_stage(hop):
        if hop == 0:
            gain_core_copy().wait_recv()
            gain_core[...] = gain_mine[...] + gain_core[...]
            gain_x_copy().start()
            return
        if hop == 1:
            gain_x_copy().wait_recv()
            gain_all[place.own] = gain_core[...] + gain_x[...]
            for way in range(2):
                gain_ring(way, 1, 0).start()
        for way in range(2):
            if 1 < hop <= hops(n, way, 0) + 1:
                distance = -ways[way][0] * (hop - 1)
                gain_ring(way, hop - 1, distance).wait_recv()
                if hop <= hops(n, way, 0):
                    gain_ring(way, hop, distance).start()

    gain_mine[...] = gains_in[...]

    @pl.when(place.core == 0)
    def _():
        run(0)
        total = gain_all[0]
        for k in range(1, n):
            total = total + gain_all[k]
        gains_out[...] = total
        gain_mine[...] = total
        gain_back_copy().start()

        for phase in (1, 3):
            grad_sent(phase, 1, place.x_partner, 1 - place.x).wait_recv()
            grad_sent(phase, 2, place.core_partner, 1 - place.x).start()

        for matrix in RETURNS:
            xs = OWNERS[matrix][4]

            @pl.when(place.x == xs)
            def _():
                answered(matrix, place.own).wait_recv()
                handed(matrix, 0, place.x_partner).start()
                handed(matrix, 1, place.core_partner).start()

            @pl.when(place.x != xs)
            def _():
                handed(matrix, 0, place.x_partner).wait_recv()
                handed(matrix, 1, place.core_partner).start()

        for matrix, (phase, _, units, _, xs, _) in enumerate(OWNERS):
            handed(matrix, 1, place.core_partner).wait_send()

            @pl.when(place.x == xs)
            def _():
                handed(matrix, 0, place.x_partner).wait_send()

        take_sums(0)
        settle_all(0)
        for phase in (1, 3):
            ring_sent(phase)
            grad_sent(phase, 2, place.core_partner, 1 - place.x).wait_send()
        gain_x_copy().wait_send()
        gain_back_copy().wait_send()
        for way in range(2):
            for h in range(1, hops(n, way, 0) + 1):
                gain_ring(way, h, -ways[way][0] * (h - 1)).wait_send()

    @pl.when(place.core == 1)
    def _():
        gain_core_copy().start()
        run(1)
        for phase in (0, 2):
            ring_sent(phase)
        newton_part(n, unit, place, pool, exact, gram, squares, at, is_owner, in_recv, in_local)
        for matrix, (_, _, units, tall, _, _) in enumerate(OWNERS):

            @pl.when(is_owner[matrix])
            def _():
                final = at["high"][1 - NS_STEPS % 2 if tall else NS_STEPS % 2]

                def send(k, carry):
                    target = lax.rem(place.own + k, n)
                    for source, part in answer_parts(matrix, final, target):
                        remote(
                            source, part, out_send.at[target], out_recv.at[matrix],
                            (place.x * 2, target),
                        ).start()
                    return carry

                lax.fori_loop(0, n, send, 0)

                def sent(k, carry):
                    answered(matrix, lax.rem(place.own + k, n)).wait_send()
                    return carry

                lax.fori_loop(0, n, sent, 0)

        gain_core_copy().wait_send()
        gain_back_copy().wait_recv()
        gains_out[...] = gain_x[...]
        take_sums(1)
        settle_all(1)
        for matrix in RETURNS:
            handed(matrix, 1, place.core_partner).wait_recv()


def newton_part(n, unit, place, pool, exact, gram, squares, at, is_owner, in_recv, in_local):
    base = unit // n
    small = min(256, unit // 2)
    per = unit // small
    wide = unit // 2
    few = 32
    count, tall = 0, 0
    for mine, (_, _, units, lies_tall, _, _) in zip(is_owner, OWNERS):
        count = count + units * mine.astype(jnp.int32)
        tall = tall + int(lies_tall) * mine.astype(jnp.int32)
    high, poly = at["high"], at["poly"]

    def rows(start, size):
        return pl.ds(pl.multiple_of(start, size), size)

    for matrix, (phase, _, units, *_) in enumerate(OWNERS):

        @pl.when(is_owner[matrix])
        def _():
            span = pool.at[pl.ds(high[1], units * base)]
            inside = summing_core(phase) == 1
            if inside:
                pltpu.make_async_copy(span, span, in_local).wait()
            for k in range(1 if inside else 0, n):
                own_index = lax.rem(place.own + k, n)
                remote(
                    span, span, in_recv.at[own_index], in_recv.at[own_index], place.core_partner
                ).wait_recv()

    @pl.when(count > 0)
    def _():
        squares[...] = jnp.zeros_like(squares)

        def square(k, carry):
            part = pool[rows(high[1] + k * few, few), :].astype(F32)
            squares[...] += jnp.sum((part * part).reshape(few // 8, 8, unit), 0)
            return carry

        lax.fori_loop(0, count * (unit // few), square, 0)
        total = jnp.sum(jnp.sum(squares[...], 1, keepdims=True), 0, keepdims=True)
        inverse = 1.0 / (jnp.sqrt(total) + 1e-07)

        @pl.when(tall == 0)
        def _():
            def scale(k, carry):
                value = pool[rows(high[1] + k * few, few), :].astype(F32) * inverse
                exact[rows(k * few, few), :] = value
                pool[rows(high[0] + k * few, few), :] = value.astype(BF16)
                return carry

            lax.fori_loop(0, count * (unit // few), scale, 0)

        @pl.when(tall == 1)
        def _():
            def scale(k, carry):
                block, row = k // per, k % per
                for column in range(per):
                    part = pool[
                        rows(high[1] + k * small, small), pl.ds(column * small, small)
                    ].astype(F32)
                    value = (part * inverse).T
                    shift = block * unit + column * small
                    columns = rows(row * small, small)
                    exact[rows(shift, small), columns] = value
                    pool[rows(high[0] + shift, small), columns] = value.astype(BF16)
                return carry

            lax.fori_loop(0, count * per, scale, 0)

        def newton(step, carry):
            even = step % 2
            now = high[0] + even * (high[1] - high[0])
            later = high[1] - even * (high[1] - high[0])

            def keep_symmetric(to, chunk, value):
                pool[pl.ds(to, (chunk + 1) * wide), pl.ds(chunk * wide, wide)] = value.astype(BF16)
                if chunk == 1:
                    pool[pl.ds(to + wide, wide), pl.ds(0, wide)] = value[:wide].T.astype(BF16)

            for chunk in range(2):
                down = (chunk + 1) * wide

                def product(block):
                    left = pool[pl.ds(pl.multiple_of(now + block * unit, unit), down), :]
                    right = pool[rows(now + block * unit + chunk * wide, wide), :]
                    return lax.dot_general(
                        left, right, (((1,), (1,)), ((), ())), preferred_element_type=F32
                    )

                gram[:down, :] = product(0)

                def more(block, carry):
                    gram[:down, :] += product(block)
                    return carry

                lax.fori_loop(1, count, more, 0)
                keep_symmetric(poly[0], chunk, gram[:down, :])

            for chunk in range(2):
                down = (chunk + 1) * wide
                columns = pl.ds(chunk * wide, wide)
                squared = jnp.dot(
                    pool[pl.ds(poly[0], down), :], pool[pl.ds(poly[0], unit), columns],
                    preferred_element_type=F32,
                )
                plain = pool[pl.ds(poly[0], down), columns].astype(F32)
                keep_symmetric(poly[1], chunk, NEWTON_B * plain + NEWTON_C * squared)

            def advance(block, carry):
                for chunk in range(2):
                    columns = pl.ds(chunk * wide, wide)
                    value = NEWTON_A * exact[rows(block * unit, unit), columns] + jnp.dot(
                        pool[pl.ds(poly[1], unit), :],
                        pool[rows(now + block * unit, unit), columns],
                        preferred_element_type=F32,
                    )
                    exact[rows(block * unit, unit), columns] = value
                    pool[rows(later + block * unit, unit), columns] = value.astype(BF16)
                return carry

            lax.fori_loop(0, count, advance, 0)
            return carry

        lax.fori_loop(0, NS_STEPS, newton, 0)

        @pl.when(tall == 1)
        def _():
            free = high[1 - NS_STEPS % 2]
            factor = jnp.sqrt(jnp.full((1, 1), count, jnp.int32).astype(F32))

            def lay(k, carry):
                block, row = k // per, k % per
                for column in range(per):
                    columns = pl.ds(column * small, small)
                    part = exact[rows(k * small, small), columns]
                    pool[
                        rows(free + block * unit + column * small, small), rows(row * small, small)
                    ] = (part * factor).T.astype(BF16)
                return carry

            lax.fori_loop(0, count * per, lay, 0)


def update_all(grads, moments, gains, n, unit):
    top = n // 2
    dma = pltpu.SemaphoreType.DMA
    vmem = pltpu.VMEM
    _, pool_rows = layout(n, unit)
    shapes = [(unit // n, 4 * unit), (2 * unit // n, unit), (unit // n, 6 * unit), (3 * unit // n, unit)]
    own = [jax.ShapeDtypeStruct(shape, BF16) for shape in shapes]
    whole = [jax.ShapeDtypeStruct(grad.shape, BF16) for grad in grads]
    in_vmem = pl.BlockSpec(memory_space=pltpu.VMEM)
    results = pl.pallas_call(
        functools.partial(update_kernel, n, unit),
        out_shape=own + own + whole + [jax.ShapeDtypeStruct(gains.shape, F32)],
        in_specs=[ANY] * 11 + [in_vmem],
        out_specs=[ANY] * 12 + [in_vmem],
        scratch_shapes=[
            vmem((pool_rows, unit), BF16),
            vmem((3 * unit, unit), F32),
            vmem((unit, unit // 2), F32),
            vmem((8, unit), F32),
            vmem(gains.shape, F32),
            vmem(gains.shape, F32),
            vmem(gains.shape, F32),
            vmem((n,) + gains.shape, F32),
            dma((4 * n,)),
            dma((4 * n,)),
            dma((TILE_SLOTS,)),
            dma((2 * n,)),
            dma((2, 2 * n)),
            pltpu.SemaphoreType.REGULAR,
            dma((16 * top,)),
            dma((16 * top,)),
            dma((2,)),
            dma((2,)),
            dma((4,)),
            dma((4,)),
            dma((4, 3)),
            dma((4, 3)),
            dma((7,)),
            dma((n,)),
            dma,
            dma((n,)),
            dma((7,)),
            dma((7, 2)),
            dma((7, 2)),
            dma((3 + 2 * top,)),
            dma((3 + 2 * top,)),
        ],
        compiler_params=pltpu.CompilerParams(
            collective_id=1, has_side_effects=True, vmem_limit_bytes=56 * 2**20
        ),
    )(*grads, *moments, gains)
    return results[:4], results[4:8], results[12]


def apply_kernel(unit, *refs):
    weights, moments, sums, orths = refs[:7], refs[7:14], refs[14:18], refs[18:22]
    new_weights, new_moments = refs[22:29], refs[29:36]
    weight, moment, grad, orth, weight_out, moment_out, load_sem, store_sem = refs[36:]
    slots, base = weight.shape[0], weight.shape[1]
    arrays = ((QKV, 0), (QKV, 2), (QKV, 3), (OUT, 0), (GU, 0), (GU, 3), (DOWN, 0))
    tiles = []
    for matrix, (array, first) in enumerate(arrays):
        for row in range(weights[matrix].shape[0] // base):
            for column in range(weights[matrix].shape[1] // unit):
                tiles.append((matrix, array, row * base, column * unit, (first + column) * unit))

    def loads(t):
        matrix, array, row, column, array_column = tiles[t]
        here = (pl.ds(row, base), pl.ds(column, unit))
        there = (pl.ds(row, base), pl.ds(array_column, unit))
        slot = t % slots
        return [
            pltpu.make_async_copy(source, target.at[slot], load_sem.at[slot, k])
            for k, (source, target) in enumerate(
                (
                    (weights[matrix].at[here], weight), (moments[matrix].at[here], moment),
                    (sums[array].at[there], grad), (orths[array].at[there], orth),
                )
            )
        ]

    def stores(t):
        matrix, _, row, column, _ = tiles[t]
        here = (pl.ds(row, base), pl.ds(column, unit))
        slot = t % slots
        return [
            pltpu.make_async_copy(weight_out.at[slot], new_weights[matrix].at[here], store_sem.at[slot, 0]),
            pltpu.make_async_copy(moment_out.at[slot], new_moments[matrix].at[here], store_sem.at[slot, 1]),
        ]

    for t in range(slots - 1):
        for copy in loads(t):
            copy.start()
    few = 16
    for t in range(len(tiles)):
        slot = t % slots
        if t + slots - 1 < len(tiles):
            for copy in loads(t + slots - 1):
                copy.start()
        for copy in loads(t):
            copy.wait()
        if t >= slots:
            for copy in stores(t - slots):
                copy.wait()

        def act(k, carry):
            rows = pl.ds(pl.multiple_of(k * few, few), few)
            weight_out[slot, rows, :] = weight[slot, rows, :] * (
                1.0 - LEARN_RATE * WEIGHT_DECAY
            ) - LEARN_RATE * orth[slot, rows, :].astype(F32)
            moment_out[slot, rows, :] = MOMENTUM * moment[slot, rows, :] + grad[
                slot, rows, :
            ].astype(F32)
            return carry

        lax.fori_loop(0, base // few, act, 0)
        for copy in stores(t):
            copy.start()
    for t in range(len(tiles) - slots, len(tiles)):
        for copy in stores(t):
            copy.wait()


def apply_all(weights, moments, sums, orths, n, unit):
    slots, base = 4, unit // n
    dma = pltpu.SemaphoreType.DMA
    vmem = pltpu.VMEM
    results = pl.pallas_call(
        functools.partial(apply_kernel, unit),
        out_shape=[jax.ShapeDtypeStruct(matrix.shape, F32) for matrix in weights] * 2,
        in_specs=[ANY] * 22,
        out_specs=[ANY] * 14,
        scratch_shapes=[
            vmem((slots, base, unit), F32),
            vmem((slots, base, unit), F32),
            vmem((slots, base, unit), BF16),
            vmem((slots, base, unit), BF16),
            vmem((slots, base, unit), F32),
            vmem((slots, base, unit), F32),
            dma((slots, 4)),
            dma((slots, 2)),
        ],
        compiler_params=pltpu.CompilerParams(vmem_limit_bytes=56 * 2**20),
    )(*weights, *moments, *sums, *orths)
    return results[:7], results[7:]


def body(
    layer_input,
    output_grad,
    lengths,
    attention_gain,
    feed_gain,
    query_gain,
    key_gain,
    query_weight,
    key_weight,
    value_weight,
    out_weight,
    gate_weight,
    up_weight,
    down_weight,
    query_moment,
    key_moment,
    value_moment,
    out_moment,
    gate_moment,
    up_moment,
    down_moment,
):
    owned = (
        query_weight, key_weight, value_weight, out_weight, gate_weight, up_weight, down_weight,
    )
    moments = (
        query_moment, key_moment, value_moment, out_moment, gate_moment, up_moment, down_moment,
    )
    n = lax.axis_size("own")
    unit = layer_input.shape[1]
    core = lax.axis_index("rep") % 2

    def halves(*matrices):
        parts = []
        for matrix in matrices:
            width = matrix.shape[1] // 2
            parts.append(lax.dynamic_slice_in_dim(matrix, core * width, width, 1))
        return jnp.concatenate(parts, 1).astype(BF16)

    step = unit // 2
    gate_half, up_half = halves(gate_weight), halves(up_weight)
    shards = (
        halves(query_weight, key_weight, value_weight),
        out_weight.astype(BF16),
        jnp.concatenate(
            [part[:, k * step : (k + 1) * step] for k in range(3) for part in (gate_half, up_half)], 1
        ),
        down_weight.astype(BF16),
    )
    row_count = layer_input.shape[0]
    _, positions = segments(lengths[0], row_count)
    cosine_table, sine_table = rope_tables(positions)
    starts = (jnp.arange(row_count, dtype=jnp.int32) - positions).astype(F32)
    table = jnp.concatenate(
        [
            cosine_table[:, 0], cosine_table[:, 0], -sine_table[:, 0], sine_table[:, 0],
            jnp.broadcast_to(starts[:, None], (row_count, HEAD_DIM)),
        ],
        1,
    )
    gain_rows = [gain[None, :] for gain in (attention_gain, feed_gain, query_gain, key_gain)]
    (block_output, input_grad), gain_grads, grads = layer_pass(
        layer_input, output_grad, table, gain_rows, shards, n
    )
    gains = jnp.concatenate([grad[0] for grad in gain_grads])
    gains = jnp.pad(gains, (0, 24 * 128 - gains.shape[0])).reshape(24, 128)
    reduced, orth, gain_sums = update_all(grads, moments, gains, n, unit)
    new_weights, moments_next = apply_all(owned, moments, reduced, orth, n, unit)
    gain_sums = gain_sums.reshape(-1)
    norm_grads = gain_sums[: 2 * unit].reshape(2, unit)
    head_grads = gain_sums[2 * unit : 2 * unit + 2 * HEAD_DIM].reshape(2, HEAD_DIM)
    return (block_output, input_grad, norm_grads, head_grads, *new_weights, *moments_next)


def solution(mesh):
    tokens, owned = P(("rep", "own"), None), P("own", None)
    return jax.shard_map(
        body,
        mesh=mesh,
        in_specs=(tokens,) * 3 + (P(),) * 4 + (owned,) * 14,
        out_specs=(tokens,) * 2 + (P(),) * 2 + (owned,) * 14,
        check_vma=False,
    )
```

```python
import functools

import jax
import jax.numpy as jnp
from jax import lax
from jax.experimental import pallas as pl
from jax.experimental.pallas import tpu as pltpu
from jax.sharding import PartitionSpec as P

HEADS = 16
KV_HEADS = 8
HEAD_DIM = 128
NS_STEPS = 5

EPSILON = 1e-06
ROPE_BASE = 1000000.0
MOMENTUM = 0.95
LEARN_RATE = 0.8
WEIGHT_DECAY = 0.01
NEWTON_A = 3.4445
NEWTON_B = -4.775
NEWTON_C = 2.0315

BF16 = jnp.bfloat16
F32 = jnp.float32
MESH = pl.DeviceIdType.MESH
ANY = pl.BlockSpec(memory_space=pltpu.HBM)

QKV, OUT, GU, DOWN = range(4)


def segments(lengths, row_count):
    seq_ends = jnp.cumsum(lengths)
    seq_starts = seq_ends - lengths
    row_ids = jnp.arange(row_count, dtype=jnp.int32)
    segment_ids = jnp.sum((row_ids[:, None] >= seq_ends[None, :]).astype(jnp.int32), 1)
    slot_ids = jnp.arange(lengths.shape[0], dtype=jnp.int32)
    row_starts = jnp.sum(
        jnp.where(segment_ids[:, None] == slot_ids[None, :], seq_starts[None, :], 0), 1
    )
    return (segment_ids, row_ids - row_starts)


def rope_tables(positions):
    inverse = ROPE_BASE ** (-jnp.arange(0, HEAD_DIM, 2, dtype=jnp.float32) / HEAD_DIM)
    angles = positions.astype(jnp.float32)[:, None] * inverse[None, :]
    return (jnp.cos(angles)[:, None, :], jnp.sin(angles)[:, None, :])


class Place:
    def __init__(self, n):
        self.n = n
        self.rep = lax.axis_index("rep")
        self.own = lax.axis_index("own")
        self.x = self.rep // 2
        self.core = self.rep % 2
        odd, pair = self.own % 2, self.own // 2
        self.ring = pair * (1 - odd) + odd * (n - 1 - pair)

    def own_at(self, ring):
        odd = ring // (self.n // 2)
        return 2 * (ring * (1 - odd) + odd * (self.n - 1 - ring)) + odd

    def shard(self, distance):
        return self.own_at(lax.rem(self.ring + distance + self.n, self.n))

    def ring_neighbour(self, way):
        return (self.rep, self.shard(way))

    @property
    def core_partner(self):
        return (self.x * 2 + 1 - self.core, self.own)

    @property
    def x_partner(self):
        return ((1 - self.x) * 2 + self.core, self.own)


def greet(devices):
    barrier = pltpu.get_barrier_semaphore()
    for device in devices:
        pl.semaphore_signal(barrier, inc=1, device_id=device, device_id_type=MESH)
    pl.semaphore_wait(barrier, len(devices))


class Several:
    def __init__(self, whole, copies):
        self.whole = whole
        self.copies = copies

    def start(self):
        for copy in self.copies:
            copy().start()

    def wait_send(self):
        self.whole().wait_send()

    def wait_recv(self):
        self.whole().wait_recv()


def remote(src, dst, send, recv, device):
    return pltpu.make_async_remote_copy(
        src_ref=src, dst_ref=dst, send_sem=send, recv_sem=recv, device_id=device, device_id_type=MESH
    )


def hops(n, way, kind):
    return n // 2 if (way == 0) == (kind == 0) else n // 2 - 1


SPREADS = ((QKV, True), (OUT, False), (GU, True), (DOWN, False))


def layer_kernel(n, tokens, unit, *refs):
    (
        x_ref, back_ref, table_ref, attention_gain, feed_gain, query_gain, key_gain,
    ) = refs[:7]
    shards = refs[7:11]
    output, input_grad, grad_attention, grad_feed, grad_query_gain, grad_key_gain = refs[11:17]
    grads = refs[17:21]
    (
        w_qkv, w_out, w_gu, w_down, normed, raw, low, probs, context, hidden, out_low, activated, gu_back, part, sent, got, middle, tables, stage, turned_left, normed_turned, context_turned, hidden_turned,
        gain_sums,
        local, ring_send, ring_recv, x_send, x_recv, swap_send, swap_recv, stage_sem,
    ) = refs[21:]
    weights = (w_qkv, w_out, w_gu, w_down)
    grad_context, attended = normed, context
    place = Place(n)
    top = n // 2
    cw, ccw = place.ring_neighbour(1), place.ring_neighbour(-1)
    ways = ((1, cw), (-1, ccw))
    greet([cw, ccw, place.core_partner, place.x_partner])
    both = 2 * tokens
    mine = pl.multiple_of(place.core * tokens, tokens)
    theirs = pl.multiple_of((1 - place.core) * tokens, tokens)
    my_rows, their_rows = pl.ds(mine, tokens), pl.ds(theirs, tokens)
    chunk = unit // 2
    ff = 3 * unit // 2
    few = 32
    base = unit // n
    heads = unit // HEAD_DIM
    kv_heads = heads // 2
    scale = HEAD_DIM ** (-0.5)

    def holds(which, own_index, act):
        if SPREADS[which][1]:
            act()
        else:
            pl.when(own_index // top == place.core)(act)

    def region(which, own_index, x):
        array, split = SPREADS[which]
        height = shards[which].shape[0]
        if split:
            width = weights[which].shape[1] // 2
            start = pl.multiple_of(own_index * height, height)
            return weights[which].at[pl.ds(start, height), pl.ds(pl.multiple_of(x * width, width), width)]
        start = pl.multiple_of(lax.rem(own_index, top) * height, height)
        return weights[which].at[pl.ds(start, height)]

    def own_copy(which):
        height = shards[which].shape[0]
        index = place.own if SPREADS[which][1] else lax.rem(place.own, top)
        start = pl.multiple_of(index * height, height)
        return pltpu.make_async_copy(
            shards[which], weights[which].at[pl.ds(start, height)], local.at[which]
        )

    def reach(which, way):
        return hops(n, way, 0 if SPREADS[which][1] else 1)

    def ring_copy(which, way, hop, act):
        step, target = ways[way]
        own_index = place.shard(-step * (hop if act == "wait_recv" else hop - 1))
        spot = region(which, own_index, place.x)
        index = (which * 2 + way) * top + hop - 1

        def do():
            copy = remote(spot, spot, ring_send.at[index], ring_recv.at[index], target)
            getattr(copy, act)()

        holds(which, own_index, do)

    def send_on(which, way, hop):
        ring_copy(which, way, hop, "start")

    def x_copy(which, way, hop, x):
        spot = region(which, place.shard(-ways[way][0] * hop), x)
        index = (which // 2 * 2 + way) * top + hop - 1
        return remote(spot, spot, x_send.at[index], x_recv.at[index], place.x_partner)

    def serve(which, hop):
        for way in range(2):
            if hop > reach(which, way):
                continue
            ring_copy(which, way, hop, "wait_recv")
            if hop < reach(which, way):
                send_on(which, way, hop + 1)
            if SPREADS[which][1]:
                x_copy(which, way, hop, place.x).start()

    def begin(which):
        def act():
            own_copy(which).wait()

        holds(which, place.own, act)
        for way in range(2):
            if reach(which, way) > 0:
                send_on(which, way, 1)

    def take_x(which):
        for way in range(2):
            for hop in range(1, reach(which, way) + 1):
                x_copy(which, way, hop, 1 - place.x).wait_recv()

    def swap(index, src, dst):
        return remote(src, dst, swap_send.at[index], swap_recv.at[index], place.core_partner)

    def rows_swap(index, ref):
        return swap(index, ref.at[my_rows], ref.at[my_rows])

    def part_swap(index, slot):
        return swap(index, sent.at[slot], got.at[slot])

    def loop(size, step, act):
        def body(k, carry):
            act(pl.multiple_of(k * step, step))
            return carry

        lax.fori_loop(0, size // step, body, 0)

    def normalize(source, gain, target):
        def act(k):
            value = source[pl.ds(k, few), :]
            value = value * lax.rsqrt(jnp.mean(value * value, -1, keepdims=True) + EPSILON)
            target[pl.ds(pl.multiple_of(mine + k, few), few), :] = (value * gain[...]).astype(BF16)

        loop(tokens, few, act)

    def normalize_back(k, source, gain, grad):
        value = source[pl.ds(k, few), :]
        inverse = lax.rsqrt(jnp.mean(value * value, -1, keepdims=True) + EPSILON)
        unscaled = value * inverse
        inner = grad * gain[...]
        back = inverse * (inner - unscaled * jnp.mean(inner * unscaled, -1, keepdims=True))
        return back, jnp.sum((grad * unscaled).reshape(few // 8, 8, unit), 0)

    def dot(left, right, across):
        return lax.dot_general(left, right, ((across[0], across[1]), ((), ())), preferred_element_type=F32)

    NN, NT, TN = ((1,), (0,)), ((1,), (1,)), ((0,), (0,))

    def partial_product(index, slot, left, right, across):
        part[...] = dot(left[...], right[...], across)

        def pack(k):
            sent[slot, pl.ds(k, few), :] = part[
                pl.ds(pl.multiple_of(theirs + k, few), few), :
            ].astype(BF16)

        loop(tokens, few, pack)
        part_swap(index, slot).start()

    def whole_rows(k, slot):
        own = part[pl.ds(pl.multiple_of(mine + k, few), few), :]
        return own + got[slot, pl.ds(k, few), :].astype(F32)

    def turn(left, target):
        def act(k):
            target[pl.ds(k, chunk), :] = left[:, pl.ds(k, chunk)].T

        loop(left.shape[1], chunk, act)

    def weight_grad(which, left, right, turned):
        columns = right.shape[1] // unit

        def by_rows(r, carry):
            row = pl.multiple_of(r * chunk, chunk)
            if turned is None:
                turned_left[...] = left[:, pl.ds(row, chunk)].T

            def by_columns(c, carry):
                column = pl.multiple_of(c * unit, unit)
                index = r * columns + c
                slot = lax.rem(index, 2)

                @pl.when(index >= 2)
                def _():
                    stage_copy(which, slot, row, column, chunk, unit).wait()

                block = turned_left[...] if turned is None else turned[pl.ds(row, chunk), :]
                value = dot(block, right[:, pl.ds(column, unit)], NN)
                stage[slot] = value.astype(BF16)
                stage_copy(which, slot, row, column, chunk, unit).start()
                return carry

            lax.fori_loop(0, columns, by_columns, 0)
            return carry

        lax.fori_loop(0, left.shape[1] // chunk, by_rows, 0)
        for slot in range(2):
            stage_copy(which, slot, 0, 0, chunk, unit).wait()

    def stage_copy(which, slot, row, column, height, width):
        return pltpu.make_async_copy(
            stage.at[slot], grads[which].at[pl.ds(row, height), pl.ds(column, width)],
            stage_sem.at[slot],
        )

    for which in range(4):
        holds(which, place.own, lambda: own_copy(which).start())
    tables[my_rows, :] = table_ref[...]
    normalize(x_ref, attention_gain, normed)
    rows_swap(0, normed).start()
    rows_swap(1, tables).start()
    begin(0)
    begin(1)

    def round_back(k):
        out_low[pl.ds(pl.multiple_of(mine + k, few), few), :] = back_ref[pl.ds(k, few), :].astype(BF16)

    loop(tokens, few, round_back)
    rows_swap(2, out_low).start()
    gain_sums[...] = jnp.zeros_like(gain_sums)

    late = [(1, top)] if top < 3 else [(1, h) for h in range(3, top + 1)]
    serve(0, 1)
    serve(1, 1)
    begin(2)
    for hop in range(2, top + 1):
        serve(0, hop)
        if (1, hop) not in late:
            serve(1, hop)
        if hop == 2:
            serve(2, 1)
    take_x(0)
    begin(3)
    pending = late + [(2, h) for h in range(2, top)] + [(3, 1), (2, top)]
    pending += [(3, h) for h in range(2, top + 1)]
    for name in (0, 1):
        rows_swap(name, (normed, tables)[name]).wait_recv()

    raw[:, pl.ds(0, unit)] = dot(normed[...], w_qkv[:, pl.ds(0, unit)], NN)
    keys_values = dot(normed[...], w_qkv[:, pl.ds(unit, unit)], NN)
    raw[:, pl.ds(unit, chunk)] = keys_values[:, :chunk]
    low[:, pl.ds(unit + chunk, chunk)] = keys_values[:, chunk:].astype(BF16)
    serve(*pending.pop(0))
    turn(normed, normed_turned)

    def turned(value, rows):
        return value * tables[rows, pl.ds(0, HEAD_DIM)] + pltpu.roll(
            value, HEAD_DIM // 2, 1
        ) * tables[rows, pl.ds(HEAD_DIM, HEAD_DIM)]

    def turned_back(value, rows):
        return value * tables[rows, pl.ds(0, HEAD_DIM)] - pltpu.roll(
            value, HEAD_DIM // 2, 1
        ) * tables[rows, pl.ds(HEAD_DIM, HEAD_DIM)]

    def head_norm(first, count, gain):
        def act(k):
            for half in range(2):
                rows = pl.ds(half * tokens, tokens)
                columns = pl.ds(pl.multiple_of(first + k, HEAD_DIM), HEAD_DIM)
                value = raw[rows, columns]
                inverse = lax.rsqrt(jnp.mean(value * value, -1, keepdims=True) + EPSILON)
                low[rows, columns] = turned(value * inverse * gain[...], rows).astype(BF16)

        loop(count * HEAD_DIM, HEAD_DIM, act)

    head_norm(0, heads, query_gain)
    if pending:
        serve(*pending.pop(0))
    head_norm(unit, kv_heads, key_gain)

    def spans(k, half):
        queries = [pl.ds(pl.multiple_of((2 * k + g) * HEAD_DIM, HEAD_DIM), HEAD_DIM) for g in range(2)]
        keys = pl.ds(pl.multiple_of(unit + k * HEAD_DIM, HEAD_DIM), HEAD_DIM)
        values = pl.ds(pl.multiple_of(unit + unit // 2 + k * HEAD_DIM, HEAD_DIM), HEAD_DIM)
        return queries, keys, values, pl.ds(half * tokens, tokens)

    def stacked(ref, rows, columns):
        return jnp.concatenate([ref[rows, columns[0]], ref[rows, columns[1]]], 0)

    def attend(k, half):
        queries, keys, values, rows = spans(k, half)
        row_id = lax.broadcasted_iota(jnp.int32, (tokens, tokens), 0)
        column_id = lax.broadcasted_iota(jnp.int32, (tokens, tokens), 1)
        start = tables[rows, pl.ds(2 * HEAD_DIM, HEAD_DIM)][:, :1]
        allowed = (column_id <= row_id) & (column_id.astype(F32) >= start)
        masks = jnp.where(allowed, 0.0, -1e30)
        scores = dot(stacked(low, rows, queries), low[rows, keys], NT) * scale
        scores = scores + jnp.concatenate([masks, masks], 0)
        exponent = jnp.exp(scores - jnp.max(scores, -1, keepdims=True))
        value = exponent / jnp.sum(exponent, -1, keepdims=True)
        probs[k * 2 + half] = value
        result = dot(value.astype(BF16), low[rows, values], NN).astype(BF16)
        for g in range(2):
            context[rows, queries[g]] = result[g * tokens : (g + 1) * tokens]

    for k in range(kv_heads):
        for half in range(2):
            attend(k, half)
        if pending and k % 2 == 0:
            serve(*pending.pop(0))

    while pending and pending[0][0] == 1:
        serve(*pending.pop(0))
    partial_product(3, 0, context, w_out, NN)
    turn(context, context_turned)
    if pending and pending[0][0] == 2:
        serve(*pending.pop(0))
    part_swap(3, 0).wait_recv()

    def add_middle(k):
        middle[pl.ds(k, few), :] = x_ref[pl.ds(k, few), :] + whole_rows(k, 0)

    loop(tokens, few, add_middle)
    normalize(middle, feed_gain, hidden)
    rows_swap(4, hidden).start()
    if pending:
        serve(*pending.pop(0))
    rows_swap(4, hidden).wait_recv()
    turn(hidden, hidden_turned)
    while pending:
        serve(*pending.pop(0))
    take_x(2)
    rows_swap(2, out_low).wait_recv()

    def feed(k):
        span = pl.ds(k, chunk)
        pair = pl.ds(pl.multiple_of(2 * k, unit), unit)
        gate_up = dot(hidden[...], w_gu[:, pair], NN)
        gate, up = gate_up[:, :chunk], gate_up[:, chunk:]
        grad = dot(out_low[...], w_down[span, :], NT)
        sigmoid = 1.0 / (1.0 + jnp.exp(-gate))
        swish = gate * sigmoid
        activated[:, span] = (swish * up).astype(BF16)
        gu_back[:, pl.ds(pl.multiple_of(2 * k, chunk), chunk)] = (
            grad * up * (sigmoid + swish * (1.0 - sigmoid))
        ).astype(BF16)
        gu_back[:, pl.ds(pl.multiple_of(2 * k + chunk, chunk), chunk)] = (grad * swish).astype(BF16)

    loop(ff, chunk, feed)
    part_swap(3, 0).wait_send()
    partial_product(6, 0, gu_back, w_gu, NT)
    weight_grad(3, activated, out_low, None)
    part_swap(6, 0).wait_recv()

    def middle_back(k):
        back, gain_part = normalize_back(k, middle, feed_gain, whole_rows(k, 0))
        back = back_ref[pl.ds(k, few), :] + back
        input_grad[pl.ds(k, few), :] = back
        attended[pl.ds(pl.multiple_of(mine + k, few), few), :] = back.astype(BF16)
        gain_sums[1] += gain_part

    loop(tokens, few, middle_back)
    rows_swap(7, attended).start()
    partial_product(5, 1, activated, w_down, NN)
    weight_grad(2, hidden, gu_back, hidden_turned)
    part_swap(5, 1).wait_recv()

    def add_output(k):
        output[pl.ds(k, few), :] = middle[pl.ds(k, few), :] + whole_rows(k, 1)

    loop(tokens, few, add_output)
    rows_swap(7, attended).wait_recv()

    rows_swap(0, normed).wait_send()
    grad_context[...] = dot(attended[...], w_out[...], NT).astype(BF16)
    weight_grad(1, context, attended, context_turned)

    def head_back(rows, columns, gain, grad, index):
        value = raw[rows, columns]
        inverse = lax.rsqrt(jnp.mean(value * value, -1, keepdims=True) + EPSILON)
        unscaled = value * inverse
        grad = turned_back(grad, rows)
        gain_sums[index, :, pl.ds(0, HEAD_DIM)] += jnp.sum(
            (grad * unscaled).reshape(tokens // 8, 8, HEAD_DIM), 0
        )
        inner = grad * gain[...]
        back = inverse * (inner - unscaled * jnp.mean(inner * unscaled, -1, keepdims=True))
        low[rows, columns] = back.astype(BF16)

    def attend_back(k, half):
        queries, keys, values, rows = spans(k, half)
        prob = probs[k * 2 + half]
        above = stacked(grad_context, rows, queries)
        query_pair = stacked(low, rows, queries)
        grad_values = dot(prob.astype(BF16), above, TN)
        grad_probs = dot(above, low[rows, values], NT)
        grad_scores = prob * (grad_probs - jnp.sum(prob * grad_probs, -1, keepdims=True))
        grad_scores = grad_scores.astype(BF16)
        grad_queries = dot(grad_scores, low[rows, keys], NN) * scale
        grad_keys = dot(grad_scores, query_pair, TN) * scale
        for g in range(2):
            head_back(rows, queries[g], query_gain, grad_queries[g * tokens : (g + 1) * tokens], 2)
        head_back(rows, keys, key_gain, grad_keys, 3)
        low[rows, values] = grad_values.astype(BF16)

    def back_body(k, carry):
        for half in range(2):
            attend_back(k, half)
        return carry

    lax.fori_loop(0, kv_heads, back_body, 0)

    part_swap(6, 0).wait_send()
    partial_product(8, 0, low, w_qkv, NT)
    weight_grad(0, normed, low, normed_turned)
    part_swap(8, 0).wait_recv()

    def input_back(k):
        back, gain_part = normalize_back(k, x_ref, attention_gain, whole_rows(k, 0))
        input_grad[pl.ds(k, few), :] += back
        gain_sums[0] += gain_part

    loop(tokens, few, input_back)
    grad_attention[...] = jnp.sum(gain_sums[0], 0, keepdims=True)
    grad_feed[...] = jnp.sum(gain_sums[1], 0, keepdims=True)
    grad_query_gain[...] = jnp.sum(gain_sums[2, :, pl.ds(0, HEAD_DIM)], 0, keepdims=True)
    grad_key_gain[...] = jnp.sum(gain_sums[3, :, pl.ds(0, HEAD_DIM)], 0, keepdims=True)

    for index, ref in ((1, tables), (2, out_low), (4, hidden), (7, attended)):
        rows_swap(index, ref).wait_send()
    part_swap(5, 1).wait_send()
    part_swap(8, 0).wait_send()
    for which in range(4):
        for way in range(2):
            for hop in range(1, reach(which, way) + 1):
                ring_copy(which, way, hop, "wait_send")
                if SPREADS[which][1]:
                    x_copy(which, way, hop, place.x).wait_send()


def layer_pass(values, back, table, gains, shards, n):
    tokens, unit = values.shape
    top = n // 2
    dma = pltpu.SemaphoreType.DMA
    vmem = pltpu.VMEM
    both = 2 * tokens
    heads = unit // HEAD_DIM
    in_vmem = pl.BlockSpec(memory_space=pltpu.VMEM)
    row = lambda width: jax.ShapeDtypeStruct((1, width), F32)
    shapes = [(unit, 2 * unit), (unit, unit), (unit, 3 * unit), (3 * unit // 2, unit)]
    results = pl.pallas_call(
        functools.partial(layer_kernel, n, tokens, unit),
        out_shape=[jax.ShapeDtypeStruct((tokens, unit), F32)] * 2
        + [row(unit), row(unit), row(HEAD_DIM), row(HEAD_DIM)]
        + [jax.ShapeDtypeStruct(shape, BF16) for shape in shapes],
        in_specs=[in_vmem] * 7 + [ANY] * 4,
        out_specs=[in_vmem] * 6 + [ANY] * 4,
        scratch_shapes=[vmem(shape, BF16) for shape in shapes]
        + [
            vmem((both, unit), BF16),
            vmem((both, 3 * unit // 2), F32),
            vmem((both, 2 * unit), BF16),
            vmem((heads, both, tokens), F32),
            vmem((both, unit), BF16),
            vmem((both, unit), BF16),
            vmem((both, unit), BF16),
            vmem((both, 3 * unit // 2), BF16),
            vmem((both, 3 * unit), BF16),
            vmem((both, unit), F32),
            vmem((2, tokens, unit), BF16),
            vmem((2, tokens, unit), BF16),
            vmem((tokens, unit), F32),
            vmem((both, 3 * HEAD_DIM), F32),
            vmem((2, unit // 2, unit), BF16),
            vmem((unit // 2, both), BF16),
            vmem((unit, both), BF16),
            vmem((unit, both), BF16),
            vmem((unit, both), BF16),
            vmem((4, 8, unit), F32),
            dma((4,)),
            dma((8 * top,)),
            dma((8 * top,)),
            dma((4 * top,)),
            dma((4 * top,)),
            dma((9,)),
            dma((9,)),
            dma((2,)),
        ],
        compiler_params=pltpu.CompilerParams(
            collective_id=0, has_side_effects=True, vmem_limit_bytes=56 * 2**20
        ),
    )(values, back, table, *gains, *shards)
    return results[:2], results[2:6], results[6:]


PHASES = ((DOWN, 3, False), (GU, 3, True), (OUT, 2, False), (QKV, 2, True))

OWNERS = (
    (3, 0, 1, False, 1, 2),
    (3, 1, 1, False, 1, 6),
    (3, 0, 2, False, 0, 2),
    (2, 0, 2, True, 1, 5),
    (1, 0, 3, False, 0, 5),
    (1, 0, 3, False, 1, 1),
    (0, 0, 3, True, 0, 1),
)
KEY, VALUE, QUERY, OUTM, GATE, UP, DOWNM = range(7)
RETURNS = (OUTM, KEY, VALUE, DOWNM, GATE, UP, QUERY)
TILE_SLOTS = 4
X_AHEAD = 8
LAND_AHEAD = 16


def summing_core(phase):
    return 0 if PHASES[phase][2] else 1


def stage_order(n, core):
    rings = ((1.0, 1.5), (4.0, 2.7), (13.0, 1.1), (26.6, 1.7))
    crossings = {1: (-6.0, 2.5), 3: (14.0, 1.5)}
    keys, needs = {}, {}
    for phase in range(4):
        first, step = rings[phase]
        for i in range(n):
            key = first + step * i * 8 / n
            if summing_core(phase) == core:
                keys["ring", phase, i] = key
                needs["ring", phase, i] = [("ring", phase, i - 1)] if i else []
                if phase in crossings:
                    needs["ring", phase, i].append(("x", phase, i))
            else:
                keys["land", phase, i] = key - 6.0
                needs["land", phase, i] = [("land", phase, i - 1)] if i else []
        if phase in crossings:
            first, step = crossings[phase]
            for i in range(n):
                keys["x", phase, i] = first + step * i * 8 / n
                needs["x", phase, i] = [("x", phase, i - 1)] if i else [("x", 1, n - 1)] * (phase == 3)
        elif core == 1:
            keys["final", phase, 0] = {0: 16.0, 2: 27.0}[phase]
            needs["final", phase, 0] = [("ring", phase, n - 1)]
    left, found = sorted(keys, key=lambda stage: (keys[stage], stage)), []
    while left:
        stage = next(stage for stage in left if all(need in found for need in needs[stage]))
        left.remove(stage)
        found.append(stage)
    return found


class Rows:
    def __init__(self):
        self.next = 0

    def take(self, rows):
        start = self.next
        self.next += rows
        return start


def layout(n, unit):
    base = unit // n
    top = n // 2
    place = {}
    rows = (Rows(), Rows())
    place["high"] = [None, rows[1].take(3 * unit)]
    for name in ("grad", "ahead"):
        place[name] = [rows[summing_core(p)].take(PHASES[p][1] * base) for p in range(4)]
    for name in ("part", "other"):
        place[name] = [0 if split else rows[1].take(units * base) for _, units, split in PHASES]
    newton = Rows()
    newton.next = -(-rows[1].next // unit) * unit
    place["high"][0] = newton.take(3 * unit)
    place["poly"] = [newton.take(unit) for _ in range(2)]
    place["x_in"] = {p: [rows[0].take(PHASES[p][1] * base) for _ in range(n)] for p in (1, 3)}
    place["own"] = [[rows[core].take(3 * base) for _ in range(TILE_SLOTS)] for core in range(2)]
    place["ring"], place["far"] = [], []
    for phase, (_, units, _) in enumerate(PHASES):
        take = rows[summing_core(phase)].take
        place["ring"].append([[take(units * base) for _ in range(top)] for _ in range(2)])
        place["far"].append(take(units * base))
    return place, max(rows[0].next, rows[1].next, newton.next)


def update_kernel(n, unit, *refs):
    grads, moments, gains_in = refs[:4], refs[4:11], refs[11]
    outs, orths, lands, gains_out = refs[12:16], refs[16:20], refs[20:24], refs[24]
    (
        pool, exact, gram, squares, gain_mine, gain_core, gain_x, gain_all,
        land_send, land_recv, tile_sem, x_send, x_recv, ring_send, ring_recv, part_send, part_recv,
        moment_sem, grad_local, grad_send, grad_recv, in_send, in_recv, in_local,
        out_send, out_recv, pass_send, pass_recv, gain_send, gain_recv,
    ) = refs[25:]
    place = Place(n)
    base = unit // n
    top = n // 2
    at, _ = layout(n, unit)
    cw, ccw = place.ring_neighbour(1), place.ring_neighbour(-1)
    ways = ((1, cw), (-1, ccw))
    side = [(place.x * 2 + core, lax.rem(place.own + k, n)) for k in range(1, n) for core in range(2)]
    across = [((1 - place.x) * 2 + core, place.own) for core in range(2)]
    greet(side + [place.core_partner] + across)
    order = [top]
    for distance in range(top - 1, 0, -1):
        order += [distance, -distance]
    order.append(0)
    moment = exact
    height = [units * base for _, units, _ in PHASES]
    moment_at = [sum(height[:phase]) for phase in range(4)]
    owners = [
        (xs * 2 + 1, place.own_at(spot * n // 8)) for _, _, _, _, xs, spot in OWNERS
    ]
    here = place.rep * n + place.own
    is_owner = [here == rep * n + own for rep, own in owners]

    def rows(start, size):
        if isinstance(start, int):
            return pl.ds(start, size)
        return pl.ds(pl.multiple_of(start, size), size)

    def block(start, size):
        return pool.at[rows(start, size)]

    def pieces_of(phase, x):
        array, units, _ = PHASES[phase]
        half = unit // 2
        found = []
        for core in range(2):
            for b in range(units):
                if array == GU:
                    own_column = b * unit + x * half
                    column = x * 3 * unit + core * (3 * half) + b * half
                else:
                    own_column = x * units * half + b * half
                    column = x * 2 * unit + core * (unit - x * half) + b * (half + x * half)
                found.append((core, b, own_column, column))
        return found

    def columns(start):
        return pl.ds(pl.multiple_of(start, unit // 2), unit // 2)

    def in_block(start, core, b):
        return pool.at[pl.ds(start + b * base, base), pl.ds(core * (unit // 2), unit // 2)]

    def shard_rows(phase, own_index):
        if PHASES[phase][2]:
            return rows(own_index * base, base)
        return rows(lax.rem(own_index, top) * height[phase], height[phase])

    def landing(phase, own_index, act):
        if PHASES[phase][2]:
            act()
        else:
            pl.when(own_index // top != summing_core(phase))(act)

    def spread(source, target, size, send, recv, device):
        step = size

        def copy(k, count):
            return remote(block(source + k, count), block(target + k, count), send, recv, device)

        return Several(
            functools.partial(copy, 0, size),
            [functools.partial(copy, k, step) for k in range(0, size, step)],
        )

    def land_copy(phase, i, act):
        array, units, split = PHASES[phase]
        own_index = place.shard(order[i])
        span = shard_rows(phase, own_index)

        def copy(at_columns):
            return remote(
                grads[array].at[span, at_columns], lands[array].at[span, at_columns],
                land_send.at[phase * n + i], land_recv.at[phase * n + i], place.core_partner,
            )

        def do():
            if not split:
                getattr(copy(pl.ds(0, unit)), act)()
            elif act == "start":
                for core, _, column, _ in pieces_of(phase, place.x):
                    if core == 1:
                        copy(columns(column)).start()
            else:
                getattr(copy(pl.ds(0, units * unit // 2)), act)()

        landing(phase, own_index, do)

    def x_index(phase, i):
        return (phase // 2) * n + i

    def x_copies(phase, i, core, act):
        index = x_index(phase, i)
        array, units, _ = PHASES[phase]
        span = shard_rows(phase, place.shard(order[i]))
        target = at["x_in"][phase][i]

        def copy(source, spot):
            return remote(
                source, spot, x_send.at[index], x_recv.at[core, index], ((1 - place.x) * 2, place.own)
            )

        if act == "start":
            for its_core, b, column, _ in pieces_of(phase, 1 - place.x):
                if its_core == core:
                    copy(grads[array].at[span, columns(column)], in_block(target, core, b)).start()
        else:
            spot = pool.at[pl.ds(target, height[phase]), pl.ds(core * (unit // 2), unit // 2)]
            getattr(copy(spot, spot), act)()

    def ring_copy(phase, way, distance, source, part):
        size = height[phase] // 2
        target = at["ring"][phase][way][distance - 1] + part * size
        index = ((phase * 2 + way) * top + distance - 1) * 2 + part
        return spread(
            source + part * size, target, size,
            ring_send.at[index], ring_recv.at[index], ways[way][1],
        )

    def ring_out(phase, distance, part):
        if distance == 0:
            return []
        if distance == top:
            return [ring_copy(phase, part, top, at["far"][phase], part)]
        way = 0 if distance > 0 else 1
        far = abs(distance)
        return [ring_copy(phase, way, far, at["ring"][phase][way][far], part)]

    def part_copy(phase):
        return spread(
            at["part"][phase], at["other"][phase], height[phase],
            part_send.at[phase // 2], part_recv.at[phase // 2], place.x_partner,
        )

    def gain_copy(src, dst, slot, device):
        return remote(src, dst, gain_send.at[slot], gain_recv.at[slot], device)

    def gain_core_copy():
        return gain_copy(gain_mine, gain_core, 0, place.core_partner)

    def gain_x_copy():
        return gain_copy(gain_core, gain_x, 1, place.x_partner)

    def gain_back_copy():
        return gain_copy(gain_mine, gain_x, 2, place.core_partner)

    def gain_ring(way, hop, distance):
        spot = gain_all.at[place.shard(distance)]
        return gain_copy(spot, spot, 3 + way * top + hop - 1, ways[way][1])

    def grad_place(phase, x):
        array = PHASES[phase][0]
        start = at["grad"][phase]
        if not PHASES[phase][2]:
            return [(outs[array], block(start, height[phase]))]
        return [
            (outs[array].at[:, columns(column)], in_block(start, core, b))
            for core, b, _, column in pieces_of(phase, x)
        ]

    def grad_span(phase, x):
        array, units, split = PHASES[phase]
        if not split:
            return outs[array]
        first = pl.multiple_of(x * units * unit, unit)
        return outs[array].at[:, pl.ds(first, units * unit)]

    def grad_sent(phase, to, device, x):
        span = grad_span(phase, x)
        return remote(span, span, grad_send.at[phase, to], grad_recv.at[phase, to], device)

    def matrix_rows(matrix, own_index):
        phase, first, units, tall, _, _ = OWNERS[matrix]
        if tall:
            return [(0, own_index * units * base, units * base)]
        return [
            ((first + k) * base, k * unit + own_index * base, base) for k in range(units)
        ]

    def matrix_span(matrix):
        phase, first, units, tall, xs, _ = OWNERS[matrix]
        array = PHASES[phase][0]
        if tall:
            return orths[array]
        start = (xs * PHASES[phase][1] + first) * unit
        return orths[array].at[:, pl.ds(start, units * unit)]

    def answer_parts(matrix, final, own_index):
        phase, first, units, tall, xs, _ = OWNERS[matrix]
        array = PHASES[phase][0]
        if tall:
            return [(block(final + own_index * units * base, units * base), orths[array])]
        return [
            (
                pool.at[
                    rows(final + (b - first) * unit + own_index * base, base),
                    pl.ds(core * (unit // 2), unit // 2),
                ],
                orths[array].at[:, columns(column)],
            )
            for core, b, _, column in pieces_of(phase, xs)
            if first <= b < first + units
        ]

    def handed(matrix, to, device):
        span = matrix_span(matrix)
        return remote(span, span, pass_send.at[matrix, to], pass_recv.at[matrix, to], device)

    def answered(matrix, target):
        span = matrix_span(matrix)
        return remote(
            span, span, out_send.at[target], out_recv.at[matrix], (place.x * 2, target)
        )

    def summed(pieces, size, store):
        step = 16
        steps = 4 if size % (4 * step) == 0 else 1

        def body(k, carry):
            for j in range(steps):
                shift = (k * steps + j) * step
                total = None
                for start in pieces:
                    value = pool[rows_at(start, shift, step), :].astype(F32)
                    total = value if total is None else total + value
                store(shift, step, total)
            return carry

        lax.fori_loop(0, size // (step * steps), body, 0)

    def rows_at(start, shift, step):
        return pl.ds(pl.multiple_of(start + shift, step), step)

    def keep(start):
        def store(shift, step, total):
            pool[rows_at(start, shift, step), :] = total.astype(BF16)

        return store

    def load_tile(phase, i, slot):
        array, _, split = PHASES[phase]
        own_index = place.shard(order[i])
        span = shard_rows(phase, own_index)
        summing = summing_core(phase)

        def load(source, target):
            pltpu.make_async_copy(source, target, tile_sem.at[slot]).start()

        if split:
            for core, b, column, _ in pieces_of(phase, place.x):
                load(
                    (grads, lands)[core][array].at[span, columns(column)],
                    in_block(at["own"][summing][slot], core, b),
                )
            return
        for core in range(2):

            @pl.when(own_index // top == core)
            def _():
                load(
                    (lands, grads)[core == summing][array].at[span],
                    block(at["own"][summing][slot], height[phase]),
                )

    def prefetch(rings, index):
        if index < len(rings):
            _, phase, i = rings[index]
            land_copy(phase, i, "wait_recv")
            load_tile(phase, i, index % TILE_SLOTS)

    def moment_copies(phase, act):
        array, units, split = PHASES[phase]
        if not split:
            act(moments[3 if array == OUT else 6], moment.at[pl.ds(moment_at[phase], height[phase])])
            return
        half = unit // 2
        for x in range(2):

            @pl.when(place.x == x)
            def _():
                for core, b, _, column in pieces_of(phase, x):
                    if array == GU:
                        source, first = 4 + x, x * 3 * unit
                    elif x == 0:
                        source, first = 0, 0
                    else:
                        source, first = 1 + b, (2 + b) * unit
                    act(
                        moments[source].at[:, pl.ds(column - first, half)],
                        moment.at[pl.ds(moment_at[phase] + b * base, base), pl.ds(core * half, half)],
                    )

    def load_moment(phase):
        moment_copies(
            phase, lambda src, dst: pltpu.make_async_copy(src, dst, moment_sem.at[phase]).start()
        )

    def finish(phase, pieces):
        span = moment.at[pl.ds(moment_at[phase], height[phase])]
        pltpu.make_async_copy(span, span, moment_sem.at[phase]).wait()

        def store(shift, step, total):
            pool[rows_at(at["grad"][phase], shift, step), :] = total.astype(BF16)
            ahead = (1.0 + MOMENTUM) * total + MOMENTUM**2 * moment[
                rows_at(moment_at[phase], shift, step), :
            ]
            pool[rows_at(at["ahead"][phase], shift, step), :] = ahead.astype(BF16)

        summed(pieces, height[phase], store)
        for matrix, (its_phase, _, _, _, xs, _) in enumerate(OWNERS):
            if its_phase != phase:
                continue

            def hand_in(local):
                for source, target, size in matrix_rows(matrix, place.own):
                    source = block(at["ahead"][phase] + source, size)
                    target = block(at["high"][1] + target, size)
                    if local:
                        pltpu.make_async_copy(source, target, in_local).start()
                    else:
                        remote(
                            source, target, in_send.at[matrix], in_recv.at[place.own], owners[matrix]
                        ).start()

            if summing_core(phase) == 0:
                pl.when(place.x == xs)(functools.partial(hand_in, False))
            else:
                pl.when(is_owner[matrix])(functools.partial(hand_in, True))
                pl.when((place.x == xs) & (here != owners[matrix][0] * n + owners[matrix][1]))(
                    functools.partial(hand_in, False)
                )

        for target, source in grad_place(phase, place.x):
            pltpu.make_async_copy(source, target, grad_local.at[phase]).start()
            remote(
                source, target, grad_send.at[phase, 0], grad_recv.at[phase, 0], place.core_partner
            ).start()
            if PHASES[phase][2]:
                remote(
                    source, target, grad_send.at[phase, 1], grad_recv.at[phase, 1], place.x_partner
                ).start()

    def settle(phase):
        span = block(at["grad"][phase], height[phase])
        pltpu.make_async_copy(span, span, grad_local.at[phase]).wait()
        remote(
            span, span, grad_send.at[phase, 0], grad_recv.at[phase, 0], place.core_partner
        ).wait_send()
        if PHASES[phase][2]:
            remote(
                span, span, grad_send.at[phase, 1], grad_recv.at[phase, 1], place.x_partner
            ).wait_send()
        for matrix, (its_phase, _, units, _, xs, _) in enumerate(OWNERS):
            if its_phase != phase:
                continue

            sends = place.x == xs
            if summing_core(phase) == 1:
                sends = sends & (here != owners[matrix][0] * n + owners[matrix][1])

            @pl.when(sends)
            def _():
                span = block(at["high"][1], units * base)
                remote(
                    span, span, in_send.at[matrix], in_recv.at[0], place.core_partner
                ).wait_send()

    def stage_x(phase, i, core):
        index = x_index(phase, i)
        if index >= X_AHEAD:
            before = index - X_AHEAD
            x_copies(1 if before < n else 3, before % n, core, "wait_send")
        x_copies(phase, i, core, "start")

    def stage_ring(phase, i, slot):
        distance = order[i]
        start = at["own"][summing_core(phase)][slot]
        span = block(start, height[phase])
        pltpu.make_async_copy(span, span, tile_sem.at[slot]).wait()
        pieces = [start]
        if PHASES[phase][2]:
            for core in range(2):
                x_copies(phase, i, core, "wait_recv")
            pieces.append(at["x_in"][phase][i])
        size = height[phase]
        mid = size // 2
        if distance == 0:
            for way in range(2):
                held = at["ring"][phase][way][0]
                for part in range(2):
                    ring_copy(phase, way, 1, held, part).wait_recv()
                pieces.append(held)
            if PHASES[phase][2]:
                finish(phase, pieces)
            else:
                summed(pieces, size, keep(at["part"][phase]))
                part_copy(phase).start()
        else:
            way = 0 if distance > 0 else 1
            far = abs(distance)
            held = at["far"][phase] if far == top else at["ring"][phase][way][far]
            for part in (1 - way, way):
                starts = [start + part * mid for start in pieces]
                if far + 1 < top or (far + 1 == top and part == way):
                    ring_copy(phase, way, far + 1, held, part).wait_recv()
                    starts.append(held + part * mid)
                summed(starts, mid, keep(held + part * mid))
                for copy in ring_out(phase, distance, part):
                    copy.start()
    def ring_sent(phase):
        for distance in order:
            for part in range(2):
                for copy in ring_out(phase, distance, part):
                    copy.wait_send()

    def run(core):
        stages = stage_order(n, core)
        rings = [stage for stage in stages if stage[0] == "ring"]
        landed = [stage for stage in stages if stage[0] == "land"]
        for phase in range(4):
            if summing_core(phase) == core:
                load_moment(phase)
        done, sent, hop = 0, 0, 0
        for index in range(min(LAND_AHEAD, len(landed))):
            land_copy(*landed[index][1:], "start")
        for index in range(TILE_SLOTS - 1):
            prefetch(rings, index)
        for kind, phase, i in stages:
            if kind == "x":
                stage_x(phase, i, core)
            elif kind == "land":
                land_copy(phase, i, "wait_send")
                if sent + LAND_AHEAD < len(landed):
                    land_copy(*landed[sent + LAND_AHEAD][1:], "start")
                sent += 1
            elif kind == "final":
                part_copy(phase).wait_recv()
                finish(phase, [at["part"][phase], at["other"][phase]])
            else:
                prefetch(rings, done + TILE_SLOTS - 1)
                stage_ring(phase, i, done % TILE_SLOTS)
                done += 1
                if core == 0 and hop <= top + 1:
                    gain_stage(hop)
                    hop += 1

    def settle_all(core):
        for phase, (_, _, split) in enumerate(PHASES):
            if summing_core(phase) == core:
                settle(phase)
                if not split:
                    part_copy(phase).wait_send()
        for index in range(2 * n - X_AHEAD, 2 * n):
            x_copies(1 if index < n else 3, index % n, core, "wait_send")

    def take_sums(core):
        for phase, (_, _, split) in enumerate(PHASES):
            if summing_core(phase) != core:
                grad_sent(phase, 0, place.core_partner, place.x).wait_recv()
                if split:
                    grad_sent(phase, 2, place.core_partner, 1 - place.x).wait_recv()

    def gain_stage(hop):
        if hop == 0:
            gain_core_copy().wait_recv()
            gain_core[...] = gain_mine[...] + gain_core[...]
            gain_x_copy().start()
            return
        if hop == 1:
            gain_x_copy().wait_recv()
            gain_all[place.own] = gain_core[...] + gain_x[...]
            for way in range(2):
                gain_ring(way, 1, 0).start()
        for way in range(2):
            if 1 < hop <= hops(n, way, 0) + 1:
                distance = -ways[way][0] * (hop - 1)
                gain_ring(way, hop - 1, distance).wait_recv()
                if hop <= hops(n, way, 0):
                    gain_ring(way, hop, distance).start()

    gain_mine[...] = gains_in[...]

    @pl.when(place.core == 0)
    def _():
        run(0)
        total = gain_all[0]
        for k in range(1, n):
            total = total + gain_all[k]
        gains_out[...] = total
        gain_mine[...] = total
        gain_back_copy().start()

        for phase in (1, 3):
            grad_sent(phase, 1, place.x_partner, 1 - place.x).wait_recv()
            grad_sent(phase, 2, place.core_partner, 1 - place.x).start()

        for matrix in RETURNS:
            xs = OWNERS[matrix][4]

            @pl.when(place.x == xs)
            def _():
                answered(matrix, place.own).wait_recv()
                handed(matrix, 0, place.x_partner).start()
                handed(matrix, 1, place.core_partner).start()

            @pl.when(place.x != xs)
            def _():
                handed(matrix, 0, place.x_partner).wait_recv()
                handed(matrix, 1, place.core_partner).start()

        for matrix, (phase, _, units, _, xs, _) in enumerate(OWNERS):
            handed(matrix, 1, place.core_partner).wait_send()

            @pl.when(place.x == xs)
            def _():
                handed(matrix, 0, place.x_partner).wait_send()

        take_sums(0)
        settle_all(0)
        for phase in (1, 3):
            ring_sent(phase)
            grad_sent(phase, 2, place.core_partner, 1 - place.x).wait_send()
        gain_x_copy().wait_send()
        gain_back_copy().wait_send()
        for way in range(2):
            for h in range(1, hops(n, way, 0) + 1):
                gain_ring(way, h, -ways[way][0] * (h - 1)).wait_send()

    @pl.when(place.core == 1)
    def _():
        gain_core_copy().start()
        run(1)
        for phase in (0, 2):
            ring_sent(phase)
        newton_part(n, unit, place, pool, exact, gram, squares, at, is_owner, in_recv, in_local)
        for matrix, (_, _, units, tall, _, _) in enumerate(OWNERS):

            @pl.when(is_owner[matrix])
            def _():
                final = at["high"][1 - NS_STEPS % 2 if tall else NS_STEPS % 2]

                def send(k, carry):
                    target = lax.rem(place.own + k, n)
                    for source, part in answer_parts(matrix, final, target):
                        remote(
                            source, part, out_send.at[target], out_recv.at[matrix],
                            (place.x * 2, target),
                        ).start()
                    return carry

                lax.fori_loop(0, n, send, 0)

                def sent(k, carry):
                    answered(matrix, lax.rem(place.own + k, n)).wait_send()
                    return carry

                lax.fori_loop(0, n, sent, 0)

        gain_core_copy().wait_send()
        gain_back_copy().wait_recv()
        gains_out[...] = gain_x[...]
        take_sums(1)
        settle_all(1)
        for matrix in RETURNS:
            handed(matrix, 1, place.core_partner).wait_recv()


def newton_part(n, unit, place, pool, exact, gram, squares, at, is_owner, in_recv, in_local):
    base = unit // n
    small = min(256, unit // 2)
    per = unit // small
    wide = unit // 2
    few = 32
    count, tall = 0, 0
    for mine, (_, _, units, lies_tall, _, _) in zip(is_owner, OWNERS):
        count = count + units * mine.astype(jnp.int32)
        tall = tall + int(lies_tall) * mine.astype(jnp.int32)
    high, poly = at["high"], at["poly"]

    def rows(start, size):
        return pl.ds(pl.multiple_of(start, size), size)

    for matrix, (phase, _, units, *_) in enumerate(OWNERS):

        @pl.when(is_owner[matrix])
        def _():
            span = pool.at[pl.ds(high[1], units * base)]
            inside = summing_core(phase) == 1
            if inside:
                pltpu.make_async_copy(span, span, in_local).wait()
            for k in range(1 if inside else 0, n):
                own_index = lax.rem(place.own + k, n)
                remote(
                    span, span, in_recv.at[own_index], in_recv.at[own_index], place.core_partner
                ).wait_recv()

    @pl.when(count > 0)
    def _():
        squares[...] = jnp.zeros_like(squares)

        def square(k, carry):
            part = pool[rows(high[1] + k * few, few), :].astype(F32)
            squares[...] += jnp.sum((part * part).reshape(few // 8, 8, unit), 0)
            return carry

        lax.fori_loop(0, count * (unit // few), square, 0)
        total = jnp.sum(jnp.sum(squares[...], 1, keepdims=True), 0, keepdims=True)
        inverse = 1.0 / (jnp.sqrt(total) + 1e-07)

        @pl.when(tall == 0)
        def _():
            def scale(k, carry):
                value = pool[rows(high[1] + k * few, few), :].astype(F32) * inverse
                exact[rows(k * few, few), :] = value
                pool[rows(high[0] + k * few, few), :] = value.astype(BF16)
                return carry

            lax.fori_loop(0, count * (unit // few), scale, 0)

        @pl.when(tall == 1)
        def _():
            def scale(k, carry):
                block, row = k // per, k % per
                for column in range(per):
                    part = pool[
                        rows(high[1] + k * small, small), pl.ds(column * small, small)
                    ].astype(F32)
                    value = (part * inverse).T
                    shift = block * unit + column * small
                    columns = rows(row * small, small)
                    exact[rows(shift, small), columns] = value
                    pool[rows(high[0] + shift, small), columns] = value.astype(BF16)
                return carry

            lax.fori_loop(0, count * per, scale, 0)

        def newton(step, carry):
            even = step % 2
            now = high[0] + even * (high[1] - high[0])
            later = high[1] - even * (high[1] - high[0])

            def keep_symmetric(to, chunk, value):
                pool[pl.ds(to, (chunk + 1) * wide), pl.ds(chunk * wide, wide)] = value.astype(BF16)
                if chunk == 1:
                    pool[pl.ds(to + wide, wide), pl.ds(0, wide)] = value[:wide].T.astype(BF16)

            for chunk in range(2):
                down = (chunk + 1) * wide

                def product(block):
                    left = pool[pl.ds(pl.multiple_of(now + block * unit, unit), down), :]
                    right = pool[rows(now + block * unit + chunk * wide, wide), :]
                    return lax.dot_general(
                        left, right, (((1,), (1,)), ((), ())), preferred_element_type=F32
                    )

                gram[:down, :] = product(0)

                def more(block, carry):
                    gram[:down, :] += product(block)
                    return carry

                lax.fori_loop(1, count, more, 0)
                keep_symmetric(poly[0], chunk, gram[:down, :])

            for chunk in range(2):
                down = (chunk + 1) * wide
                columns = pl.ds(chunk * wide, wide)
                squared = jnp.dot(
                    pool[pl.ds(poly[0], down), :], pool[pl.ds(poly[0], unit), columns],
                    preferred_element_type=F32,
                )
                plain = pool[pl.ds(poly[0], down), columns].astype(F32)
                keep_symmetric(poly[1], chunk, NEWTON_B * plain + NEWTON_C * squared)

            def advance(block, carry):
                for chunk in range(2):
                    columns = pl.ds(chunk * wide, wide)
                    value = NEWTON_A * exact[rows(block * unit, unit), columns] + jnp.dot(
                        pool[pl.ds(poly[1], unit), :],
                        pool[rows(now + block * unit, unit), columns],
                        preferred_element_type=F32,
                    )
                    exact[rows(block * unit, unit), columns] = value
                    pool[rows(later + block * unit, unit), columns] = value.astype(BF16)
                return carry

            lax.fori_loop(0, count, advance, 0)
            return carry

        lax.fori_loop(0, NS_STEPS, newton, 0)

        @pl.when(tall == 1)
        def _():
            free = high[1 - NS_STEPS % 2]
            factor = jnp.sqrt(jnp.full((1, 1), count, jnp.int32).astype(F32))

            def lay(k, carry):
                block, row = k // per, k % per
                for column in range(per):
                    columns = pl.ds(column * small, small)
                    part = exact[rows(k * small, small), columns]
                    pool[
                        rows(free + block * unit + column * small, small), rows(row * small, small)
                    ] = (part * factor).T.astype(BF16)
                return carry

            lax.fori_loop(0, count * per, lay, 0)


def update_all(grads, moments, gains, n, unit):
    top = n // 2
    dma = pltpu.SemaphoreType.DMA
    vmem = pltpu.VMEM
    _, pool_rows = layout(n, unit)
    shapes = [(unit // n, 4 * unit), (2 * unit // n, unit), (unit // n, 6 * unit), (3 * unit // n, unit)]
    own = [jax.ShapeDtypeStruct(shape, BF16) for shape in shapes]
    whole = [jax.ShapeDtypeStruct(grad.shape, BF16) for grad in grads]
    in_vmem = pl.BlockSpec(memory_space=pltpu.VMEM)
    results = pl.pallas_call(
        functools.partial(update_kernel, n, unit),
        out_shape=own + own + whole + [jax.ShapeDtypeStruct(gains.shape, F32)],
        in_specs=[ANY] * 11 + [in_vmem],
        out_specs=[ANY] * 12 + [in_vmem],
        scratch_shapes=[
            vmem((pool_rows, unit), BF16),
            vmem((3 * unit, unit), F32),
            vmem((unit, unit // 2), F32),
            vmem((8, unit), F32),
            vmem(gains.shape, F32),
            vmem(gains.shape, F32),
            vmem(gains.shape, F32),
            vmem((n,) + gains.shape, F32),
            dma((4 * n,)),
            dma((4 * n,)),
            dma((TILE_SLOTS,)),
            dma((2 * n,)),
            dma((2, 2 * n)),
            dma((16 * top,)),
            dma((16 * top,)),
            dma((2,)),
            dma((2,)),
            dma((4,)),
            dma((4,)),
            dma((4, 3)),
            dma((4, 3)),
            dma((7,)),
            dma((n,)),
            dma,
            dma((n,)),
            dma((7,)),
            dma((7, 2)),
            dma((7, 2)),
            dma((3 + 2 * top,)),
            dma((3 + 2 * top,)),
        ],
        compiler_params=pltpu.CompilerParams(
            collective_id=1, has_side_effects=True, vmem_limit_bytes=56 * 2**20
        ),
    )(*grads, *moments, gains)
    return results[:4], results[4:8], results[12]


def apply_kernel(unit, *refs):
    weights, moments, sums, orths = refs[:7], refs[7:14], refs[14:18], refs[18:22]
    new_weights, new_moments = refs[22:29], refs[29:36]
    weight, moment, grad, orth, weight_out, moment_out, load_sem, store_sem = refs[36:]
    slots, base = weight.shape[0], weight.shape[1]
    arrays = ((QKV, 0), (QKV, 2), (QKV, 3), (OUT, 0), (GU, 0), (GU, 3), (DOWN, 0))
    tiles = []
    for matrix, (array, first) in enumerate(arrays):
        for row in range(weights[matrix].shape[0] // base):
            for column in range(weights[matrix].shape[1] // unit):
                tiles.append((matrix, array, row * base, column * unit, (first + column) * unit))

    def loads(t):
        matrix, array, row, column, array_column = tiles[t]
        here = (pl.ds(row, base), pl.ds(column, unit))
        there = (pl.ds(row, base), pl.ds(array_column, unit))
        slot = t % slots
        return [
            pltpu.make_async_copy(source, target.at[slot], load_sem.at[slot, k])
            for k, (source, target) in enumerate(
                (
                    (weights[matrix].at[here], weight), (moments[matrix].at[here], moment),
                    (sums[array].at[there], grad), (orths[array].at[there], orth),
                )
            )
        ]

    def stores(t):
        matrix, _, row, column, _ = tiles[t]
        here = (pl.ds(row, base), pl.ds(column, unit))
        slot = t % slots
        return [
            pltpu.make_async_copy(weight_out.at[slot], new_weights[matrix].at[here], store_sem.at[slot, 0]),
            pltpu.make_async_copy(moment_out.at[slot], new_moments[matrix].at[here], store_sem.at[slot, 1]),
        ]

    for t in range(slots - 1):
        for copy in loads(t):
            copy.start()
    few = 16
    for t in range(len(tiles)):
        slot = t % slots
        if t + slots - 1 < len(tiles):
            for copy in loads(t + slots - 1):
                copy.start()
        for copy in loads(t):
            copy.wait()
        if t >= slots:
            for copy in stores(t - slots):
                copy.wait()

        def act(k, carry):
            rows = pl.ds(pl.multiple_of(k * few, few), few)
            weight_out[slot, rows, :] = weight[slot, rows, :] * (
                1.0 - LEARN_RATE * WEIGHT_DECAY
            ) - LEARN_RATE * orth[slot, rows, :].astype(F32)
            moment_out[slot, rows, :] = MOMENTUM * moment[slot, rows, :] + grad[
                slot, rows, :
            ].astype(F32)
            return carry

        lax.fori_loop(0, base // few, act, 0)
        for copy in stores(t):
            copy.start()
    for t in range(len(tiles) - slots, len(tiles)):
        for copy in stores(t):
            copy.wait()


def apply_all(weights, moments, sums, orths, n, unit):
    slots, base = 4, unit // n
    dma = pltpu.SemaphoreType.DMA
    vmem = pltpu.VMEM
    results = pl.pallas_call(
        functools.partial(apply_kernel, unit),
        out_shape=[jax.ShapeDtypeStruct(matrix.shape, F32) for matrix in weights] * 2,
        in_specs=[ANY] * 22,
        out_specs=[ANY] * 14,
        scratch_shapes=[
            vmem((slots, base, unit), F32),
            vmem((slots, base, unit), F32),
            vmem((slots, base, unit), BF16),
            vmem((slots, base, unit), BF16),
            vmem((slots, base, unit), F32),
            vmem((slots, base, unit), F32),
            dma((slots, 4)),
            dma((slots, 2)),
        ],
        compiler_params=pltpu.CompilerParams(vmem_limit_bytes=56 * 2**20),
    )(*weights, *moments, *sums, *orths)
    return results[:7], results[7:]


def body(
    layer_input,
    output_grad,
    lengths,
    attention_gain,
    feed_gain,
    query_gain,
    key_gain,
    query_weight,
    key_weight,
    value_weight,
    out_weight,
    gate_weight,
    up_weight,
    down_weight,
    query_moment,
    key_moment,
    value_moment,
    out_moment,
    gate_moment,
    up_moment,
    down_moment,
):
    owned = (
        query_weight, key_weight, value_weight, out_weight, gate_weight, up_weight, down_weight,
    )
    moments = (
        query_moment, key_moment, value_moment, out_moment, gate_moment, up_moment, down_moment,
    )
    n = lax.axis_size("own")
    unit = layer_input.shape[1]
    core = lax.axis_index("rep") % 2

    def halves(*matrices):
        parts = []
        for matrix in matrices:
            width = matrix.shape[1] // 2
            parts.append(lax.dynamic_slice_in_dim(matrix, core * width, width, 1))
        return jnp.concatenate(parts, 1).astype(BF16)

    step = unit // 2
    gate_half, up_half = halves(gate_weight), halves(up_weight)
    shards = (
        halves(query_weight, key_weight, value_weight),
        out_weight.astype(BF16),
        jnp.concatenate(
            [part[:, k * step : (k + 1) * step] for k in range(3) for part in (gate_half, up_half)], 1
        ),
        down_weight.astype(BF16),
    )
    row_count = layer_input.shape[0]
    _, positions = segments(lengths[0], row_count)
    cosine_table, sine_table = rope_tables(positions)
    starts = (jnp.arange(row_count, dtype=jnp.int32) - positions).astype(F32)
    table = jnp.concatenate(
        [
            cosine_table[:, 0], cosine_table[:, 0], -sine_table[:, 0], sine_table[:, 0],
            jnp.broadcast_to(starts[:, None], (row_count, HEAD_DIM)),
        ],
        1,
    )
    gain_rows = [gain[None, :] for gain in (attention_gain, feed_gain, query_gain, key_gain)]
    (block_output, input_grad), gain_grads, grads = layer_pass(
        layer_input, output_grad, table, gain_rows, shards, n
    )
    gains = jnp.concatenate([grad[0] for grad in gain_grads])
    gains = jnp.pad(gains, (0, 24 * 128 - gains.shape[0])).reshape(24, 128)
    reduced, orth, gain_sums = update_all(grads, moments, gains, n, unit)
    new_weights, moments_next = apply_all(owned, moments, reduced, orth, n, unit)
    gain_sums = gain_sums.reshape(-1)
    norm_grads = gain_sums[: 2 * unit].reshape(2, unit)
    head_grads = gain_sums[2 * unit : 2 * unit + 2 * HEAD_DIM].reshape(2, HEAD_DIM)
    return (block_output, input_grad, norm_grads, head_grads, *new_weights, *moments_next)


def solution(mesh):
    tokens, owned = P(("rep", "own"), None), P("own", None)
    return jax.shard_map(
        body,
        mesh=mesh,
        in_specs=(tokens,) * 3 + (P(),) * 4 + (owned,) * 14,
        out_specs=(tokens,) * 2 + (P(),) * 2 + (owned,) * 14,
        check_vma=False,
    )
```
